32 devices in a mesh: blk: 8 (over z, x), mb: 4 (over y, core).
Axes of the slice: x: 2, y: 2, z: 4, core: 2. Of those that a mesh axis runs over, the one named last changes fastest.
Arguments:
- patches: bfloat16 [8, 1024, 1024], P('mb', 'blk'), may hold values from -6 to 6
- seg_lengths: int32 [8, 8], P('mb'), may hold values from 1 to 960, as said below
- w_query: bfloat16 [1024, 1024], replicated, may hold values from -0.1875 to 0.1875
- w_key: bfloat16 [1024, 1024], replicated, may hold values from -0.1875 to 0.1875
- w_value: bfloat16 [1024, 1024], replicated, may hold values from -0.1875 to 0.1875
- w_out: bfloat16 [1024, 1024], replicated, may hold values from -2 to 2
- w_up: bfloat16 [1024, 4096], replicated, may hold values from -0.1875 to 0.1875
- w_down: bfloat16 [4096, 1024], replicated, may hold values from -0.09375 to 0.09375
- norm1_gain: float32 [1024], replicated, may hold values from 0.25 to 1.75
- norm1_bias: float32 [1024], replicated, may hold values from -1.5 to 1.5
- norm2_gain: float32 [1024], replicated, may hold values from 0.25 to 1.75
- norm2_bias: float32 [1024], replicated, may hold values from -1.5 to 1.5
- out_grad: bfloat16 [8, 1024, 1024], P('mb', 'blk'), may hold values from -6 to 6
Outputs:
- layer_out: bfloat16 [8, 1024, 1024], P('mb', 'blk')
- patches_grad: bfloat16 [8, 1024, 1024], P('mb', 'blk')
- query_weight_grad: float32 [1024, 1024], P(('blk', 'mb'))
- key_weight_grad: float32 [1024, 1024], P(('blk', 'mb'))
- value_weight_grad: float32 [1024, 1024], P(('blk', 'mb'))
- out_weight_grad: float32 [1024, 1024], P(('blk', 'mb'))
- up_weight_grad: float32 [1024, 4096], P(('blk', 'mb'))
- down_weight_grad: float32 [4096, 1024], P(('blk', 'mb'))
- norm1_gain_grad: float32 [1024], P(('blk', 'mb'))
- norm1_bias_grad: float32 [1024], P(('blk', 'mb'))
- norm2_gain_grad: float32 [1024], P(('blk', 'mb'))
- norm2_bias_grad: float32 [1024], P(('blk', 'mb'))
The draws below stay inside these ranges and needn't reach their ends.
Inputs may be any that keep to these rules, and one draw needn't show every extreme that they name: `seg_lengths`: row b lists the lengths of the 8 documents of micro-batch b, laid end to end from position 0; the positions after them, at most 128, are padding. Of the 2 rows on each index of mb, one holds a document of exactly 960 positions and no padding.
All inputs are finite; a program needn't handle non-finite values.
Results may differ from the reference program's by a relative error of at most 0.012.
Values may be sent and summed in bfloat16 or wider, within the bound.
No kernel may reach another device: no remote copies, remote signals or barrier semaphores. Data moves between devices by JAX's collectives and lax.ppermute only.
A program may use at most 256 MiB of HBM per device.

```python
import math
import jax
import jax.numpy as jnp
from jax import lax

D = 1024
H = 16
HD = 64
FF = 4096
TOK_DEV = 128
MB_LOC = 2
SEGS = 8
SEQ = 1024
MICRO = 8


def composition(key, total_len, part_count):
    cut_points = jnp.sort(jax.random.permutation(key, total_len - 1)[:part_count - 1] + 1).astype(jnp.int32)
    bounds = jnp.concatenate([jnp.zeros((1,), jnp.int32), cut_points, jnp.full((1,), total_len, jnp.int32)])
    return bounds[1:] - bounds[:-1]


def spanning_row(key):
    short_total = TOK_DEV // 2
    first_key, place_key = jax.random.split(key)
    shorts = composition(first_key, short_total, SEGS - 1)
    long_place = jax.random.randint(place_key, (), 0, SEGS)
    slot_index = jnp.arange(SEGS)
    before = shorts[jnp.clip(slot_index, 0, SEGS - 2)]
    shifted = shorts[jnp.clip(slot_index - 1, 0, SEGS - 2)]
    longest = jnp.full((SEGS,), SEQ - short_total, jnp.int32)
    return jnp.where(slot_index < long_place, before, jnp.where(slot_index == long_place, longest, shifted)).astype(jnp.int32)


def ragged_row(key):
    half_length = SEQ // 2
    key_first, key_second, key_pad = jax.random.split(key, 3)
    first_half = composition(key_first, half_length, SEGS // 2)
    padding = jax.random.randint(key_pad, (), 0, TOK_DEV + 1)
    second = composition(key_second, half_length - TOK_DEV, SEGS // 2)
    second = second.at[SEGS // 2 - 1].add(TOK_DEV - padding)
    return jnp.concatenate([first_half, second]).astype(jnp.int32)


def draw_seg_lengths(key, part):
    key = jax.random.fold_in(key, 11)
    slot_key, row_key = jax.random.split(key)
    group_total = MICRO // MB_LOC
    chosen = jax.random.randint(slot_key, (group_total,), 0, MB_LOC)
    row_index = jnp.arange(MICRO)
    spanning = row_index % MB_LOC == jnp.repeat(chosen, MB_LOC)
    row_keys = jax.random.split(row_key, MICRO)
    return jnp.where(spanning[:, None], jax.vmap(spanning_row)(row_keys), jax.vmap(ragged_row)(row_keys)).astype(jnp.int32)


def steps_of(key, shape, cuts, low, largest):
    gain = 1.0
    for dim, blocks in cuts:
        heights = jax.random.uniform(jax.random.fold_in(jax.random.fold_in(key, 6), dim), (blocks,), jnp.float32, low / len(cuts), largest / len(cuts))
        gain = gain * jnp.repeat(jnp.exp(heights), shape[dim] // blocks).reshape((-1,) + (1,) * (len(shape) - 1 - dim))
    return gain


def gaussian(stream_key, extent, width, most, cuts=(), dtype=jnp.bfloat16):
    entries = width * jax.random.normal(stream_key, extent, jnp.float32)
    if cuts:
        entries = entries * steps_of(stream_key, extent, cuts, -0.22, 0.18)
    return jnp.clip(entries, -most, most).astype(dtype)


def setup_inputs(seed: int = 0) -> dict:
    key_of = jax.random.split(jax.random.key(seed), 14)
    return {
        "patches": gaussian(key_of[0], (MICRO, SEQ, D), 1.0, 6.0, ((0, 4), (1, 8))),
        "seg_lengths": draw_seg_lengths(jax.random.fold_in(key_of[13], 71), 0),
        "w_query": gaussian(key_of[2], (D, D), D ** -0.5, 0.1875),
        "w_key": gaussian(key_of[3], (D, D), D ** -0.5, 0.1875),
        "w_value": gaussian(key_of[4], (D, D), D ** -0.5, 0.1875),
        "w_out": gaussian(key_of[5], (D, D), (D // 128) ** -0.5, 2.0),
        "w_up": gaussian(key_of[6], (D, FF), D ** -0.5, 0.1875),
        "w_down": gaussian(key_of[7], (FF, D), FF ** -0.5, 0.09375),
        "norm1_gain": jnp.clip(1.0 + 0.15 * jax.random.normal(key_of[8], (D,), jnp.float32), 0.25, 1.75),
        "norm1_bias": gaussian(key_of[9], (D,), 0.3, 1.5, (), jnp.float32),
        "norm2_gain": jnp.clip(1.0 + 0.15 * jax.random.normal(key_of[10], (D,), jnp.float32), 0.25, 1.75),
        "norm2_bias": gaussian(key_of[11], (D,), 0.3, 1.5, (), jnp.float32),
        "out_grad": gaussian(key_of[12], (MICRO, SEQ, D), 1.0, 6.0, ((0, 4), (1, 8))),
    }


@jax.custom_vjp
def low(v):
    return lax.optimization_barrier(v.astype(jnp.bfloat16)).astype(jnp.float32)

@jax.custom_vjp
def low_back(v):
    return v

def low_keep(v):
    return (low(v), None)

def low_pass(kept, grad):
    return (grad,)

def back_keep(v):
    return (v, None)

def back_low(kept, grad):
    return (low(grad),)
low.defvjp(low_keep, low_pass)
low_back.defvjp(back_keep, back_low)

def layer_norm(values, norm_gain, norm_bias):
    center = values - lax.optimization_barrier(jnp.mean(values, axis=-1, keepdims=True))
    variance = lax.optimization_barrier(jnp.mean(center * center, axis=-1, keepdims=True))
    return center * lax.rsqrt(variance + 1e-05) * norm_gain + norm_bias

def product(left_side, right_side):
    return jnp.dot(left_side, right_side, precision=lax.Precision.HIGHEST)

def segment_ids(lengths, positions):
    doc_ends = jnp.cumsum(lengths, axis=-1).astype(jnp.int32)
    return lax.optimization_barrier(jnp.sum((positions[None, :, None] >= doc_ends[:, None, :]).astype(jnp.int32), axis=-1))

def head_attention(operands, same_doc):
    query_head, key_head, value_head = operands
    scores = low_back(product(query_head, key_head.T) * (1.0 / math.sqrt(HD)))
    scores = jnp.where(same_doc, scores, -1e+30)
    row_max = lax.optimization_barrier(jnp.max(scores, axis=-1, keepdims=True))
    exponent = jnp.exp(scores - row_max)
    weights_soft = exponent / lax.optimization_barrier(jnp.sum(exponent, axis=-1, keepdims=True))
    return product(low(weights_soft), value_head)

def one_micro(inputs, segments, valid_mask, params):
    w_query, w_key, w_value, w_out, w_up, w_down, gain_one, bias_one, gain_two, bias_two = params
    norm_one = low(layer_norm(inputs, gain_one, bias_one))
    queries = low_back(low(product(norm_one, w_query)))
    keys_proj = low_back(low(product(norm_one, w_key)))
    values_proj = low_back(low(product(norm_one, w_value)))

    def split_heads(values):
        return values.reshape(SEQ, H, HD).transpose(1, 0, 2)
    same_doc = segments[:, None] == segments[None, :]
    attend = jax.checkpoint(lambda operands: head_attention(operands, same_doc))
    heads_out = lax.map(attend, (split_heads(queries), split_heads(keys_proj), split_heads(values_proj)))
    attended = low_back(low(heads_out.transpose(1, 0, 2).reshape(SEQ, D) * valid_mask[:, None]))
    mixed_rows = inputs + low_back(product(attended, w_out))
    norm_two = low(layer_norm(mixed_rows, gain_two, bias_two))
    upper_proj = low_back(product(norm_two, w_up))
    active = low(jax.nn.gelu(upper_proj, approximate=False))
    return mixed_rows + low_back(product(active, w_down))

def reference(patches, seg_lengths, w_query, w_key, w_value, w_out, w_up, w_down, norm1_gain, norm1_bias, norm2_gain, norm2_bias, out_grad):
    positions = jnp.arange(SEQ).astype(jnp.int32)
    segments = segment_ids(seg_lengths, positions)
    valid_mask = (segments < SEGS).astype(jnp.float32)

    def forward(inputs, params):

        def micro_step(operands):
            return one_micro(operands[0], operands[1], operands[2], params)
        return lax.map(micro_step, (inputs, segments, valid_mask))
    params = (w_query.astype(jnp.float32), w_key.astype(jnp.float32), w_value.astype(jnp.float32), w_out.astype(jnp.float32), w_up.astype(jnp.float32), w_down.astype(jnp.float32), norm1_gain.astype(jnp.float32), norm1_bias.astype(jnp.float32), norm2_gain.astype(jnp.float32), norm2_bias.astype(jnp.float32))
    result, pullback = jax.vjp(forward, patches.astype(jnp.float32), params)
    input_grad, param_grads = pullback(out_grad.astype(jnp.float32))
    return (result.astype(jnp.bfloat16), input_grad.astype(jnp.bfloat16), param_grads[0], param_grads[1], param_grads[2], param_grads[3], param_grads[4], param_grads[5], param_grads[6], param_grads[7], param_grads[8], param_grads[9])
```

```python
import math

import jax
import jax.numpy as jnp
from jax import lax
from jax.experimental import pallas as pl
from jax.experimental.pallas import tpu as pltpu
from jax.sharding import PartitionSpec as P

H = 16


epsilon = 1e-05
masked_score = -1e30


def layer_norm(values, norm_gain, norm_bias):
    center = values - jnp.mean(values, axis=-1, keepdims=True)
    variance = jnp.mean(center * center, axis=-1, keepdims=True)
    return center * lax.rsqrt(variance + epsilon) * norm_gain + norm_bias


def gelu_exact(values):
    return jax.nn.gelu(values, approximate=False)


def matmul(left_side, right_side):
    return jnp.dot(left_side, right_side, preferred_element_type=jnp.float32)


def contract_rows(left_side, right_side):
    return lax.dot_general(
        left_side, right_side, (((0,), (0,)), ((), ())), preferred_element_type=jnp.float32
    )


def contract_cols(left_side, right_side):
    return lax.dot_general(
        left_side, right_side, (((1,), (1,)), ((), ())), preferred_element_type=jnp.float32
    )


def segment_ids(lengths, positions):
    doc_ends = jnp.cumsum(lengths, axis=-1)
    return jnp.sum((positions[None, :, None] >= doc_ends[:, None, :]).astype(jnp.int32), axis=-1)


def masked_scores(query_piece, keys_all, query_docs, key_docs, score_scale):
    scores = contract_cols(query_piece, keys_all) * score_scale
    return jnp.where(query_docs[:, None] == key_docs[None, :], scores, masked_score)


def soft_rows(scores):
    row_max = jnp.max(scores, axis=-1, keepdims=True)
    exponent = jnp.exp(scores - row_max)
    return exponent / jnp.sum(exponent, axis=-1, keepdims=True)


def body(
    patches,
    seg_lengths,
    w_query,
    w_key,
    w_value,
    w_out,
    w_up,
    w_down,
    norm1_gain,
    norm1_bias,
    norm2_gain,
    norm2_bias,
    out_grad,
):
    micro_count, tokens, features = patches.shape
    row_count = micro_count * tokens
    blocks = lax.axis_size("blk")
    block_index = lax.axis_index("blk")
    head_count = H
    head_dim = features // head_count
    repeat = max(1, blocks // head_count)
    per_slot = max(1, head_count // blocks)
    groups = head_count // per_slot
    rows_part = tokens // repeat
    query_rows = blocks * rows_part
    seq_length = blocks * tokens
    item_count = micro_count * per_slot
    block_rows = min(512, query_rows)
    block_count = query_rows // block_rows
    slot_width = micro_count * per_slot * head_dim
    score_scale = 1.0 / math.sqrt(head_dim)
    doc_count = seg_lengths.shape[1]

    def query_layout(values):
        shaped = values.reshape(micro_count, repeat, rows_part, groups, per_slot * head_dim)
        return shaped.transpose(3, 1, 2, 0, 4).reshape(blocks, rows_part, slot_width)

    def key_layout(values):
        shaped = values.reshape(micro_count, tokens, groups, per_slot * head_dim).transpose(
            2, 1, 0, 3
        )
        shaped = jnp.broadcast_to(
            shaped[:, None], (groups, repeat, tokens, micro_count, per_slot * head_dim)
        )
        return shaped.reshape(blocks, tokens, slot_width)

    def token_layout(values):
        shaped = values.reshape(groups, repeat, rows_part, micro_count, per_slot * head_dim)
        return shaped.transpose(3, 1, 2, 0, 4).reshape(row_count, features)

    def key_sum(values):
        shaped = values.reshape(groups, repeat, tokens, micro_count, per_slot * head_dim).sum(
            axis=1
        )
        return shaped.transpose(2, 1, 0, 3).reshape(row_count, features)

    def to_items(received):
        row_total = received.shape[1]
        shaped = received.reshape(row_total, micro_count, per_slot, head_dim).transpose(1, 2, 0, 3)
        return shaped.reshape(item_count, row_total, head_dim)

    def from_items(values):
        row_total = values.shape[1]
        shaped = values.reshape(micro_count, per_slot, row_total, head_dim).transpose(2, 0, 1, 3)
        return shaped.reshape(1, row_total, slot_width)

    row_ids = jnp.arange(query_rows)
    query_pos = (
        row_ids // rows_part * tokens + block_index % repeat * rows_part + row_ids % rows_part
    )
    query_docs = jnp.repeat(segment_ids(seg_lengths, query_pos), per_slot, axis=0)
    key_docs = jnp.repeat(segment_ids(seg_lengths, jnp.arange(seq_length)), per_slot, axis=0)
    query_valid = (query_docs < doc_count).astype(jnp.float32)
    local_pos = block_index * tokens + jnp.arange(tokens)
    row_valid = (
        (segment_ids(seg_lengths, local_pos) < doc_count).astype(jnp.float32).reshape(row_count, 1)
    )

    def forward_item(operands):
        queries_item, keys_item, values_item, docs_item, key_docs_item = operands

        def forward_one_block(block_operands):
            query_piece, docs_piece = block_operands
            weights_soft = soft_rows(
                masked_scores(query_piece, keys_item, docs_piece, key_docs_item, score_scale)
            )
            return matmul(weights_soft.astype(jnp.bfloat16), values_item)

        outputs = lax.map(
            forward_one_block,
            (
                queries_item.reshape(block_count, block_rows, head_dim),
                docs_item.reshape(block_count, block_rows),
            ),
        )
        return outputs.reshape(query_rows, head_dim)

    def backward_item(operands):
        queries_item, keys_item, values_item, grads_item, docs_item, key_docs_item = operands

        def backward_one_block(totals, block_operands):
            key_total, value_total = totals
            query_piece, grad_piece, docs_piece = block_operands
            weights_soft = soft_rows(
                masked_scores(query_piece, keys_item, docs_piece, key_docs_item, score_scale)
            )
            weights_low = weights_soft.astype(jnp.bfloat16)
            weight_grads = contract_cols(grad_piece, values_item)
            row_inner = jnp.sum(weights_soft * weight_grads, axis=-1, keepdims=True)
            score_grads = (weights_soft * (weight_grads - row_inner)).astype(jnp.bfloat16)
            query_grad = matmul(score_grads, keys_item) * score_scale
            key_total = key_total + contract_rows(score_grads, query_piece) * score_scale
            value_total = value_total + contract_rows(weights_low, grad_piece)
            return ((key_total, value_total), query_grad)

        zero_block = jnp.zeros((seq_length, head_dim), jnp.float32)
        totals, query_grads = lax.scan(
            backward_one_block,
            (zero_block, zero_block),
            (
                queries_item.reshape(block_count, block_rows, head_dim),
                grads_item.reshape(block_count, block_rows, head_dim),
                docs_item.reshape(block_count, block_rows),
            ),
        )
        return (query_grads.reshape(query_rows, head_dim), totals[0], totals[1])

    inputs = patches.astype(jnp.float32).reshape(row_count, features)
    norm_one_full, norm_one_pull = jax.vjp(layer_norm, inputs, norm1_gain, norm1_bias)
    norm_one = norm_one_full.astype(jnp.bfloat16)
    queries = matmul(norm_one, w_query).astype(jnp.bfloat16)
    keys_proj = matmul(norm_one, w_key).astype(jnp.bfloat16)
    values_proj = matmul(norm_one, w_value).astype(jnp.bfloat16)
    query_send = query_layout(queries)
    key_send = key_layout(keys_proj)
    value_send = key_layout(values_proj)
    query_heads, key_heads, value_heads = (
        lax.all_to_all(query_send, "blk", split_axis=0, concat_axis=1, tiled=True),
        lax.all_to_all(key_send, "blk", split_axis=0, concat_axis=1, tiled=True),
        lax.all_to_all(value_send, "blk", split_axis=0, concat_axis=1, tiled=True),
    )
    query_items = to_items(query_heads)
    key_items = to_items(key_heads)
    value_items = to_items(value_heads)
    attended_items = lax.map(
        forward_item, (query_items, key_items, value_items, query_docs, key_docs)
    )
    attended_items = (attended_items * query_valid[:, :, None]).astype(jnp.bfloat16)
    attended = token_layout(
        lax.all_to_all(from_items(attended_items), "blk", split_axis=1, concat_axis=0, tiled=True)
    )
    mixed_rows = inputs + matmul(attended, w_out)
    norm_two_full, norm_two_pull = jax.vjp(layer_norm, mixed_rows, norm2_gain, norm2_bias)
    norm_two = norm_two_full.astype(jnp.bfloat16)
    upper_proj = matmul(norm_two, w_up)
    active_full, gelu_pull = jax.vjp(gelu_exact, upper_proj)
    active = active_full.astype(jnp.bfloat16)
    result = mixed_rows + matmul(active, w_down)
    layer_out = result.astype(jnp.bfloat16).reshape(micro_count, tokens, features)
    dout_low = out_grad.reshape(row_count, features)
    down_grad = contract_rows(active, dout_low)
    active_grad = contract_cols(dout_low, w_down)
    upper_grad = gelu_pull(active_grad)[0].astype(jnp.bfloat16)
    up_grad = contract_rows(norm_two, upper_grad)
    norm_two_grad = contract_cols(upper_grad, w_up)
    mixed_part, gain_two_grad, bias_two_grad = norm_two_pull(norm_two_grad)
    mixed_grad = dout_low.astype(jnp.float32) + mixed_part
    mixed_low = mixed_grad.astype(jnp.bfloat16)
    out_proj_grad = contract_rows(attended, mixed_low)
    attended_grad = (contract_cols(mixed_low, w_out) * row_valid).astype(jnp.bfloat16)
    grad_send = query_layout(attended_grad)
    query_again, key_again, value_again, grad_heads = (
        lax.all_to_all(query_send, "blk", split_axis=0, concat_axis=1, tiled=True),
        lax.all_to_all(key_send, "blk", split_axis=0, concat_axis=1, tiled=True),
        lax.all_to_all(value_send, "blk", split_axis=0, concat_axis=1, tiled=True),
        lax.all_to_all(grad_send, "blk", split_axis=0, concat_axis=1, tiled=True),
    )
    back_queries = to_items(query_again)
    back_keys = to_items(key_again)
    back_values = to_items(value_again)
    grad_items = to_items(grad_heads)
    query_grad_items, key_grad_items, value_grad_items = lax.map(
        backward_item, (back_queries, back_keys, back_values, grad_items, query_docs, key_docs)
    )
    query_back, key_back, value_back = (
        lax.all_to_all(
            from_items(query_grad_items).astype(jnp.bfloat16),
            "blk",
            split_axis=1,
            concat_axis=0,
            tiled=True,
        ).astype(jnp.float32),
        lax.all_to_all(
            from_items(key_grad_items).astype(jnp.bfloat16),
            "blk",
            split_axis=1,
            concat_axis=0,
            tiled=True,
        ).astype(jnp.float32),
        lax.all_to_all(
            from_items(value_grad_items).astype(jnp.bfloat16),
            "blk",
            split_axis=1,
            concat_axis=0,
            tiled=True,
        ).astype(jnp.float32),
    )
    query_grad = token_layout(query_back).astype(jnp.bfloat16)
    key_grad = key_sum(key_back).astype(jnp.bfloat16)
    value_grad = key_sum(value_back).astype(jnp.bfloat16)
    query_proj_grad = contract_rows(norm_one, query_grad)
    key_proj_grad = contract_rows(norm_one, key_grad)
    value_proj_grad = contract_rows(norm_one, value_grad)
    norm_one_grad = (
        contract_cols(query_grad, w_query)
        + contract_cols(key_grad, w_key)
        + contract_cols(value_grad, w_value)
    )
    input_part, gain_one_grad, bias_one_grad = norm_one_pull(norm_one_grad)
    patches_grad = (
        (mixed_grad + input_part).astype(jnp.bfloat16).reshape(micro_count, tokens, features)
    )
    gradients = (
        query_proj_grad,
        key_proj_grad,
        value_proj_grad,
        out_proj_grad,
        up_grad,
        down_grad,
        gain_one_grad,
        bias_one_grad,
        gain_two_grad,
        bias_two_grad,
    )
    summed = (
        lax.psum_scatter(gradients[0], ("blk", "mb"), scatter_dimension=0, tiled=True),
        lax.psum_scatter(gradients[1], ("blk", "mb"), scatter_dimension=0, tiled=True),
        lax.psum_scatter(gradients[2], ("blk", "mb"), scatter_dimension=0, tiled=True),
        lax.psum_scatter(gradients[3], ("blk", "mb"), scatter_dimension=0, tiled=True),
        lax.psum_scatter(gradients[4], ("blk", "mb"), scatter_dimension=0, tiled=True),
        lax.psum_scatter(gradients[5], ("blk", "mb"), scatter_dimension=0, tiled=True),
        lax.psum_scatter(gradients[6], ("blk", "mb"), scatter_dimension=0, tiled=True),
        lax.psum_scatter(gradients[7], ("blk", "mb"), scatter_dimension=0, tiled=True),
        lax.psum_scatter(gradients[8], ("blk", "mb"), scatter_dimension=0, tiled=True),
        lax.psum_scatter(gradients[9], ("blk", "mb"), scatter_dimension=0, tiled=True),
    )
    return (
        layer_out,
        patches_grad,
        summed[0],
        summed[1],
        summed[2],
        summed[3],
        summed[4],
        summed[5],
        summed[6],
        summed[7],
        summed[8],
        summed[9],
    )


def _normalize(values):
    center = values - jnp.mean(values, axis=-1, keepdims=True)
    variance = jnp.mean(center * center, axis=-1, keepdims=True)
    inverse = lax.rsqrt(variance + epsilon)
    return center * inverse, inverse


def _normalize_back(grads, gain, unit, inverse):
    scaled = grads * gain
    mean_scaled = jnp.mean(scaled, axis=-1, keepdims=True)
    mean_product = jnp.mean(scaled * unit, axis=-1, keepdims=True)
    return (scaled - mean_scaled - unit * mean_product) * inverse


def _doc_ids(lengths_ref, micro, doc_count, positions):
    end = jnp.int32(0)
    ids = jnp.zeros_like(positions)
    for doc in range(doc_count):
        end = end + lengths_ref[micro, doc]
        ids = ids + (positions >= end).astype(jnp.int32)
    return ids


def _params(mib):
    return pltpu.CompilerParams(vmem_limit_bytes=mib << 20)


def _cost(flops, moved, exps=0):
    return pl.CostEstimate(flops=int(flops), bytes_accessed=int(moved), transcendentals=int(exps))


def project_call(rows, gain, bias, w_query, w_key, w_value, blocks):
    row_count, features = rows.shape
    slot = features // blocks
    per_step = max(1, min(blocks, 256 // slot))
    wide = slot * per_step

    def kernel(rows_ref, gain_ref, bias_ref, wq_ref, wk_ref, wv_ref, send_ref, norm_ref):
        @pl.when(pl.program_id(0) == 0)
        def _():
            unit, _unused = _normalize(rows_ref[...].astype(jnp.float32))
            norm_ref[...] = (unit * gain_ref[...] + bias_ref[...]).astype(jnp.bfloat16)

        for part, weight_ref in enumerate((wq_ref, wk_ref, wv_ref)):
            made = matmul(norm_ref[...], weight_ref[...]).astype(jnp.bfloat16)
            for piece in range(per_step):
                send_ref[piece, :, part * slot : (part + 1) * slot] = made[
                    :, piece * slot : (piece + 1) * slot
                ]

    whole = pl.BlockSpec((row_count, features), lambda i: (0, 0))
    vector = pl.BlockSpec((1, features), lambda i: (0, 0))
    columns = pl.BlockSpec((features, wide), lambda i: (0, i))
    return pl.pallas_call(
        kernel,
        grid=(blocks // per_step,),
        in_specs=[whole, vector, vector, columns, columns, columns],
        out_specs=[pl.BlockSpec((per_step, row_count, 3 * slot), lambda i: (i, 0, 0)), whole],
        out_shape=[
            jax.ShapeDtypeStruct((blocks, row_count, 3 * slot), jnp.bfloat16),
            jax.ShapeDtypeStruct((row_count, features), jnp.bfloat16),
        ],
        compiler_params=_params(40),
        cost_estimate=_cost(6 * row_count * features * features, 6 * features * features + 4 * row_count * features),
        name="project",
    )(rows, gain, bias, w_query, w_key, w_value)


def _head_masks(slot, head_dim, dtype):
    lanes = lax.broadcasted_iota(jnp.int32, (1, slot), 1)
    return [(lanes // head_dim == head).astype(dtype) for head in range(slot // head_dim)]


def attend_call(received, lengths, head_dim):
    blocks, micro_count, tokens, width = received.shape
    slot = width // 3
    seq = blocks * tokens
    doc_count = lengths.shape[1]
    step_blocks = max(1, min(blocks, 256 // tokens))
    rows = step_blocks * tokens
    scale = 1.0 / math.sqrt(head_dim)

    def kernel(lengths_ref, data_ref, out_ref):
        micro = pl.program_id(0)
        step = pl.program_id(1)
        key_docs = _doc_ids(lengths_ref, micro, doc_count, lax.broadcasted_iota(jnp.int32, (1, seq), 1))
        row_docs = _doc_ids(
            lengths_ref, micro, doc_count, lax.broadcasted_iota(jnp.int32, (rows, 1), 0) + step * rows
        )
        same = row_docs == key_docs
        queries = data_ref[pl.ds(step * step_blocks, step_blocks), 0, :, 0:slot].reshape(rows, slot)
        keys = data_ref[:, 0, :, slot : 2 * slot].reshape(seq, slot)
        values = data_ref[:, 0, :, 2 * slot : 3 * slot].reshape(seq, slot)
        queries = queries * scale
        total = jnp.zeros((rows, slot), jnp.float32)
        for mask, mask_wide in zip(
            _head_masks(slot, head_dim, jnp.bfloat16), _head_masks(slot, head_dim, jnp.float32)
        ):
            scores = jnp.where(same, contract_cols(queries * mask, keys), masked_score)
            exponent = jnp.exp(scores - jnp.max(scores, axis=-1, keepdims=True))
            share = 1.0 / jnp.sum(exponent, axis=-1, keepdims=True)
            total = total + matmul(exponent.astype(jnp.bfloat16), values) * (share * mask_wide)
        total = jnp.where(row_docs < doc_count, total, 0.0)
        out_ref[...] = total.astype(jnp.bfloat16).reshape(step_blocks, 1, tokens, slot)

    items = micro_count * slot // head_dim
    return pl.pallas_call(
        kernel,
        grid=(micro_count, blocks // step_blocks),
        in_specs=[
            pl.BlockSpec(memory_space=pltpu.SMEM),
            pl.BlockSpec((blocks, 1, tokens, width), lambda m, s: (0, m, 0, 0)),
        ],
        out_specs=pl.BlockSpec((step_blocks, 1, tokens, slot), lambda m, s: (s, m, 0, 0)),
        out_shape=jax.ShapeDtypeStruct((blocks, micro_count, tokens, slot), jnp.bfloat16),
        compiler_params=_params(40),
        cost_estimate=_cost(16 * items * seq * seq * head_dim, 8 * seq * micro_count * slot, items * seq * seq),
        name="attend",
    )(lengths, received)


def attend_back_call(received, grads, lengths, head_dim):
    blocks, micro_count, tokens, width = received.shape
    slot = width // 3
    seq = blocks * tokens
    doc_count = lengths.shape[1]
    step_blocks = max(1, min(blocks, 256 // tokens))
    rows = step_blocks * tokens
    steps = blocks // step_blocks
    scale = 1.0 / math.sqrt(head_dim)

    def kernel(lengths_ref, data_ref, grads_ref, out_ref, key_total, value_total):
        micro = pl.program_id(0)
        step = pl.program_id(1)

        @pl.when(step == 0)
        def _():
            key_total[...] = jnp.zeros_like(key_total)
            value_total[...] = jnp.zeros_like(value_total)

        key_docs = _doc_ids(lengths_ref, micro, doc_count, lax.broadcasted_iota(jnp.int32, (seq, 1), 0))
        row_docs = _doc_ids(
            lengths_ref, micro, doc_count, lax.broadcasted_iota(jnp.int32, (1, rows), 1) + step * rows
        )
        column_docs = _doc_ids(
            lengths_ref, micro, doc_count, lax.broadcasted_iota(jnp.int32, (rows, 1), 0) + step * rows
        )
        same = row_docs == key_docs
        queries = data_ref[pl.ds(step * step_blocks, step_blocks), 0, :, 0:slot].reshape(rows, slot)
        keys = data_ref[:, 0, :, slot : 2 * slot].reshape(seq, slot)
        values = data_ref[:, 0, :, 2 * slot : 3 * slot].reshape(seq, slot)
        queries = queries * scale
        out_grads = grads_ref[...].reshape(rows, slot)
        out_grads = out_grads * (column_docs < doc_count).astype(jnp.float32).astype(jnp.bfloat16)
        query_total = jnp.zeros((rows, slot), jnp.float32)
        for mask, mask_wide in zip(
            _head_masks(slot, head_dim, jnp.bfloat16), _head_masks(slot, head_dim, jnp.float32)
        ):
            queries_head = queries * mask
            grads_head = out_grads * mask
            scores = jnp.where(same, contract_cols(keys, queries_head), masked_score)
            exponent = jnp.exp(scores - jnp.max(scores, axis=0, keepdims=True))
            probs = exponent * (1.0 / jnp.sum(exponent, axis=0, keepdims=True))
            prob_grads = contract_cols(values, grads_head)
            inner = jnp.sum(probs * prob_grads, axis=0, keepdims=True)
            score_grads = (probs * (prob_grads - inner)).astype(jnp.bfloat16)
            value_total[...] += matmul(probs.astype(jnp.bfloat16), grads_head)
            key_total[...] += matmul(score_grads, queries_head)
            query_total = query_total + contract_rows(score_grads, keys) * mask_wide
        out_ref[pl.ds(step * step_blocks, step_blocks), 0, :, 0:slot] = (
            (query_total * scale).astype(jnp.bfloat16).reshape(step_blocks, tokens, slot)
        )

        @pl.when(step == steps - 1)
        def _():
            out_ref[:, 0, :, slot : 2 * slot] = (
                key_total[...].astype(jnp.bfloat16).reshape(blocks, tokens, slot)
            )
            out_ref[:, 0, :, 2 * slot : 3 * slot] = (
                value_total[...].astype(jnp.bfloat16).reshape(blocks, tokens, slot)
            )

    items = micro_count * slot // head_dim
    return pl.pallas_call(
        kernel,
        grid=(micro_count, steps),
        in_specs=[
            pl.BlockSpec(memory_space=pltpu.SMEM),
            pl.BlockSpec((blocks, 1, tokens, width), lambda m, s: (0, m, 0, 0)),
            pl.BlockSpec((step_blocks, 1, tokens, slot), lambda m, s: (s, m, 0, 0)),
        ],
        out_specs=pl.BlockSpec((blocks, 1, tokens, width), lambda m, s: (0, m, 0, 0)),
        out_shape=jax.ShapeDtypeStruct(received.shape, jnp.bfloat16),
        scratch_shapes=[pltpu.VMEM((seq, slot), jnp.float32), pltpu.VMEM((seq, slot), jnp.float32)],
        compiler_params=_params(48),
        cost_estimate=_cost(40 * items * seq * seq * head_dim, 14 * seq * micro_count * slot, items * seq * seq),
        name="attend_back",
    )(lengths, received, grads)


def middle_call(attended, rows, out_grad, gain, bias, w_out, w_up, w_down):
    blocks, row_count, slot = attended.shape
    features = rows.shape[1]
    hidden = w_up.shape[1]
    wide = min(512, hidden)
    steps = hidden // wide
    acts_width = 2 * hidden + 3 * features

    def kernel(
        att_ref, rows_ref, grad_ref, gain_ref, bias_ref, wo_ref, wu_ref, wd_ref,
        out_ref, acts_ref, mixed_grad_ref, back_ref, sums_ref,
        mixed, inverse, total, grad_total,
    ):
        step = pl.program_id(0)
        norm_at, att_at, low_at = 2 * hidden, 2 * hidden + features, 2 * hidden + 2 * features

        @pl.when(step == 0)
        def _():
            for block in range(blocks):
                acts_ref[:, att_at + block * slot : att_at + (block + 1) * slot] = att_ref[block]
            value = rows_ref[...].astype(jnp.float32) + matmul(
                acts_ref[:, att_at : att_at + features], wo_ref[...]
            )
            mixed[...] = value
            unit, scale = _normalize(value)
            inverse[...] = scale
            acts_ref[:, norm_at : norm_at + features] = (unit * gain_ref[...] + bias_ref[...]).astype(jnp.bfloat16)
            total[...] = jnp.zeros_like(total)
            grad_total[...] = jnp.zeros_like(grad_total)

        upper = matmul(acts_ref[:, norm_at : norm_at + features], wu_ref[...])
        active_grad = contract_cols(grad_ref[...], wd_ref[...])
        half = (1.0 + lax.erf(upper * (1.0 / math.sqrt(2.0)))) * 0.5
        active = (upper * half).astype(jnp.bfloat16)
        slope = half + upper * jnp.exp(upper * upper * -0.5) * (1.0 / math.sqrt(2.0 * math.pi))
        upper_grad = (active_grad * slope).astype(jnp.bfloat16)
        acts_ref[:, pl.ds(pl.multiple_of(step * wide, wide), wide)] = active
        acts_ref[:, pl.ds(pl.multiple_of(hidden + step * wide, wide), wide)] = upper_grad
        total[...] += matmul(active, wd_ref[...])
        grad_total[...] += contract_cols(upper_grad, wu_ref[...])

        @pl.when(step == steps - 1)
        def _():
            out_ref[...] = (mixed[...] + total[...]).astype(jnp.bfloat16)
            unit = (mixed[...] - jnp.mean(mixed[...], axis=-1, keepdims=True)) * inverse[...]
            grads = grad_total[...]
            sums_ref[0:1, :] = jnp.sum(grads * unit, axis=0, keepdims=True)
            sums_ref[1:2, :] = jnp.sum(grads, axis=0, keepdims=True)
            mixed_grad = grad_ref[...].astype(jnp.float32) + _normalize_back(grads, gain_ref[...], unit, inverse[...])
            mixed_grad_ref[...] = mixed_grad
            low = mixed_grad.astype(jnp.bfloat16)
            acts_ref[:, low_at : low_at + features] = low
            back = contract_cols(low, wo_ref[...]).astype(jnp.bfloat16)
            for block in range(blocks):
                back_ref[block] = back[:, block * slot : (block + 1) * slot]

    def fixed(*shape):
        return pl.BlockSpec(shape, lambda i: (0,) * len(shape))

    return pl.pallas_call(
        kernel,
        grid=(steps,),
        in_specs=[
            fixed(blocks, row_count, slot),
            fixed(row_count, features),
            fixed(row_count, features),
            fixed(1, features),
            fixed(1, features),
            fixed(features, features),
            pl.BlockSpec((features, wide), lambda i: (0, i)),
            pl.BlockSpec((wide, features), lambda i: (i, 0)),
        ],
        out_specs=[
            fixed(row_count, features),
            fixed(row_count, acts_width),
            fixed(row_count, features),
            fixed(blocks, row_count, slot),
            fixed(2, features),
        ],
        out_shape=[
            jax.ShapeDtypeStruct((row_count, features), jnp.bfloat16),
            jax.ShapeDtypeStruct((row_count, acts_width), jnp.bfloat16),
            jax.ShapeDtypeStruct((row_count, features), jnp.float32),
            jax.ShapeDtypeStruct((blocks, row_count, slot), jnp.bfloat16),
            jax.ShapeDtypeStruct((2, features), jnp.float32),
        ],
        scratch_shapes=[
            pltpu.VMEM((row_count, features), jnp.float32),
            pltpu.VMEM((row_count, 1), jnp.float32),
            pltpu.VMEM((row_count, features), jnp.float32),
            pltpu.VMEM((row_count, features), jnp.float32),
        ],
        compiler_params=_params(56),
        cost_estimate=_cost(
            8 * row_count * features * hidden + 4 * row_count * features * features,
            4 * features * hidden + 2 * features * features + 2 * row_count * acts_width,
            2 * row_count * hidden,
        ),
        name="middle",
    )(attended, rows, out_grad, gain, bias, w_out, w_up, w_down)


def finish_call(received, rows, mixed_grad, gain, sums, w_query, w_key, w_value):
    blocks, row_count, width = received.shape
    slot = width // 3
    features = rows.shape[1]
    per_step = max(1, min(blocks, 256 // slot))
    wide = slot * per_step
    steps = blocks // per_step

    def kernel(data_ref, rows_ref, mixed_ref, gain_ref, more_ref, wq_ref, wk_ref, wv_ref, out_ref, acts_ref, total):
        step = pl.program_id(0)

        @pl.when(step == 0)
        def _():
            total[...] = jnp.zeros_like(total)

        for part, weight_ref in enumerate((wq_ref, wk_ref, wv_ref)):
            for piece in range(per_step):
                at = pl.multiple_of(part * features + step * wide + piece * slot, 128)
                acts_ref[0:row_count, pl.ds(at, slot)] = data_ref[piece, :, part * slot : (part + 1) * slot]
            at = pl.multiple_of(part * features + step * wide, 128)
            total[...] += contract_cols(acts_ref[0:row_count, pl.ds(at, wide)], weight_ref[...])

        @pl.when(step == steps - 1)
        def _():
            unit, inverse = _normalize(rows_ref[...].astype(jnp.float32))
            grads = total[...]
            sums = jnp.concatenate(
                [
                    jnp.sum(grads * unit, axis=0, keepdims=True),
                    jnp.sum(grads, axis=0, keepdims=True),
                    more_ref[...],
                    jnp.zeros((12, features), jnp.float32),
                ],
                axis=0,
            )
            acts_ref[row_count:, 0:features] = sums.astype(jnp.bfloat16)
            out_ref[...] = (
                mixed_ref[...] + _normalize_back(grads, gain_ref[...], unit, inverse)
            ).astype(jnp.bfloat16)

    def fixed(*shape):
        return pl.BlockSpec(shape, lambda i: (0,) * len(shape))

    columns = pl.BlockSpec((features, wide), lambda i: (0, i))
    return pl.pallas_call(
        kernel,
        grid=(steps,),
        in_specs=[
            pl.BlockSpec((per_step, row_count, width), lambda i: (i, 0, 0)),
            fixed(row_count, features),
            fixed(row_count, features),
            fixed(1, features),
            fixed(2, features),
            columns,
            columns,
            columns,
        ],
        out_specs=[fixed(row_count, features), fixed(row_count + 16, 3 * features)],
        out_shape=[
            jax.ShapeDtypeStruct((row_count, features), jnp.bfloat16),
            jax.ShapeDtypeStruct((row_count + 16, 3 * features), jnp.bfloat16),
        ],
        scratch_shapes=[pltpu.VMEM((row_count, features), jnp.float32)],
        compiler_params=_params(48),
        cost_estimate=_cost(6 * row_count * features * features, 6 * features * features + 14 * row_count * features),
        name="finish",
    )(received, rows, mixed_grad, gain, sums, w_query, w_key, w_value)


def _bits(count):
    return [1 << place for place in range(count.bit_length() - 1)]


def _ordered(bits):
    places = [0]
    for bit in bits:
        places = [at + step for at in places for step in (0, bit)]
    return places


def _paired(values, axis, bit):
    count = lax.axis_size(axis)
    return lax.ppermute(values, axis, [(i, i ^ bit) for i in range(count)])


def _bit_of(axis, bit):
    return (lax.axis_index(axis) // bit) % 2


def grad_rows_call(chosen, own, peer, picks, features, wide, orders, blocks, shares, out_dtype, extra=False):
    (own_left, own_right), (peer_left, peer_right) = own, peer
    row_count = own_left.shape[0]
    group = features // (blocks * shares)
    kept = len(orders) * group
    steps = [width // wide for _, _, width in picks]
    starts = [sum(steps[:part]) for part in range(len(picks))]
    columns = sum(width for _, _, width in picks)
    right_rows = own_right.shape[0]

    def choose(step, per_part):
        value = per_part[0](step)
        for part in range(1, len(picks)):
            value = jnp.where(step >= starts[part], per_part[part](step), value)
        return value

    def kernel(chosen_ref, ol_ref, or_ref, pl_ref, pr_ref, out_ref, turned, left, *columns_ref):
        step = pl.program_id(0)
        for start in starts:

            @pl.when(step == start)
            def _():
                for side, ref in enumerate((ol_ref, pl_ref)):
                    turned[:, :, :, side * row_count : (side + 1) * row_count] = ref[...].T.reshape(
                        blocks, shares, group, row_count
                    )
                for place, (block, share) in enumerate(orders):
                    left[place * group : (place + 1) * group, :] = turned[
                        block + chosen_ref[0], share + chosen_ref[1]
                    ]

        made = matmul(left[:, 0:row_count], or_ref[0:row_count, :]) + matmul(
            left[:, row_count:], pr_ref[0:row_count, :]
        )
        if not extra:
            out_ref[...] = made.astype(out_dtype)
        else:
            out_ref[:, 0:wide] = made.astype(out_dtype)
            sums = or_ref[row_count:, 0:features].astype(jnp.float32) + pr_ref[row_count:, 0:features].astype(jnp.float32)
            sums = jnp.concatenate([sums, jnp.zeros((128 - sums.shape[0], features), jnp.float32)], axis=0)
            columns_ref[0][...] = sums.T.reshape(blocks, shares, group, 128)
            for place, (block, share) in enumerate(orders):
                out_ref[place * group : (place + 1) * group, wide:] = columns_ref[0][
                    block + chosen_ref[0], share + chosen_ref[1]
                ].astype(out_dtype)

    left_at = [lambda step, at=at // features: at for at, _, _ in picks]
    right_at = [lambda step, at=at // wide, start=start: at + step - start for (_, at, _), start in zip(picks, starts)]
    left_spec = pl.BlockSpec((row_count, features), lambda i, chosen: (0, choose(i, left_at)))
    right_spec = pl.BlockSpec((right_rows, wide), lambda i, chosen: (0, choose(i, right_at)))
    more = 128 if extra else 0
    return pl.pallas_call(
        kernel,
        grid_spec=pltpu.PrefetchScalarGridSpec(
            num_scalar_prefetch=1,
            grid=(sum(steps),),
            in_specs=[left_spec, right_spec, left_spec, right_spec],
            out_specs=pl.BlockSpec((kept, wide + more), lambda i, chosen: (0, i)),
            scratch_shapes=[
                pltpu.VMEM((blocks, shares, group, 2 * row_count), jnp.bfloat16),
                pltpu.VMEM((kept, 2 * row_count), jnp.bfloat16),
            ]
            + [pltpu.VMEM((blocks, shares, group, 128), jnp.float32)] * bool(extra),
        ),
        out_shape=jax.ShapeDtypeStruct((kept, columns + more), out_dtype),
        compiler_params=_params(40),
        cost_estimate=_cost(4 * row_count * kept * columns, 4 * row_count * (columns + features) + 4 * kept * columns),
        name="grad_rows",
    )(chosen, own_left, own_right, peer_left, peer_right)


def grad_down_call(chosen, own_acts, peer_acts, own_right, peer_right, orders, shares, rows_each, out_dtype):
    row_count, features = own_right.shape
    span = len(orders)
    strides = []
    for place in range(span.bit_length() - 1):
        strides.append(orders[1 << place] - orders[0])

    def block_of(step, chosen):
        value = chosen[0]
        for place, stride in enumerate(strides):
            value = value + (step // (1 << place)) % 2 * stride
        return value

    def kernel(chosen_ref, ol_ref, pl_ref, or_ref, pr_ref, out_ref):
        out_ref[...] = (
            contract_rows(ol_ref[...], or_ref[...]) + contract_rows(pl_ref[...], pr_ref[...])
        ).astype(out_dtype)

    left_spec = pl.BlockSpec((row_count, rows_each), lambda i, chosen: (0, block_of(i, chosen)))
    whole = pl.BlockSpec((row_count, features), lambda i, chosen: (0, 0))
    return pl.pallas_call(
        kernel,
        grid_spec=pltpu.PrefetchScalarGridSpec(
            num_scalar_prefetch=1,
            grid=(span,),
            in_specs=[left_spec, left_spec, whole, whole],
            out_specs=pl.BlockSpec((rows_each, features), lambda i, chosen: (i, 0)),
        ),
        out_shape=jax.ShapeDtypeStruct((span * rows_each, features), out_dtype),
        compiler_params=_params(40),
        cost_estimate=_cost(
            4 * row_count * span * rows_each * features, 4 * row_count * (span * rows_each + features) + 4 * span * rows_each * features
        ),
        name="grad_down",
    )(chosen, own_acts, peer_acts, own_right, peer_right)


def halving(keep, received, rest):
    for axis, bit in rest:
        pair = (2, keep.shape[0] // 2) + keep.shape[1:]
        keep, received = keep.reshape(pair), received.reshape(pair)
        mine = _bit_of(axis, bit)

        def half(index):
            return lax.dynamic_index_in_dim(keep, index, 0, False) + lax.dynamic_index_in_dim(
                received, index, 0, False
            ).astype(jnp.float32)

        theirs, keep = half(1 - mine), half(mine)
        received = _paired(theirs.astype(jnp.bfloat16), axis, bit)
    return keep + received.astype(jnp.float32)


def fast_body(
    patches, seg_lengths, w_query, w_key, w_value, w_out, w_up, w_down,
    norm1_gain, norm1_bias, norm2_gain, norm2_bias, out_grad,
):
    micro_count, tokens, features = patches.shape
    hidden = w_up.shape[1]
    row_count = micro_count * tokens
    blocks, shares = lax.axis_size("blk"), lax.axis_size("mb")
    head_dim = features // H
    slot = features // blocks
    rows = patches.reshape(row_count, features)
    dout = out_grad.reshape(row_count, features)
    gain_one, bias_one, gain_two, bias_two = (
        value.reshape(1, features) for value in (norm1_gain, norm1_bias, norm2_gain, norm2_bias)
    )

    def swap(values):
        return lax.all_to_all(values, "blk", split_axis=0, concat_axis=0, tiled=True)

    def by_micro(values):
        return values.reshape(blocks, micro_count, tokens, values.shape[-1])

    send, norm_one = project_call(rows, gain_one, bias_one, w_query, w_key, w_value, blocks)
    received = by_micro(swap(send))
    dout_peer = _paired(dout, "mb", 1)
    norm_peer = _paired(norm_one, "mb", 1)
    attended = swap(attend_call(received, seg_lengths, head_dim).reshape(blocks, row_count, slot))
    layer_out, acts, mixed_grad, back, sums_two = middle_call(
        attended, rows, dout, gain_two, bias_two, w_out, w_up, w_down
    )
    grads = by_micro(swap(back))
    acts_peer = _paired(acts, "mb", 1)

    core, other = _bit_of("mb", 1), _bit_of("mb", 2)
    x_bit = _bit_of("blk", 1)
    blk_bits = _bits(blocks)
    z_order = _ordered(blk_bits[1:])
    rest_z = [("blk", bit) for bit in blk_bits[1:]]

    def picked(*values):
        return jnp.stack([jnp.asarray(value, jnp.int32) for value in values])

    down_rows = hidden // (blocks * shares)
    down_order = [at * shares for at in _ordered(blk_bits)]
    down_made = [
        grad_down_call(
            picked(2 * which + core), acts, acts_peer, dout, dout_peer, down_order, shares, down_rows, dtype
        )
        for which, dtype in ((1 - other, jnp.bfloat16), (other, jnp.float32))
    ]
    up_orders = [(at, 2 * share) for share in (0, 1) for at in z_order]
    norm_at = 2 * hidden
    up_picks = [(norm_at, hidden, hidden), (norm_at + features, norm_at + 2 * features, features)]
    up_made = [
        grad_rows_call(
            picked(which, core), (acts, acts), (acts_peer, acts_peer), up_picks, features, 512, up_orders, blocks, shares, dtype
        )
        for which, dtype in ((1 - x_bit, jnp.bfloat16), (x_bit, jnp.float32))
    ]

    def pieces(values, height):
        return values.reshape(-1, height, values.shape[-1])

    down_received = _paired(pieces(down_made[0], down_rows), "mb", 2)
    up_received = _paired(pieces(up_made[0], features // (blocks * shares)), "blk", 1)
    down_total = halving(pieces(down_made[1], down_rows), down_received, [("blk", 1)] + rest_z)
    up_total = halving(pieces(up_made[1], features // (blocks * shares)), up_received, [("mb", 2)] + rest_z)

    (grads, _, _) = lax.optimization_barrier((grads, down_made, up_made))
    made = attend_back_call(received, grads, seg_lengths, head_dim)
    returned = swap(made.reshape(blocks, row_count, 3 * slot))
    patches_grad, acts_one = finish_call(returned, rows, mixed_grad, gain_one, sums_two, w_query, w_key, w_value)
    acts_one_peer = _paired(acts_one, "mb", 1)
    one_made = [
        grad_rows_call(
            picked(which, core), (norm_one, acts_one), (norm_peer, acts_one_peer), [(0, 0, 3 * features)], features, 3 * features,
            up_orders, blocks, shares, dtype, True,
        )
        for which, dtype in ((1 - x_bit, jnp.bfloat16), (x_bit, jnp.float32))
    ]
    one_received = _paired(pieces(one_made[0], features // (blocks * shares)), "blk", 1)
    one_total = halving(
        pieces(one_made[1], features // (blocks * shares)), one_received, [("mb", 2)] + rest_z
    )

    up_total, one_total, down_total = up_total[0], one_total[0], down_total[0]
    return (
        layer_out.reshape(patches.shape),
        patches_grad.reshape(patches.shape),
        one_total[:, 0:features],
        one_total[:, features : 2 * features],
        one_total[:, 2 * features : 3 * features],
        up_total[:, hidden:],
        up_total[:, 0:hidden],
        down_total,
        one_total[:, 3 * features],
        one_total[:, 3 * features + 1],
        one_total[:, 3 * features + 2],
        one_total[:, 3 * features + 3],
    )


def solution(mesh):
    in_specs = (
        P("mb", "blk", None),
        P("mb", None),
        P(),
        P(),
        P(),
        P(),
        P(),
        P(),
        P(),
        P(),
        P(),
        P(),
        P("mb", "blk", None),
    )
    out_specs = (
        P("mb", "blk", None),
        P("mb", "blk", None),
        P(("blk", "mb"), None),
        P(("blk", "mb"), None),
        P(("blk", "mb"), None),
        P(("blk", "mb"), None),
        P(("blk", "mb"), None),
        P(("blk", "mb"), None),
        P(("blk", "mb")),
        P(("blk", "mb")),
        P(("blk", "mb")),
        P(("blk", "mb")),
    )
    blocks, shares = mesh.shape["blk"], mesh.shape["mb"]
    paired = blocks >= 2 and blocks & (blocks - 1) == 0 and shares == 4
    chosen_body = fast_body if paired and H % blocks == 0 else body
    return jax.shard_map(chosen_body, mesh=mesh, in_specs=in_specs, out_specs=out_specs, check_vma=False)
```

```python
import math

import jax
import jax.numpy as jnp
from jax import lax
from jax.experimental import pallas as pl
from jax.experimental.pallas import tpu as pltpu
from jax.sharding import PartitionSpec as P

H = 16


epsilon = 1e-05
masked_score = -1e30


def layer_norm(values, norm_gain, norm_bias):
    center = values - jnp.mean(values, axis=-1, keepdims=True)
    variance = jnp.mean(center * center, axis=-1, keepdims=True)
    return center * lax.rsqrt(variance + epsilon) * norm_gain + norm_bias


def gelu_exact(values):
    return jax.nn.gelu(values, approximate=False)


def matmul(left_side, right_side):
    return jnp.dot(left_side, right_side, preferred_element_type=jnp.float32)


def contract_rows(left_side, right_side):
    return lax.dot_general(
        left_side, right_side, (((0,), (0,)), ((), ())), preferred_element_type=jnp.float32
    )


def contract_cols(left_side, right_side):
    return lax.dot_general(
        left_side, right_side, (((1,), (1,)), ((), ())), preferred_element_type=jnp.float32
    )


def segment_ids(lengths, positions):
    doc_ends = jnp.cumsum(lengths, axis=-1)
    return jnp.sum((positions[None, :, None] >= doc_ends[:, None, :]).astype(jnp.int32), axis=-1)


def masked_scores(query_piece, keys_all, query_docs, key_docs, score_scale):
    scores = contract_cols(query_piece, keys_all) * score_scale
    return jnp.where(query_docs[:, None] == key_docs[None, :], scores, masked_score)


def soft_rows(scores):
    row_max = jnp.max(scores, axis=-1, keepdims=True)
    exponent = jnp.exp(scores - row_max)
    return exponent / jnp.sum(exponent, axis=-1, keepdims=True)


def body(
    patches,
    seg_lengths,
    w_query,
    w_key,
    w_value,
    w_out,
    w_up,
    w_down,
    norm1_gain,
    norm1_bias,
    norm2_gain,
    norm2_bias,
    out_grad,
):
    micro_count, tokens, features = patches.shape
    row_count = micro_count * tokens
    blocks = lax.axis_size("blk")
    block_index = lax.axis_index("blk")
    head_count = H
    head_dim = features // head_count
    repeat = max(1, blocks // head_count)
    per_slot = max(1, head_count // blocks)
    groups = head_count // per_slot
    rows_part = tokens // repeat
    query_rows = blocks * rows_part
    seq_length = blocks * tokens
    item_count = micro_count * per_slot
    block_rows = min(512, query_rows)
    block_count = query_rows // block_rows
    slot_width = micro_count * per_slot * head_dim
    score_scale = 1.0 / math.sqrt(head_dim)
    doc_count = seg_lengths.shape[1]

    def query_layout(values):
        shaped = values.reshape(micro_count, repeat, rows_part, groups, per_slot * head_dim)
        return shaped.transpose(3, 1, 2, 0, 4).reshape(blocks, rows_part, slot_width)

    def key_layout(values):
        shaped = values.reshape(micro_count, tokens, groups, per_slot * head_dim).transpose(
            2, 1, 0, 3
        )
        shaped = jnp.broadcast_to(
            shaped[:, None], (groups, repeat, tokens, micro_count, per_slot * head_dim)
        )
        return shaped.reshape(blocks, tokens, slot_width)

    def token_layout(values):
        shaped = values.reshape(groups, repeat, rows_part, micro_count, per_slot * head_dim)
        return shaped.transpose(3, 1, 2, 0, 4).reshape(row_count, features)

    def key_sum(values):
        shaped = values.reshape(groups, repeat, tokens, micro_count, per_slot * head_dim).sum(
            axis=1
        )
        return shaped.transpose(2, 1, 0, 3).reshape(row_count, features)

    def to_items(received):
        row_total = received.shape[1]
        shaped = received.reshape(row_total, micro_count, per_slot, head_dim).transpose(1, 2, 0, 3)
        return shaped.reshape(item_count, row_total, head_dim)

    def from_items(values):
        row_total = values.shape[1]
        shaped = values.reshape(micro_count, per_slot, row_total, head_dim).transpose(2, 0, 1, 3)
        return shaped.reshape(1, row_total, slot_width)

    row_ids = jnp.arange(query_rows)
    query_pos = (
        row_ids // rows_part * tokens + block_index % repeat * rows_part + row_ids % rows_part
    )
    query_docs = jnp.repeat(segment_ids(seg_lengths, query_pos), per_slot, axis=0)
    key_docs = jnp.repeat(segment_ids(seg_lengths, jnp.arange(seq_length)), per_slot, axis=0)
    query_valid = (query_docs < doc_count).astype(jnp.float32)
    local_pos = block_index * tokens + jnp.arange(tokens)
    row_valid = (
        (segment_ids(seg_lengths, local_pos) < doc_count).astype(jnp.float32).reshape(row_count, 1)
    )

    def forward_item(operands):
        queries_item, keys_item, values_item, docs_item, key_docs_item = operands

        def forward_one_block(block_operands):
            query_piece, docs_piece = block_operands
            weights_soft = soft_rows(
                masked_scores(query_piece, keys_item, docs_piece, key_docs_item, score_scale)
            )
            return matmul(weights_soft.astype(jnp.bfloat16), values_item)

        outputs = lax.map(
            forward_one_block,
            (
                queries_item.reshape(block_count, block_rows, head_dim),
                docs_item.reshape(block_count, block_rows),
            ),
        )
        return outputs.reshape(query_rows, head_dim)

    def backward_item(operands):
        queries_item, keys_item, values_item, grads_item, docs_item, key_docs_item = operands

        def backward_one_block(totals, block_operands):
            key_total, value_total = totals
            query_piece, grad_piece, docs_piece = block_operands
            weights_soft = soft_rows(
                masked_scores(query_piece, keys_item, docs_piece, key_docs_item, score_scale)
            )
            weights_low = weights_soft.astype(jnp.bfloat16)
            weight_grads = contract_cols(grad_piece, values_item)
            row_inner = jnp.sum(weights_soft * weight_grads, axis=-1, keepdims=True)
            score_grads = (weights_soft * (weight_grads - row_inner)).astype(jnp.bfloat16)
            query_grad = matmul(score_grads, keys_item) * score_scale
            key_total = key_total + contract_rows(score_grads, query_piece) * score_scale
            value_total = value_total + contract_rows(weights_low, grad_piece)
            return ((key_total, value_total), query_grad)

        zero_block = jnp.zeros((seq_length, head_dim), jnp.float32)
        totals, query_grads = lax.scan(
            backward_one_block,
            (zero_block, zero_block),
            (
                queries_item.reshape(block_count, block_rows, head_dim),
                grads_item.reshape(block_count, block_rows, head_dim),
                docs_item.reshape(block_count, block_rows),
            ),
        )
        return (query_grads.reshape(query_rows, head_dim), totals[0], totals[1])

    inputs = patches.astype(jnp.float32).reshape(row_count, features)
    norm_one_full, norm_one_pull = jax.vjp(layer_norm, inputs, norm1_gain, norm1_bias)
    norm_one = norm_one_full.astype(jnp.bfloat16)
    queries = matmul(norm_one, w_query).astype(jnp.bfloat16)
    keys_proj = matmul(norm_one, w_key).astype(jnp.bfloat16)
    values_proj = matmul(norm_one, w_value).astype(jnp.bfloat16)
    query_send = query_layout(queries)
    key_send = key_layout(keys_proj)
    value_send = key_layout(values_proj)
    query_heads, key_heads, value_heads = (
        lax.all_to_all(query_send, "blk", split_axis=0, concat_axis=1, tiled=True),
        lax.all_to_all(key_send, "blk", split_axis=0, concat_axis=1, tiled=True),
        lax.all_to_all(value_send, "blk", split_axis=0, concat_axis=1, tiled=True),
    )
    query_items = to_items(query_heads)
    key_items = to_items(key_heads)
    value_items = to_items(value_heads)
    attended_items = lax.map(
        forward_item, (query_items, key_items, value_items, query_docs, key_docs)
    )
    attended_items = (attended_items * query_valid[:, :, None]).astype(jnp.bfloat16)
    attended = token_layout(
        lax.all_to_all(from_items(attended_items), "blk", split_axis=1, concat_axis=0, tiled=True)
    )
    mixed_rows = inputs + matmul(attended, w_out)
    norm_two_full, norm_two_pull = jax.vjp(layer_norm, mixed_rows, norm2_gain, norm2_bias)
    norm_two = norm_two_full.astype(jnp.bfloat16)
    upper_proj = matmul(norm_two, w_up)
    active_full, gelu_pull = jax.vjp(gelu_exact, upper_proj)
    active = active_full.astype(jnp.bfloat16)
    result = mixed_rows + matmul(active, w_down)
    layer_out = result.astype(jnp.bfloat16).reshape(micro_count, tokens, features)
    dout_low = out_grad.reshape(row_count, features)
    down_grad = contract_rows(active, dout_low)
    active_grad = contract_cols(dout_low, w_down)
    upper_grad = gelu_pull(active_grad)[0].astype(jnp.bfloat16)
    up_grad = contract_rows(norm_two, upper_grad)
    norm_two_grad = contract_cols(upper_grad, w_up)
    mixed_part, gain_two_grad, bias_two_grad = norm_two_pull(norm_two_grad)
    mixed_grad = dout_low.astype(jnp.float32) + mixed_part
    mixed_low = mixed_grad.astype(jnp.bfloat16)
    out_proj_grad = contract_rows(attended, mixed_low)
    attended_grad = (contract_cols(mixed_low, w_out) * row_valid).astype(jnp.bfloat16)
    grad_send = query_layout(attended_grad)
    query_again, key_again, value_again, grad_heads = (
        lax.all_to_all(query_send, "blk", split_axis=0, concat_axis=1, tiled=True),
        lax.all_to_all(key_send, "blk", split_axis=0, concat_axis=1, tiled=True),
        lax.all_to_all(value_send, "blk", split_axis=0, concat_axis=1, tiled=True),
        lax.all_to_all(grad_send, "blk", split_axis=0, concat_axis=1, tiled=True),
    )
    back_queries = to_items(query_again)
    back_keys = to_items(key_again)
    back_values = to_items(value_again)
    grad_items = to_items(grad_heads)
    query_grad_items, key_grad_items, value_grad_items = lax.map(
        backward_item, (back_queries, back_keys, back_values, grad_items, query_docs, key_docs)
    )
    query_back, key_back, value_back = (
        lax.all_to_all(
            from_items(query_grad_items).astype(jnp.bfloat16),
            "blk",
            split_axis=1,
            concat_axis=0,
            tiled=True,
        ).astype(jnp.float32),
        lax.all_to_all(
            from_items(key_grad_items).astype(jnp.bfloat16),
            "blk",
            split_axis=1,
            concat_axis=0,
            tiled=True,
        ).astype(jnp.float32),
        lax.all_to_all(
            from_items(value_grad_items).astype(jnp.bfloat16),
            "blk",
            split_axis=1,
            concat_axis=0,
            tiled=True,
        ).astype(jnp.float32),
    )
    query_grad = token_layout(query_back).astype(jnp.bfloat16)
    key_grad = key_sum(key_back).astype(jnp.bfloat16)
    value_grad = key_sum(value_back).astype(jnp.bfloat16)
    query_proj_grad = contract_rows(norm_one, query_grad)
    key_proj_grad = contract_rows(norm_one, key_grad)
    value_proj_grad = contract_rows(norm_one, value_grad)
    norm_one_grad = (
        contract_cols(query_grad, w_query)
        + contract_cols(key_grad, w_key)
        + contract_cols(value_grad, w_value)
    )
    input_part, gain_one_grad, bias_one_grad = norm_one_pull(norm_one_grad)
    patches_grad = (
        (mixed_grad + input_part).astype(jnp.bfloat16).reshape(micro_count, tokens, features)
    )
    gradients = (
        query_proj_grad,
        key_proj_grad,
        value_proj_grad,
        out_proj_grad,
        up_grad,
        down_grad,
        gain_one_grad,
        bias_one_grad,
        gain_two_grad,
        bias_two_grad,
    )
    summed = (
        lax.psum_scatter(gradients[0], ("blk", "mb"), scatter_dimension=0, tiled=True),
        lax.psum_scatter(gradients[1], ("blk", "mb"), scatter_dimension=0, tiled=True),
        lax.psum_scatter(gradients[2], ("blk", "mb"), scatter_dimension=0, tiled=True),
        lax.psum_scatter(gradients[3], ("blk", "mb"), scatter_dimension=0, tiled=True),
        lax.psum_scatter(gradients[4], ("blk", "mb"), scatter_dimension=0, tiled=True),
        lax.psum_scatter(gradients[5], ("blk", "mb"), scatter_dimension=0, tiled=True),
        lax.psum_scatter(gradients[6], ("blk", "mb"), scatter_dimension=0, tiled=True),
        lax.psum_scatter(gradients[7], ("blk", "mb"), scatter_dimension=0, tiled=True),
        lax.psum_scatter(gradients[8], ("blk", "mb"), scatter_dimension=0, tiled=True),
        lax.psum_scatter(gradients[9], ("blk", "mb"), scatter_dimension=0, tiled=True),
    )
    return (
        layer_out,
        patches_grad,
        summed[0],
        summed[1],
        summed[2],
        summed[3],
        summed[4],
        summed[5],
        summed[6],
        summed[7],
        summed[8],
        summed[9],
    )


def _normalize(values):
    center = values - jnp.mean(values, axis=-1, keepdims=True)
    variance = jnp.mean(center * center, axis=-1, keepdims=True)
    inverse = lax.rsqrt(variance + epsilon)
    return center * inverse, inverse


def _normalize_back(grads, gain, unit, inverse):
    scaled = grads * gain
    mean_scaled = jnp.mean(scaled, axis=-1, keepdims=True)
    mean_product = jnp.mean(scaled * unit, axis=-1, keepdims=True)
    return (scaled - mean_scaled - unit * mean_product) * inverse


def _doc_ids(lengths_ref, micro, doc_count, positions):
    end = jnp.int32(0)
    ids = jnp.zeros_like(positions)
    for doc in range(doc_count):
        end = end + lengths_ref[micro, doc]
        ids = ids + (positions >= end).astype(jnp.int32)
    return ids


def _params(mib):
    return pltpu.CompilerParams(vmem_limit_bytes=max(mib, 60) << 20)


def _cost(microseconds):
    return pl.CostEstimate(flops=int(microseconds * 1e9) + 1, bytes_accessed=1, transcendentals=0)


def project_call(rows, gain, bias, w_query, w_key, w_value, blocks, tokens):
    row_count, features = rows.shape
    slot = features // blocks
    per_step = max(1, min(blocks, 256 // slot))
    wide = slot * per_step

    def kernel(rows_ref, gain_ref, bias_ref, wq_ref, wk_ref, wv_ref, send_ref, *refs):
        unit_refs, norm_ref = refs[:-1], refs[-1]


        @pl.when(pl.program_id(0) == 0)
        def _():
            unit, _unused = _normalize(rows_ref[...].astype(jnp.float32))
            for micro, unit_ref in enumerate(unit_refs):
                unit_ref[...] = unit[micro * tokens : (micro + 1) * tokens].astype(jnp.bfloat16)
            norm_ref[...] = (unit * gain_ref[...] + bias_ref[...]).astype(jnp.bfloat16)

        for part, weight_ref in enumerate((wq_ref, wk_ref, wv_ref)):
            made = matmul(norm_ref[...], weight_ref[...]).astype(jnp.bfloat16)
            for piece in range(per_step):
                send_ref[piece, :, part * slot : (part + 1) * slot] = made[
                    :, piece * slot : (piece + 1) * slot
                ]

    whole = pl.BlockSpec((row_count, features), lambda i: (0, 0))
    vector = pl.BlockSpec((1, features), lambda i: (0, 0))
    columns = pl.BlockSpec((features, wide), lambda i: (0, i))
    return pl.pallas_call(
        kernel,
        grid=(blocks // per_step,),
        in_specs=[whole, vector, vector, columns, columns, columns],
        out_specs=[pl.BlockSpec((per_step, row_count, 3 * slot), lambda i: (i, 0, 0))]
        + [pl.BlockSpec((tokens, features), lambda i: (0, 0))] * (row_count // tokens),
        out_shape=[jax.ShapeDtypeStruct((blocks, row_count, 3 * slot), jnp.bfloat16)]
        + [jax.ShapeDtypeStruct((tokens, features), jnp.bfloat16)] * (row_count // tokens),
        scratch_shapes=[pltpu.VMEM((row_count, features), jnp.bfloat16)],
        compiler_params=_params(40),
        cost_estimate=_cost(6),
        name="project",
    )(rows, gain, bias, w_query, w_key, w_value)


def _head_masks(slot, head_dim, dtype):
    lanes = lax.broadcasted_iota(jnp.int32, (1, slot), 1)
    return [(lanes // head_dim == head).astype(dtype) for head in range(slot // head_dim)]


def _key_range(lengths_ref, micro, doc_count, first_row, last_row, seq):
    low, high, end = jnp.int32(0), jnp.int32(seq), jnp.int32(0)
    for doc in range(doc_count):
        end = end + lengths_ref[micro, doc]
        low = jnp.where(end <= first_row, jnp.maximum(low, end), low)
        high = jnp.where(end >= last_row, jnp.minimum(high, end), high)
    return low, high


def _by_key_range(lengths_ref, micro, doc_count, step, rows, blocks, tokens, compute):
    low, high = _key_range(lengths_ref, micro, doc_count, step * rows, (step + 1) * rows, blocks * tokens)
    half = blocks // 2
    in_low, in_high = high <= half * tokens, low >= half * tokens

    @pl.when(in_low | in_high)
    def _():
        compute(jnp.where(in_low, 0, half), half)

    @pl.when(jnp.logical_not(in_low | in_high))
    def _():
        compute(0, blocks)


def attend_call(received, lengths, head_dim):
    blocks, micro_count, tokens, width = received.shape
    slot = width // 3
    doc_count = lengths.shape[1]
    step_blocks = max(1, min(blocks, 256 // tokens))
    rows = step_blocks * tokens
    scale = 1.0 / math.sqrt(head_dim)

    def kernel(lengths_ref, data_ref, out_ref):
        micro = pl.program_id(0)
        step = pl.program_id(1)
        row_docs = _doc_ids(
            lengths_ref, micro, doc_count, lax.broadcasted_iota(jnp.int32, (rows, 1), 0) + step * rows
        )
        queries = data_ref[pl.ds(step * step_blocks, step_blocks), 0, :, 0:slot].reshape(rows, slot) * scale

        def compute(first, count):
            seq = count * tokens
            key_docs = _doc_ids(
                lengths_ref, micro, doc_count, lax.broadcasted_iota(jnp.int32, (1, seq), 1) + first * tokens
            )
            same = row_docs == key_docs
            keys = data_ref[pl.ds(first, count), 0, :, slot : 2 * slot].reshape(seq, slot)
            values = data_ref[pl.ds(first, count), 0, :, 2 * slot : 3 * slot].reshape(seq, slot)
            total = jnp.zeros((rows, slot), jnp.float32)
            for mask, mask_wide in zip(
                _head_masks(slot, head_dim, jnp.bfloat16), _head_masks(slot, head_dim, jnp.float32)
            ):
                scores = jnp.where(same, contract_cols(queries * mask, keys), masked_score)
                exponent = jnp.exp(scores - jnp.max(scores, axis=-1, keepdims=True))
                share = 1.0 / jnp.sum(exponent, axis=-1, keepdims=True)
                total = total + matmul(exponent.astype(jnp.bfloat16), values) * (share * mask_wide)
            total = jnp.where(row_docs < doc_count, total, 0.0)
            out_ref[...] = total.astype(jnp.bfloat16).reshape(step_blocks, 1, tokens, slot)

        _by_key_range(lengths_ref, micro, doc_count, step, rows, blocks, tokens, compute)

    return pl.pallas_call(
        kernel,
        grid=(micro_count, blocks // step_blocks),
        in_specs=[
            pl.BlockSpec(memory_space=pltpu.SMEM),
            pl.BlockSpec((blocks, 1, tokens, width), lambda m, s: (0, m, 0, 0)),
        ],
        out_specs=pl.BlockSpec((step_blocks, 1, tokens, slot), lambda m, s: (s, m, 0, 0)),
        out_shape=jax.ShapeDtypeStruct((blocks, micro_count, tokens, slot), jnp.bfloat16),
        compiler_params=_params(40),
        cost_estimate=_cost(11),
        name="attend",
    )(lengths, received)


def attend_back_call(received, grads, lengths, head_dim):
    blocks, micro_count, tokens, width = received.shape
    slot = width // 3
    doc_count = lengths.shape[1]
    step_blocks = max(1, min(blocks, 256 // tokens))
    rows = step_blocks * tokens
    steps = blocks // step_blocks
    scale = 1.0 / math.sqrt(head_dim)

    def kernel(lengths_ref, data_ref, grads_ref, *refs):
        out_refs, (key_total, value_total) = refs[:micro_count], refs[micro_count:]
        micro = pl.program_id(0)
        step = pl.program_id(1)

        @pl.when(step == 0)
        def _():
            key_total[...] = jnp.zeros_like(key_total)
            value_total[...] = jnp.zeros_like(value_total)

        row_docs = _doc_ids(
            lengths_ref, micro, doc_count, lax.broadcasted_iota(jnp.int32, (1, rows), 1) + step * rows
        )
        column_docs = _doc_ids(
            lengths_ref, micro, doc_count, lax.broadcasted_iota(jnp.int32, (rows, 1), 0) + step * rows
        )
        queries = data_ref[pl.ds(step * step_blocks, step_blocks), 0, :, 0:slot].reshape(rows, slot) * scale
        out_grads = grads_ref[...].reshape(rows, slot)
        out_grads = out_grads * (column_docs < doc_count).astype(jnp.float32).astype(jnp.bfloat16)

        def compute(first, count):
            seq = count * tokens
            key_docs = _doc_ids(
                lengths_ref, micro, doc_count, lax.broadcasted_iota(jnp.int32, (seq, 1), 0) + first * tokens
            )
            same = row_docs == key_docs
            keys = data_ref[pl.ds(first, count), 0, :, slot : 2 * slot].reshape(seq, slot)
            values = data_ref[pl.ds(first, count), 0, :, 2 * slot : 3 * slot].reshape(seq, slot)
            query_total = jnp.zeros((rows, slot), jnp.float32)
            key_parts, value_parts = [], []
            for mask, mask_wide in zip(
                _head_masks(slot, head_dim, jnp.bfloat16), _head_masks(slot, head_dim, jnp.float32)
            ):
                queries_head = queries * mask
                grads_head = out_grads * mask
                scores = jnp.where(same, contract_cols(keys, queries_head), masked_score)
                exponent = jnp.exp(scores - jnp.max(scores, axis=0, keepdims=True))
                probs = exponent * (1.0 / jnp.sum(exponent, axis=0, keepdims=True))
                prob_grads = contract_cols(values, grads_head)
                inner = jnp.sum(probs * prob_grads, axis=0, keepdims=True)
                score_grads = (probs * (prob_grads - inner)).astype(jnp.bfloat16)
                value_parts.append(matmul(probs.astype(jnp.bfloat16), grads_head))
                key_parts.append(matmul(score_grads, queries_head))
                query_total = query_total + contract_rows(score_grads, keys) * mask_wide
            at = pl.ds(pl.multiple_of(first * tokens, tokens), seq)
            key_total[at, :] += sum(key_parts)
            value_total[at, :] += sum(value_parts)
            query_grads = (query_total * scale).astype(jnp.bfloat16).reshape(step_blocks, tokens, slot)
            for at, out_ref in enumerate(out_refs):

                @pl.when(micro == at)
                def _():
                    out_ref[pl.ds(step * step_blocks, step_blocks), :, 0:slot] = query_grads

        _by_key_range(lengths_ref, micro, doc_count, step, rows, blocks, tokens, compute)

        for at, out_ref in enumerate(out_refs):

            @pl.when((step == steps - 1) & (micro == at))
            def _():
                out_ref[:, :, slot : 2 * slot] = key_total[...].astype(jnp.bfloat16).reshape(blocks, tokens, slot)
                out_ref[:, :, 2 * slot :] = value_total[...].astype(jnp.bfloat16).reshape(blocks, tokens, slot)

    return pl.pallas_call(
        kernel,
        grid=(micro_count, steps),
        in_specs=[
            pl.BlockSpec(memory_space=pltpu.SMEM),
            pl.BlockSpec((blocks, 1, tokens, width), lambda m, s: (0, m, 0, 0)),
            pl.BlockSpec((step_blocks, 1, tokens, slot), lambda m, s: (s, m, 0, 0)),
        ],
        out_specs=[pl.BlockSpec((blocks, tokens, width), lambda m, s: (0, 0, 0))] * micro_count,
        out_shape=[jax.ShapeDtypeStruct((blocks, tokens, width), jnp.bfloat16)] * micro_count,
        scratch_shapes=[pltpu.VMEM((blocks * tokens, slot), jnp.float32)] * 2,
        compiler_params=_params(48),
        cost_estimate=_cost(0),
        name="attend_back",
    )(lengths, received, grads)


def _fixed(*shape):
    return pl.BlockSpec(shape, lambda *_unused: (0,) * len(shape))


def mix_call(attended, rows, gain, bias, w_out):
    blocks, row_count, slot = attended.shape
    features = rows.shape[1]

    def kernel(att_ref, rows_ref, gain_ref, bias_ref, wo_ref, mixed_ref, norm_ref, side_ref):
        for block in range(blocks):
            side_ref[:, block * slot : (block + 1) * slot] = att_ref[block]
        value = rows_ref[...].astype(jnp.float32) + matmul(side_ref[...], wo_ref[...])
        mixed_ref[...] = value
        unit, _unused = _normalize(value)
        norm_ref[...] = (unit * gain_ref[...] + bias_ref[...]).astype(jnp.bfloat16)

    rows_spec, vector = _fixed(row_count, features), _fixed(1, features)
    return pl.pallas_call(
        kernel,
        grid=(1,),
        in_specs=[_fixed(blocks, row_count, slot), rows_spec, vector, vector, _fixed(features, features)],
        out_specs=[rows_spec] * 3,
        out_shape=[
            jax.ShapeDtypeStruct((row_count, features), jnp.float32),
            jax.ShapeDtypeStruct((row_count, features), jnp.bfloat16),
            jax.ShapeDtypeStruct((row_count, features), jnp.bfloat16),
        ],
        compiler_params=_params(56),
        cost_estimate=_cost(4),
        name="mix",
    )(attended, rows, gain, bias, w_out)


def _hidden_parts(norm, out_grad, up_columns, down_rows):
    upper = matmul(norm, up_columns)
    active_grad = contract_cols(out_grad, down_rows)
    half = (1.0 + lax.erf(upper * (1.0 / math.sqrt(2.0)))) * 0.5
    slope = half + upper * jnp.exp(upper * upper * -0.5) * (1.0 / math.sqrt(2.0 * math.pi))
    return (upper * half).astype(jnp.bfloat16), (active_grad * slope).astype(jnp.bfloat16)


def middle_call(norm, mixed, out_grad, w_up, w_down):
    row_count, features = mixed.shape
    hidden = w_up.shape[1]
    wide = min(1024, hidden)
    sub = min(512, wide)
    steps = hidden // wide

    def kernel(norm_ref, mixed_ref, grad_ref, wu_ref, wd_ref, out_ref, grad_total, total, active_all, upper_all):
        step = pl.program_id(0)

        @pl.when(step == 0)
        def _():
            total[...] = mixed_ref[...]
            grad_total[...] = jnp.zeros_like(grad_total)

        for chunk in range(0, wide, sub):
            active, upper_grad = _hidden_parts(
                norm_ref[...], grad_ref[...], wu_ref[:, chunk : chunk + sub], wd_ref[chunk : chunk + sub, :]
            )
            active_all[:, chunk : chunk + sub] = active
            upper_all[:, chunk : chunk + sub] = upper_grad
        total[...] += matmul(active_all[...], wd_ref[...])
        grad_total[...] += contract_cols(upper_all[...], wu_ref[...])

        @pl.when(step == steps - 1)
        def _():
            out_ref[...] = total[...].astype(jnp.bfloat16)

    rows_spec = _fixed(row_count, features)
    return pl.pallas_call(
        kernel,
        grid=(steps,),
        in_specs=[
            rows_spec,
            rows_spec,
            rows_spec,
            pl.BlockSpec((features, wide), lambda i: (0, i)),
            pl.BlockSpec((wide, features), lambda i: (i, 0)),
        ],
        out_specs=[rows_spec] * 2,
        scratch_shapes=[
            pltpu.VMEM((row_count, features), jnp.float32),
            pltpu.VMEM((row_count, wide), jnp.bfloat16),
            pltpu.VMEM((row_count, wide), jnp.bfloat16),
        ],
        out_shape=[
            jax.ShapeDtypeStruct((row_count, features), jnp.bfloat16),
            jax.ShapeDtypeStruct((row_count, features), jnp.float32),
        ],
        compiler_params=_params(56),
        cost_estimate=_cost(20),
        name="middle",
    )(norm, mixed, out_grad, w_up, w_down)


def middle_back_call(place, mixed, norm_grads, out_grad, gain, w_out, blocks, shares):
    row_count, features = mixed.shape
    slot = features // blocks
    part = features // shares

    def kernel(place_ref, mixed_ref, norm_ref, grad_ref, gain_ref, wo_ref, mixed_grad_ref, back_ref, sums_ref, *refs):
        low_refs, low_all = refs[:shares], refs[shares]
        unit, inverse = _normalize(mixed_ref[...])
        grads = norm_ref[...]
        sums_ref[0:1, :] = jnp.sum(grads * unit, axis=0, keepdims=True)
        sums_ref[1:2, :] = jnp.sum(grads, axis=0, keepdims=True)
        mixed_grad = grad_ref[...].astype(jnp.float32) + _normalize_back(grads, gain_ref[...], unit, inverse)
        mixed_grad_ref[...] = mixed_grad
        low = mixed_grad.astype(jnp.bfloat16)
        low_all[...] = low
        for share, low_ref in enumerate(low_refs):
            low_ref[...] = low_all[:, pl.ds(pl.multiple_of((place_ref[1] ^ share) * part, 128), part)]
        back = contract_cols(low, wo_ref[...]).astype(jnp.bfloat16)
        for block in range(blocks):
            back_ref[block] = back[:, block * slot : (block + 1) * slot]

    rows_spec = _fixed(row_count, features)
    return pl.pallas_call(
        kernel,
        grid_spec=pltpu.PrefetchScalarGridSpec(
            num_scalar_prefetch=1,
            grid=(1,),
            in_specs=[rows_spec, rows_spec, rows_spec, _fixed(1, features), _fixed(features, features)],
            out_specs=[rows_spec, _fixed(blocks, row_count, slot), _fixed(2, features)]
            + [_fixed(row_count, part)] * shares,
            scratch_shapes=[pltpu.VMEM((row_count, features), jnp.bfloat16)],
        ),
        out_shape=[
            jax.ShapeDtypeStruct((row_count, features), jnp.float32),
            jax.ShapeDtypeStruct((blocks, row_count, slot), jnp.bfloat16),
            jax.ShapeDtypeStruct((2, features), jnp.float32),
        ]
        + [jax.ShapeDtypeStruct((row_count, part), jnp.bfloat16)] * shares,
        compiler_params=_params(56),
        cost_estimate=_cost(0),
        name="middle_back",
    )(place, mixed, norm_grads, out_grad, gain, w_out)


def finish_call(received, rows, mixed_grad, gain, w_query, w_key, w_value):
    micro_count = len(received)
    blocks, tokens, width = received[0].shape
    slot = width // 3
    row_count, features = rows.shape
    per_step = max(1, min(blocks, 256 // slot))
    wide = slot * per_step
    steps = blocks // per_step

    def kernel(*refs):
        data_refs, refs = refs[:micro_count], refs[micro_count:]
        rows_ref, mixed_ref, gain_ref, wq_ref, wk_ref, wv_ref, out_ref, total, side = refs
        step = pl.program_id(0)

        @pl.when(step == 0)
        def _():
            total[...] = jnp.zeros_like(total)

        for part, weight_ref in enumerate((wq_ref, wk_ref, wv_ref)):
            for micro, data_ref in enumerate(data_refs):
                for piece in range(per_step):
                    side[part, micro * tokens : (micro + 1) * tokens, piece * slot : (piece + 1) * slot] = data_ref[
                        piece, :, part * slot : (part + 1) * slot
                    ]
            total[...] += contract_cols(side[part], weight_ref[...])

        @pl.when(step == steps - 1)
        def _():
            unit, inverse = _normalize(rows_ref[...].astype(jnp.float32))
            out_ref[...] = (
                mixed_ref[...] + _normalize_back(total[...], gain_ref[...], unit, inverse)
            ).astype(jnp.bfloat16)

    def fixed(*shape):
        return pl.BlockSpec(shape, lambda i: (0,) * len(shape))

    columns = pl.BlockSpec((features, wide), lambda i: (0, i))
    return pl.pallas_call(
        kernel,
        grid=(steps,),
        in_specs=[pl.BlockSpec((per_step, tokens, width), lambda i: (i, 0, 0))] * micro_count
        + [
            fixed(row_count, features),
            fixed(row_count, features),
            fixed(1, features),
            columns,
            columns,
            columns,
        ],
        out_specs=fixed(row_count, features),
        out_shape=jax.ShapeDtypeStruct((row_count, features), jnp.bfloat16),
        scratch_shapes=[
            pltpu.VMEM((row_count, features), jnp.float32),
            pltpu.VMEM((3, row_count, wide), jnp.bfloat16),
        ],
        compiler_params=_params(48),
        cost_estimate=_cost(0),
        name="finish",
    )(*received, rows, mixed_grad, gain, w_query, w_key, w_value)


def grad_heads_call(place, units, places, made, gain, bias, sums, w_query, w_key, w_value, shares):
    micro_count = len(made)
    blocks, tokens, width = made[0].shape
    slot = width // 3
    features = gain.shape[1]
    group = features // (blocks * shares)
    full = width + 128
    kept = blocks * (shares // 2) * group

    def kernel(place_ref, *refs):
        unit_refs, refs = refs[: 2 * micro_count], refs[2 * micro_count :]
        made_refs, refs = refs[:micro_count], refs[micro_count:]
        gain_ref, bias_ref, sums_ref, wq_ref, wk_ref, wv_ref, send_ref, keep_ref, spread, ordered = refs
        product = jnp.zeros((features, width), jnp.float32)
        column_sum = jnp.zeros((1, width), jnp.float32)
        for micro, made_ref in enumerate(made_refs):
            for at, relative in enumerate(places[micro]):
                ordered[at * tokens : (at + 1) * tokens, :] = made_ref[place_ref[0] ^ relative]
            half = blocks * tokens // 2
            for side in range(2):
                rows = ordered[side * half : (side + 1) * half, :]
                product = product + contract_rows(unit_refs[2 * micro + side][...], rows)
                column_sum = column_sum + jnp.sum(rows.astype(jnp.float32), axis=0, keepdims=True)
        vectors = jnp.concatenate(
            [gain_ref[...], bias_ref[...], sums_ref[...], jnp.zeros((124, features), jnp.float32)], axis=0
        ).T
        total = vectors[:, 0:1] * product + vectors[:, 1:2] * column_sum
        weights = jnp.concatenate([wq_ref[...], wk_ref[...], wv_ref[...]], axis=1).astype(jnp.float32)
        gain_sum = jnp.sum(weights * product, axis=1, keepdims=True)
        bias_sum = jnp.sum(weights * column_sum, axis=1, keepdims=True)
        lanes = lax.broadcasted_iota(jnp.int32, (1, 128), 1)
        norms = jnp.where(
            lanes == 0, gain_sum, jnp.where(lanes == 1, bias_sum, jnp.where(lanes < 4, vectors, 0.0))
        )
        spread[:, :, :, 0:width] = total.reshape(blocks, shares, group, width)
        spread[:, :, :, width:] = norms.reshape(blocks, shares, group, 128)
        core = place_ref[1] % 2
        for which, out_ref in enumerate((send_ref, keep_ref)):
            for share in range(0, shares, 2):
                for block in range(blocks):
                    out_ref[share // 2, block] = spread[block, share + (core if which else 1 - core)].astype(out_ref.dtype)

    def fixed(*shape):
        return pl.BlockSpec(shape, lambda i, place: (0,) * len(shape))

    columns = pl.BlockSpec((features, slot), lambda i, place: (0, place[0]))
    out = (shares // 2, blocks, group, full)
    return pl.pallas_call(
        kernel,
        grid_spec=pltpu.PrefetchScalarGridSpec(
            num_scalar_prefetch=1,
            grid=(1,),
            in_specs=[fixed(*part.shape) for part in (*units, *made)]
            + [fixed(1, features), fixed(1, features), fixed(2, features), columns, columns, columns],
            out_specs=[fixed(*out), fixed(*out)],
            scratch_shapes=[
                pltpu.VMEM((blocks, shares, group, full), jnp.float32),
                pltpu.VMEM((blocks * tokens, width), jnp.bfloat16),
            ],
        ),
        out_shape=[jax.ShapeDtypeStruct(out, jnp.bfloat16), jax.ShapeDtypeStruct(out, jnp.float32)],
        compiler_params=_params(48),
        cost_estimate=_cost(0),
        name="grad_heads",
    )(place, *units, *made, gain, bias, sums, w_query, w_key, w_value)


def _bits(count):
    return [1 << place for place in range(count.bit_length() - 1)]


def _ordered(bits):
    places = [0]
    for bit in bits:
        places = [at + step for at in places for step in (0, bit)]
    return places


def _ordered_low(bits):
    places = [0]
    for bit in bits:
        places = places + [at + bit for at in places]
    return places


def _paired(values, axis, bit):
    count = lax.axis_size(axis)
    return lax.ppermute(values, axis, [(i, i ^ bit) for i in range(count)])


def _bit_of(axis, bit):
    return (lax.axis_index(axis) // bit) % 2


def _place_at(bits, step):
    places = _ordered(bits)
    at = jnp.int32(places[0])
    for other in range(1, len(places)):
        at = jnp.where(step == other, places[other], at)
    return at


def grad_middle_call(place, norms, out_grads, sides, lows, w_up, w_down, down_bits, up_bits):
    shares = len(norms)
    row_count, features = norms[0].shape
    all_rows = shares * row_count
    hidden = w_up.shape[1]
    blocks = 1 << len(up_bits)
    owned = hidden // (blocks * shares)
    part = lows[0].shape[1]
    half = blocks // 2
    pair = min(2, half)
    half_steps = half // pair
    block_rows = features // blocks
    sub = min(2, shares)

    def kernel(place_ref, *refs):
        groups, refs = [refs[at * shares : (at + 1) * shares] for at in range(4)], refs[4 * shares :]
        up_refs, down_refs, refs = refs[:pair], refs[pair : 2 * pair], refs[2 * pair :]
        down_send, down_keep, up_send, up_keep, norm_all, grad_all, active_all, upper_all, up_all = refs
        step = pl.program_id(0)
        low = place_ref[0] // up_bits[0] % 2

        def spread():
            for at, block in enumerate(_ordered(up_bits[1:])):
                rows = slice(at * block_rows, (at + 1) * block_rows)
                up_send[rows, :] = up_all[block + up_bits[0] * (1 - low)].astype(jnp.bfloat16)
                up_keep[rows, :] = up_all[block + up_bits[0] * low]

        @pl.when(step == 0)
        def _():
            for at in range(shares):
                norm_all[at * row_count : (at + 1) * row_count, :] = groups[0][at][...]
                grad_all[at * row_count : (at + 1) * row_count, :] = groups[1][at][...]

        @pl.when(step < 2 * half_steps)
        def _():
            up_columns = jnp.concatenate([ref[...] for ref in up_refs], axis=1)
            down_rows = jnp.concatenate([ref[...] for ref in down_refs], axis=0)
            for at in range(0, all_rows, all_rows // sub):
                rows = slice(at, at + all_rows // sub)
                active_all[rows, :], upper_all[rows, :] = _hidden_parts(
                    norm_all[rows, :], grad_all[rows, :], up_columns, down_rows
                )
            down_made = contract_rows(active_all[...], grad_all[...])

            @pl.when(step < half_steps)
            def _():
                down_send[...] = down_made.astype(jnp.bfloat16)

            @pl.when(step >= half_steps)
            def _():
                down_keep[...] = down_made

            up_all[...] = contract_rows(norm_all[...], upper_all[...]).reshape(blocks, block_rows, pair * owned)
            spread()

        @pl.when(step == 2 * half_steps)
        def _():
            made = jnp.zeros((features, part), jnp.float32)
            for side_ref, low_ref in zip(groups[2], groups[3]):
                made = made + contract_rows(side_ref[...], low_ref[...])
            up_all[...] = made.reshape(blocks, block_rows, part)
            spread()

    def first_bit(i, place):
        return (place[0] // down_bits[0] + 1 + jnp.minimum(i, 2 * half_steps - 1) // half_steps) % 2

    def unit_block(i, place, at):
        inner = _place_at(down_bits[1:], jnp.minimum(i, 2 * half_steps - 1) % half_steps * pair + at)
        return (inner + down_bits[0] * first_bit(i, place)) * shares + place[1]

    ups = [
        pl.BlockSpec((features, owned), lambda i, place, at=at: (0, unit_block(i, place, at))) for at in range(pair)
    ]
    downs = [
        pl.BlockSpec((owned, features), lambda i, place, at=at: (unit_block(i, place, at), 0)) for at in range(pair)
    ]
    def up_block(i, place):
        return (0, jnp.where(i == 2 * half_steps, i, first_bit(i, place) * half_steps + i % half_steps))

    up_out = pl.BlockSpec((features // 2, pair * owned), up_block)
    shapes = [(half * owned, features), (features // 2, blocks * owned + part)]
    return pl.pallas_call(
        kernel,
        grid_spec=pltpu.PrefetchScalarGridSpec(
            num_scalar_prefetch=1,
            grid=(2 * half_steps + 1,),
            in_specs=[_fixed(row_count, features)] * (3 * shares) + [_fixed(row_count, part)] * shares + ups + downs,
            out_specs=[
                pl.BlockSpec((pair * owned, features), lambda i, place: (jnp.minimum(i, half_steps - 1), 0)),
                pl.BlockSpec((pair * owned, features), lambda i, place: (jnp.clip(i - half_steps, 0, half_steps - 1), 0)),
                up_out,
                up_out,
            ],
            scratch_shapes=[
                pltpu.VMEM((all_rows, features), jnp.bfloat16),
                pltpu.VMEM((all_rows, features), jnp.bfloat16),
                pltpu.VMEM((all_rows, pair * owned), jnp.bfloat16),
                pltpu.VMEM((all_rows, pair * owned), jnp.bfloat16),
                pltpu.VMEM((blocks, block_rows, pair * owned), jnp.float32),
            ],
        ),
        out_shape=[jax.ShapeDtypeStruct(shape, dtype) for shape in shapes for dtype in (jnp.bfloat16, jnp.float32)],
        compiler_params=_params(56),
        cost_estimate=_cost(0),
        name="grad_middle",
    )(place, *norms, *out_grads, *sides, *lows, *([w_up] * pair), *([w_down] * pair))


def halved(keep, received, axis, bit):
    pair = (2, keep.shape[0] // 2) + keep.shape[1:]
    keep, received = keep.reshape(pair), received.reshape(pair)
    mine = _bit_of(axis, bit)

    def half(index):
        return lax.dynamic_index_in_dim(keep, index, 0, False) + lax.dynamic_index_in_dim(
            received, index, 0, False
        ).astype(jnp.float32)

    return half(1 - mine).astype(jnp.bfloat16), half(mine)


def fast_body(
    patches, seg_lengths, w_query, w_key, w_value, w_out, w_up, w_down,
    norm1_gain, norm1_bias, norm2_gain, norm2_bias, out_grad,
):
    micro_count, tokens, features = patches.shape
    hidden = w_up.shape[1]
    row_count = micro_count * tokens
    blocks, shares = lax.axis_size("blk"), lax.axis_size("mb")
    head_dim = features // H
    slot = features // blocks
    rows = patches.reshape(row_count, features)
    dout = out_grad.reshape(row_count, features)
    gain_one, bias_one, gain_two, bias_two = (
        value.reshape(1, features) for value in (norm1_gain, norm1_bias, norm2_gain, norm2_bias)
    )

    def swap(values):
        return lax.all_to_all(values, "blk", split_axis=0, concat_axis=0, tiled=True)

    def by_micro(values):
        return values.reshape(blocks, micro_count, tokens, values.shape[-1])

    place = jnp.stack([lax.axis_index("blk"), lax.axis_index("mb")]).astype(jnp.int32)
    blk_bits = _bits(blocks)
    down_bits = [blk_bits[1], blk_bits[0], *blk_bits[2:]]
    each, owned, block_rows = features // (blocks * shares), hidden // (blocks * shares), features // blocks
    tie = lax.optimization_barrier

    def grown(values, bit):
        return jnp.concatenate([values, _paired(values, "blk", bit)], axis=0)

    def shared(values):
        over = _paired(values, "mb", 2)
        return [values, _paired(values, "mb", 1), over, _paired(over, "mb", 1)]

    send, units_first, units_last = project_call(
        rows, gain_one, bias_one, w_query, w_key, w_value, blocks, tokens
    )
    received = by_micro(swap(send))
    douts = shared(dout)
    units_last = grown(units_last, blk_bits[0])
    units_last, received, douts = tie((units_last, received, douts))
    units_first, received = tie((units_first, received))
    units_first = grown(units_first, blk_bits[-1])
    attended = attend_call(received, seg_lengths, head_dim).reshape(blocks, row_count, slot)
    attended, units_first = tie((attended, units_first))
    attended, units_first, units_last = tie((swap(attended), units_first, units_last))
    for bit in blk_bits[-2:0:-1]:
        units_first = grown(units_first, bit)
    for bit in blk_bits[:1:-1]:
        units_last = grown(units_last, bit)
    places_first = _ordered_low([*blk_bits[:0:-1], blk_bits[0]])
    places_last = _ordered_low([blk_bits[0], *blk_bits[:1:-1], blk_bits[1]])

    mixed, norm, side = mix_call(attended, rows, gain_two, bias_two, w_out)
    norm_peer, norm_over = _paired(norm, "mb", 1), _paired(norm, "mb", 2)
    layer_out, norm_grads = middle_call(norm, mixed, dout, w_up, w_down)
    norm_grads, units_first, units_last, norm_peer, norm_over, side = tie(
        (norm_grads, units_first, units_last, norm_peer, norm_over, side)
    )
    norms = [norm, norm_peer, norm_over, _paired(norm_over, "mb", 1)]
    sides = shared(side)
    units_first_peer = _paired(units_first, "blk", blk_bits[0])
    units_last_peer = _paired(units_last, "blk", blk_bits[1])
    mixed_grad, back, sums_two, *lows = middle_back_call(
        place, mixed, norm_grads, dout, gain_two, w_out, blocks, shares
    )
    grads = by_micro(swap(back))
    lows = [lows[0]] + [_paired(lows[share], "mb", share) for share in range(1, shares)]
    down_theirs, down_keep, up_theirs, up_keep = grad_middle_call(
        place, norms, douts, sides, lows, w_up, w_down, down_bits, blk_bits
    )
    down_theirs, down_keep = (value.reshape(-1, owned, features) for value in (down_theirs, down_keep))
    up_theirs, up_keep = (value.reshape(-1, block_rows, value.shape[-1]) for value in (up_theirs, up_keep))
    sums = {"down": (down_theirs, down_keep, down_bits), "up": (up_theirs, up_keep, blk_bits)}

    def sent(name, step):
        return _paired(sums[name][0], "blk", sums[name][2][step])

    def added(name, received, step):
        theirs, keep = halved(sums[name][1], received, "blk", sums[name][2][step])
        sums[name] = (theirs, keep, sums[name][2])

    down_received, up_received = sent("down", 0), sent("up", 0)
    grads, down_keep, units_first_peer, units_last_peer = tie(
        (grads, sums["down"][1], units_first_peer, units_last_peer)
    )
    sums["down"] = (sums["down"][0], down_keep, down_bits)
    made = attend_back_call(received, grads, seg_lengths, head_dim)
    returned = [swap(made[0])]
    added("down", down_received, 1)
    made, theirs = tie((made, sums["down"][0]))
    sums["down"] = (theirs, *sums["down"][1:])
    down_received = sent("down", 1)
    heads_send, heads_keep = grad_heads_call(
        place, (units_first, units_first_peer, units_last, units_last_peer), (places_first, places_last),
        made, gain_one, bias_one, sums_two, w_query, w_key, w_value, shares,
    )
    added("up", up_received, 1)
    returned[0], theirs, down_received, heads_send = tie((returned[0], sums["up"][0], down_received, heads_send))
    sums["up"] = (theirs, *sums["up"][1:])
    returned += [swap(tie((values, returned[0]))[0]) for values in made[1:]]
    up_received = sent("up", 1)
    flat = (-1,) + heads_keep.shape[2:]
    heads_received = _paired(heads_send, "mb", 1).reshape(flat)
    for step in range(2, len(blk_bits)):
        added("down", down_received, step)
        down_received = sent("down", step)
        added("up", up_received, step)
        up_received = sent("up", step)
    heads_theirs, heads_keep = halved(heads_keep.reshape(flat), heads_received, "mb", 2)
    heads_total = heads_keep + _paired(heads_theirs, "mb", 2).astype(jnp.float32)
    heads_total, returned = tie((heads_total, returned))
    heads_total = lax.all_to_all(heads_total.astype(jnp.bfloat16), "blk", split_axis=0, concat_axis=0, tiled=True)
    patches_grad = finish_call(returned, rows, mixed_grad, gain_one, w_query, w_key, w_value)
    patches_grad, heads_total, up_received = tie((patches_grad, heads_total, up_received))
    heads_total = heads_total.astype(jnp.float32)
    down_total = (sums["down"][1] + down_received.astype(jnp.float32))[0]
    wide_total = (sums["up"][1] + up_received.astype(jnp.float32))[0]
    wide_total = lax.all_to_all(
        wide_total.astype(jnp.bfloat16).reshape(shares, each, -1), "mb", split_axis=0, concat_axis=0, tiled=True
    ).astype(jnp.float32)
    places = len(blk_bits)
    up_total = wide_total[:, :, 0 : blocks * owned].reshape((shares, each) + (2,) * places + (owned,))
    order = [2 + down_bits.index(bit) for bit in reversed(blk_bits)]
    up_total = up_total.transpose((1, *order, 0, 2 + places)).reshape(each, hidden)
    out_total = wide_total[:, :, blocks * owned :].transpose(1, 0, 2).reshape(each, features)

    def of_heads(part):
        return heads_total[:, :, part * slot : (part + 1) * slot].transpose(1, 0, 2).reshape(each, features)

    sums = jnp.sum(heads_total[:, :, 3 * slot : 3 * slot + 4], axis=0)
    return (
        layer_out.reshape(patches.shape),
        patches_grad.reshape(patches.shape),
        of_heads(0),
        of_heads(1),
        of_heads(2),
        out_total,
        up_total,
        down_total,
        sums[:, 0],
        sums[:, 1],
        sums[:, 2],
        sums[:, 3],
    )


def solution(mesh):
    in_specs = (
        P("mb", "blk", None),
        P("mb", None),
        P(),
        P(),
        P(),
        P(),
        P(),
        P(),
        P(),
        P(),
        P(),
        P(),
        P("mb", "blk", None),
    )
    out_specs = (
        P("mb", "blk", None),
        P("mb", "blk", None),
        P(("blk", "mb"), None),
        P(("blk", "mb"), None),
        P(("blk", "mb"), None),
        P(("blk", "mb"), None),
        P(("blk", "mb"), None),
        P(("blk", "mb"), None),
        P(("blk", "mb")),
        P(("blk", "mb")),
        P(("blk", "mb")),
        P(("blk", "mb")),
    )
    blocks, shares = mesh.shape["blk"], mesh.shape["mb"]
    paired = blocks >= 4 and blocks & (blocks - 1) == 0 and shares == 4
    chosen_body = fast_body if paired and H % blocks == 0 else body
    return jax.shard_map(chosen_body, mesh=mesh, in_specs=in_specs, out_specs=out_specs, check_vma=False)
```

```python
import math

import jax
import jax.numpy as jnp
from jax import lax
from jax.experimental import pallas as pl
from jax.experimental.pallas import tpu as pltpu
from jax.sharding import PartitionSpec as P

H = 16
CHUNK = 8


epsilon = 1e-05
masked_score = -1e30


def layer_norm(values, norm_gain, norm_bias):
    center = values - jnp.mean(values, axis=-1, keepdims=True)
    variance = jnp.mean(center * center, axis=-1, keepdims=True)
    return center * lax.rsqrt(variance + epsilon) * norm_gain + norm_bias


def gelu_exact(values):
    return jax.nn.gelu(values, approximate=False)


def matmul(left_side, right_side):
    return jnp.dot(left_side, right_side, preferred_element_type=jnp.float32)


def contract_rows(left_side, right_side):
    return lax.dot_general(
        left_side, right_side, (((0,), (0,)), ((), ())), preferred_element_type=jnp.float32
    )


def contract_cols(left_side, right_side):
    return lax.dot_general(
        left_side, right_side, (((1,), (1,)), ((), ())), preferred_element_type=jnp.float32
    )


def segment_ids(lengths, positions):
    doc_ends = jnp.cumsum(lengths, axis=-1)
    return jnp.sum((positions[None, :, None] >= doc_ends[:, None, :]).astype(jnp.int32), axis=-1)


def masked_scores(query_piece, keys_all, query_docs, key_docs, score_scale):
    scores = contract_cols(query_piece, keys_all) * score_scale
    return jnp.where(query_docs[:, None] == key_docs[None, :], scores, masked_score)


def soft_rows(scores):
    row_max = jnp.max(scores, axis=-1, keepdims=True)
    exponent = jnp.exp(scores - row_max)
    return exponent / jnp.sum(exponent, axis=-1, keepdims=True)


def body(
    patches,
    seg_lengths,
    w_query,
    w_key,
    w_value,
    w_out,
    w_up,
    w_down,
    norm1_gain,
    norm1_bias,
    norm2_gain,
    norm2_bias,
    out_grad,
):
    micro_count, tokens, features = patches.shape
    row_count = micro_count * tokens
    blocks = lax.axis_size("blk")
    block_index = lax.axis_index("blk")
    head_count = H
    head_dim = features // head_count
    repeat = max(1, blocks // head_count)
    per_slot = max(1, head_count // blocks)
    groups = head_count // per_slot
    rows_part = tokens // repeat
    query_rows = blocks * rows_part
    seq_length = blocks * tokens
    item_count = micro_count * per_slot
    block_rows = min(512, query_rows)
    block_count = query_rows // block_rows
    slot_width = micro_count * per_slot * head_dim
    score_scale = 1.0 / math.sqrt(head_dim)
    doc_count = seg_lengths.shape[1]

    def query_layout(values):
        shaped = values.reshape(micro_count, repeat, rows_part, groups, per_slot * head_dim)
        return shaped.transpose(3, 1, 2, 0, 4).reshape(blocks, rows_part, slot_width)

    def key_layout(values):
        shaped = values.reshape(micro_count, tokens, groups, per_slot * head_dim).transpose(
            2, 1, 0, 3
        )
        shaped = jnp.broadcast_to(
            shaped[:, None], (groups, repeat, tokens, micro_count, per_slot * head_dim)
        )
        return shaped.reshape(blocks, tokens, slot_width)

    def token_layout(values):
        shaped = values.reshape(groups, repeat, rows_part, micro_count, per_slot * head_dim)
        return shaped.transpose(3, 1, 2, 0, 4).reshape(row_count, features)

    def key_sum(values):
        shaped = values.reshape(groups, repeat, tokens, micro_count, per_slot * head_dim).sum(
            axis=1
        )
        return shaped.transpose(2, 1, 0, 3).reshape(row_count, features)

    def to_items(received):
        row_total = received.shape[1]
        shaped = received.reshape(row_total, micro_count, per_slot, head_dim).transpose(1, 2, 0, 3)
        return shaped.reshape(item_count, row_total, head_dim)

    def from_items(values):
        row_total = values.shape[1]
        shaped = values.reshape(micro_count, per_slot, row_total, head_dim).transpose(2, 0, 1, 3)
        return shaped.reshape(1, row_total, slot_width)

    row_ids = jnp.arange(query_rows)
    query_pos = (
        row_ids // rows_part * tokens + block_index % repeat * rows_part + row_ids % rows_part
    )
    query_docs = jnp.repeat(segment_ids(seg_lengths, query_pos), per_slot, axis=0)
    key_docs = jnp.repeat(segment_ids(seg_lengths, jnp.arange(seq_length)), per_slot, axis=0)
    query_valid = (query_docs < doc_count).astype(jnp.float32)
    local_pos = block_index * tokens + jnp.arange(tokens)
    row_valid = (
        (segment_ids(seg_lengths, local_pos) < doc_count).astype(jnp.float32).reshape(row_count, 1)
    )

    def forward_item(operands):
        queries_item, keys_item, values_item, docs_item, key_docs_item = operands

        def forward_one_block(block_operands):
            query_piece, docs_piece = block_operands
            weights_soft = soft_rows(
                masked_scores(query_piece, keys_item, docs_piece, key_docs_item, score_scale)
            )
            return matmul(weights_soft.astype(jnp.bfloat16), values_item)

        outputs = lax.map(
            forward_one_block,
            (
                queries_item.reshape(block_count, block_rows, head_dim),
                docs_item.reshape(block_count, block_rows),
            ),
        )
        return outputs.reshape(query_rows, head_dim)

    def backward_item(operands):
        queries_item, keys_item, values_item, grads_item, docs_item, key_docs_item = operands

        def backward_one_block(totals, block_operands):
            key_total, value_total = totals
            query_piece, grad_piece, docs_piece = block_operands
            weights_soft = soft_rows(
                masked_scores(query_piece, keys_item, docs_piece, key_docs_item, score_scale)
            )
            weights_low = weights_soft.astype(jnp.bfloat16)
            weight_grads = contract_cols(grad_piece, values_item)
            row_inner = jnp.sum(weights_soft * weight_grads, axis=-1, keepdims=True)
            score_grads = (weights_soft * (weight_grads - row_inner)).astype(jnp.bfloat16)
            query_grad = matmul(score_grads, keys_item) * score_scale
            key_total = key_total + contract_rows(score_grads, query_piece) * score_scale
            value_total = value_total + contract_rows(weights_low, grad_piece)
            return ((key_total, value_total), query_grad)

        zero_block = jnp.zeros((seq_length, head_dim), jnp.float32)
        totals, query_grads = lax.scan(
            backward_one_block,
            (zero_block, zero_block),
            (
                queries_item.reshape(block_count, block_rows, head_dim),
                grads_item.reshape(block_count, block_rows, head_dim),
                docs_item.reshape(block_count, block_rows),
            ),
        )
        return (query_grads.reshape(query_rows, head_dim), totals[0], totals[1])

    inputs = patches.astype(jnp.float32).reshape(row_count, features)
    norm_one_full, norm_one_pull = jax.vjp(layer_norm, inputs, norm1_gain, norm1_bias)
    norm_one = norm_one_full.astype(jnp.bfloat16)
    queries = matmul(norm_one, w_query).astype(jnp.bfloat16)
    keys_proj = matmul(norm_one, w_key).astype(jnp.bfloat16)
    values_proj = matmul(norm_one, w_value).astype(jnp.bfloat16)
    query_send = query_layout(queries)
    key_send = key_layout(keys_proj)
    value_send = key_layout(values_proj)
    query_heads, key_heads, value_heads = (
        lax.all_to_all(query_send, "blk", split_axis=0, concat_axis=1, tiled=True),
        lax.all_to_all(key_send, "blk", split_axis=0, concat_axis=1, tiled=True),
        lax.all_to_all(value_send, "blk", split_axis=0, concat_axis=1, tiled=True),
    )
    query_items = to_items(query_heads)
    key_items = to_items(key_heads)
    value_items = to_items(value_heads)
    attended_items = lax.map(
        forward_item, (query_items, key_items, value_items, query_docs, key_docs)
    )
    attended_items = (attended_items * query_valid[:, :, None]).astype(jnp.bfloat16)
    attended = token_layout(
        lax.all_to_all(from_items(attended_items), "blk", split_axis=1, concat_axis=0, tiled=True)
    )
    mixed_rows = inputs + matmul(attended, w_out)
    norm_two_full, norm_two_pull = jax.vjp(layer_norm, mixed_rows, norm2_gain, norm2_bias)
    norm_two = norm_two_full.astype(jnp.bfloat16)
    upper_proj = matmul(norm_two, w_up)
    active_full, gelu_pull = jax.vjp(gelu_exact, upper_proj)
    active = active_full.astype(jnp.bfloat16)
    result = mixed_rows + matmul(active, w_down)
    layer_out = result.astype(jnp.bfloat16).reshape(micro_count, tokens, features)
    dout_low = out_grad.reshape(row_count, features)
    down_grad = contract_rows(active, dout_low)
    active_grad = contract_cols(dout_low, w_down)
    upper_grad = gelu_pull(active_grad)[0].astype(jnp.bfloat16)
    up_grad = contract_rows(norm_two, upper_grad)
    norm_two_grad = contract_cols(upper_grad, w_up)
    mixed_part, gain_two_grad, bias_two_grad = norm_two_pull(norm_two_grad)
    mixed_grad = dout_low.astype(jnp.float32) + mixed_part
    mixed_low = mixed_grad.astype(jnp.bfloat16)
    out_proj_grad = contract_rows(attended, mixed_low)
    attended_grad = (contract_cols(mixed_low, w_out) * row_valid).astype(jnp.bfloat16)
    grad_send = query_layout(attended_grad)
    query_again, key_again, value_again, grad_heads = (
        lax.all_to_all(query_send, "blk", split_axis=0, concat_axis=1, tiled=True),
        lax.all_to_all(key_send, "blk", split_axis=0, concat_axis=1, tiled=True),
        lax.all_to_all(value_send, "blk", split_axis=0, concat_axis=1, tiled=True),
        lax.all_to_all(grad_send, "blk", split_axis=0, concat_axis=1, tiled=True),
    )
    back_queries = to_items(query_again)
    back_keys = to_items(key_again)
    back_values = to_items(value_again)
    grad_items = to_items(grad_heads)
    query_grad_items, key_grad_items, value_grad_items = lax.map(
        backward_item, (back_queries, back_keys, back_values, grad_items, query_docs, key_docs)
    )
    query_back, key_back, value_back = (
        lax.all_to_all(
            from_items(query_grad_items).astype(jnp.bfloat16),
            "blk",
            split_axis=1,
            concat_axis=0,
            tiled=True,
        ).astype(jnp.float32),
        lax.all_to_all(
            from_items(key_grad_items).astype(jnp.bfloat16),
            "blk",
            split_axis=1,
            concat_axis=0,
            tiled=True,
        ).astype(jnp.float32),
        lax.all_to_all(
            from_items(value_grad_items).astype(jnp.bfloat16),
            "blk",
            split_axis=1,
            concat_axis=0,
            tiled=True,
        ).astype(jnp.float32),
    )
    query_grad = token_layout(query_back).astype(jnp.bfloat16)
    key_grad = key_sum(key_back).astype(jnp.bfloat16)
    value_grad = key_sum(value_back).astype(jnp.bfloat16)
    query_proj_grad = contract_rows(norm_one, query_grad)
    key_proj_grad = contract_rows(norm_one, key_grad)
    value_proj_grad = contract_rows(norm_one, value_grad)
    norm_one_grad = (
        contract_cols(query_grad, w_query)
        + contract_cols(key_grad, w_key)
        + contract_cols(value_grad, w_value)
    )
    input_part, gain_one_grad, bias_one_grad = norm_one_pull(norm_one_grad)
    patches_grad = (
        (mixed_grad + input_part).astype(jnp.bfloat16).reshape(micro_count, tokens, features)
    )
    gradients = (
        query_proj_grad,
        key_proj_grad,
        value_proj_grad,
        out_proj_grad,
        up_grad,
        down_grad,
        gain_one_grad,
        bias_one_grad,
        gain_two_grad,
        bias_two_grad,
    )
    summed = (
        lax.psum_scatter(gradients[0], ("blk", "mb"), scatter_dimension=0, tiled=True),
        lax.psum_scatter(gradients[1], ("blk", "mb"), scatter_dimension=0, tiled=True),
        lax.psum_scatter(gradients[2], ("blk", "mb"), scatter_dimension=0, tiled=True),
        lax.psum_scatter(gradients[3], ("blk", "mb"), scatter_dimension=0, tiled=True),
        lax.psum_scatter(gradients[4], ("blk", "mb"), scatter_dimension=0, tiled=True),
        lax.psum_scatter(gradients[5], ("blk", "mb"), scatter_dimension=0, tiled=True),
        lax.psum_scatter(gradients[6], ("blk", "mb"), scatter_dimension=0, tiled=True),
        lax.psum_scatter(gradients[7], ("blk", "mb"), scatter_dimension=0, tiled=True),
        lax.psum_scatter(gradients[8], ("blk", "mb"), scatter_dimension=0, tiled=True),
        lax.psum_scatter(gradients[9], ("blk", "mb"), scatter_dimension=0, tiled=True),
    )
    return (
        layer_out,
        patches_grad,
        summed[0],
        summed[1],
        summed[2],
        summed[3],
        summed[4],
        summed[5],
        summed[6],
        summed[7],
        summed[8],
        summed[9],
    )


def _normalize(values):
    center = values - jnp.mean(values, axis=-1, keepdims=True)
    variance = jnp.mean(center * center, axis=-1, keepdims=True)
    inverse = lax.rsqrt(variance + epsilon)
    return center * inverse, inverse


def _normalize_back(grads, gain, unit, inverse):
    scaled = grads * gain
    mean_scaled = jnp.mean(scaled, axis=-1, keepdims=True)
    mean_product = jnp.mean(scaled * unit, axis=-1, keepdims=True)
    return (scaled - mean_scaled - unit * mean_product) * inverse


def _doc_ids(lengths_ref, micro, doc_count, positions):
    end = jnp.int32(0)
    ids = jnp.zeros_like(positions)
    for doc in range(doc_count):
        end = end + lengths_ref[micro, doc]
        ids = ids + (positions >= end).astype(jnp.int32)
    return ids


def _params(mib):
    return pltpu.CompilerParams(vmem_limit_bytes=mib << 20)


def _cost(microseconds):
    return pl.CostEstimate(flops=int(microseconds * 1e9) + 1, bytes_accessed=1, transcendentals=0)


def project_call(rows, gain, bias, w_query, w_key, w_value, blocks, tokens):
    row_count, features = rows.shape
    slot = features // blocks
    per_step = max(1, min(blocks, 256 // slot))
    wide = slot * per_step

    def kernel(rows_ref, gain_ref, bias_ref, wq_ref, wk_ref, wv_ref, send_ref, *refs):
        unit_refs, norm_ref = refs[:-1], refs[-1]


        @pl.when(pl.program_id(0) == 0)
        def _():
            unit, _unused = _normalize(rows_ref[...].astype(jnp.float32))
            for micro, unit_ref in enumerate(unit_refs):
                unit_ref[...] = unit[micro * tokens : (micro + 1) * tokens].astype(jnp.bfloat16)
            norm_ref[...] = (unit * gain_ref[...] + bias_ref[...]).astype(jnp.bfloat16)

        for part, weight_ref in enumerate((wq_ref, wk_ref, wv_ref)):
            made = matmul(norm_ref[...], weight_ref[...]).astype(jnp.bfloat16)
            for piece in range(per_step):
                send_ref[piece, :, part * slot : (part + 1) * slot] = made[
                    :, piece * slot : (piece + 1) * slot
                ]

    whole = pl.BlockSpec((row_count, features), lambda i: (0, 0))
    vector = pl.BlockSpec((1, features), lambda i: (0, 0))
    columns = pl.BlockSpec((features, wide), lambda i: (0, i))
    return pl.pallas_call(
        kernel,
        grid=(blocks // per_step,),
        in_specs=[whole, vector, vector, columns, columns, columns],
        out_specs=[pl.BlockSpec((per_step, row_count, 3 * slot), lambda i: (i, 0, 0))]
        + [pl.BlockSpec((tokens, features), lambda i: (0, 0))] * (row_count // tokens),
        out_shape=[jax.ShapeDtypeStruct((blocks, row_count, 3 * slot), jnp.bfloat16)]
        + [jax.ShapeDtypeStruct((tokens, features), jnp.bfloat16)] * (row_count // tokens),
        scratch_shapes=[pltpu.VMEM((row_count, features), jnp.bfloat16)],
        compiler_params=_params(60),
        cost_estimate=_cost(6),
        name="project",
    )(rows, gain, bias, w_query, w_key, w_value)


def _head_masks(slot, head_dim, dtype):
    lanes = lax.broadcasted_iota(jnp.int32, (1, slot), 1)
    return [(lanes // head_dim == head).astype(dtype) for head in range(slot // head_dim)]


def _key_range(lengths_ref, micro, doc_count, first_row, last_row, seq):
    low, high, end = jnp.int32(0), jnp.int32(seq), jnp.int32(0)
    for doc in range(doc_count):
        end = end + lengths_ref[micro, doc]
        low = jnp.where(end <= first_row, jnp.maximum(low, end), low)
        high = jnp.where(end >= last_row, jnp.minimum(high, end), high)
    return low, high


def _by_key_range(lengths_ref, micro, doc_count, step, rows, blocks, tokens, compute):
    low, high = _key_range(lengths_ref, micro, doc_count, step * rows, (step + 1) * rows, blocks * tokens)
    half = blocks // 2
    in_low, in_high = high <= half * tokens, low >= half * tokens

    @pl.when(in_low | in_high)
    def _():
        compute(jnp.where(in_low, 0, half), half)

    @pl.when(jnp.logical_not(in_low | in_high))
    def _():
        compute(0, blocks)


def attend_call(received, lengths, head_dim):
    blocks, micro_count, tokens, width = received.shape
    slot = width // 3
    doc_count = lengths.shape[1]
    step_blocks = max(1, min(blocks, 256 // tokens))
    rows = step_blocks * tokens
    scale = 1.0 / math.sqrt(head_dim)

    def kernel(lengths_ref, data_ref, out_ref, exact_ref, log_ref):
        micro = pl.program_id(0)
        step = pl.program_id(1)
        row_docs = _doc_ids(
            lengths_ref, micro, doc_count, lax.broadcasted_iota(jnp.int32, (rows, 1), 0) + step * rows
        )
        queries = data_ref[pl.ds(step * step_blocks, step_blocks), 0, :, 0:slot].reshape(rows, slot) * scale

        def compute(first, count):
            seq = count * tokens
            key_docs = _doc_ids(
                lengths_ref, micro, doc_count, lax.broadcasted_iota(jnp.int32, (1, seq), 1) + first * tokens
            )
            same = row_docs == key_docs
            keys = data_ref[pl.ds(first, count), 0, :, slot : 2 * slot].reshape(seq, slot)
            values = data_ref[pl.ds(first, count), 0, :, 2 * slot : 3 * slot].reshape(seq, slot)
            total = jnp.zeros((rows, slot), jnp.float32)
            logs = jnp.zeros((rows, 128), jnp.float32)
            lanes = lax.broadcasted_iota(jnp.int32, (1, 128), 1)
            for head, (mask, mask_wide) in enumerate(
                zip(_head_masks(slot, head_dim, jnp.bfloat16), _head_masks(slot, head_dim, jnp.float32))
            ):
                scores = jnp.where(same, contract_cols(queries * mask, keys), masked_score)
                most = jnp.max(scores, axis=-1, keepdims=True)
                exponent = jnp.exp(scores - most)
                exponent_sum = jnp.sum(exponent, axis=-1, keepdims=True)
                share = 1.0 / exponent_sum
                logs = jnp.where(lanes == head, most + jnp.log(exponent_sum), logs)
                total = total + matmul(exponent.astype(jnp.bfloat16), values) * (share * mask_wide)
            total = jnp.where(row_docs < doc_count, total, 0.0)
            out_ref[...] = total.astype(jnp.bfloat16).reshape(step_blocks, 1, tokens, slot)
            exact_ref[...] = total.reshape(step_blocks, 1, tokens, slot)
            log_ref[0] = logs.T[0:8, :]

        _by_key_range(lengths_ref, micro, doc_count, step, rows, blocks, tokens, compute)

    return pl.pallas_call(
        kernel,
        grid=(micro_count, blocks // step_blocks),
        in_specs=[
            pl.BlockSpec(memory_space=pltpu.SMEM),
            pl.BlockSpec((blocks, 1, tokens, width), lambda m, s: (0, m, 0, 0)),
        ],
        out_specs=[
            pl.BlockSpec((step_blocks, 1, tokens, slot), lambda m, s: (s, m, 0, 0)),
            pl.BlockSpec((step_blocks, 1, tokens, slot), lambda m, s: (s, m, 0, 0)),
            pl.BlockSpec((1, 8, rows), lambda m, s: (m, 0, s)),
        ],
        out_shape=[
            jax.ShapeDtypeStruct((blocks, micro_count, tokens, slot), jnp.bfloat16),
            jax.ShapeDtypeStruct((blocks, micro_count, tokens, slot), jnp.float32),
            jax.ShapeDtypeStruct((micro_count, 8, blocks * tokens), jnp.float32),
        ],
        compiler_params=_params(32),
        cost_estimate=_cost(11),
        name="attend",
    )(lengths, received)


def attend_back_call(received, grads, attended, logs, lengths, head_dim):
    blocks, micro_count, tokens, width = received.shape
    slot = width // 3
    doc_count = lengths.shape[1]
    step_blocks = max(1, min(blocks, 256 // tokens))
    rows = step_blocks * tokens
    steps = blocks // step_blocks
    scale = 1.0 / math.sqrt(head_dim)

    def kernel(lengths_ref, data_ref, grads_ref, att_ref, log_ref, *refs):
        out_refs, (key_total, value_total, turned) = refs[:micro_count], refs[micro_count:]
        micro = pl.program_id(0)
        step = pl.program_id(1)

        @pl.when(step == 0)
        def _():
            key_total[...] = jnp.zeros_like(key_total)
            value_total[...] = jnp.zeros_like(value_total)
            for block in range(blocks):
                turned[block] = data_ref[block, 0, :, slot : 2 * slot].T

        row_docs = _doc_ids(
            lengths_ref, micro, doc_count, lax.broadcasted_iota(jnp.int32, (1, rows), 1) + step * rows
        )
        column_docs = _doc_ids(
            lengths_ref, micro, doc_count, lax.broadcasted_iota(jnp.int32, (rows, 1), 0) + step * rows
        )
        queries = data_ref[pl.ds(step * step_blocks, step_blocks), 0, :, 0:slot].reshape(rows, slot) * scale
        out_grads = grads_ref[...].reshape(rows, slot)
        out_grads = out_grads * (column_docs < doc_count).astype(jnp.float32).astype(jnp.bfloat16)

        inner = (out_grads.astype(jnp.float32) * att_ref[...].reshape(rows, slot)).T

        def compute(first, count):
            chunk = min(CHUNK, count)
            query_parts = [jnp.zeros((head_dim, rows), jnp.float32) for _ in range(slot // head_dim)]
            masks = _head_masks(slot, head_dim, jnp.bfloat16)
            for at in range(0, count, chunk):
                seq = chunk * tokens
                key_docs = _doc_ids(
                    lengths_ref,
                    micro,
                    doc_count,
                    lax.broadcasted_iota(jnp.int32, (seq, 1), 0) + (first + at) * tokens,
                )
                same = row_docs == key_docs
                keys = data_ref[pl.ds(first + at, chunk), 0, :, slot : 2 * slot].reshape(seq, slot)
                values = data_ref[pl.ds(first + at, chunk), 0, :, 2 * slot : 3 * slot].reshape(seq, slot)
                keys_turned = jnp.concatenate([turned[first + at + other] for other in range(chunk)], axis=1)
                key_made = jnp.zeros((seq, slot), jnp.float32)
                value_made = jnp.zeros((seq, slot), jnp.float32)
                for head, mask in enumerate(masks):
                    lanes = slice(head * head_dim, (head + 1) * head_dim)
                    queries_head, grads_head = queries * mask, out_grads * mask
                    scores = jnp.where(same, contract_cols(keys, queries_head), masked_score)
                    probs = jnp.exp(scores - log_ref[0, head : head + 1, :])
                    prob_grads = contract_cols(values, grads_head)
                    head_inner = jnp.sum(inner[lanes], axis=0, keepdims=True)
                    score_grads = (probs * (prob_grads - head_inner)).astype(jnp.bfloat16)
                    value_made = value_made + matmul(probs.astype(jnp.bfloat16), grads_head)
                    key_made = key_made + matmul(score_grads, queries_head)
                    query_parts[head] = query_parts[head] + matmul(keys_turned[lanes], score_grads)
                to = pl.ds(pl.multiple_of((first + at) * tokens, tokens), seq)
                key_total[to, :] += key_made
                value_total[to, :] += value_made
            query_grads = (jnp.concatenate(query_parts, axis=0).T * scale).astype(jnp.bfloat16).reshape(step_blocks, tokens, slot)
            for at, out_ref in enumerate(out_refs):

                @pl.when(micro == at)
                def _():
                    out_ref[pl.ds(step * step_blocks, step_blocks), :, 0:slot] = query_grads

        _by_key_range(lengths_ref, micro, doc_count, step, rows, blocks, tokens, compute)

        for at, out_ref in enumerate(out_refs):

            @pl.when((step == steps - 1) & (micro == at))
            def _():
                out_ref[:, :, slot : 2 * slot] = key_total[...].astype(jnp.bfloat16).reshape(blocks, tokens, slot)
                out_ref[:, :, 2 * slot :] = value_total[...].astype(jnp.bfloat16).reshape(blocks, tokens, slot)

    return pl.pallas_call(
        kernel,
        grid=(micro_count, steps),
        in_specs=[
            pl.BlockSpec(memory_space=pltpu.SMEM),
            pl.BlockSpec((blocks, 1, tokens, width), lambda m, s: (0, m, 0, 0)),
            pl.BlockSpec((step_blocks, 1, tokens, slot), lambda m, s: (s, m, 0, 0)),
            pl.BlockSpec((step_blocks, 1, tokens, slot), lambda m, s: (s, m, 0, 0)),
            pl.BlockSpec((1, 8, rows), lambda m, s: (m, 0, s)),
        ],
        out_specs=[pl.BlockSpec((blocks, tokens, width), lambda m, s: (0, 0, 0))] * micro_count,
        out_shape=[jax.ShapeDtypeStruct((blocks, tokens, width), jnp.bfloat16)] * micro_count,
        scratch_shapes=[pltpu.VMEM((blocks * tokens, slot), jnp.float32)] * 2
        + [pltpu.VMEM((blocks, slot, tokens), jnp.bfloat16)],
        compiler_params=_params(60),
        cost_estimate=_cost(3),
        name="attend_back",
    )(lengths, received, grads, attended, logs)


def _fixed(*shape):
    return pl.BlockSpec(shape, lambda *_unused: (0,) * len(shape))


def mix_call(attended, rows, gain, bias, w_out):
    blocks, row_count, slot = attended.shape
    features = rows.shape[1]

    def kernel(att_ref, rows_ref, gain_ref, bias_ref, wo_ref, mixed_ref, both_ref):
        for block in range(blocks):
            both_ref[1, :, block * slot : (block + 1) * slot] = att_ref[block]
        value = rows_ref[...].astype(jnp.float32) + matmul(both_ref[1], wo_ref[...])
        mixed_ref[...] = value
        unit, _unused = _normalize(value)
        both_ref[0] = (unit * gain_ref[...] + bias_ref[...]).astype(jnp.bfloat16)

    rows_spec, vector = _fixed(row_count, features), _fixed(1, features)
    return pl.pallas_call(
        kernel,
        grid=(1,),
        in_specs=[_fixed(blocks, row_count, slot), rows_spec, vector, vector, _fixed(features, features)],
        out_specs=[rows_spec, _fixed(2, row_count, features)],
        out_shape=[
            jax.ShapeDtypeStruct((row_count, features), jnp.float32),
            jax.ShapeDtypeStruct((2, row_count, features), jnp.bfloat16),
        ],
        compiler_params=_params(24),
        cost_estimate=_cost(4),
        name="mix",
    )(attended, rows, gain, bias, w_out)


def _hidden_parts(norm, out_grad, up_columns, down_rows):
    upper = matmul(norm, up_columns)
    active_grad = contract_cols(out_grad, down_rows)
    half = (1.0 + lax.erf(upper * (1.0 / math.sqrt(2.0)))) * 0.5
    slope = half + upper * jnp.exp(upper * upper * -0.5) * (1.0 / math.sqrt(2.0 * math.pi))
    return (upper * half).astype(jnp.bfloat16), (active_grad * slope).astype(jnp.bfloat16)


def middle_call(place, both, mixed, out_grad, gain, w_out, w_up, w_down, blocks, shares):
    row_count, features = mixed.shape
    hidden = w_up.shape[1]
    wide = min(1024, hidden)
    sub = min(512, wide)
    steps = hidden // wide
    slot, part = features // blocks, features // shares

    def kernel(place_ref, norm_ref, mixed_ref, grad_ref, gain_ref, wo_ref, wu_ref, wd_ref, *refs):
        out_ref, mixed_grad_ref, back_ref, sums_ref = refs[:4]
        low_refs, (total, grad_total, active_all, upper_all, low_all) = refs[4 : 4 + shares], refs[4 + shares :]
        step = pl.program_id(0)

        @pl.when(step == 0)
        def _():
            total[...] = mixed_ref[...]
            grad_total[...] = jnp.zeros_like(grad_total)

        for chunk in range(0, wide, sub):
            active, upper_grad = _hidden_parts(
                norm_ref[0], grad_ref[...], wu_ref[:, chunk : chunk + sub], wd_ref[chunk : chunk + sub, :]
            )
            active_all[:, chunk : chunk + sub] = active
            upper_all[:, chunk : chunk + sub] = upper_grad
        total[...] += matmul(active_all[...], wd_ref[...])
        grad_total[...] += contract_cols(upper_all[...], wu_ref[...])

        @pl.when(step == steps - 1)
        def _():
            out_ref[...] = total[...].astype(jnp.bfloat16)
            unit, inverse = _normalize(mixed_ref[...])
            grads = grad_total[...]
            sums_ref[0:1, :] = jnp.sum(grads * unit, axis=0, keepdims=True)
            sums_ref[1:2, :] = jnp.sum(grads, axis=0, keepdims=True)
            mixed_grad = grad_ref[...].astype(jnp.float32) + _normalize_back(grads, gain_ref[...], unit, inverse)
            mixed_grad_ref[...] = mixed_grad
            low = mixed_grad.astype(jnp.bfloat16)
            low_all[...] = low
            for share, low_ref in enumerate(low_refs):
                low_ref[...] = low_all[:, pl.ds(pl.multiple_of((place_ref[2] ^ share) * part, 128), part)]
            back = contract_cols(low, wo_ref[...]).astype(jnp.bfloat16)
            for block in range(blocks):
                back_ref[block] = back[:, block * slot : (block + 1) * slot]

    rows_spec = _fixed(row_count, features)
    return pl.pallas_call(
        kernel,
        grid_spec=pltpu.PrefetchScalarGridSpec(
            num_scalar_prefetch=1,
            grid=(steps,),
            in_specs=[
                _fixed(1, row_count, features),
                rows_spec,
                rows_spec,
                _fixed(1, features),
                _fixed(features, features),
                pl.BlockSpec((features, wide), lambda i, place: (0, i)),
                pl.BlockSpec((wide, features), lambda i, place: (i, 0)),
            ],
            out_specs=[rows_spec, rows_spec, _fixed(blocks, row_count, slot), _fixed(2, features)]
            + [_fixed(row_count, part)] * shares,
            scratch_shapes=[
                pltpu.VMEM((row_count, features), jnp.float32),
                pltpu.VMEM((row_count, features), jnp.float32),
                pltpu.VMEM((row_count, wide), jnp.bfloat16),
                pltpu.VMEM((row_count, wide), jnp.bfloat16),
                pltpu.VMEM((row_count, features), jnp.bfloat16),
            ],
        ),
        out_shape=[
            jax.ShapeDtypeStruct((row_count, features), jnp.bfloat16),
            jax.ShapeDtypeStruct((row_count, features), jnp.float32),
            jax.ShapeDtypeStruct((blocks, row_count, slot), jnp.bfloat16),
            jax.ShapeDtypeStruct((2, features), jnp.float32),
        ]
        + [jax.ShapeDtypeStruct((row_count, part), jnp.bfloat16)] * shares,
        compiler_params=_params(44),
        cost_estimate=_cost(20),
        name="middle",
    )(place, both, mixed, out_grad, gain, w_out, w_up, w_down)


def finish_call(received, rows, mixed_grad, gain, w_query, w_key, w_value):
    micro_count = len(received)
    blocks, tokens, width = received[0].shape
    slot = width // 3
    row_count, features = rows.shape
    per_step = max(1, min(blocks, 256 // slot))
    wide = slot * per_step
    steps = blocks // per_step

    def kernel(*refs):
        data_refs, refs = refs[:micro_count], refs[micro_count:]
        rows_ref, mixed_ref, gain_ref, wq_ref, wk_ref, wv_ref, out_ref, total, side = refs
        step = pl.program_id(0)

        @pl.when(step == 0)
        def _():
            total[...] = jnp.zeros_like(total)

        for part, weight_ref in enumerate((wq_ref, wk_ref, wv_ref)):
            for micro, data_ref in enumerate(data_refs):
                for piece in range(per_step):
                    side[part, micro * tokens : (micro + 1) * tokens, piece * slot : (piece + 1) * slot] = data_ref[
                        piece, :, part * slot : (part + 1) * slot
                    ]
            total[...] += contract_cols(side[part], weight_ref[...])

        @pl.when(step == steps - 1)
        def _():
            unit, inverse = _normalize(rows_ref[...].astype(jnp.float32))
            out_ref[...] = (
                mixed_ref[...] + _normalize_back(total[...], gain_ref[...], unit, inverse)
            ).astype(jnp.bfloat16)

    def fixed(*shape):
        return pl.BlockSpec(shape, lambda i: (0,) * len(shape))

    columns = pl.BlockSpec((features, wide), lambda i: (0, i))
    return pl.pallas_call(
        kernel,
        grid=(steps,),
        in_specs=[pl.BlockSpec((per_step, tokens, width), lambda i: (i, 0, 0))] * micro_count
        + [
            fixed(row_count, features),
            fixed(row_count, features),
            fixed(1, features),
            columns,
            columns,
            columns,
        ],
        out_specs=fixed(row_count, features),
        out_shape=jax.ShapeDtypeStruct((row_count, features), jnp.bfloat16),
        scratch_shapes=[
            pltpu.VMEM((row_count, features), jnp.float32),
            pltpu.VMEM((3, row_count, wide), jnp.bfloat16),
        ],
        compiler_params=_params(60),
        cost_estimate=_cost(20),
        name="finish",
    )(*received, rows, mixed_grad, gain, w_query, w_key, w_value)


def grad_heads_call(place, units, places, made, gain, bias, sums, w_query, w_key, w_value, shares):
    micro_count = len(made)
    blocks, tokens, width = made[0].shape
    slot = width // 3
    features = gain.shape[1]
    group = features // (blocks * shares)
    full = width + 128
    kept = blocks * (shares // 2) * group

    def kernel(place_ref, *refs):
        unit_refs, refs = refs[: 2 * micro_count], refs[2 * micro_count :]
        made_refs, refs = refs[:micro_count], refs[micro_count:]
        gain_ref, bias_ref, sums_ref, wq_ref, wk_ref, wv_ref, send_ref, keep_ref, spread, ordered = refs
        product = jnp.zeros((features, width), jnp.float32)
        column_sum = jnp.zeros((1, width), jnp.float32)
        for micro, made_ref in enumerate(made_refs):
            for at, relative in enumerate(places[micro]):
                ordered[at * tokens : (at + 1) * tokens, :] = made_ref[place_ref[0] ^ relative]
            half = blocks * tokens // 2
            for side in range(2):
                rows = ordered[side * half : (side + 1) * half, :]
                product = product + contract_rows(unit_refs[2 * micro + side][...], rows)
                column_sum = column_sum + jnp.sum(rows.astype(jnp.float32), axis=0, keepdims=True)
        vectors = jnp.concatenate(
            [gain_ref[...], bias_ref[...], sums_ref[...], jnp.zeros((124, features), jnp.float32)], axis=0
        ).T
        total = vectors[:, 0:1] * product + vectors[:, 1:2] * column_sum
        weights = jnp.concatenate([wq_ref[...], wk_ref[...], wv_ref[...]], axis=1).astype(jnp.float32)
        gain_sum = jnp.sum(weights * product, axis=1, keepdims=True)
        bias_sum = jnp.sum(weights * column_sum, axis=1, keepdims=True)
        lanes = lax.broadcasted_iota(jnp.int32, (1, 128), 1)
        norms = jnp.where(
            lanes == 0, gain_sum, jnp.where(lanes == 1, bias_sum, jnp.where(lanes < 4, vectors, 0.0))
        )
        spread[:, :, :, 0:width] = total.reshape(blocks, shares, group, width)
        spread[:, :, :, width:] = norms.reshape(blocks, shares, group, 128)
        core = place_ref[1] % 2
        for which, out_ref in enumerate((send_ref, keep_ref)):
            for share in range(0, shares, 2):
                for block in range(blocks):
                    out_ref[share // 2, block] = spread[block, share + (core if which else 1 - core)].astype(out_ref.dtype)

    def fixed(*shape):
        return pl.BlockSpec(shape, lambda i, place: (0,) * len(shape))

    columns = pl.BlockSpec((features, slot), lambda i, place: (0, place[0]))
    out = (shares // 2, blocks, group, full)
    return pl.pallas_call(
        kernel,
        grid_spec=pltpu.PrefetchScalarGridSpec(
            num_scalar_prefetch=1,
            grid=(1,),
            in_specs=[fixed(*part.shape) for part in (*units, *made)]
            + [fixed(1, features), fixed(1, features), fixed(2, features), columns, columns, columns],
            out_specs=[fixed(*out), fixed(*out)],
            scratch_shapes=[
                pltpu.VMEM((blocks, shares, group, full), jnp.float32),
                pltpu.VMEM((blocks * tokens, width), jnp.bfloat16),
            ],
        ),
        out_shape=[jax.ShapeDtypeStruct(out, jnp.bfloat16), jax.ShapeDtypeStruct(out, jnp.float32)],
        compiler_params=_params(60),
        cost_estimate=_cost(20),
        name="grad_heads",
    )(place, *units, *made, gain, bias, sums, w_query, w_key, w_value)


def assemble_call(place, parts, down_steps, blocks, owned):
    shares = len(parts)
    rows, width = parts[0].shape
    part = width - blocks * owned

    def kernel(place_ref, *refs):
        part_refs, (up_ref, out_ref) = refs[:shares], refs[shares:]
        for other, part_ref in enumerate(part_refs):
            share = place_ref[2] ^ other
            for at, block in enumerate(_ordered([_owner_stride(*step, shares) for step in down_steps])):
                to = pl.multiple_of((block + share % 2 + share // 2 * shares) * owned, 128)
                up_ref[:, pl.ds(to, owned)] = part_ref[:, at * owned : (at + 1) * owned].astype(jnp.float32)
            out_ref[:, pl.ds(pl.multiple_of(share * part, 128), part)] = part_ref[:, blocks * owned :].astype(jnp.float32)

    return pl.pallas_call(
        kernel,
        grid_spec=pltpu.PrefetchScalarGridSpec(
            num_scalar_prefetch=1,
            grid=(1,),
            in_specs=[_fixed(rows, width)] * shares,
            out_specs=[_fixed(rows, blocks * shares * owned), _fixed(rows, shares * part)],
        ),
        out_shape=[
            jax.ShapeDtypeStruct((rows, blocks * shares * owned), jnp.float32),
            jax.ShapeDtypeStruct((rows, shares * part), jnp.float32),
        ],
        compiler_params=_params(8),
        cost_estimate=_cost(0),
        name="assemble",
    )(place, *parts)


def _bits(count):
    return [1 << place for place in range(count.bit_length() - 1)]


def _ordered(bits):
    places = [0]
    for bit in bits:
        places = [at + step for at in places for step in (0, bit)]
    return places


def _ordered_low(bits):
    places = [0]
    for bit in bits:
        places = places + [at + bit for at in places]
    return places


def _paired(values, axis, bit):
    count = lax.axis_size(axis)
    return lax.ppermute(values, axis, [(i, i ^ bit) for i in range(count)])


def _bit_of(axis, bit):
    return (lax.axis_index(axis) // bit) % 2


def _mesh_bit(place, step):
    axis, bit = step
    return place[("blk", "mb").index(axis)] // bit % 2


def _owner_stride(axis, bit, shares):
    return bit * shares if axis == "blk" else bit


def _share_places(shares):
    return [0, 1, shares, shares + 1]


def _place_at(bits, step):
    places = _ordered(bits)
    at = jnp.int32(places[0])
    for other in range(1, len(places)):
        at = jnp.where(step == other, places[other], at)
    return at


def grad_middle_call(place, boths, out_grads, lows, w_up, w_down, down_steps, up_steps):
    shares = len(boths)
    _, row_count, features = boths[0].shape
    all_rows = shares * row_count
    hidden = w_up.shape[1]
    blocks = 1 << len(up_steps)
    owned, each = hidden // (blocks * shares), features // (blocks * shares)
    down_places = [_owner_stride(*step, shares) for step in down_steps]
    up_places = [_owner_stride(*step, shares) for step in up_steps]
    share_places = _share_places(shares)
    part = lows[0].shape[1]
    half = blocks // 2
    pair = min(2, half)
    half_steps = half // pair
    sub = min(2, shares)

    def kernel(place_ref, *refs):
        groups, refs = [refs[at * shares : (at + 1) * shares] for at in range(3)], refs[3 * shares :]
        up_refs, down_refs, refs = refs[:pair], refs[pair : 2 * pair], refs[2 * pair :]
        down_send, down_keep, up_send, up_keep, norm_all, norm_turned, grad_all, active_all, upper_all, up_all = refs
        step = pl.program_id(0)
        mine = _mesh_bit(place_ref, up_steps[0])

        def spread():
            for at, block in enumerate(_ordered(up_places[1:])):
                for share, other in enumerate(share_places):
                    rows = slice((at * shares + share) * each, (at * shares + share + 1) * each)
                    up_send[rows, :] = up_all[block + other + up_places[0] * (1 - mine)].astype(jnp.bfloat16)
                    up_keep[rows, :] = up_all[block + other + up_places[0] * mine]

        @pl.when(step == 0)
        def _():
            for at in range(shares):
                rows = slice(at * row_count, (at + 1) * row_count)
                norm_all[rows, :] = groups[0][at][0]
                norm_turned[:, rows] = groups[0][at][0].T
                grad_all[rows, :] = groups[1][at][...]

        @pl.when(step < 2 * half_steps)
        def _():
            up_columns = jnp.concatenate([ref[...] for ref in up_refs], axis=1)
            down_rows = jnp.concatenate([ref[...] for ref in down_refs], axis=0)
            for at in range(0, all_rows, all_rows // sub):
                rows = slice(at, at + all_rows // sub)
                active_all[rows, :], upper_all[rows, :] = _hidden_parts(
                    norm_all[rows, :], grad_all[rows, :], up_columns, down_rows
                )
            down_made = contract_rows(active_all[...], grad_all[...])

            @pl.when(step < half_steps)
            def _():
                down_send[...] = down_made.astype(jnp.bfloat16)

            @pl.when(step >= half_steps)
            def _():
                down_keep[...] = down_made

            up_all[...] = matmul(norm_turned[...], upper_all[...]).reshape(blocks * shares, each, pair * owned)
            spread()

        @pl.when(step == 2 * half_steps)
        def _():
            made = jnp.zeros((features, part), jnp.float32)
            for both_ref, low_ref in zip(groups[0], groups[2]):
                made = made + contract_rows(both_ref[1], low_ref[...])
            up_all[...] = made.reshape(blocks * shares, each, part)
            spread()

    def first_bit(i, place):
        return (_mesh_bit(place, down_steps[0]) + 1 + jnp.minimum(i, 2 * half_steps - 1) // half_steps) % 2

    def unit_block(i, place, at):
        inner = _place_at(down_places[1:], jnp.minimum(i, 2 * half_steps - 1) % half_steps * pair + at)
        return inner + down_places[0] * first_bit(i, place) + place[0] % 2 * shares + place[1] % 2

    ups = [
        pl.BlockSpec((features, owned), lambda i, place, at=at: (0, unit_block(i, place, at))) for at in range(pair)
    ]
    downs = [
        pl.BlockSpec((owned, features), lambda i, place, at=at: (unit_block(i, place, at), 0)) for at in range(pair)
    ]
    def up_block(i, place):
        return (0, jnp.where(i == 2 * half_steps, i, first_bit(i, place) * half_steps + i % half_steps))

    up_out = pl.BlockSpec((features // 2, pair * owned), up_block)
    shapes = [(half * owned, features), (features // 2, blocks * owned + part)]
    return pl.pallas_call(
        kernel,
        grid_spec=pltpu.PrefetchScalarGridSpec(
            num_scalar_prefetch=1,
            grid=(2 * half_steps + 1,),
            in_specs=[_fixed(2, row_count, features)] * shares
            + [_fixed(row_count, features)] * shares
            + [_fixed(row_count, part)] * shares
            + ups
            + downs,
            out_specs=[
                pl.BlockSpec((pair * owned, features), lambda i, place: (jnp.minimum(i, half_steps - 1), 0)),
                pl.BlockSpec((pair * owned, features), lambda i, place: (jnp.clip(i - half_steps, 0, half_steps - 1), 0)),
                up_out,
                up_out,
            ],
            scratch_shapes=[
                pltpu.VMEM((all_rows, features), jnp.bfloat16),
                pltpu.VMEM((features, all_rows), jnp.bfloat16),
                pltpu.VMEM((all_rows, features), jnp.bfloat16),
                pltpu.VMEM((all_rows, pair * owned), jnp.bfloat16),
                pltpu.VMEM((all_rows, pair * owned), jnp.bfloat16),
                pltpu.VMEM((blocks * shares, each, pair * owned), jnp.float32),
            ],
        ),
        out_shape=[jax.ShapeDtypeStruct(shape, dtype) for shape in shapes for dtype in (jnp.bfloat16, jnp.float32)],
        compiler_params=_params(60),
        cost_estimate=_cost(20),
        name="grad_middle",
    )(place, *boths, *out_grads, *lows, *([w_up] * pair), *([w_down] * pair))


def halve_call(place, keep, received, step, cost):
    count, rows, columns = keep.shape
    half = count // 2

    def kernel(place_ref, keep_theirs, keep_mine, got_theirs, got_mine, theirs_ref, mine_ref):
        theirs_ref[...] = (keep_theirs[...] + got_theirs[...].astype(jnp.float32)).astype(jnp.bfloat16)
        mine_ref[...] = keep_mine[...] + got_mine[...].astype(jnp.float32)

    def block(which):
        return pl.BlockSpec(
            (1, rows, columns), lambda i, place: (i + half * ((_mesh_bit(place, step) + which) % 2), 0, 0)
        )

    out = pl.BlockSpec((1, rows, columns), lambda i, place: (i, 0, 0))
    return pl.pallas_call(
        kernel,
        grid_spec=pltpu.PrefetchScalarGridSpec(
            num_scalar_prefetch=1,
            grid=(half,),
            in_specs=[block(1), block(0), block(1), block(0)],
            out_specs=[out, out],
        ),
        out_shape=[
            jax.ShapeDtypeStruct((half, rows, columns), jnp.bfloat16),
            jax.ShapeDtypeStruct((half, rows, columns), jnp.float32),
        ],
        compiler_params=_params(16),
        cost_estimate=_cost(cost),
        name="halve",
    )(place, keep, keep, received, received)


def close_call(place, keep, received, shares):
    rows, width = keep.shape
    each = rows // shares

    def kernel(place_ref, keep_ref, got_ref, *refs):
        out_refs, total = refs[:-1], refs[-1]
        total[...] = (keep_ref[...] + got_ref[...].astype(jnp.float32)).reshape(shares, each, width)
        for share, out_ref in enumerate(out_refs):
            out_ref[...] = total[place_ref[2] ^ share].astype(jnp.bfloat16)

    return pl.pallas_call(
        kernel,
        grid_spec=pltpu.PrefetchScalarGridSpec(
            num_scalar_prefetch=1,
            grid=(1,),
            in_specs=[_fixed(rows, width)] * 2,
            out_specs=[_fixed(each, width)] * shares,
            scratch_shapes=[pltpu.VMEM((shares, each, width), jnp.float32)],
        ),
        out_shape=[jax.ShapeDtypeStruct((each, width), jnp.bfloat16)] * shares,
        compiler_params=_params(8),
        cost_estimate=_cost(0),
        name="close",
    )(place, keep, received)


def assemble_heads_call(parts, slot):
    blocks, rows, _ = parts.shape

    def kernel(parts_ref, *refs):
        weight_refs, norm_refs = refs[:3], refs[3:]
        for part, ref in enumerate(weight_refs):
            for block in range(blocks):
                ref[:, block * slot : (block + 1) * slot] = parts_ref[
                    block, :, part * slot : (part + 1) * slot
                ].astype(jnp.float32)
        sums = jnp.zeros((rows, 128), jnp.float32)
        for block in range(blocks):
            sums = sums + parts_ref[block, :, 3 * slot :].astype(jnp.float32)
        turned = jnp.concatenate([sums, jnp.zeros((128 - rows, 128), jnp.float32)], axis=0).T
        for at, ref in enumerate(norm_refs):
            ref[...] = turned[at : at + 1, 0:rows]

    return pl.pallas_call(
        kernel,
        out_shape=[jax.ShapeDtypeStruct((rows, blocks * slot), jnp.float32)] * 3
        + [jax.ShapeDtypeStruct((1, rows), jnp.float32)] * 4,
        compiler_params=_params(8),
        cost_estimate=_cost(0),
        name="assemble_heads",
    )(parts)


def fast_body(
    patches, seg_lengths, w_query, w_key, w_value, w_out, w_up, w_down,
    norm1_gain, norm1_bias, norm2_gain, norm2_bias, out_grad,
):
    micro_count, tokens, features = patches.shape
    hidden = w_up.shape[1]
    row_count = micro_count * tokens
    blocks, shares = lax.axis_size("blk"), lax.axis_size("mb")
    head_dim = features // H
    slot = features // blocks
    rows = patches.reshape(row_count, features)
    dout = out_grad.reshape(row_count, features)
    gain_one, bias_one, gain_two, bias_two = (
        value.reshape(1, features) for value in (norm1_gain, norm1_bias, norm2_gain, norm2_bias)
    )

    def swap(values):
        return lax.all_to_all(values, "blk", split_axis=0, concat_axis=0, tiled=True)

    def by_micro(values):
        return values.reshape(blocks, micro_count, tokens, values.shape[-1])

    at_blk, at_mb = lax.axis_index("blk"), lax.axis_index("mb")
    place = jnp.stack([at_blk, at_mb, at_mb % 2 + at_blk % 2 * 2]).astype(jnp.int32)
    blk_bits = _bits(blocks)
    up_steps = [("mb", 2), *(("blk", bit) for bit in blk_bits[1:])]
    down_steps = [up_steps[1], up_steps[0], *up_steps[2:]]
    each, owned, block_rows = features // (blocks * shares), hidden // (blocks * shares), features // blocks
    tie = lax.optimization_barrier

    def grown(values, bit):
        return jnp.concatenate([values, _paired(values, "blk", bit)], axis=0)

    def to_share(values, other):
        if other == 1:
            return _paired(values, "mb", 1)
        if other == 2:
            return _paired(values, "blk", 1)
        return lax.ppermute(values, ("blk", "mb"), [(i, i ^ (shares + 1)) for i in range(blocks * shares)])

    def shared(values):
        over = to_share(values, 2)
        return [values, to_share(values, 1), over, to_share(over, 1)]

    send, units_first, units_last = project_call(
        rows, gain_one, bias_one, w_query, w_key, w_value, blocks, tokens
    )
    received = by_micro(swap(send))
    dout_parts = [out_grad[micro] for micro in range(micro_count)]
    dout_over = [to_share(part, 2) for part in dout_parts]
    units_last = grown(units_last, blk_bits[0])
    units_last, received, dout_over[0] = tie((units_last, received, dout_over[0]))
    units_first, received = tie((units_first, received))
    units_first = grown(units_first, blk_bits[-1])
    own_attended, exact, logs = attend_call(received, seg_lengths, head_dim)
    attended, units_first, dout_over = tie((own_attended.reshape(blocks, row_count, slot), units_first, dout_over))
    attended, units_first, units_last = tie((swap(attended), units_first, units_last))
    dout_peer = to_share(dout, 1)
    dout_over = jnp.concatenate(dout_over, axis=0)
    douts = [dout, dout_peer, dout_over, to_share(dout_over, 1)]
    for bit in blk_bits[-2:0:-1]:
        units_first = grown(units_first, bit)
    for bit in blk_bits[:1:-1]:
        units_last = grown(units_last, bit)
    places_first = _ordered_low([*blk_bits[:0:-1], blk_bits[0]])
    places_last = _ordered_low([blk_bits[0], *blk_bits[:1:-1], blk_bits[1]])

    mixed, both = mix_call(attended, rows, gain_two, bias_two, w_out)
    both_peer, both_over = to_share(both, 1), to_share(both, 2)
    layer_out, mixed_grad, back, sums_two, *lows = middle_call(
        place, both, mixed, dout, gain_two, w_out, w_up, w_down, blocks, shares
    )
    back, lows, units_first, units_last, both_peer, both_over = tie(
        (back, lows, units_first, units_last, both_peer, both_over)
    )
    boths = [both, both_peer, both_over, to_share(both_over, 1)]
    units_first_peer = _paired(units_first, "blk", blk_bits[0])
    units_last_peer = _paired(units_last, "blk", blk_bits[1])
    grads = by_micro(swap(back))
    lows = [lows[0]] + [to_share(lows[share], share) for share in range(1, shares)]
    down_theirs, down_keep, up_theirs, up_keep = grad_middle_call(
        place, boths, douts, lows, w_up, w_down, down_steps, up_steps
    )
    down_theirs, down_keep = (value.reshape(-1, owned, features) for value in (down_theirs, down_keep))
    up_theirs, up_keep = (value.reshape(-1, block_rows, value.shape[-1]) for value in (up_theirs, up_keep))
    down_received, up_received = _paired(down_theirs, *down_steps[0]), _paired(up_theirs, *up_steps[0])
    grads, down_keep, units_first_peer, units_last_peer = tie((grads, down_keep, units_first_peer, units_last_peer))
    made = attend_back_call(received, grads, exact, logs, seg_lengths, head_dim)
    returned = [swap(made[0])]

    def then(done, *values):
        return tie((done, values))[1]

    returned += [swap(tie((values, returned[0]))[0]) for values in made[1:]]
    made = tie(made)
    down_theirs, down_keep = halve_call(place, *then(made[0], down_keep, down_received), down_steps[1], 0)
    down_received = _paired(down_theirs, *down_steps[1])
    up_theirs, up_keep = halve_call(place, *then(down_keep, up_keep, up_received), up_steps[1], 5)
    up_received = _paired(up_theirs, *up_steps[1])
    made = then(up_keep, *made)
    heads_send, heads_keep = grad_heads_call(
        place, (units_first, units_first_peer, units_last, units_last_peer), (places_first, places_last),
        made, gain_one, bias_one, sums_two, w_query, w_key, w_value, shares,
    )
    pair = (shares // 2, -1, heads_keep.shape[-1])
    heads_received = _paired(heads_send, "mb", 1).reshape(pair)
    down_keep, down_received = then(heads_keep, down_keep, down_received)
    for step in down_steps[2:]:
        down_theirs, down_keep = halve_call(place, down_keep, down_received, step, 0)
        down_received = _paired(down_theirs, *step)
    up_keep, up_received = then(down_keep, up_keep, up_received)
    for step in up_steps[2:]:
        up_theirs, up_keep = halve_call(place, up_keep, up_received, step, 3)
        up_received = _paired(up_theirs, *step)
    heads_theirs, heads_keep = halve_call(
        place, *then(up_keep, heads_keep.reshape(pair), heads_received), ("mb", 2), 0
    )
    heads_received = _paired(heads_theirs, "mb", 2)
    returned = list(then(heads_keep, *returned))
    patches_grad = finish_call(returned, rows, mixed_grad, gain_one, w_query, w_key, w_value)
    up_keep, up_received = then(patches_grad, up_keep, up_received)
    parts = close_call(place, up_keep[0], up_received[0], shares)
    heads_keep, heads_received = then(parts, heads_keep, heads_received)
    heads_total = (heads_keep + heads_received.astype(jnp.float32)).astype(jnp.bfloat16)
    heads_total = swap(heads_total.reshape(blocks, each, heads_keep.shape[-1]))
    parts = [parts[0]] + [to_share(parts[share], share) for share in range(1, shares)]
    up_total, out_total = assemble_call(place, parts, down_steps, blocks, owned)
    down_keep, down_received = then(up_total, down_keep, down_received)
    down_total = (down_keep + down_received.astype(jnp.float32))[0]
    query_total, key_total, value_total, *sums = assemble_heads_call(then(down_total, heads_total)[0], slot)
    return (
        layer_out.reshape(patches.shape),
        patches_grad.reshape(patches.shape),
        query_total,
        key_total,
        value_total,
        out_total,
        up_total,
        down_total,
        *(value.reshape(each) for value in sums),
    )


def solution(mesh):
    in_specs = (
        P("mb", "blk", None),
        P("mb", None),
        P(),
        P(),
        P(),
        P(),
        P(),
        P(),
        P(),
        P(),
        P(),
        P(),
        P("mb", "blk", None),
    )
    out_specs = (
        P("mb", "blk", None),
        P("mb", "blk", None),
        P(("blk", "mb"), None),
        P(("blk", "mb"), None),
        P(("blk", "mb"), None),
        P(("blk", "mb"), None),
        P(("blk", "mb"), None),
        P(("blk", "mb"), None),
        P(("blk", "mb")),
        P(("blk", "mb")),
        P(("blk", "mb")),
        P(("blk", "mb")),
    )
    blocks, shares = mesh.shape["blk"], mesh.shape["mb"]
    paired = blocks >= 4 and blocks & (blocks - 1) == 0 and shares == 4
    chosen_body = fast_body if paired and H % blocks == 0 else body
    return jax.shard_map(chosen_body, mesh=mesh, in_specs=in_specs, out_specs=out_specs, check_vma=False)
```

```python
import math

import jax
import jax.numpy as jnp
from jax import lax
from jax.experimental import pallas as pl
from jax.experimental.pallas import tpu as pltpu
from jax.sharding import PartitionSpec as P

H = 16
CHUNK = 8


epsilon = 1e-05
masked_score = -1e30


def layer_norm(values, norm_gain, norm_bias):
    center = values - jnp.mean(values, axis=-1, keepdims=True)
    variance = jnp.mean(center * center, axis=-1, keepdims=True)
    return center * lax.rsqrt(variance + epsilon) * norm_gain + norm_bias


def gelu_exact(values):
    return jax.nn.gelu(values, approximate=False)


def matmul(left_side, right_side):
    return jnp.dot(left_side, right_side, preferred_element_type=jnp.float32)


def contract_rows(left_side, right_side):
    return lax.dot_general(
        left_side, right_side, (((0,), (0,)), ((), ())), preferred_element_type=jnp.float32
    )


def contract_cols(left_side, right_side):
    return lax.dot_general(
        left_side, right_side, (((1,), (1,)), ((), ())), preferred_element_type=jnp.float32
    )


def segment_ids(lengths, positions):
    doc_ends = jnp.cumsum(lengths, axis=-1)
    return jnp.sum((positions[None, :, None] >= doc_ends[:, None, :]).astype(jnp.int32), axis=-1)


def masked_scores(query_piece, keys_all, query_docs, key_docs, score_scale):
    scores = contract_cols(query_piece, keys_all) * score_scale
    return jnp.where(query_docs[:, None] == key_docs[None, :], scores, masked_score)


def soft_rows(scores):
    row_max = jnp.max(scores, axis=-1, keepdims=True)
    exponent = jnp.exp(scores - row_max)
    return exponent / jnp.sum(exponent, axis=-1, keepdims=True)


def body(
    patches,
    seg_lengths,
    w_query,
    w_key,
    w_value,
    w_out,
    w_up,
    w_down,
    norm1_gain,
    norm1_bias,
    norm2_gain,
    norm2_bias,
    out_grad,
):
    micro_count, tokens, features = patches.shape
    row_count = micro_count * tokens
    blocks = lax.axis_size("blk")
    block_index = lax.axis_index("blk")
    head_count = H
    head_dim = features // head_count
    repeat = max(1, blocks // head_count)
    per_slot = max(1, head_count // blocks)
    groups = head_count // per_slot
    rows_part = tokens // repeat
    query_rows = blocks * rows_part
    seq_length = blocks * tokens
    item_count = micro_count * per_slot
    block_rows = min(512, query_rows)
    block_count = query_rows // block_rows
    slot_width = micro_count * per_slot * head_dim
    score_scale = 1.0 / math.sqrt(head_dim)
    doc_count = seg_lengths.shape[1]

    def query_layout(values):
        shaped = values.reshape(micro_count, repeat, rows_part, groups, per_slot * head_dim)
        return shaped.transpose(3, 1, 2, 0, 4).reshape(blocks, rows_part, slot_width)

    def key_layout(values):
        shaped = values.reshape(micro_count, tokens, groups, per_slot * head_dim).transpose(
            2, 1, 0, 3
        )
        shaped = jnp.broadcast_to(
            shaped[:, None], (groups, repeat, tokens, micro_count, per_slot * head_dim)
        )
        return shaped.reshape(blocks, tokens, slot_width)

    def token_layout(values):
        shaped = values.reshape(groups, repeat, rows_part, micro_count, per_slot * head_dim)
        return shaped.transpose(3, 1, 2, 0, 4).reshape(row_count, features)

    def key_sum(values):
        shaped = values.reshape(groups, repeat, tokens, micro_count, per_slot * head_dim).sum(
            axis=1
        )
        return shaped.transpose(2, 1, 0, 3).reshape(row_count, features)

    def to_items(received):
        row_total = received.shape[1]
        shaped = received.reshape(row_total, micro_count, per_slot, head_dim).transpose(1, 2, 0, 3)
        return shaped.reshape(item_count, row_total, head_dim)

    def from_items(values):
        row_total = values.shape[1]
        shaped = values.reshape(micro_count, per_slot, row_total, head_dim).transpose(2, 0, 1, 3)
        return shaped.reshape(1, row_total, slot_width)

    row_ids = jnp.arange(query_rows)
    query_pos = (
        row_ids // rows_part * tokens + block_index % repeat * rows_part + row_ids % rows_part
    )
    query_docs = jnp.repeat(segment_ids(seg_lengths, query_pos), per_slot, axis=0)
    key_docs = jnp.repeat(segment_ids(seg_lengths, jnp.arange(seq_length)), per_slot, axis=0)
    query_valid = (query_docs < doc_count).astype(jnp.float32)
    local_pos = block_index * tokens + jnp.arange(tokens)
    row_valid = (
        (segment_ids(seg_lengths, local_pos) < doc_count).astype(jnp.float32).reshape(row_count, 1)
    )

    def forward_item(operands):
        queries_item, keys_item, values_item, docs_item, key_docs_item = operands

        def forward_one_block(block_operands):
            query_piece, docs_piece = block_operands
            weights_soft = soft_rows(
                masked_scores(query_piece, keys_item, docs_piece, key_docs_item, score_scale)
            )
            return matmul(weights_soft.astype(jnp.bfloat16), values_item)

        outputs = lax.map(
            forward_one_block,
            (
                queries_item.reshape(block_count, block_rows, head_dim),
                docs_item.reshape(block_count, block_rows),
            ),
        )
        return outputs.reshape(query_rows, head_dim)

    def backward_item(operands):
        queries_item, keys_item, values_item, grads_item, docs_item, key_docs_item = operands

        def backward_one_block(totals, block_operands):
            key_total, value_total = totals
            query_piece, grad_piece, docs_piece = block_operands
            weights_soft = soft_rows(
                masked_scores(query_piece, keys_item, docs_piece, key_docs_item, score_scale)
            )
            weights_low = weights_soft.astype(jnp.bfloat16)
            weight_grads = contract_cols(grad_piece, values_item)
            row_inner = jnp.sum(weights_soft * weight_grads, axis=-1, keepdims=True)
            score_grads = (weights_soft * (weight_grads - row_inner)).astype(jnp.bfloat16)
            query_grad = matmul(score_grads, keys_item) * score_scale
            key_total = key_total + contract_rows(score_grads, query_piece) * score_scale
            value_total = value_total + contract_rows(weights_low, grad_piece)
            return ((key_total, value_total), query_grad)

        zero_block = jnp.zeros((seq_length, head_dim), jnp.float32)
        totals, query_grads = lax.scan(
            backward_one_block,
            (zero_block, zero_block),
            (
                queries_item.reshape(block_count, block_rows, head_dim),
                grads_item.reshape(block_count, block_rows, head_dim),
                docs_item.reshape(block_count, block_rows),
            ),
        )
        return (query_grads.reshape(query_rows, head_dim), totals[0], totals[1])

    inputs = patches.astype(jnp.float32).reshape(row_count, features)
    norm_one_full, norm_one_pull = jax.vjp(layer_norm, inputs, norm1_gain, norm1_bias)
    norm_one = norm_one_full.astype(jnp.bfloat16)
    queries = matmul(norm_one, w_query).astype(jnp.bfloat16)
    keys_proj = matmul(norm_one, w_key).astype(jnp.bfloat16)
    values_proj = matmul(norm_one, w_value).astype(jnp.bfloat16)
    query_send = query_layout(queries)
    key_send = key_layout(keys_proj)
    value_send = key_layout(values_proj)
    query_heads, key_heads, value_heads = (
        lax.all_to_all(query_send, "blk", split_axis=0, concat_axis=1, tiled=True),
        lax.all_to_all(key_send, "blk", split_axis=0, concat_axis=1, tiled=True),
        lax.all_to_all(value_send, "blk", split_axis=0, concat_axis=1, tiled=True),
    )
    query_items = to_items(query_heads)
    key_items = to_items(key_heads)
    value_items = to_items(value_heads)
    attended_items = lax.map(
        forward_item, (query_items, key_items, value_items, query_docs, key_docs)
    )
    attended_items = (attended_items * query_valid[:, :, None]).astype(jnp.bfloat16)
    attended = token_layout(
        lax.all_to_all(from_items(attended_items), "blk", split_axis=1, concat_axis=0, tiled=True)
    )
    mixed_rows = inputs + matmul(attended, w_out)
    norm_two_full, norm_two_pull = jax.vjp(layer_norm, mixed_rows, norm2_gain, norm2_bias)
    norm_two = norm_two_full.astype(jnp.bfloat16)
    upper_proj = matmul(norm_two, w_up)
    active_full, gelu_pull = jax.vjp(gelu_exact, upper_proj)
    active = active_full.astype(jnp.bfloat16)
    result = mixed_rows + matmul(active, w_down)
    layer_out = result.astype(jnp.bfloat16).reshape(micro_count, tokens, features)
    dout_low = out_grad.reshape(row_count, features)
    down_grad = contract_rows(active, dout_low)
    active_grad = contract_cols(dout_low, w_down)
    upper_grad = gelu_pull(active_grad)[0].astype(jnp.bfloat16)
    up_grad = contract_rows(norm_two, upper_grad)
    norm_two_grad = contract_cols(upper_grad, w_up)
    mixed_part, gain_two_grad, bias_two_grad = norm_two_pull(norm_two_grad)
    mixed_grad = dout_low.astype(jnp.float32) + mixed_part
    mixed_low = mixed_grad.astype(jnp.bfloat16)
    out_proj_grad = contract_rows(attended, mixed_low)
    attended_grad = (contract_cols(mixed_low, w_out) * row_valid).astype(jnp.bfloat16)
    grad_send = query_layout(attended_grad)
    query_again, key_again, value_again, grad_heads = (
        lax.all_to_all(query_send, "blk", split_axis=0, concat_axis=1, tiled=True),
        lax.all_to_all(key_send, "blk", split_axis=0, concat_axis=1, tiled=True),
        lax.all_to_all(value_send, "blk", split_axis=0, concat_axis=1, tiled=True),
        lax.all_to_all(grad_send, "blk", split_axis=0, concat_axis=1, tiled=True),
    )
    back_queries = to_items(query_again)
    back_keys = to_items(key_again)
    back_values = to_items(value_again)
    grad_items = to_items(grad_heads)
    query_grad_items, key_grad_items, value_grad_items = lax.map(
        backward_item, (back_queries, back_keys, back_values, grad_items, query_docs, key_docs)
    )
    query_back, key_back, value_back = (
        lax.all_to_all(
            from_items(query_grad_items).astype(jnp.bfloat16),
            "blk",
            split_axis=1,
            concat_axis=0,
            tiled=True,
        ).astype(jnp.float32),
        lax.all_to_all(
            from_items(key_grad_items).astype(jnp.bfloat16),
            "blk",
            split_axis=1,
            concat_axis=0,
            tiled=True,
        ).astype(jnp.float32),
        lax.all_to_all(
            from_items(value_grad_items).astype(jnp.bfloat16),
            "blk",
            split_axis=1,
            concat_axis=0,
            tiled=True,
        ).astype(jnp.float32),
    )
    query_grad = token_layout(query_back).astype(jnp.bfloat16)
    key_grad = key_sum(key_back).astype(jnp.bfloat16)
    value_grad = key_sum(value_back).astype(jnp.bfloat16)
    query_proj_grad = contract_rows(norm_one, query_grad)
    key_proj_grad = contract_rows(norm_one, key_grad)
    value_proj_grad = contract_rows(norm_one, value_grad)
    norm_one_grad = (
        contract_cols(query_grad, w_query)
        + contract_cols(key_grad, w_key)
        + contract_cols(value_grad, w_value)
    )
    input_part, gain_one_grad, bias_one_grad = norm_one_pull(norm_one_grad)
    patches_grad = (
        (mixed_grad + input_part).astype(jnp.bfloat16).reshape(micro_count, tokens, features)
    )
    gradients = (
        query_proj_grad,
        key_proj_grad,
        value_proj_grad,
        out_proj_grad,
        up_grad,
        down_grad,
        gain_one_grad,
        bias_one_grad,
        gain_two_grad,
        bias_two_grad,
    )
    summed = (
        lax.psum_scatter(gradients[0], ("blk", "mb"), scatter_dimension=0, tiled=True),
        lax.psum_scatter(gradients[1], ("blk", "mb"), scatter_dimension=0, tiled=True),
        lax.psum_scatter(gradients[2], ("blk", "mb"), scatter_dimension=0, tiled=True),
        lax.psum_scatter(gradients[3], ("blk", "mb"), scatter_dimension=0, tiled=True),
        lax.psum_scatter(gradients[4], ("blk", "mb"), scatter_dimension=0, tiled=True),
        lax.psum_scatter(gradients[5], ("blk", "mb"), scatter_dimension=0, tiled=True),
        lax.psum_scatter(gradients[6], ("blk", "mb"), scatter_dimension=0, tiled=True),
        lax.psum_scatter(gradients[7], ("blk", "mb"), scatter_dimension=0, tiled=True),
        lax.psum_scatter(gradients[8], ("blk", "mb"), scatter_dimension=0, tiled=True),
        lax.psum_scatter(gradients[9], ("blk", "mb"), scatter_dimension=0, tiled=True),
    )
    return (
        layer_out,
        patches_grad,
        summed[0],
        summed[1],
        summed[2],
        summed[3],
        summed[4],
        summed[5],
        summed[6],
        summed[7],
        summed[8],
        summed[9],
    )


def _normalize(values):
    center = values - jnp.mean(values, axis=-1, keepdims=True)
    variance = jnp.mean(center * center, axis=-1, keepdims=True)
    inverse = lax.rsqrt(variance + epsilon)
    return center * inverse, inverse


def _normalize_back(grads, gain, unit, inverse):
    scaled = grads * gain
    mean_scaled = jnp.mean(scaled, axis=-1, keepdims=True)
    mean_product = jnp.mean(scaled * unit, axis=-1, keepdims=True)
    return (scaled - mean_scaled - unit * mean_product) * inverse


def _doc_ids(lengths_ref, micro, doc_count, positions):
    end = jnp.int32(0)
    ids = jnp.zeros_like(positions)
    for doc in range(doc_count):
        end = end + lengths_ref[micro, doc]
        ids = ids + (positions >= end).astype(jnp.int32)
    return ids


def _params(mib):
    return pltpu.CompilerParams(vmem_limit_bytes=mib << 20)


def _cost(microseconds):
    return pl.CostEstimate(flops=int(microseconds * 1e9) + 1, bytes_accessed=1, transcendentals=0)


def project_call(rows, gain, bias, w_query, w_key, w_value, blocks, tokens):
    row_count, features = rows.shape
    slot = features // blocks
    per_step = max(1, min(blocks, 512 // slot))
    wide = slot * per_step

    def kernel(rows_ref, gain_ref, bias_ref, wq_ref, wk_ref, wv_ref, send_ref, *refs):
        unit_refs, norm_ref = refs[:-1], refs[-1]


        @pl.when(pl.program_id(0) == 0)
        def _():
            unit, _unused = _normalize(rows_ref[...].astype(jnp.float32))
            for micro, unit_ref in enumerate(unit_refs):
                unit_ref[...] = unit[micro * tokens : (micro + 1) * tokens].astype(jnp.bfloat16)
            norm_ref[...] = (unit * gain_ref[...] + bias_ref[...]).astype(jnp.bfloat16)

        for part, weight_ref in enumerate((wq_ref, wk_ref, wv_ref)):
            made = matmul(norm_ref[...], weight_ref[...]).astype(jnp.bfloat16)
            for piece in range(per_step):
                send_ref[piece, :, part * slot : (part + 1) * slot] = made[
                    :, piece * slot : (piece + 1) * slot
                ]

    whole = pl.BlockSpec((row_count, features), lambda i: (0, 0))
    vector = pl.BlockSpec((1, features), lambda i: (0, 0))
    columns = pl.BlockSpec((features, wide), lambda i: (0, i))
    return pl.pallas_call(
        kernel,
        grid=(blocks // per_step,),
        in_specs=[whole, vector, vector, columns, columns, columns],
        out_specs=[pl.BlockSpec((per_step, row_count, 3 * slot), lambda i: (i, 0, 0))]
        + [pl.BlockSpec((tokens, features), lambda i: (0, 0))] * (row_count // tokens),
        out_shape=[jax.ShapeDtypeStruct((blocks, row_count, 3 * slot), jnp.bfloat16)]
        + [jax.ShapeDtypeStruct((tokens, features), jnp.bfloat16)] * (row_count // tokens),
        scratch_shapes=[pltpu.VMEM((row_count, features), jnp.bfloat16)],
        compiler_params=_params(60),
        cost_estimate=_cost(6),
        name="project",
    )(rows, gain, bias, w_query, w_key, w_value)


def _head_masks(slot, head_dim, dtype):
    lanes = lax.broadcasted_iota(jnp.int32, (1, slot), 1)
    return [(lanes // head_dim == head).astype(dtype) for head in range(slot // head_dim)]


def _key_range(lengths_ref, micro, doc_count, first_row, last_row, seq):
    low, high, end = jnp.int32(0), jnp.int32(seq), jnp.int32(0)
    for doc in range(doc_count):
        end = end + lengths_ref[micro, doc]
        low = jnp.where(end <= first_row, jnp.maximum(low, end), low)
        high = jnp.where(end >= last_row, jnp.minimum(high, end), high)
    return low, high


def _by_key_range(lengths_ref, micro, doc_count, step, rows, blocks, tokens, compute):
    low, high = _key_range(lengths_ref, micro, doc_count, step * rows, (step + 1) * rows, blocks * tokens)
    half = blocks // 2
    in_low, in_high = high <= half * tokens, low >= half * tokens

    @pl.when(in_low | in_high)
    def _():
        compute(jnp.where(in_low, 0, half), half)

    @pl.when(jnp.logical_not(in_low | in_high))
    def _():
        compute(0, blocks)


def attend_call(received, lengths, head_dim):
    blocks, micro_count, tokens, width = received.shape
    slot = width // 3
    doc_count = lengths.shape[1]
    step_blocks = max(1, min(blocks // 2, 512 // tokens))
    rows = step_blocks * tokens
    scale = 1.0 / math.sqrt(head_dim)

    def kernel(lengths_ref, data_ref, out_ref, exact_ref, log_ref):
        micro = pl.program_id(0)
        step = pl.program_id(1)
        row_docs = _doc_ids(
            lengths_ref, micro, doc_count, lax.broadcasted_iota(jnp.int32, (rows, 1), 0) + step * rows
        )
        queries = data_ref[pl.ds(step * step_blocks, step_blocks), 0, :, 0:slot].reshape(rows, slot) * scale

        def compute(first, count):
            seq = count * tokens
            key_docs = _doc_ids(
                lengths_ref, micro, doc_count, lax.broadcasted_iota(jnp.int32, (1, seq), 1) + first * tokens
            )
            same = row_docs == key_docs
            keys = data_ref[pl.ds(first, count), 0, :, slot : 2 * slot].reshape(seq, slot)
            values = data_ref[pl.ds(first, count), 0, :, 2 * slot : 3 * slot].reshape(seq, slot)
            total = jnp.zeros((rows, slot), jnp.float32)
            logs = jnp.zeros((rows, 128), jnp.float32)
            lanes = lax.broadcasted_iota(jnp.int32, (1, 128), 1)
            for head, (mask, mask_wide) in enumerate(
                zip(_head_masks(slot, head_dim, jnp.bfloat16), _head_masks(slot, head_dim, jnp.float32))
            ):
                scores = jnp.where(same, contract_cols(queries * mask, keys), masked_score)
                most = jnp.max(scores, axis=-1, keepdims=True)
                exponent = jnp.exp(scores - most)
                exponent_sum = jnp.sum(exponent, axis=-1, keepdims=True)
                share = 1.0 / exponent_sum
                logs = jnp.where(lanes == head, most + jnp.log(exponent_sum), logs)
                total = total + matmul(exponent.astype(jnp.bfloat16), values) * (share * mask_wide)
            total = jnp.where(row_docs < doc_count, total, 0.0)
            out_ref[...] = total.astype(jnp.bfloat16).reshape(step_blocks, 1, tokens, slot)
            exact_ref[...] = total.reshape(step_blocks, 1, tokens, slot)
            log_ref[0] = logs.T[0:8, :]

        _by_key_range(lengths_ref, micro, doc_count, step, rows, blocks, tokens, compute)

    return pl.pallas_call(
        kernel,
        grid=(micro_count, blocks // step_blocks),
        in_specs=[
            pl.BlockSpec(memory_space=pltpu.SMEM),
            pl.BlockSpec((blocks, 1, tokens, width), lambda m, s: (0, m, 0, 0)),
        ],
        out_specs=[
            pl.BlockSpec((step_blocks, 1, tokens, slot), lambda m, s: (s, m, 0, 0)),
            pl.BlockSpec((step_blocks, 1, tokens, slot), lambda m, s: (s, m, 0, 0)),
            pl.BlockSpec((1, 8, rows), lambda m, s: (m, 0, s)),
        ],
        out_shape=[
            jax.ShapeDtypeStruct((blocks, micro_count, tokens, slot), jnp.bfloat16),
            jax.ShapeDtypeStruct((blocks, micro_count, tokens, slot), jnp.float32),
            jax.ShapeDtypeStruct((micro_count, 8, blocks * tokens), jnp.float32),
        ],
        compiler_params=_params(32),
        cost_estimate=_cost(11),
        name="attend",
    )(lengths, received)


def attend_back_call(received, grads, attended, logs, lengths, head_dim):
    blocks, micro_count, tokens, width = received.shape
    slot = width // 3
    doc_count = lengths.shape[1]
    step_blocks = max(1, min(blocks // 2, 512 // tokens))
    rows = step_blocks * tokens
    steps = blocks // step_blocks
    scale = 1.0 / math.sqrt(head_dim)

    def kernel(lengths_ref, data_ref, grads_ref, att_ref, log_ref, *refs):
        out_refs, (key_total, value_total, turned) = refs[:micro_count], refs[micro_count:]
        micro = pl.program_id(0)
        step = pl.program_id(1)

        @pl.when(step == 0)
        def _():
            key_total[...] = jnp.zeros_like(key_total)
            value_total[...] = jnp.zeros_like(value_total)
            for block in range(blocks):
                turned[block] = data_ref[block, 0, :, slot : 2 * slot].T

        row_docs = _doc_ids(
            lengths_ref, micro, doc_count, lax.broadcasted_iota(jnp.int32, (1, rows), 1) + step * rows
        )
        column_docs = _doc_ids(
            lengths_ref, micro, doc_count, lax.broadcasted_iota(jnp.int32, (rows, 1), 0) + step * rows
        )
        queries = data_ref[pl.ds(step * step_blocks, step_blocks), 0, :, 0:slot].reshape(rows, slot) * scale
        out_grads = grads_ref[...].reshape(rows, slot)
        out_grads = out_grads * (column_docs < doc_count).astype(jnp.float32).astype(jnp.bfloat16)

        inner = (out_grads.astype(jnp.float32) * att_ref[...].reshape(rows, slot)).T

        def compute(first, count):
            chunk = min(CHUNK, count)
            query_parts = [jnp.zeros((head_dim, rows), jnp.float32) for _ in range(slot // head_dim)]
            masks = _head_masks(slot, head_dim, jnp.bfloat16)
            for at in range(0, count, chunk):
                seq = chunk * tokens
                key_docs = _doc_ids(
                    lengths_ref,
                    micro,
                    doc_count,
                    lax.broadcasted_iota(jnp.int32, (seq, 1), 0) + (first + at) * tokens,
                )
                same = row_docs == key_docs
                keys = data_ref[pl.ds(first + at, chunk), 0, :, slot : 2 * slot].reshape(seq, slot)
                values = data_ref[pl.ds(first + at, chunk), 0, :, 2 * slot : 3 * slot].reshape(seq, slot)
                keys_turned = jnp.concatenate([turned[first + at + other] for other in range(chunk)], axis=1)
                key_made = jnp.zeros((seq, slot), jnp.float32)
                value_made = jnp.zeros((seq, slot), jnp.float32)
                for head, mask in enumerate(masks):
                    lanes = slice(head * head_dim, (head + 1) * head_dim)
                    queries_head, grads_head = queries * mask, out_grads * mask
                    scores = jnp.where(same, contract_cols(keys, queries_head), masked_score)
                    probs = jnp.exp(scores - log_ref[0, head : head + 1, :])
                    prob_grads = contract_cols(values, grads_head)
                    head_inner = jnp.sum(inner[lanes], axis=0, keepdims=True)
                    score_grads = (probs * (prob_grads - head_inner)).astype(jnp.bfloat16)
                    value_made = value_made + matmul(probs.astype(jnp.bfloat16), grads_head)
                    key_made = key_made + matmul(score_grads, queries_head)
                    query_parts[head] = query_parts[head] + matmul(keys_turned[lanes], score_grads)
                to = pl.ds(pl.multiple_of((first + at) * tokens, tokens), seq)
                key_total[to, :] += key_made
                value_total[to, :] += value_made
            query_grads = (jnp.concatenate(query_parts, axis=0).T * scale).astype(jnp.bfloat16).reshape(step_blocks, tokens, slot)
            for at, out_ref in enumerate(out_refs):

                @pl.when(micro == at)
                def _():
                    out_ref[pl.ds(step * step_blocks, step_blocks), :, 0:slot] = query_grads

        _by_key_range(lengths_ref, micro, doc_count, step, rows, blocks, tokens, compute)

        for at, out_ref in enumerate(out_refs):

            @pl.when((step == steps - 1) & (micro == at))
            def _():
                out_ref[:, :, slot : 2 * slot] = key_total[...].astype(jnp.bfloat16).reshape(blocks, tokens, slot)
                out_ref[:, :, 2 * slot :] = value_total[...].astype(jnp.bfloat16).reshape(blocks, tokens, slot)

    return pl.pallas_call(
        kernel,
        grid=(micro_count, steps),
        in_specs=[
            pl.BlockSpec(memory_space=pltpu.SMEM),
            pl.BlockSpec((blocks, 1, tokens, width), lambda m, s: (0, m, 0, 0)),
            pl.BlockSpec((step_blocks, 1, tokens, slot), lambda m, s: (s, m, 0, 0)),
            pl.BlockSpec((step_blocks, 1, tokens, slot), lambda m, s: (s, m, 0, 0)),
            pl.BlockSpec((1, 8, rows), lambda m, s: (m, 0, s)),
        ],
        out_specs=[pl.BlockSpec((blocks, tokens, width), lambda m, s: (0, 0, 0))] * micro_count,
        out_shape=[jax.ShapeDtypeStruct((blocks, tokens, width), jnp.bfloat16)] * micro_count,
        scratch_shapes=[pltpu.VMEM((blocks * tokens, slot), jnp.float32)] * 2
        + [pltpu.VMEM((blocks, slot, tokens), jnp.bfloat16)],
        compiler_params=_params(60),
        cost_estimate=_cost(3),
        name="attend_back",
    )(lengths, received, grads, attended, logs)


def _fixed(*shape):
    return pl.BlockSpec(shape, lambda *_unused: (0,) * len(shape))


def mix_call(attended, rows, gain, bias, w_out):
    blocks, row_count, slot = attended.shape
    features = rows.shape[1]

    def kernel(att_ref, rows_ref, gain_ref, bias_ref, wo_ref, mixed_ref, both_ref):
        for block in range(blocks):
            both_ref[1, :, block * slot : (block + 1) * slot] = att_ref[block]
        value = rows_ref[...].astype(jnp.float32) + matmul(both_ref[1], wo_ref[...])
        mixed_ref[...] = value
        unit, _unused = _normalize(value)
        both_ref[0] = (unit * gain_ref[...] + bias_ref[...]).astype(jnp.bfloat16)

    rows_spec, vector = _fixed(row_count, features), _fixed(1, features)
    return pl.pallas_call(
        kernel,
        grid=(1,),
        in_specs=[_fixed(blocks, row_count, slot), rows_spec, vector, vector, _fixed(features, features)],
        out_specs=[rows_spec, _fixed(2, row_count, features)],
        out_shape=[
            jax.ShapeDtypeStruct((row_count, features), jnp.float32),
            jax.ShapeDtypeStruct((2, row_count, features), jnp.bfloat16),
        ],
        compiler_params=_params(24),
        cost_estimate=_cost(4),
        name="mix",
    )(attended, rows, gain, bias, w_out)


def _hidden_parts(norm, out_grad, up_columns, down_rows):
    upper = matmul(norm, up_columns)
    active_grad = contract_cols(out_grad, down_rows)
    half = (1.0 + lax.erf(upper * (1.0 / math.sqrt(2.0)))) * 0.5
    slope = half + upper * jnp.exp(upper * upper * -0.5) * (1.0 / math.sqrt(2.0 * math.pi))
    return (upper * half).astype(jnp.bfloat16), (active_grad * slope).astype(jnp.bfloat16)


def middle_call(place, both, mixed, out_grad, gain, w_out, w_up, w_down, blocks, shares):
    row_count, features = mixed.shape
    hidden = w_up.shape[1]
    wide = min(1024, hidden)
    sub = min(512, wide)
    steps = hidden // wide
    slot, part = features // blocks, features // shares

    def kernel(place_ref, norm_ref, mixed_ref, grad_ref, gain_ref, wo_ref, wu_ref, wd_ref, *refs):
        out_ref, mixed_grad_ref, back_ref, sums_ref = refs[:4]
        low_refs, (total, grad_total, active_all, upper_all, low_all) = refs[4 : 4 + shares], refs[4 + shares :]
        step = pl.program_id(0)

        @pl.when(step == 0)
        def _():
            total[...] = mixed_ref[...]
            grad_total[...] = jnp.zeros_like(grad_total)

        for chunk in range(0, wide, sub):
            active, upper_grad = _hidden_parts(
                norm_ref[0], grad_ref[...], wu_ref[:, chunk : chunk + sub], wd_ref[chunk : chunk + sub, :]
            )
            active_all[:, chunk : chunk + sub] = active
            upper_all[:, chunk : chunk + sub] = upper_grad
        total[...] += matmul(active_all[...], wd_ref[...])
        grad_total[...] += contract_cols(upper_all[...], wu_ref[...])

        @pl.when(step == steps - 1)
        def _():
            out_ref[...] = total[...].astype(jnp.bfloat16)
            unit, inverse = _normalize(mixed_ref[...])
            grads = grad_total[...]
            sums_ref[0:1, :] = jnp.sum(grads * unit, axis=0, keepdims=True)
            sums_ref[1:2, :] = jnp.sum(grads, axis=0, keepdims=True)
            mixed_grad = grad_ref[...].astype(jnp.float32) + _normalize_back(grads, gain_ref[...], unit, inverse)
            mixed_grad_ref[...] = mixed_grad
            low = mixed_grad.astype(jnp.bfloat16)
            low_all[...] = low
            for share, low_ref in enumerate(low_refs):
                low_ref[...] = low_all[:, pl.ds(pl.multiple_of((place_ref[2] ^ share) * part, 128), part)]
            back = contract_cols(low, wo_ref[...]).astype(jnp.bfloat16)
            for block in range(blocks):
                back_ref[block] = back[:, block * slot : (block + 1) * slot]

    rows_spec = _fixed(row_count, features)
    return pl.pallas_call(
        kernel,
        grid_spec=pltpu.PrefetchScalarGridSpec(
            num_scalar_prefetch=1,
            grid=(steps,),
            in_specs=[
                _fixed(1, row_count, features),
                rows_spec,
                rows_spec,
                _fixed(1, features),
                _fixed(features, features),
                pl.BlockSpec((features, wide), lambda i, place: (0, i)),
                pl.BlockSpec((wide, features), lambda i, place: (i, 0)),
            ],
            out_specs=[rows_spec, rows_spec, _fixed(blocks, row_count, slot), _fixed(2, features)]
            + [_fixed(row_count, part)] * shares,
            scratch_shapes=[
                pltpu.VMEM((row_count, features), jnp.float32),
                pltpu.VMEM((row_count, features), jnp.float32),
                pltpu.VMEM((row_count, wide), jnp.bfloat16),
                pltpu.VMEM((row_count, wide), jnp.bfloat16),
                pltpu.VMEM((row_count, features), jnp.bfloat16),
            ],
        ),
        out_shape=[
            jax.ShapeDtypeStruct((row_count, features), jnp.bfloat16),
            jax.ShapeDtypeStruct((row_count, features), jnp.float32),
            jax.ShapeDtypeStruct((blocks, row_count, slot), jnp.bfloat16),
            jax.ShapeDtypeStruct((2, features), jnp.float32),
        ]
        + [jax.ShapeDtypeStruct((row_count, part), jnp.bfloat16)] * shares,
        compiler_params=_params(44),
        cost_estimate=_cost(20),
        name="middle",
    )(place, both, mixed, out_grad, gain, w_out, w_up, w_down)


def finish_call(received, rows, mixed_grad, gain, w_query, w_key, w_value):
    micro_count = len(received)
    blocks, tokens, width = received[0].shape
    slot = width // 3
    row_count, features = rows.shape
    per_step = max(1, min(blocks, 512 // slot))
    wide = slot * per_step
    steps = blocks // per_step

    def kernel(*refs):
        data_refs, refs = refs[:micro_count], refs[micro_count:]
        rows_ref, mixed_ref, gain_ref, wq_ref, wk_ref, wv_ref, out_ref, total, side = refs
        step = pl.program_id(0)

        @pl.when(step == 0)
        def _():
            total[...] = jnp.zeros_like(total)

        for part, weight_ref in enumerate((wq_ref, wk_ref, wv_ref)):
            for micro, data_ref in enumerate(data_refs):
                for piece in range(per_step):
                    side[part, micro * tokens : (micro + 1) * tokens, piece * slot : (piece + 1) * slot] = data_ref[
                        piece, :, part * slot : (part + 1) * slot
                    ]
            total[...] += contract_cols(side[part], weight_ref[...])

        @pl.when(step == steps - 1)
        def _():
            unit, inverse = _normalize(rows_ref[...].astype(jnp.float32))
            out_ref[...] = (
                mixed_ref[...] + _normalize_back(total[...], gain_ref[...], unit, inverse)
            ).astype(jnp.bfloat16)

    def fixed(*shape):
        return pl.BlockSpec(shape, lambda i: (0,) * len(shape))

    columns = pl.BlockSpec((features, wide), lambda i: (0, i))
    return pl.pallas_call(
        kernel,
        grid=(steps,),
        in_specs=[pl.BlockSpec((per_step, tokens, width), lambda i: (i, 0, 0))] * micro_count
        + [
            fixed(row_count, features),
            fixed(row_count, features),
            fixed(1, features),
            columns,
            columns,
            columns,
        ],
        out_specs=fixed(row_count, features),
        out_shape=jax.ShapeDtypeStruct((row_count, features), jnp.bfloat16),
        scratch_shapes=[
            pltpu.VMEM((row_count, features), jnp.float32),
            pltpu.VMEM((3, row_count, wide), jnp.bfloat16),
        ],
        compiler_params=_params(60),
        cost_estimate=_cost(20),
        name="finish",
    )(*received, rows, mixed_grad, gain, w_query, w_key, w_value)


def grad_heads_call(place, units, places, made, gain, bias, sums, w_query, w_key, w_value, shares):
    micro_count = len(made)
    blocks, tokens, width = made[0].shape
    slot = width // 3
    features = gain.shape[1]
    group = features // (blocks * shares)
    full = width + 128
    kept = blocks * (shares // 2) * group

    def kernel(place_ref, *refs):
        unit_refs, refs = refs[: 2 * micro_count], refs[2 * micro_count :]
        made_refs, refs = refs[:micro_count], refs[micro_count:]
        gain_ref, bias_ref, sums_ref, wq_ref, wk_ref, wv_ref, send_ref, keep_ref, spread, ordered = refs
        product = jnp.zeros((features, width), jnp.float32)
        column_sum = jnp.zeros((1, width), jnp.float32)
        for micro, made_ref in enumerate(made_refs):
            for at, relative in enumerate(places[micro]):
                ordered[at * tokens : (at + 1) * tokens, :] = made_ref[place_ref[0] ^ relative]
            half = blocks * tokens // 2
            for side in range(2):
                rows = ordered[side * half : (side + 1) * half, :]
                product = product + contract_rows(unit_refs[2 * micro + side][...], rows)
                column_sum = column_sum + jnp.sum(rows.astype(jnp.float32), axis=0, keepdims=True)
        vectors = jnp.concatenate(
            [gain_ref[...], bias_ref[...], sums_ref[...], jnp.zeros((124, features), jnp.float32)], axis=0
        ).T
        total = vectors[:, 0:1] * product + vectors[:, 1:2] * column_sum
        weights = jnp.concatenate([wq_ref[...], wk_ref[...], wv_ref[...]], axis=1).astype(jnp.float32)
        gain_sum = jnp.sum(weights * product, axis=1, keepdims=True)
        bias_sum = jnp.sum(weights * column_sum, axis=1, keepdims=True)
        lanes = lax.broadcasted_iota(jnp.int32, (1, 128), 1)
        norms = jnp.where(
            lanes == 0, gain_sum, jnp.where(lanes == 1, bias_sum, jnp.where(lanes < 4, vectors, 0.0))
        )
        spread[:, :, :, 0:width] = total.reshape(blocks, shares, group, width)
        spread[:, :, :, width:] = norms.reshape(blocks, shares, group, 128)
        core = place_ref[1] % 2
        for which, out_ref in enumerate((send_ref, keep_ref)):
            for share in range(0, shares, 2):
                for block in range(blocks):
                    out_ref[share // 2, block] = spread[block, share + (core if which else 1 - core)].astype(out_ref.dtype)

    def fixed(*shape):
        return pl.BlockSpec(shape, lambda i, place: (0,) * len(shape))

    columns = pl.BlockSpec((features, slot), lambda i, place: (0, place[0]))
    out = (shares // 2, blocks, group, full)
    return pl.pallas_call(
        kernel,
        grid_spec=pltpu.PrefetchScalarGridSpec(
            num_scalar_prefetch=1,
            grid=(1,),
            in_specs=[fixed(*part.shape) for part in (*units, *made)]
            + [fixed(1, features), fixed(1, features), fixed(2, features), columns, columns, columns],
            out_specs=[fixed(*out), fixed(*out)],
            scratch_shapes=[
                pltpu.VMEM((blocks, shares, group, full), jnp.float32),
                pltpu.VMEM((blocks * tokens, width), jnp.bfloat16),
            ],
        ),
        out_shape=[jax.ShapeDtypeStruct(out, jnp.bfloat16), jax.ShapeDtypeStruct(out, jnp.float32)],
        compiler_params=_params(60),
        cost_estimate=_cost(20),
        name="grad_heads",
    )(place, *units, *made, gain, bias, sums, w_query, w_key, w_value)


def assemble_call(place, parts, down_steps, blocks, owned):
    shares = len(parts)
    rows, width = parts[0].shape
    part = width - blocks * owned

    def kernel(place_ref, *refs):
        part_refs, (up_ref, out_ref) = refs[:shares], refs[shares:]
        for other, part_ref in enumerate(part_refs):
            share = place_ref[2] ^ other
            for at, block in enumerate(_ordered([_owner_stride(*step, shares) for step in down_steps])):
                to = pl.multiple_of((block + share % 2 + share // 2 * shares) * owned, 128)
                up_ref[:, pl.ds(to, owned)] = part_ref[:, at * owned : (at + 1) * owned].astype(jnp.float32)
            out_ref[:, pl.ds(pl.multiple_of(share * part, 128), part)] = part_ref[:, blocks * owned :].astype(jnp.float32)

    return pl.pallas_call(
        kernel,
        grid_spec=pltpu.PrefetchScalarGridSpec(
            num_scalar_prefetch=1,
            grid=(1,),
            in_specs=[_fixed(rows, width)] * shares,
            out_specs=[_fixed(rows, blocks * shares * owned), _fixed(rows, shares * part)],
        ),
        out_shape=[
            jax.ShapeDtypeStruct((rows, blocks * shares * owned), jnp.float32),
            jax.ShapeDtypeStruct((rows, shares * part), jnp.float32),
        ],
        compiler_params=_params(8),
        cost_estimate=_cost(0),
        name="assemble",
    )(place, *parts)


def _bits(count):
    return [1 << place for place in range(count.bit_length() - 1)]


def _ordered(bits):
    places = [0]
    for bit in bits:
        places = [at + step for at in places for step in (0, bit)]
    return places


def _ordered_low(bits):
    places = [0]
    for bit in bits:
        places = places + [at + bit for at in places]
    return places


def _paired(values, axis, bit):
    count = lax.axis_size(axis)
    return lax.ppermute(values, axis, [(i, i ^ bit) for i in range(count)])


def _bit_of(axis, bit):
    return (lax.axis_index(axis) // bit) % 2


def _mesh_bit(place, step):
    axis, bit = step
    return place[("blk", "mb").index(axis)] // bit % 2


def _owner_stride(axis, bit, shares):
    return bit * shares if axis == "blk" else bit


def _share_places(shares):
    return [0, 1, shares, shares + 1]


def _place_at(bits, step):
    places = _ordered(bits)
    at = jnp.int32(places[0])
    for other in range(1, len(places)):
        at = jnp.where(step == other, places[other], at)
    return at


def grad_middle_call(place, boths, out_grads, lows, w_up, w_down, down_steps, up_steps):
    shares = len(boths)
    _, row_count, features = boths[0].shape
    all_rows = shares * row_count
    hidden = w_up.shape[1]
    blocks = 1 << len(up_steps)
    owned, each = hidden // (blocks * shares), features // (blocks * shares)
    down_places = [_owner_stride(*step, shares) for step in down_steps]
    up_places = [_owner_stride(*step, shares) for step in up_steps]
    share_places = _share_places(shares)
    part = lows[0].shape[1]
    half = blocks // 2
    pair = min(2, half)
    half_steps = half // pair
    sub = min(2, shares)

    def kernel(place_ref, *refs):
        groups, refs = [refs[at * shares : (at + 1) * shares] for at in range(3)], refs[3 * shares :]
        up_refs, down_refs, refs = refs[:pair], refs[pair : 2 * pair], refs[2 * pair :]
        down_send, down_keep, up_send, up_keep, norm_all, norm_turned, grad_all, active_all, upper_all, up_all = refs
        step = pl.program_id(0)
        mine = _mesh_bit(place_ref, up_steps[0])

        def spread():
            for at, block in enumerate(_ordered(up_places[1:])):
                for share, other in enumerate(share_places):
                    rows = slice((at * shares + share) * each, (at * shares + share + 1) * each)
                    up_send[rows, :] = up_all[block + other + up_places[0] * (1 - mine)].astype(jnp.bfloat16)
                    up_keep[rows, :] = up_all[block + other + up_places[0] * mine]

        @pl.when(step == 0)
        def _():
            for at in range(shares):
                rows = slice(at * row_count, (at + 1) * row_count)
                norm_all[rows, :] = groups[0][at][0]
                norm_turned[:, rows] = groups[0][at][0].T
                grad_all[rows, :] = groups[1][at][...]

        @pl.when(step < 2 * half_steps)
        def _():
            up_columns = jnp.concatenate([ref[...] for ref in up_refs], axis=1)
            down_rows = jnp.concatenate([ref[...] for ref in down_refs], axis=0)
            for at in range(0, all_rows, all_rows // sub):
                rows = slice(at, at + all_rows // sub)
                active_all[rows, :], upper_all[rows, :] = _hidden_parts(
                    norm_all[rows, :], grad_all[rows, :], up_columns, down_rows
                )
            down_made = contract_rows(active_all[...], grad_all[...])

            @pl.when(step < half_steps)
            def _():
                down_send[...] = down_made.astype(jnp.bfloat16)

            @pl.when(step >= half_steps)
            def _():
                down_keep[...] = down_made

            up_all[...] = matmul(norm_turned[...], upper_all[...]).reshape(blocks * shares, each, pair * owned)
            spread()

        @pl.when(step == 2 * half_steps)
        def _():
            made = jnp.zeros((features, part), jnp.float32)
            for both_ref, low_ref in zip(groups[0], groups[2]):
                made = made + contract_rows(both_ref[1], low_ref[...])
            up_all[...] = made.reshape(blocks * shares, each, part)
            spread()

    def first_bit(i, place):
        return (_mesh_bit(place, down_steps[0]) + 1 + jnp.minimum(i, 2 * half_steps - 1) // half_steps) % 2

    def unit_block(i, place, at):
        inner = _place_at(down_places[1:], jnp.minimum(i, 2 * half_steps - 1) % half_steps * pair + at)
        return inner + down_places[0] * first_bit(i, place) + place[0] % 2 * shares + place[1] % 2

    ups = [
        pl.BlockSpec((features, owned), lambda i, place, at=at: (0, unit_block(i, place, at))) for at in range(pair)
    ]
    downs = [
        pl.BlockSpec((owned, features), lambda i, place, at=at: (unit_block(i, place, at), 0)) for at in range(pair)
    ]
    def up_block(i, place):
        return (0, jnp.where(i == 2 * half_steps, i, first_bit(i, place) * half_steps + i % half_steps))

    up_out = pl.BlockSpec((features // 2, pair * owned), up_block)
    shapes = [(half * owned, features), (features // 2, blocks * owned + part)]
    return pl.pallas_call(
        kernel,
        grid_spec=pltpu.PrefetchScalarGridSpec(
            num_scalar_prefetch=1,
            grid=(2 * half_steps + 1,),
            in_specs=[_fixed(2, row_count, features)] * shares
            + [_fixed(row_count, features)] * shares
            + [_fixed(row_count, part)] * shares
            + ups
            + downs,
            out_specs=[
                pl.BlockSpec((pair * owned, features), lambda i, place: (jnp.minimum(i, half_steps - 1), 0)),
                pl.BlockSpec((pair * owned, features), lambda i, place: (jnp.clip(i - half_steps, 0, half_steps - 1), 0)),
                up_out,
                up_out,
            ],
            scratch_shapes=[
                pltpu.VMEM((all_rows, features), jnp.bfloat16),
                pltpu.VMEM((features, all_rows), jnp.bfloat16),
                pltpu.VMEM((all_rows, features), jnp.bfloat16),
                pltpu.VMEM((all_rows, pair * owned), jnp.bfloat16),
                pltpu.VMEM((all_rows, pair * owned), jnp.bfloat16),
                pltpu.VMEM((blocks * shares, each, pair * owned), jnp.float32),
            ],
        ),
        out_shape=[jax.ShapeDtypeStruct(shape, dtype) for shape in shapes for dtype in (jnp.bfloat16, jnp.float32)],
        compiler_params=_params(60),
        cost_estimate=_cost(20),
        name="grad_middle",
    )(place, *boths, *out_grads, *lows, *([w_up] * pair), *([w_down] * pair))


def halve_call(place, keep, received, step, cost):
    count, rows, columns = keep.shape
    half = count // 2

    def kernel(place_ref, keep_theirs, keep_mine, got_theirs, got_mine, theirs_ref, mine_ref):
        theirs_ref[...] = (keep_theirs[...] + got_theirs[...].astype(jnp.float32)).astype(jnp.bfloat16)
        mine_ref[...] = keep_mine[...] + got_mine[...].astype(jnp.float32)

    def block(which):
        return pl.BlockSpec(
            (1, rows, columns), lambda i, place: (i + half * ((_mesh_bit(place, step) + which) % 2), 0, 0)
        )

    out = pl.BlockSpec((1, rows, columns), lambda i, place: (i, 0, 0))
    return pl.pallas_call(
        kernel,
        grid_spec=pltpu.PrefetchScalarGridSpec(
            num_scalar_prefetch=1,
            grid=(half,),
            in_specs=[block(1), block(0), block(1), block(0)],
            out_specs=[out, out],
        ),
        out_shape=[
            jax.ShapeDtypeStruct((half, rows, columns), jnp.bfloat16),
            jax.ShapeDtypeStruct((half, rows, columns), jnp.float32),
        ],
        compiler_params=_params(16),
        cost_estimate=_cost(cost),
        name="halve",
    )(place, keep, keep, received, received)


def close_call(place, keep, received, shares):
    rows, width = keep.shape
    each = rows // shares

    def kernel(place_ref, keep_ref, got_ref, *refs):
        out_refs, total = refs[:-1], refs[-1]
        total[...] = (keep_ref[...] + got_ref[...].astype(jnp.float32)).reshape(shares, each, width)
        for share, out_ref in enumerate(out_refs):
            out_ref[...] = total[place_ref[2] ^ share].astype(jnp.bfloat16)

    return pl.pallas_call(
        kernel,
        grid_spec=pltpu.PrefetchScalarGridSpec(
            num_scalar_prefetch=1,
            grid=(1,),
            in_specs=[_fixed(rows, width)] * 2,
            out_specs=[_fixed(each, width)] * shares,
            scratch_shapes=[pltpu.VMEM((shares, each, width), jnp.float32)],
        ),
        out_shape=[jax.ShapeDtypeStruct((each, width), jnp.bfloat16)] * shares,
        compiler_params=_params(8),
        cost_estimate=_cost(0),
        name="close",
    )(place, keep, received)


def assemble_heads_call(parts, slot):
    blocks, rows, _ = parts.shape

    def kernel(parts_ref, *refs):
        weight_refs, norm_refs = refs[:3], refs[3:]
        for part, ref in enumerate(weight_refs):
            for block in range(blocks):
                ref[:, block * slot : (block + 1) * slot] = parts_ref[
                    block, :, part * slot : (part + 1) * slot
                ].astype(jnp.float32)
        sums = jnp.zeros((rows, 128), jnp.float32)
        for block in range(blocks):
            sums = sums + parts_ref[block, :, 3 * slot :].astype(jnp.float32)
        turned = jnp.concatenate([sums, jnp.zeros((128 - rows, 128), jnp.float32)], axis=0).T
        for at, ref in enumerate(norm_refs):
            ref[...] = turned[at : at + 1, 0:rows]

    return pl.pallas_call(
        kernel,
        out_shape=[jax.ShapeDtypeStruct((rows, blocks * slot), jnp.float32)] * 3
        + [jax.ShapeDtypeStruct((1, rows), jnp.float32)] * 4,
        compiler_params=_params(8),
        cost_estimate=_cost(0),
        name="assemble_heads",
    )(parts)


def fast_body(
    patches, seg_lengths, w_query, w_key, w_value, w_out, w_up, w_down,
    norm1_gain, norm1_bias, norm2_gain, norm2_bias, out_grad,
):
    micro_count, tokens, features = patches.shape
    hidden = w_up.shape[1]
    row_count = micro_count * tokens
    blocks, shares = lax.axis_size("blk"), lax.axis_size("mb")
    head_dim = features // H
    slot = features // blocks
    rows = patches.reshape(row_count, features)
    dout = out_grad.reshape(row_count, features)
    gain_one, bias_one, gain_two, bias_two = (
        value.reshape(1, features) for value in (norm1_gain, norm1_bias, norm2_gain, norm2_bias)
    )

    def swap(values):
        return lax.all_to_all(values, "blk", split_axis=0, concat_axis=0, tiled=True)

    def by_micro(values):
        return values.reshape(blocks, micro_count, tokens, values.shape[-1])

    at_blk, at_mb = lax.axis_index("blk"), lax.axis_index("mb")
    place = jnp.stack([at_blk, at_mb, at_mb % 2 + at_blk % 2 * 2]).astype(jnp.int32)
    blk_bits = _bits(blocks)
    up_steps = [("mb", 2), *(("blk", bit) for bit in blk_bits[1:])]
    down_steps = [up_steps[1], up_steps[0], *up_steps[2:]]
    each, owned, block_rows = features // (blocks * shares), hidden // (blocks * shares), features // blocks
    tie = lax.optimization_barrier

    def grown(values, bit):
        return jnp.concatenate([values, _paired(values, "blk", bit)], axis=0)

    def to_share(values, other):
        if other == 1:
            return _paired(values, "mb", 1)
        if other == 2:
            return _paired(values, "blk", 1)
        return lax.ppermute(values, ("blk", "mb"), [(i, i ^ (shares + 1)) for i in range(blocks * shares)])

    def shared(values):
        over = to_share(values, 2)
        return [values, to_share(values, 1), over, to_share(over, 1)]

    send, units_first, units_last = project_call(
        rows, gain_one, bias_one, w_query, w_key, w_value, blocks, tokens
    )
    received = by_micro(swap(send))
    dout_parts = [out_grad[micro] for micro in range(micro_count)]
    dout_over = [to_share(part, 2) for part in dout_parts]
    received, dout_over[0] = tie((received, dout_over[0]))
    units_first, received = tie((units_first, received))
    units_first = grown(units_first, blk_bits[-1])
    own_attended, exact, logs = attend_call(received, seg_lengths, head_dim)
    attended, units_first, dout_over = tie((own_attended.reshape(blocks, row_count, slot), units_first, dout_over))
    dout_over = jnp.concatenate(dout_over, axis=0)
    attended, units_first, units_last, *douts = tie(
        (swap(attended), units_first, units_last, dout, to_share(dout, 1), dout_over, to_share(dout_over, 1))
    )
    for bit in blk_bits[-2:0:-1]:
        units_first = grown(units_first, bit)
    units_last = grown(units_last, blk_bits[-1])
    places = _ordered_low([*blk_bits[:0:-1], blk_bits[0]])

    mixed, both = mix_call(attended, rows, gain_two, bias_two, w_out)
    both_peer, both_over = to_share(both, 1), to_share(both, 2)
    layer_out, mixed_grad, back, sums_two, *lows = middle_call(
        place, both, mixed, dout, gain_two, w_out, w_up, w_down, blocks, shares
    )
    back, lows, units_first, units_last, both_peer, both_over = tie(
        (back, lows, units_first, units_last, both_peer, both_over)
    )
    boths = [both, both_peer, both_over, to_share(both_over, 1)]
    units_first_peer = _paired(units_first, "blk", blk_bits[0])
    for bit in blk_bits[-2:0:-1]:
        units_last = grown(units_last, bit)
    grads = by_micro(swap(back))
    lows = [lows[0]] + [to_share(lows[share], share) for share in range(1, shares)]
    down_theirs, down_keep, up_theirs, up_keep = grad_middle_call(
        place, boths, douts, lows, w_up, w_down, down_steps, up_steps
    )
    down_theirs, down_keep = (value.reshape(-1, owned, features) for value in (down_theirs, down_keep))
    up_theirs, up_keep = (value.reshape(-1, block_rows, value.shape[-1]) for value in (up_theirs, up_keep))
    down_received, up_received = _paired(down_theirs, *down_steps[0]), _paired(up_theirs, *up_steps[0])
    grads, down_keep, units_last = tie((grads, down_keep, units_last))
    units_last_peer = _paired(units_last, "blk", blk_bits[0])
    made = attend_back_call(received, grads, exact, logs, seg_lengths, head_dim)
    returned = [swap(made[0])]

    def then(done, *values):
        return tie((done, values))[1]

    returned += [swap(tie((values, returned[0]))[0]) for values in made[1:]]
    made = tie(made)
    up_keep, up_received, units_first_peer = then(made[0], up_keep, up_received, units_first_peer)
    up_theirs, up_keep = halve_call(place, up_keep, up_received, up_steps[1], 0)
    up_received = _paired(up_theirs, *up_steps[1])
    down_keep, down_received, units_last_peer = then(up_keep, down_keep, down_received, units_last_peer)
    down_theirs, down_keep = halve_call(place, down_keep, down_received, down_steps[1], 5)
    down_received = _paired(down_theirs, *down_steps[1])
    made = then(down_keep, *made)
    heads_send, heads_keep = grad_heads_call(
        place, (units_first, units_first_peer, units_last, units_last_peer), (places, places),
        made, gain_one, bias_one, sums_two, w_query, w_key, w_value, shares,
    )
    pair = (shares // 2, -1, heads_keep.shape[-1])
    heads_received = _paired(heads_send, "mb", 1).reshape(pair)
    down_keep, down_received = then(heads_keep, down_keep, down_received)
    for step in down_steps[2:]:
        down_theirs, down_keep = halve_call(place, down_keep, down_received, step, 0)
        down_received = _paired(down_theirs, *step)
    up_keep, up_received = then(down_keep, up_keep, up_received)
    for step in up_steps[2:]:
        up_theirs, up_keep = halve_call(place, up_keep, up_received, step, 3)
        up_received = _paired(up_theirs, *step)
    heads_theirs, heads_keep = halve_call(
        place, *then(up_keep, heads_keep.reshape(pair), heads_received), ("mb", 2), 0
    )
    heads_received = _paired(heads_theirs, "mb", 2)
    returned = list(then(heads_keep, *returned))
    patches_grad = finish_call(returned, rows, mixed_grad, gain_one, w_query, w_key, w_value)
    up_keep, up_received = then(patches_grad, up_keep, up_received)
    parts = close_call(place, up_keep[0], up_received[0], shares)
    heads_keep, heads_received = then(parts, heads_keep, heads_received)
    heads_total = (heads_keep + heads_received.astype(jnp.float32)).astype(jnp.bfloat16)
    heads_total = swap(heads_total.reshape(blocks, each, heads_keep.shape[-1]))
    parts = [parts[0]] + [to_share(parts[share], share) for share in range(1, shares)]
    up_total, out_total = assemble_call(place, parts, down_steps, blocks, owned)
    down_keep, down_received = then(up_total, down_keep, down_received)
    down_total = (down_keep + down_received.astype(jnp.float32))[0]
    query_total, key_total, value_total, *sums = assemble_heads_call(then(down_total, heads_total)[0], slot)
    return (
        layer_out.reshape(patches.shape),
        patches_grad.reshape(patches.shape),
        query_total,
        key_total,
        value_total,
        out_total,
        up_total,
        down_total,
        *(value.reshape(each) for value in sums),
    )


def solution(mesh):
    in_specs = (
        P("mb", "blk", None),
        P("mb", None),
        P(),
        P(),
        P(),
        P(),
        P(),
        P(),
        P(),
        P(),
        P(),
        P(),
        P("mb", "blk", None),
    )
    out_specs = (
        P("mb", "blk", None),
        P("mb", "blk", None),
        P(("blk", "mb"), None),
        P(("blk", "mb"), None),
        P(("blk", "mb"), None),
        P(("blk", "mb"), None),
        P(("blk", "mb"), None),
        P(("blk", "mb"), None),
        P(("blk", "mb")),
        P(("blk", "mb")),
        P(("blk", "mb")),
        P(("blk", "mb")),
    )
    blocks, shares = mesh.shape["blk"], mesh.shape["mb"]
    paired = blocks >= 4 and blocks & (blocks - 1) == 0 and shares == 4
    chosen_body = fast_body if paired and H % blocks == 0 else body
    return jax.shard_map(chosen_body, mesh=mesh, in_specs=in_specs, out_specs=out_specs, check_vma=False)
```

```python
import math

import jax
import jax.numpy as jnp
from jax import lax
from jax.experimental import pallas as pl
from jax.experimental.pallas import tpu as pltpu
from jax.sharding import PartitionSpec as P

H = 16
CHUNK = 8


epsilon = 1e-05
masked_score = -1e30


def layer_norm(values, norm_gain, norm_bias):
    center = values - jnp.mean(values, axis=-1, keepdims=True)
    variance = jnp.mean(center * center, axis=-1, keepdims=True)
    return center * lax.rsqrt(variance + epsilon) * norm_gain + norm_bias


def gelu_exact(values):
    return jax.nn.gelu(values, approximate=False)


def matmul(left_side, right_side):
    return jnp.dot(left_side, right_side, preferred_element_type=jnp.float32)


def contract_rows(left_side, right_side):
    return lax.dot_general(
        left_side, right_side, (((0,), (0,)), ((), ())), preferred_element_type=jnp.float32
    )


def contract_cols(left_side, right_side):
    return lax.dot_general(
        left_side, right_side, (((1,), (1,)), ((), ())), preferred_element_type=jnp.float32
    )


def segment_ids(lengths, positions):
    doc_ends = jnp.cumsum(lengths, axis=-1)
    return jnp.sum((positions[None, :, None] >= doc_ends[:, None, :]).astype(jnp.int32), axis=-1)


def masked_scores(query_piece, keys_all, query_docs, key_docs, score_scale):
    scores = contract_cols(query_piece, keys_all) * score_scale
    return jnp.where(query_docs[:, None] == key_docs[None, :], scores, masked_score)


def soft_rows(scores):
    row_max = jnp.max(scores, axis=-1, keepdims=True)
    exponent = jnp.exp(scores - row_max)
    return exponent / jnp.sum(exponent, axis=-1, keepdims=True)


def body(
    patches,
    seg_lengths,
    w_query,
    w_key,
    w_value,
    w_out,
    w_up,
    w_down,
    norm1_gain,
    norm1_bias,
    norm2_gain,
    norm2_bias,
    out_grad,
):
    micro_count, tokens, features = patches.shape
    row_count = micro_count * tokens
    blocks = lax.axis_size("blk")
    block_index = lax.axis_index("blk")
    head_count = H
    head_dim = features // head_count
    repeat = max(1, blocks // head_count)
    per_slot = max(1, head_count // blocks)
    groups = head_count // per_slot
    rows_part = tokens // repeat
    query_rows = blocks * rows_part
    seq_length = blocks * tokens
    item_count = micro_count * per_slot
    block_rows = min(512, query_rows)
    block_count = query_rows // block_rows
    slot_width = micro_count * per_slot * head_dim
    score_scale = 1.0 / math.sqrt(head_dim)
    doc_count = seg_lengths.shape[1]

    def query_layout(values):
        shaped = values.reshape(micro_count, repeat, rows_part, groups, per_slot * head_dim)
        return shaped.transpose(3, 1, 2, 0, 4).reshape(blocks, rows_part, slot_width)

    def key_layout(values):
        shaped = values.reshape(micro_count, tokens, groups, per_slot * head_dim).transpose(
            2, 1, 0, 3
        )
        shaped = jnp.broadcast_to(
            shaped[:, None], (groups, repeat, tokens, micro_count, per_slot * head_dim)
        )
        return shaped.reshape(blocks, tokens, slot_width)

    def token_layout(values):
        shaped = values.reshape(groups, repeat, rows_part, micro_count, per_slot * head_dim)
        return shaped.transpose(3, 1, 2, 0, 4).reshape(row_count, features)

    def key_sum(values):
        shaped = values.reshape(groups, repeat, tokens, micro_count, per_slot * head_dim).sum(
            axis=1
        )
        return shaped.transpose(2, 1, 0, 3).reshape(row_count, features)

    def to_items(received):
        row_total = received.shape[1]
        shaped = received.reshape(row_total, micro_count, per_slot, head_dim).transpose(1, 2, 0, 3)
        return shaped.reshape(item_count, row_total, head_dim)

    def from_items(values):
        row_total = values.shape[1]
        shaped = values.reshape(micro_count, per_slot, row_total, head_dim).transpose(2, 0, 1, 3)
        return shaped.reshape(1, row_total, slot_width)

    row_ids = jnp.arange(query_rows)
    query_pos = (
        row_ids // rows_part * tokens + block_index % repeat * rows_part + row_ids % rows_part
    )
    query_docs = jnp.repeat(segment_ids(seg_lengths, query_pos), per_slot, axis=0)
    key_docs = jnp.repeat(segment_ids(seg_lengths, jnp.arange(seq_length)), per_slot, axis=0)
    query_valid = (query_docs < doc_count).astype(jnp.float32)
    local_pos = block_index * tokens + jnp.arange(tokens)
    row_valid = (
        (segment_ids(seg_lengths, local_pos) < doc_count).astype(jnp.float32).reshape(row_count, 1)
    )

    def forward_item(operands):
        queries_item, keys_item, values_item, docs_item, key_docs_item = operands

        def forward_one_block(block_operands):
            query_piece, docs_piece = block_operands
            weights_soft = soft_rows(
                masked_scores(query_piece, keys_item, docs_piece, key_docs_item, score_scale)
            )
            return matmul(weights_soft.astype(jnp.bfloat16), values_item)

        outputs = lax.map(
            forward_one_block,
            (
                queries_item.reshape(block_count, block_rows, head_dim),
                docs_item.reshape(block_count, block_rows),
            ),
        )
        return outputs.reshape(query_rows, head_dim)

    def backward_item(operands):
        queries_item, keys_item, values_item, grads_item, docs_item, key_docs_item = operands

        def backward_one_block(totals, block_operands):
            key_total, value_total = totals
            query_piece, grad_piece, docs_piece = block_operands
            weights_soft = soft_rows(
                masked_scores(query_piece, keys_item, docs_piece, key_docs_item, score_scale)
            )
            weights_low = weights_soft.astype(jnp.bfloat16)
            weight_grads = contract_cols(grad_piece, values_item)
            row_inner = jnp.sum(weights_soft * weight_grads, axis=-1, keepdims=True)
            score_grads = (weights_soft * (weight_grads - row_inner)).astype(jnp.bfloat16)
            query_grad = matmul(score_grads, keys_item) * score_scale
            key_total = key_total + contract_rows(score_grads, query_piece) * score_scale
            value_total = value_total + contract_rows(weights_low, grad_piece)
            return ((key_total, value_total), query_grad)

        zero_block = jnp.zeros((seq_length, head_dim), jnp.float32)
        totals, query_grads = lax.scan(
            backward_one_block,
            (zero_block, zero_block),
            (
                queries_item.reshape(block_count, block_rows, head_dim),
                grads_item.reshape(block_count, block_rows, head_dim),
                docs_item.reshape(block_count, block_rows),
            ),
        )
        return (query_grads.reshape(query_rows, head_dim), totals[0], totals[1])

    inputs = patches.astype(jnp.float32).reshape(row_count, features)
    norm_one_full, norm_one_pull = jax.vjp(layer_norm, inputs, norm1_gain, norm1_bias)
    norm_one = norm_one_full.astype(jnp.bfloat16)
    queries = matmul(norm_one, w_query).astype(jnp.bfloat16)
    keys_proj = matmul(norm_one, w_key).astype(jnp.bfloat16)
    values_proj = matmul(norm_one, w_value).astype(jnp.bfloat16)
    query_send = query_layout(queries)
    key_send = key_layout(keys_proj)
    value_send = key_layout(values_proj)
    query_heads, key_heads, value_heads = (
        lax.all_to_all(query_send, "blk", split_axis=0, concat_axis=1, tiled=True),
        lax.all_to_all(key_send, "blk", split_axis=0, concat_axis=1, tiled=True),
        lax.all_to_all(value_send, "blk", split_axis=0, concat_axis=1, tiled=True),
    )
    query_items = to_items(query_heads)
    key_items = to_items(key_heads)
    value_items = to_items(value_heads)
    attended_items = lax.map(
        forward_item, (query_items, key_items, value_items, query_docs, key_docs)
    )
    attended_items = (attended_items * query_valid[:, :, None]).astype(jnp.bfloat16)
    attended = token_layout(
        lax.all_to_all(from_items(attended_items), "blk", split_axis=1, concat_axis=0, tiled=True)
    )
    mixed_rows = inputs + matmul(attended, w_out)
    norm_two_full, norm_two_pull = jax.vjp(layer_norm, mixed_rows, norm2_gain, norm2_bias)
    norm_two = norm_two_full.astype(jnp.bfloat16)
    upper_proj = matmul(norm_two, w_up)
    active_full, gelu_pull = jax.vjp(gelu_exact, upper_proj)
    active = active_full.astype(jnp.bfloat16)
    result = mixed_rows + matmul(active, w_down)
    layer_out = result.astype(jnp.bfloat16).reshape(micro_count, tokens, features)
    dout_low = out_grad.reshape(row_count, features)
    down_grad = contract_rows(active, dout_low)
    active_grad = contract_cols(dout_low, w_down)
    upper_grad = gelu_pull(active_grad)[0].astype(jnp.bfloat16)
    up_grad = contract_rows(norm_two, upper_grad)
    norm_two_grad = contract_cols(upper_grad, w_up)
    mixed_part, gain_two_grad, bias_two_grad = norm_two_pull(norm_two_grad)
    mixed_grad = dout_low.astype(jnp.float32) + mixed_part
    mixed_low = mixed_grad.astype(jnp.bfloat16)
    out_proj_grad = contract_rows(attended, mixed_low)
    attended_grad = (contract_cols(mixed_low, w_out) * row_valid).astype(jnp.bfloat16)
    grad_send = query_layout(attended_grad)
    query_again, key_again, value_again, grad_heads = (
        lax.all_to_all(query_send, "blk", split_axis=0, concat_axis=1, tiled=True),
        lax.all_to_all(key_send, "blk", split_axis=0, concat_axis=1, tiled=True),
        lax.all_to_all(value_send, "blk", split_axis=0, concat_axis=1, tiled=True),
        lax.all_to_all(grad_send, "blk", split_axis=0, concat_axis=1, tiled=True),
    )
    back_queries = to_items(query_again)
    back_keys = to_items(key_again)
    back_values = to_items(value_again)
    grad_items = to_items(grad_heads)
    query_grad_items, key_grad_items, value_grad_items = lax.map(
        backward_item, (back_queries, back_keys, back_values, grad_items, query_docs, key_docs)
    )
    query_back, key_back, value_back = (
        lax.all_to_all(
            from_items(query_grad_items).astype(jnp.bfloat16),
            "blk",
            split_axis=1,
            concat_axis=0,
            tiled=True,
        ).astype(jnp.float32),
        lax.all_to_all(
            from_items(key_grad_items).astype(jnp.bfloat16),
            "blk",
            split_axis=1,
            concat_axis=0,
            tiled=True,
        ).astype(jnp.float32),
        lax.all_to_all(
            from_items(value_grad_items).astype(jnp.bfloat16),
            "blk",
            split_axis=1,
            concat_axis=0,
            tiled=True,
        ).astype(jnp.float32),
    )
    query_grad = token_layout(query_back).astype(jnp.bfloat16)
    key_grad = key_sum(key_back).astype(jnp.bfloat16)
    value_grad = key_sum(value_back).astype(jnp.bfloat16)
    query_proj_grad = contract_rows(norm_one, query_grad)
    key_proj_grad = contract_rows(norm_one, key_grad)
    value_proj_grad = contract_rows(norm_one, value_grad)
    norm_one_grad = (
        contract_cols(query_grad, w_query)
        + contract_cols(key_grad, w_key)
        + contract_cols(value_grad, w_value)
    )
    input_part, gain_one_grad, bias_one_grad = norm_one_pull(norm_one_grad)
    patches_grad = (
        (mixed_grad + input_part).astype(jnp.bfloat16).reshape(micro_count, tokens, features)
    )
    gradients = (
        query_proj_grad,
        key_proj_grad,
        value_proj_grad,
        out_proj_grad,
        up_grad,
        down_grad,
        gain_one_grad,
        bias_one_grad,
        gain_two_grad,
        bias_two_grad,
    )
    summed = (
        lax.psum_scatter(gradients[0], ("blk", "mb"), scatter_dimension=0, tiled=True),
        lax.psum_scatter(gradients[1], ("blk", "mb"), scatter_dimension=0, tiled=True),
        lax.psum_scatter(gradients[2], ("blk", "mb"), scatter_dimension=0, tiled=True),
        lax.psum_scatter(gradients[3], ("blk", "mb"), scatter_dimension=0, tiled=True),
        lax.psum_scatter(gradients[4], ("blk", "mb"), scatter_dimension=0, tiled=True),
        lax.psum_scatter(gradients[5], ("blk", "mb"), scatter_dimension=0, tiled=True),
        lax.psum_scatter(gradients[6], ("blk", "mb"), scatter_dimension=0, tiled=True),
        lax.psum_scatter(gradients[7], ("blk", "mb"), scatter_dimension=0, tiled=True),
        lax.psum_scatter(gradients[8], ("blk", "mb"), scatter_dimension=0, tiled=True),
        lax.psum_scatter(gradients[9], ("blk", "mb"), scatter_dimension=0, tiled=True),
    )
    return (
        layer_out,
        patches_grad,
        summed[0],
        summed[1],
        summed[2],
        summed[3],
        summed[4],
        summed[5],
        summed[6],
        summed[7],
        summed[8],
        summed[9],
    )


def _normalize(values):
    center = values - jnp.mean(values, axis=-1, keepdims=True)
    variance = jnp.mean(center * center, axis=-1, keepdims=True)
    inverse = lax.rsqrt(variance + epsilon)
    return center * inverse, inverse


def _normalize_back(grads, gain, unit, inverse):
    scaled = grads * gain
    mean_scaled = jnp.mean(scaled, axis=-1, keepdims=True)
    mean_product = jnp.mean(scaled * unit, axis=-1, keepdims=True)
    return (scaled - mean_scaled - unit * mean_product) * inverse


def _doc_ids(lengths_ref, micro, doc_count, positions):
    end = jnp.int32(0)
    ids = jnp.zeros_like(positions)
    for doc in range(doc_count):
        end = end + lengths_ref[micro, doc]
        ids = ids + (positions >= end).astype(jnp.int32)
    return ids


def _params(mib):
    return pltpu.CompilerParams(vmem_limit_bytes=mib << 20)


def _cost(microseconds):
    return pl.CostEstimate(flops=int(microseconds * 1e9) + 1, bytes_accessed=1, transcendentals=0)


def project_call(rows, gain, bias, w_query, w_key, w_value, blocks, tokens):
    row_count, features = rows.shape
    slot = features // blocks
    per_step = max(1, min(blocks, 512 // slot))
    wide = slot * per_step

    def kernel(rows_ref, gain_ref, bias_ref, wq_ref, wk_ref, wv_ref, send_ref, *refs):
        unit_refs, norm_ref = refs[:-1], refs[-1]


        @pl.when(pl.program_id(0) == 0)
        def _():
            unit, _unused = _normalize(rows_ref[...].astype(jnp.float32))
            for micro, unit_ref in enumerate(unit_refs):
                unit_ref[...] = unit[micro * tokens : (micro + 1) * tokens].astype(jnp.bfloat16)
            norm_ref[...] = (unit * gain_ref[...] + bias_ref[...]).astype(jnp.bfloat16)

        for part, weight_ref in enumerate((wq_ref, wk_ref, wv_ref)):
            made = matmul(norm_ref[...], weight_ref[...]).astype(jnp.bfloat16)
            for piece in range(per_step):
                send_ref[piece, :, part * slot : (part + 1) * slot] = made[
                    :, piece * slot : (piece + 1) * slot
                ]

    whole = pl.BlockSpec((row_count, features), lambda i: (0, 0))
    vector = pl.BlockSpec((1, features), lambda i: (0, 0))
    columns = pl.BlockSpec((features, wide), lambda i: (0, i))
    return pl.pallas_call(
        kernel,
        grid=(blocks // per_step,),
        in_specs=[whole, vector, vector, columns, columns, columns],
        out_specs=[pl.BlockSpec((per_step, row_count, 3 * slot), lambda i: (i, 0, 0))]
        + [pl.BlockSpec((tokens, features), lambda i: (0, 0))] * (row_count // tokens),
        out_shape=[jax.ShapeDtypeStruct((blocks, row_count, 3 * slot), jnp.bfloat16)]
        + [jax.ShapeDtypeStruct((tokens, features), jnp.bfloat16)] * (row_count // tokens),
        scratch_shapes=[pltpu.VMEM((row_count, features), jnp.bfloat16)],
        compiler_params=_params(60),
        cost_estimate=_cost(6),
        name="project",
    )(rows, gain, bias, w_query, w_key, w_value)


def _head_masks(slot, head_dim, dtype):
    lanes = lax.broadcasted_iota(jnp.int32, (1, slot), 1)
    return [(lanes // head_dim == head).astype(dtype) for head in range(slot // head_dim)]


def _key_range(lengths_ref, micro, doc_count, first_row, last_row, seq):
    low, high, end = jnp.int32(0), jnp.int32(seq), jnp.int32(0)
    for doc in range(doc_count):
        end = end + lengths_ref[micro, doc]
        low = jnp.where(end <= first_row, jnp.maximum(low, end), low)
        high = jnp.where(end >= last_row, jnp.minimum(high, end), high)
    return low, high


def _by_key_range(lengths_ref, micro, doc_count, step, rows, blocks, tokens, compute):
    low, high = _key_range(lengths_ref, micro, doc_count, step * rows, (step + 1) * rows, blocks * tokens)
    half = blocks // 2
    in_low, in_high = high <= half * tokens, low >= half * tokens

    @pl.when(in_low | in_high)
    def _():
        compute(jnp.where(in_low, 0, half), half)

    @pl.when(jnp.logical_not(in_low | in_high))
    def _():
        compute(0, blocks)


def attend_call(received, lengths, head_dim):
    blocks, micro_count, tokens, width = received.shape
    slot = width // 3
    doc_count = lengths.shape[1]
    step_blocks = max(1, min(blocks // 2, 512 // tokens))
    rows = step_blocks * tokens
    scale = 1.0 / math.sqrt(head_dim)

    def kernel(lengths_ref, data_ref, out_ref, exact_ref, log_ref):
        micro = pl.program_id(0)
        step = pl.program_id(1)
        row_docs = _doc_ids(
            lengths_ref, micro, doc_count, lax.broadcasted_iota(jnp.int32, (rows, 1), 0) + step * rows
        )
        queries = data_ref[pl.ds(step * step_blocks, step_blocks), 0, :, 0:slot].reshape(rows, slot) * scale

        def compute(first, count):
            seq = count * tokens
            key_docs = _doc_ids(
                lengths_ref, micro, doc_count, lax.broadcasted_iota(jnp.int32, (1, seq), 1) + first * tokens
            )
            same = row_docs == key_docs
            keys = data_ref[pl.ds(first, count), 0, :, slot : 2 * slot].reshape(seq, slot)
            values = data_ref[pl.ds(first, count), 0, :, 2 * slot : 3 * slot].reshape(seq, slot)
            total = jnp.zeros((rows, slot), jnp.float32)
            logs = jnp.zeros((rows, 128), jnp.float32)
            lanes = lax.broadcasted_iota(jnp.int32, (1, 128), 1)
            for head, (mask, mask_wide) in enumerate(
                zip(_head_masks(slot, head_dim, jnp.bfloat16), _head_masks(slot, head_dim, jnp.float32))
            ):
                scores = jnp.where(same, contract_cols(queries * mask, keys), masked_score)
                most = jnp.max(scores, axis=-1, keepdims=True)
                exponent = jnp.exp(scores - most)
                exponent_sum = jnp.sum(exponent, axis=-1, keepdims=True)
                share = 1.0 / exponent_sum
                logs = jnp.where(lanes == head, most + jnp.log(exponent_sum), logs)
                total = total + matmul(exponent.astype(jnp.bfloat16), values) * (share * mask_wide)
            total = jnp.where(row_docs < doc_count, total, 0.0)
            out_ref[...] = total.astype(jnp.bfloat16).reshape(step_blocks, 1, tokens, slot)
            exact_ref[...] = total.reshape(step_blocks, 1, tokens, slot)
            log_ref[0] = logs.T[0:8, :]

        _by_key_range(lengths_ref, micro, doc_count, step, rows, blocks, tokens, compute)

    return pl.pallas_call(
        kernel,
        grid=(micro_count, blocks // step_blocks),
        in_specs=[
            pl.BlockSpec(memory_space=pltpu.SMEM),
            pl.BlockSpec((blocks, 1, tokens, width), lambda m, s: (0, m, 0, 0)),
        ],
        out_specs=[
            pl.BlockSpec((step_blocks, 1, tokens, slot), lambda m, s: (s, m, 0, 0)),
            pl.BlockSpec((step_blocks, 1, tokens, slot), lambda m, s: (s, m, 0, 0)),
            pl.BlockSpec((1, 8, rows), lambda m, s: (m, 0, s)),
        ],
        out_shape=[
            jax.ShapeDtypeStruct((blocks, micro_count, tokens, slot), jnp.bfloat16),
            jax.ShapeDtypeStruct((blocks, micro_count, tokens, slot), jnp.float32),
            jax.ShapeDtypeStruct((micro_count, 8, blocks * tokens), jnp.float32),
        ],
        compiler_params=_params(32),
        cost_estimate=_cost(11),
        name="attend",
    )(lengths, received)


def attend_back_call(received, grads, attended, logs, lengths, head_dim):
    blocks, micro_count, tokens, width = received.shape
    slot = width // 3
    doc_count = lengths.shape[1]
    step_blocks = max(1, min(blocks // 2, 512 // tokens))
    rows = step_blocks * tokens
    steps = blocks // step_blocks
    scale = 1.0 / math.sqrt(head_dim)

    def kernel(lengths_ref, data_ref, grads_ref, att_ref, log_ref, *refs):
        out_refs, (key_total, value_total, turned) = refs[:micro_count], refs[micro_count:]
        micro = pl.program_id(0)
        step = pl.program_id(1)

        @pl.when(step == 0)
        def _():
            key_total[...] = jnp.zeros_like(key_total)
            value_total[...] = jnp.zeros_like(value_total)
            for block in range(blocks):
                turned[block] = data_ref[block, 0, :, slot : 2 * slot].T

        row_docs = _doc_ids(
            lengths_ref, micro, doc_count, lax.broadcasted_iota(jnp.int32, (1, rows), 1) + step * rows
        )
        column_docs = _doc_ids(
            lengths_ref, micro, doc_count, lax.broadcasted_iota(jnp.int32, (rows, 1), 0) + step * rows
        )
        queries = data_ref[pl.ds(step * step_blocks, step_blocks), 0, :, 0:slot].reshape(rows, slot) * scale
        out_grads = grads_ref[...].reshape(rows, slot)
        out_grads = out_grads * (column_docs < doc_count).astype(jnp.float32).astype(jnp.bfloat16)

        inner = (out_grads.astype(jnp.float32) * att_ref[...].reshape(rows, slot)).T

        def compute(first, count):
            chunk = min(CHUNK, count)
            query_parts = [jnp.zeros((head_dim, rows), jnp.float32) for _ in range(slot // head_dim)]
            masks = _head_masks(slot, head_dim, jnp.bfloat16)
            for at in range(0, count, chunk):
                seq = chunk * tokens
                key_docs = _doc_ids(
                    lengths_ref,
                    micro,
                    doc_count,
                    lax.broadcasted_iota(jnp.int32, (seq, 1), 0) + (first + at) * tokens,
                )
                same = row_docs == key_docs
                keys = data_ref[pl.ds(first + at, chunk), 0, :, slot : 2 * slot].reshape(seq, slot)
                values = data_ref[pl.ds(first + at, chunk), 0, :, 2 * slot : 3 * slot].reshape(seq, slot)
                keys_turned = jnp.concatenate([turned[first + at + other] for other in range(chunk)], axis=1)
                key_made = jnp.zeros((seq, slot), jnp.float32)
                value_made = jnp.zeros((seq, slot), jnp.float32)
                for head, mask in enumerate(masks):
                    lanes = slice(head * head_dim, (head + 1) * head_dim)
                    queries_head, grads_head = queries * mask, out_grads * mask
                    scores = jnp.where(same, contract_cols(keys, queries_head), masked_score)
                    probs = jnp.exp(scores - log_ref[0, head : head + 1, :])
                    prob_grads = contract_cols(values, grads_head)
                    head_inner = jnp.sum(inner[lanes], axis=0, keepdims=True)
                    score_grads = (probs * (prob_grads - head_inner)).astype(jnp.bfloat16)
                    value_made = value_made + matmul(probs.astype(jnp.bfloat16), grads_head)
                    key_made = key_made + matmul(score_grads, queries_head)
                    query_parts[head] = query_parts[head] + matmul(keys_turned[lanes], score_grads)
                to = pl.ds(pl.multiple_of((first + at) * tokens, tokens), seq)
                key_total[to, :] += key_made
                value_total[to, :] += value_made
            query_grads = (jnp.concatenate(query_parts, axis=0).T * scale).astype(jnp.bfloat16).reshape(step_blocks, tokens, slot)
            for at, out_ref in enumerate(out_refs):

                @pl.when(micro == at)
                def _():
                    out_ref[pl.ds(step * step_blocks, step_blocks), :, 0:slot] = query_grads

        _by_key_range(lengths_ref, micro, doc_count, step, rows, blocks, tokens, compute)

        for at, out_ref in enumerate(out_refs):

            @pl.when((step == steps - 1) & (micro == at))
            def _():
                out_ref[:, :, slot : 2 * slot] = key_total[...].astype(jnp.bfloat16).reshape(blocks, tokens, slot)
                out_ref[:, :, 2 * slot :] = value_total[...].astype(jnp.bfloat16).reshape(blocks, tokens, slot)

    return pl.pallas_call(
        kernel,
        grid=(micro_count, steps),
        in_specs=[
            pl.BlockSpec(memory_space=pltpu.SMEM),
            pl.BlockSpec((blocks, 1, tokens, width), lambda m, s: (0, m, 0, 0)),
            pl.BlockSpec((step_blocks, 1, tokens, slot), lambda m, s: (s, m, 0, 0)),
            pl.BlockSpec((step_blocks, 1, tokens, slot), lambda m, s: (s, m, 0, 0)),
            pl.BlockSpec((1, 8, rows), lambda m, s: (m, 0, s)),
        ],
        out_specs=[pl.BlockSpec((blocks, tokens, width), lambda m, s: (0, 0, 0))] * micro_count,
        out_shape=[jax.ShapeDtypeStruct((blocks, tokens, width), jnp.bfloat16)] * micro_count,
        scratch_shapes=[pltpu.VMEM((blocks * tokens, slot), jnp.float32)] * 2
        + [pltpu.VMEM((blocks, slot, tokens), jnp.bfloat16)],
        compiler_params=_params(60),
        cost_estimate=_cost(3),
        name="attend_back",
    )(lengths, received, grads, attended, logs)


def _fixed(*shape):
    return pl.BlockSpec(shape, lambda *_unused: (0,) * len(shape))


def mix_call(attended, rows, gain, bias, w_out):
    blocks, row_count, slot = attended.shape
    features = rows.shape[1]

    def kernel(att_ref, rows_ref, gain_ref, bias_ref, wo_ref, mixed_ref, both_ref):
        for block in range(blocks):
            both_ref[1, :, block * slot : (block + 1) * slot] = att_ref[block]
        value = rows_ref[...].astype(jnp.float32) + matmul(both_ref[1], wo_ref[...])
        mixed_ref[...] = value
        unit, _unused = _normalize(value)
        both_ref[0] = (unit * gain_ref[...] + bias_ref[...]).astype(jnp.bfloat16)

    rows_spec, vector = _fixed(row_count, features), _fixed(1, features)
    return pl.pallas_call(
        kernel,
        grid=(1,),
        in_specs=[_fixed(blocks, row_count, slot), rows_spec, vector, vector, _fixed(features, features)],
        out_specs=[rows_spec, _fixed(2, row_count, features)],
        out_shape=[
            jax.ShapeDtypeStruct((row_count, features), jnp.float32),
            jax.ShapeDtypeStruct((2, row_count, features), jnp.bfloat16),
        ],
        compiler_params=_params(24),
        cost_estimate=_cost(4),
        name="mix",
    )(attended, rows, gain, bias, w_out)


def _hidden_parts(norm, out_grad, up_columns, down_rows):
    upper = matmul(norm, up_columns)
    active_grad = contract_cols(out_grad, down_rows)
    half = (1.0 + lax.erf(upper * (1.0 / math.sqrt(2.0)))) * 0.5
    slope = half + upper * jnp.exp(upper * upper * -0.5) * (1.0 / math.sqrt(2.0 * math.pi))
    return (upper * half).astype(jnp.bfloat16), (active_grad * slope).astype(jnp.bfloat16)


def middle_call(place, both, mixed, out_grad, gain, w_out, w_up, w_down, blocks, shares):
    row_count, features = mixed.shape
    hidden = w_up.shape[1]
    wide = min(1024, hidden)
    sub = min(512, wide)
    steps = hidden // wide
    slot, part = features // blocks, features // shares

    def kernel(place_ref, norm_ref, mixed_ref, grad_ref, gain_ref, wo_ref, wu_ref, wd_ref, *refs):
        out_ref, mixed_grad_ref, back_ref, sums_ref = refs[:4]
        low_refs, (total, grad_total, active_all, upper_all, low_all) = refs[4 : 4 + shares], refs[4 + shares :]
        step = pl.program_id(0)

        @pl.when(step == 0)
        def _():
            total[...] = mixed_ref[...]
            grad_total[...] = jnp.zeros_like(grad_total)

        for chunk in range(0, wide, sub):
            active, upper_grad = _hidden_parts(
                norm_ref[0], grad_ref[...], wu_ref[:, chunk : chunk + sub], wd_ref[chunk : chunk + sub, :]
            )
            active_all[:, chunk : chunk + sub] = active
            upper_all[:, chunk : chunk + sub] = upper_grad
        total[...] += matmul(active_all[...], wd_ref[...])
        grad_total[...] += contract_cols(upper_all[...], wu_ref[...])

        @pl.when(step == steps - 1)
        def _():
            out_ref[...] = total[...].astype(jnp.bfloat16)
            unit, inverse = _normalize(mixed_ref[...])
            grads = grad_total[...]
            sums_ref[0:1, :] = jnp.sum(grads * unit, axis=0, keepdims=True)
            sums_ref[1:2, :] = jnp.sum(grads, axis=0, keepdims=True)
            mixed_grad = grad_ref[...].astype(jnp.float32) + _normalize_back(grads, gain_ref[...], unit, inverse)
            mixed_grad_ref[...] = mixed_grad
            low = mixed_grad.astype(jnp.bfloat16)
            low_all[...] = low
            for share, low_ref in enumerate(low_refs):
                low_ref[...] = low_all[:, pl.ds(pl.multiple_of((place_ref[2] ^ share) * part, 128), part)]
            back = contract_cols(low, wo_ref[...]).astype(jnp.bfloat16)
            for block in range(blocks):
                back_ref[block] = back[:, block * slot : (block + 1) * slot]

    rows_spec = _fixed(row_count, features)
    return pl.pallas_call(
        kernel,
        grid_spec=pltpu.PrefetchScalarGridSpec(
            num_scalar_prefetch=1,
            grid=(steps,),
            in_specs=[
                _fixed(1, row_count, features),
                rows_spec,
                rows_spec,
                _fixed(1, features),
                _fixed(features, features),
                pl.BlockSpec((features, wide), lambda i, place: (0, i)),
                pl.BlockSpec((wide, features), lambda i, place: (i, 0)),
            ],
            out_specs=[rows_spec, rows_spec, _fixed(blocks, row_count, slot), _fixed(2, features)]
            + [_fixed(row_count, part)] * shares,
            scratch_shapes=[
                pltpu.VMEM((row_count, features), jnp.float32),
                pltpu.VMEM((row_count, features), jnp.float32),
                pltpu.VMEM((row_count, wide), jnp.bfloat16),
                pltpu.VMEM((row_count, wide), jnp.bfloat16),
                pltpu.VMEM((row_count, features), jnp.bfloat16),
            ],
        ),
        out_shape=[
            jax.ShapeDtypeStruct((row_count, features), jnp.bfloat16),
            jax.ShapeDtypeStruct((row_count, features), jnp.float32),
            jax.ShapeDtypeStruct((blocks, row_count, slot), jnp.bfloat16),
            jax.ShapeDtypeStruct((2, features), jnp.float32),
        ]
        + [jax.ShapeDtypeStruct((row_count, part), jnp.bfloat16)] * shares,
        compiler_params=_params(44),
        cost_estimate=_cost(20),
        name="middle",
    )(place, both, mixed, out_grad, gain, w_out, w_up, w_down)


def finish_call(received, patches, mixed_grad, gain, w_query, w_key, w_value, micro, before, cost):
    blocks, row_count, width = received.shape
    slot = width // 3
    features = patches.shape[2]
    per_step = max(1, min(blocks, 512 // slot))
    wide = slot * per_step
    steps = blocks // per_step

    def kernel(data_ref, rows_ref, mixed_ref, gain_ref, wq_ref, wk_ref, wv_ref, *refs):
        out_ref, total, side = refs[-3:]
        step = pl.program_id(0)

        @pl.when(step == 0)
        def _():
            total[...] = jnp.zeros_like(total)

        for part, weight_ref in enumerate((wq_ref, wk_ref, wv_ref)):
            for piece in range(per_step):
                side[part, :, piece * slot : (piece + 1) * slot] = data_ref[
                    piece, :, part * slot : (part + 1) * slot
                ]
            total[...] += contract_cols(side[part], weight_ref[...])

        @pl.when(step == steps - 1)
        def _():
            unit, inverse = _normalize(rows_ref[0].astype(jnp.float32))
            out_ref[0] = (
                mixed_ref[...] + _normalize_back(total[...], gain_ref[...], unit, inverse)
            ).astype(jnp.bfloat16)

    def fixed(*shape):
        return pl.BlockSpec(shape, lambda i: (0,) * len(shape))

    columns = pl.BlockSpec((features, wide), lambda i: (0, i))
    return pl.pallas_call(
        kernel,
        grid=(steps,),
        in_specs=[
            pl.BlockSpec((per_step, row_count, width), lambda i: (i, 0, 0)),
            pl.BlockSpec((1, row_count, features), lambda i: (micro, 0, 0)),
            pl.BlockSpec((row_count, features), lambda i: (micro, 0)),
            fixed(1, features),
            columns,
            columns,
            columns,
        ]
        + [pl.BlockSpec(memory_space=pl.ANY)] * (before is not None),
        out_specs=pl.BlockSpec((1, row_count, features), lambda i: (micro, 0, 0)),
        out_shape=jax.ShapeDtypeStruct(patches.shape, jnp.bfloat16),
        input_output_aliases={7: 0} if before is not None else {},
        scratch_shapes=[
            pltpu.VMEM((row_count, features), jnp.float32),
            pltpu.VMEM((3, row_count, wide), jnp.bfloat16),
        ],
        compiler_params=_params(60),
        cost_estimate=_cost(cost),
        name="finish",
    )(received, patches, mixed_grad, gain, w_query, w_key, w_value, *([before] if before is not None else []))


def grad_heads_call(place, units, places, made, gain, bias, sums, w_query, w_key, w_value, shares):
    micro_count = len(made)
    blocks, tokens, width = made[0].shape
    slot = width // 3
    features = gain.shape[1]
    group = features // (blocks * shares)
    full = width + 128
    kept = blocks * (shares // 2) * group

    def kernel(place_ref, *refs):
        unit_refs, refs = refs[: 2 * micro_count], refs[2 * micro_count :]
        made_refs, refs = refs[:micro_count], refs[micro_count:]
        gain_ref, bias_ref, sums_ref, wq_ref, wk_ref, wv_ref, send_ref, keep_ref, spread, ordered = refs
        product = jnp.zeros((features, width), jnp.float32)
        column_sum = jnp.zeros((1, width), jnp.float32)
        for micro, made_ref in enumerate(made_refs):
            for at, relative in enumerate(places[micro]):
                ordered[at * tokens : (at + 1) * tokens, :] = made_ref[place_ref[0] ^ relative]
            half = blocks * tokens // 2
            for side in range(2):
                rows = ordered[side * half : (side + 1) * half, :]
                product = product + contract_rows(unit_refs[2 * micro + side][...], rows)
                column_sum = column_sum + jnp.sum(rows.astype(jnp.float32), axis=0, keepdims=True)
        vectors = jnp.concatenate(
            [gain_ref[...], bias_ref[...], sums_ref[...], jnp.zeros((124, features), jnp.float32)], axis=0
        ).T
        total = vectors[:, 0:1] * product + vectors[:, 1:2] * column_sum
        weights = jnp.concatenate([wq_ref[...], wk_ref[...], wv_ref[...]], axis=1).astype(jnp.float32)
        gain_sum = jnp.sum(weights * product, axis=1, keepdims=True)
        bias_sum = jnp.sum(weights * column_sum, axis=1, keepdims=True)
        lanes = lax.broadcasted_iota(jnp.int32, (1, 128), 1)
        norms = jnp.where(
            lanes == 0, gain_sum, jnp.where(lanes == 1, bias_sum, jnp.where(lanes < 4, vectors, 0.0))
        )
        spread[:, :, :, 0:width] = total.reshape(blocks, shares, group, width)
        spread[:, :, :, width:] = norms.reshape(blocks, shares, group, 128)
        core = place_ref[1] % 2
        for which, out_ref in enumerate((send_ref, keep_ref)):
            for share in range(0, shares, 2):
                for block in range(blocks):
                    out_ref[share // 2, block] = spread[block, share + (core if which else 1 - core)].astype(out_ref.dtype)

    def fixed(*shape):
        return pl.BlockSpec(shape, lambda i, place: (0,) * len(shape))

    columns = pl.BlockSpec((features, slot), lambda i, place: (0, place[0]))
    out = (shares // 2, blocks, group, full)
    return pl.pallas_call(
        kernel,
        grid_spec=pltpu.PrefetchScalarGridSpec(
            num_scalar_prefetch=1,
            grid=(1,),
            in_specs=[fixed(*part.shape) for part in (*units, *made)]
            + [fixed(1, features), fixed(1, features), fixed(2, features), columns, columns, columns],
            out_specs=[fixed(*out), fixed(*out)],
            scratch_shapes=[
                pltpu.VMEM((blocks, shares, group, full), jnp.float32),
                pltpu.VMEM((blocks * tokens, width), jnp.bfloat16),
            ],
        ),
        out_shape=[jax.ShapeDtypeStruct(out, jnp.bfloat16), jax.ShapeDtypeStruct(out, jnp.float32)],
        compiler_params=_params(60),
        cost_estimate=_cost(20),
        name="grad_heads",
    )(place, *units, *made, gain, bias, sums, w_query, w_key, w_value)


def assemble_call(place, parts, down_steps, blocks, owned):
    shares = len(parts)
    rows, width = parts[0].shape
    part = width - blocks * owned

    def kernel(place_ref, *refs):
        part_refs, (up_ref, out_ref) = refs[:shares], refs[shares:]
        for other, part_ref in enumerate(part_refs):
            share = place_ref[2] ^ other
            for at, block in enumerate(_ordered([_owner_stride(*step, shares) for step in down_steps])):
                to = pl.multiple_of((block + share % 2 + share // 2 * shares) * owned, 128)
                up_ref[:, pl.ds(to, owned)] = part_ref[:, at * owned : (at + 1) * owned].astype(jnp.float32)
            out_ref[:, pl.ds(pl.multiple_of(share * part, 128), part)] = part_ref[:, blocks * owned :].astype(jnp.float32)

    return pl.pallas_call(
        kernel,
        grid_spec=pltpu.PrefetchScalarGridSpec(
            num_scalar_prefetch=1,
            grid=(1,),
            in_specs=[_fixed(rows, width)] * shares,
            out_specs=[_fixed(rows, blocks * shares * owned), _fixed(rows, shares * part)],
        ),
        out_shape=[
            jax.ShapeDtypeStruct((rows, blocks * shares * owned), jnp.float32),
            jax.ShapeDtypeStruct((rows, shares * part), jnp.float32),
        ],
        compiler_params=_params(8),
        cost_estimate=_cost(0),
        name="assemble",
    )(place, *parts)


def _bits(count):
    return [1 << place for place in range(count.bit_length() - 1)]


def _ordered(bits):
    places = [0]
    for bit in bits:
        places = [at + step for at in places for step in (0, bit)]
    return places


def _ordered_low(bits):
    places = [0]
    for bit in bits:
        places = places + [at + bit for at in places]
    return places


def _paired(values, axis, bit):
    count = lax.axis_size(axis)
    return lax.ppermute(values, axis, [(i, i ^ bit) for i in range(count)])


def _bit_of(axis, bit):
    return (lax.axis_index(axis) // bit) % 2


def _mesh_bit(place, step):
    axis, bit = step
    return place[("blk", "mb").index(axis)] // bit % 2


def _owner_stride(axis, bit, shares):
    return bit * shares if axis == "blk" else bit


def _share_places(shares):
    return [0, 1, shares, shares + 1]


def _place_at(bits, step):
    places = _ordered(bits)
    at = jnp.int32(places[0])
    for other in range(1, len(places)):
        at = jnp.where(step == other, places[other], at)
    return at


def grad_middle_call(place, boths, out_grads, lows, w_up, w_down, down_steps, up_steps):
    shares = len(boths)
    _, row_count, features = boths[0].shape
    all_rows = shares * row_count
    hidden = w_up.shape[1]
    blocks = 1 << len(up_steps)
    owned, each = hidden // (blocks * shares), features // (blocks * shares)
    down_places = [_owner_stride(*step, shares) for step in down_steps]
    up_places = [_owner_stride(*step, shares) for step in up_steps]
    share_places = _share_places(shares)
    part = lows[0].shape[1]
    half = blocks // 2
    pair = min(2, half)
    half_steps = half // pair
    sub = min(2, shares)

    def kernel(place_ref, *refs):
        groups, refs = [refs[at * shares : (at + 1) * shares] for at in range(3)], refs[3 * shares :]
        up_refs, down_refs, refs = refs[:pair], refs[pair : 2 * pair], refs[2 * pair :]
        down_send, down_keep, up_send, up_keep, norm_all, norm_turned, grad_all, active_all, upper_all, up_all = refs
        step = pl.program_id(0)
        mine = _mesh_bit(place_ref, up_steps[0])

        def spread():
            for at, block in enumerate(_ordered(up_places[1:])):
                for share, other in enumerate(share_places):
                    rows = slice((at * shares + share) * each, (at * shares + share + 1) * each)
                    up_send[rows, :] = up_all[block + other + up_places[0] * (1 - mine)].astype(jnp.bfloat16)
                    up_keep[rows, :] = up_all[block + other + up_places[0] * mine]

        @pl.when(step == 0)
        def _():
            for at in range(shares):
                rows = slice(at * row_count, (at + 1) * row_count)
                norm_all[rows, :] = groups[0][at][0]
                norm_turned[:, rows] = groups[0][at][0].T
                grad_all[rows, :] = groups[1][at][...]

        @pl.when(step < 2 * half_steps)
        def _():
            up_columns = jnp.concatenate([ref[...] for ref in up_refs], axis=1)
            down_rows = jnp.concatenate([ref[...] for ref in down_refs], axis=0)
            for at in range(0, all_rows, all_rows // sub):
                rows = slice(at, at + all_rows // sub)
                active_all[rows, :], upper_all[rows, :] = _hidden_parts(
                    norm_all[rows, :], grad_all[rows, :], up_columns, down_rows
                )
            down_made = contract_rows(active_all[...], grad_all[...])

            @pl.when(step < half_steps)
            def _():
                down_send[...] = down_made.astype(jnp.bfloat16)

            @pl.when(step >= half_steps)
            def _():
                down_keep[...] = down_made

            up_all[...] = matmul(norm_turned[...], upper_all[...]).reshape(blocks * shares, each, pair * owned)
            spread()

        @pl.when(step == 2 * half_steps)
        def _():
            made = jnp.zeros((features, part), jnp.float32)
            for both_ref, low_ref in zip(groups[0], groups[2]):
                made = made + contract_rows(both_ref[1], low_ref[...])
            up_all[...] = made.reshape(blocks * shares, each, part)
            spread()

    def first_bit(i, place):
        return (_mesh_bit(place, down_steps[0]) + 1 + jnp.minimum(i, 2 * half_steps - 1) // half_steps) % 2

    def unit_block(i, place, at):
        inner = _place_at(down_places[1:], jnp.minimum(i, 2 * half_steps - 1) % half_steps * pair + at)
        return inner + down_places[0] * first_bit(i, place) + place[0] % 2 * shares + place[1] % 2

    ups = [
        pl.BlockSpec((features, owned), lambda i, place, at=at: (0, unit_block(i, place, at))) for at in range(pair)
    ]
    downs = [
        pl.BlockSpec((owned, features), lambda i, place, at=at: (unit_block(i, place, at), 0)) for at in range(pair)
    ]
    def up_block(i, place):
        return (0, jnp.where(i == 2 * half_steps, i, first_bit(i, place) * half_steps + i % half_steps))

    up_out = pl.BlockSpec((features // 2, pair * owned), up_block)
    shapes = [(half * owned, features), (features // 2, blocks * owned + part)]
    return pl.pallas_call(
        kernel,
        grid_spec=pltpu.PrefetchScalarGridSpec(
            num_scalar_prefetch=1,
            grid=(2 * half_steps + 1,),
            in_specs=[_fixed(2, row_count, features)] * shares
            + [_fixed(row_count, features)] * shares
            + [_fixed(row_count, part)] * shares
            + ups
            + downs,
            out_specs=[
                pl.BlockSpec((pair * owned, features), lambda i, place: (jnp.minimum(i, half_steps - 1), 0)),
                pl.BlockSpec((pair * owned, features), lambda i, place: (jnp.clip(i - half_steps, 0, half_steps - 1), 0)),
                up_out,
                up_out,
            ],
            scratch_shapes=[
                pltpu.VMEM((all_rows, features), jnp.bfloat16),
                pltpu.VMEM((features, all_rows), jnp.bfloat16),
                pltpu.VMEM((all_rows, features), jnp.bfloat16),
                pltpu.VMEM((all_rows, pair * owned), jnp.bfloat16),
                pltpu.VMEM((all_rows, pair * owned), jnp.bfloat16),
                pltpu.VMEM((blocks * shares, each, pair * owned), jnp.float32),
            ],
        ),
        out_shape=[jax.ShapeDtypeStruct(shape, dtype) for shape in shapes for dtype in (jnp.bfloat16, jnp.float32)],
        compiler_params=_params(60),
        cost_estimate=_cost(20),
        name="grad_middle",
    )(place, *boths, *out_grads, *lows, *([w_up] * pair), *([w_down] * pair))


def halve_call(place, keep, received, step, cost):
    count, rows, columns = keep.shape
    half = count // 2

    def kernel(place_ref, keep_theirs, keep_mine, got_theirs, got_mine, theirs_ref, mine_ref):
        theirs_ref[...] = (keep_theirs[...] + got_theirs[...].astype(jnp.float32)).astype(jnp.bfloat16)
        mine_ref[...] = keep_mine[...] + got_mine[...].astype(jnp.float32)

    def block(which):
        return pl.BlockSpec(
            (1, rows, columns), lambda i, place: (i + half * ((_mesh_bit(place, step) + which) % 2), 0, 0)
        )

    out = pl.BlockSpec((1, rows, columns), lambda i, place: (i, 0, 0))
    return pl.pallas_call(
        kernel,
        grid_spec=pltpu.PrefetchScalarGridSpec(
            num_scalar_prefetch=1,
            grid=(half,),
            in_specs=[block(1), block(0), block(1), block(0)],
            out_specs=[out, out],
        ),
        out_shape=[
            jax.ShapeDtypeStruct((half, rows, columns), jnp.bfloat16),
            jax.ShapeDtypeStruct((half, rows, columns), jnp.float32),
        ],
        compiler_params=_params(16),
        cost_estimate=_cost(cost),
        name="halve",
    )(place, keep, keep, received, received)


def heads_total_call(keep, received):
    def kernel(keep_ref, got_ref, out_ref):
        out_ref[...] = (keep_ref[...] + got_ref[...].astype(jnp.float32)).astype(jnp.bfloat16)

    return pl.pallas_call(
        kernel,
        out_shape=jax.ShapeDtypeStruct(keep.shape, jnp.bfloat16),
        compiler_params=_params(8),
        cost_estimate=_cost(20),
        name="heads_total",
    )(keep, received)


def close_call(place, keep, received, shares):
    rows, width = keep.shape
    each = rows // shares

    def kernel(place_ref, keep_ref, got_ref, *refs):
        out_refs, total = refs[:-1], refs[-1]
        total[...] = (keep_ref[...] + got_ref[...].astype(jnp.float32)).reshape(shares, each, width)
        for share, out_ref in enumerate(out_refs):
            out_ref[...] = total[place_ref[2] ^ share].astype(jnp.bfloat16)

    return pl.pallas_call(
        kernel,
        grid_spec=pltpu.PrefetchScalarGridSpec(
            num_scalar_prefetch=1,
            grid=(1,),
            in_specs=[_fixed(rows, width)] * 2,
            out_specs=[_fixed(each, width)] * shares,
            scratch_shapes=[pltpu.VMEM((shares, each, width), jnp.float32)],
        ),
        out_shape=[jax.ShapeDtypeStruct((each, width), jnp.bfloat16)] * shares,
        compiler_params=_params(8),
        cost_estimate=_cost(6),
        name="close",
    )(place, keep, received)


def assemble_heads_call(parts, slot):
    blocks, rows, _ = parts.shape

    def kernel(parts_ref, *refs):
        weight_refs, norm_refs = refs[:3], refs[3:]
        for part, ref in enumerate(weight_refs):
            for block in range(blocks):
                ref[:, block * slot : (block + 1) * slot] = parts_ref[
                    block, :, part * slot : (part + 1) * slot
                ].astype(jnp.float32)
        sums = jnp.zeros((rows, 128), jnp.float32)
        for block in range(blocks):
            sums = sums + parts_ref[block, :, 3 * slot :].astype(jnp.float32)
        turned = jnp.concatenate([sums, jnp.zeros((128 - rows, 128), jnp.float32)], axis=0).T
        for at, ref in enumerate(norm_refs):
            ref[...] = turned[at : at + 1, 0:rows]

    return pl.pallas_call(
        kernel,
        out_shape=[jax.ShapeDtypeStruct((rows, blocks * slot), jnp.float32)] * 3
        + [jax.ShapeDtypeStruct((1, rows), jnp.float32)] * 4,
        compiler_params=_params(8),
        cost_estimate=_cost(0),
        name="assemble_heads",
    )(parts)


def fast_body(
    patches, seg_lengths, w_query, w_key, w_value, w_out, w_up, w_down,
    norm1_gain, norm1_bias, norm2_gain, norm2_bias, out_grad,
):
    micro_count, tokens, features = patches.shape
    hidden = w_up.shape[1]
    row_count = micro_count * tokens
    blocks, shares = lax.axis_size("blk"), lax.axis_size("mb")
    head_dim = features // H
    slot = features // blocks
    rows = patches.reshape(row_count, features)
    dout = out_grad.reshape(row_count, features)
    gain_one, bias_one, gain_two, bias_two = (
        value.reshape(1, features) for value in (norm1_gain, norm1_bias, norm2_gain, norm2_bias)
    )

    def swap(values):
        return lax.all_to_all(values, "blk", split_axis=0, concat_axis=0, tiled=True)

    def by_micro(values):
        return values.reshape(blocks, micro_count, tokens, values.shape[-1])

    at_blk, at_mb = lax.axis_index("blk"), lax.axis_index("mb")
    place = jnp.stack([at_blk, at_mb, at_mb % 2 + at_blk % 2 * 2]).astype(jnp.int32)
    blk_bits = _bits(blocks)
    down_steps = [("mb", 2), *(("blk", bit) for bit in blk_bits[1:])]
    up_steps = [down_steps[1], down_steps[0], *down_steps[2:]]
    each, owned, block_rows = features // (blocks * shares), hidden // (blocks * shares), features // blocks
    tie = lax.optimization_barrier

    def grown(values, bit):
        return jnp.concatenate([values, _paired(values, "blk", bit)], axis=0)

    def to_share(values, other):
        if other == 1:
            return _paired(values, "mb", 1)
        if other == 2:
            return _paired(values, "blk", 1)
        return lax.ppermute(values, ("blk", "mb"), [(i, i ^ (shares + 1)) for i in range(blocks * shares)])

    def shared(values):
        over = to_share(values, 2)
        return [values, to_share(values, 1), over, to_share(over, 1)]

    send, units_first, units_last = project_call(
        rows, gain_one, bias_one, w_query, w_key, w_value, blocks, tokens
    )
    received = by_micro(swap(send))
    dout_parts = [out_grad[micro] for micro in range(micro_count)]
    dout_over = [to_share(part, 2) for part in dout_parts]
    received, dout_over[0] = tie((received, dout_over[0]))
    units_first, received = tie((units_first, received))
    units_first = grown(units_first, blk_bits[-1])
    own_attended, exact, logs = attend_call(received, seg_lengths, head_dim)
    attended, units_first, dout_over = tie((own_attended.reshape(blocks, row_count, slot), units_first, dout_over))
    dout_over = jnp.concatenate(dout_over, axis=0)
    attended, units_first, units_last, *douts = tie(
        (swap(attended), units_first, units_last, dout, to_share(dout, 1), dout_over, to_share(dout_over, 1))
    )
    for bit in blk_bits[-2:0:-1]:
        units_first = grown(units_first, bit)
    units_last = grown(units_last, blk_bits[-1])
    places = _ordered_low([*blk_bits[:0:-1], blk_bits[0]])

    mixed, both = mix_call(attended, rows, gain_two, bias_two, w_out)
    both_peer, both_over = to_share(both, 1), to_share(both, 2)
    layer_out, mixed_grad, back, sums_two, *lows = middle_call(
        place, both, mixed, dout, gain_two, w_out, w_up, w_down, blocks, shares
    )
    back, lows, units_first, units_last, both_peer, both_over = tie(
        (back, lows, units_first, units_last, both_peer, both_over)
    )
    boths = [both, both_peer, both_over, to_share(both_over, 1)]
    units_first_peer = _paired(units_first, "blk", blk_bits[0])
    for bit in blk_bits[-2:0:-1]:
        units_last = grown(units_last, bit)
    grads = by_micro(swap(back))
    lows = [lows[0]] + [to_share(lows[share], share) for share in range(1, shares)]
    down_theirs, down_keep, up_theirs, up_keep = grad_middle_call(
        place, boths, douts, lows, w_up, w_down, down_steps, up_steps
    )
    down_theirs, down_keep = (value.reshape(-1, owned, features) for value in (down_theirs, down_keep))
    up_theirs, up_keep = (value.reshape(-1, block_rows, value.shape[-1]) for value in (up_theirs, up_keep))
    down_received, up_received = _paired(down_theirs, *down_steps[0]), _paired(up_theirs, *up_steps[0])
    grads, down_keep, units_last = tie((grads, down_keep, units_last))
    units_last_peer = _paired(units_last, "blk", blk_bits[0])
    made = attend_back_call(received, grads, exact, logs, seg_lengths, head_dim)
    returned = [swap(made[0])]

    def then(done, *values):
        return tie((done, values))[1]

    returned += [swap(tie((values, returned[0]))[0]) for values in made[1:]]
    made = tie(made)
    up_keep, up_received, units_first_peer = then(made[0], up_keep, up_received, units_first_peer)
    up_theirs, up_keep = halve_call(place, up_keep, up_received, up_steps[1], 0)
    up_received = _paired(up_theirs, *up_steps[1])
    down_keep, down_received, units_last_peer = then(up_keep, down_keep, down_received, units_last_peer)
    down_theirs, down_keep = halve_call(place, down_keep, down_received, down_steps[1], 5)
    down_received = _paired(down_theirs, *down_steps[1])
    made = then(down_keep, *made)
    heads_send, heads_keep = grad_heads_call(
        place, (units_first, units_first_peer, units_last, units_last_peer), (places, places),
        made, gain_one, bias_one, sums_two, w_query, w_key, w_value, shares,
    )
    pair = (shares // 2, -1, heads_keep.shape[-1])
    heads_received = _paired(heads_send, "mb", 1).reshape(pair)
    down_keep, down_received = then(heads_keep, down_keep, down_received)
    for step in down_steps[2:-1]:
        down_theirs, down_keep = halve_call(place, down_keep, down_received, step, 0)
        down_received = _paired(down_theirs, *step)
    down_theirs, down_keep = halve_call(place, down_keep, down_received, down_steps[-1], 0)
    up_keep, up_received = then(down_keep, up_keep, up_received)
    for step in up_steps[2:]:
        up_theirs, up_keep = halve_call(place, up_keep, up_received, step, 3)
        up_received = _paired(up_theirs, *step)
    heads_theirs, heads_keep = halve_call(
        place, *then(up_keep, heads_keep.reshape(pair), heads_received), ("mb", 2), 0
    )
    heads_theirs, down_theirs = tie((heads_theirs, down_theirs))
    heads_received = _paired(heads_theirs, "mb", 2)
    down_received = _paired(down_theirs, *down_steps[-1])
    finish = (patches, mixed_grad, gain_one, w_query, w_key, w_value)
    patches_grad = None
    for micro in range(micro_count - 1):
        first, heads_keep, heads_received = then(down_keep, returned[micro], heads_keep, heads_received)
        patches_grad = finish_call(first, *finish, micro, patches_grad, 0)
        heads_keep, heads_received = then(patches_grad, heads_keep, heads_received)
    returned[-1], heads_keep, heads_received = tie((returned[-1], heads_keep, heads_received))
    heads_total = heads_total_call(heads_keep[0], heads_received[0]).reshape(blocks, each, heads_keep.shape[-1])
    heads_parts = swap(heads_total)
    up_keep, up_received = then(heads_total, up_keep, up_received)
    parts = close_call(place, up_keep[0], up_received[0], shares)
    last = then(parts[0], returned[-1])[0]
    parts = [parts[0]] + [to_share(parts[share], share) for share in range(1, shares)]
    patches_grad = finish_call(last, *finish, micro_count - 1, patches_grad, 20)
    up_total, out_total = assemble_call(place, then(patches_grad, *parts), down_steps, blocks, owned)
    down_keep, down_received = then(up_total, down_keep, down_received)
    down_total = (down_keep + down_received.astype(jnp.float32))[0]
    query_total, key_total, value_total, *sums = assemble_heads_call(then(down_total, heads_parts)[0], slot)
    return (
        layer_out.reshape(patches.shape),
        patches_grad.reshape(patches.shape),
        query_total,
        key_total,
        value_total,
        out_total,
        up_total,
        down_total,
        *(value.reshape(each) for value in sums),
    )


def solution(mesh):
    in_specs = (
        P("mb", "blk", None),
        P("mb", None),
        P(),
        P(),
        P(),
        P(),
        P(),
        P(),
        P(),
        P(),
        P(),
        P(),
        P("mb", "blk", None),
    )
    out_specs = (
        P("mb", "blk", None),
        P("mb", "blk", None),
        P(("blk", "mb"), None),
        P(("blk", "mb"), None),
        P(("blk", "mb"), None),
        P(("blk", "mb"), None),
        P(("blk", "mb"), None),
        P(("blk", "mb"), None),
        P(("blk", "mb")),
        P(("blk", "mb")),
        P(("blk", "mb")),
        P(("blk", "mb")),
    )
    blocks, shares = mesh.shape["blk"], mesh.shape["mb"]
    paired = blocks >= 4 and blocks & (blocks - 1) == 0 and shares == 4
    chosen_body = fast_body if paired and H % blocks == 0 else body
    return jax.shard_map(chosen_body, mesh=mesh, in_specs=in_specs, out_specs=out_specs, check_vma=False)
```

```python
import math

import jax
import jax.numpy as jnp
from jax import lax
from jax.experimental import pallas as pl
from jax.experimental.pallas import tpu as pltpu
from jax.sharding import PartitionSpec as P

H = 16
CHUNK = 8


epsilon = 1e-05
masked_score = -1e30


def layer_norm(values, norm_gain, norm_bias):
    center = values - jnp.mean(values, axis=-1, keepdims=True)
    variance = jnp.mean(center * center, axis=-1, keepdims=True)
    return center * lax.rsqrt(variance + epsilon) * norm_gain + norm_bias


def gelu_exact(values):
    return jax.nn.gelu(values, approximate=False)


def matmul(left_side, right_side):
    return jnp.dot(left_side, right_side, preferred_element_type=jnp.float32)


def contract_rows(left_side, right_side):
    return lax.dot_general(
        left_side, right_side, (((0,), (0,)), ((), ())), preferred_element_type=jnp.float32
    )


def contract_cols(left_side, right_side):
    return lax.dot_general(
        left_side, right_side, (((1,), (1,)), ((), ())), preferred_element_type=jnp.float32
    )


def segment_ids(lengths, positions):
    doc_ends = jnp.cumsum(lengths, axis=-1)
    return jnp.sum((positions[None, :, None] >= doc_ends[:, None, :]).astype(jnp.int32), axis=-1)


def masked_scores(query_piece, keys_all, query_docs, key_docs, score_scale):
    scores = contract_cols(query_piece, keys_all) * score_scale
    return jnp.where(query_docs[:, None] == key_docs[None, :], scores, masked_score)


def soft_rows(scores):
    row_max = jnp.max(scores, axis=-1, keepdims=True)
    exponent = jnp.exp(scores - row_max)
    return exponent / jnp.sum(exponent, axis=-1, keepdims=True)


def body(
    patches,
    seg_lengths,
    w_query,
    w_key,
    w_value,
    w_out,
    w_up,
    w_down,
    norm1_gain,
    norm1_bias,
    norm2_gain,
    norm2_bias,
    out_grad,
):
    micro_count, tokens, features = patches.shape
    row_count = micro_count * tokens
    blocks = lax.axis_size("blk")
    block_index = lax.axis_index("blk")
    head_count = H
    head_dim = features // head_count
    repeat = max(1, blocks // head_count)
    per_slot = max(1, head_count // blocks)
    groups = head_count // per_slot
    rows_part = tokens // repeat
    query_rows = blocks * rows_part
    seq_length = blocks * tokens
    item_count = micro_count * per_slot
    block_rows = min(512, query_rows)
    block_count = query_rows // block_rows
    slot_width = micro_count * per_slot * head_dim
    score_scale = 1.0 / math.sqrt(head_dim)
    doc_count = seg_lengths.shape[1]

    def query_layout(values):
        shaped = values.reshape(micro_count, repeat, rows_part, groups, per_slot * head_dim)
        return shaped.transpose(3, 1, 2, 0, 4).reshape(blocks, rows_part, slot_width)

    def key_layout(values):
        shaped = values.reshape(micro_count, tokens, groups, per_slot * head_dim).transpose(
            2, 1, 0, 3
        )
        shaped = jnp.broadcast_to(
            shaped[:, None], (groups, repeat, tokens, micro_count, per_slot * head_dim)
        )
        return shaped.reshape(blocks, tokens, slot_width)

    def token_layout(values):
        shaped = values.reshape(groups, repeat, rows_part, micro_count, per_slot * head_dim)
        return shaped.transpose(3, 1, 2, 0, 4).reshape(row_count, features)

    def key_sum(values):
        shaped = values.reshape(groups, repeat, tokens, micro_count, per_slot * head_dim).sum(
            axis=1
        )
        return shaped.transpose(2, 1, 0, 3).reshape(row_count, features)

    def to_items(received):
        row_total = received.shape[1]
        shaped = received.reshape(row_total, micro_count, per_slot, head_dim).transpose(1, 2, 0, 3)
        return shaped.reshape(item_count, row_total, head_dim)

    def from_items(values):
        row_total = values.shape[1]
        shaped = values.reshape(micro_count, per_slot, row_total, head_dim).transpose(2, 0, 1, 3)
        return shaped.reshape(1, row_total, slot_width)

    row_ids = jnp.arange(query_rows)
    query_pos = (
        row_ids // rows_part * tokens + block_index % repeat * rows_part + row_ids % rows_part
    )
    query_docs = jnp.repeat(segment_ids(seg_lengths, query_pos), per_slot, axis=0)
    key_docs = jnp.repeat(segment_ids(seg_lengths, jnp.arange(seq_length)), per_slot, axis=0)
    query_valid = (query_docs < doc_count).astype(jnp.float32)
    local_pos = block_index * tokens + jnp.arange(tokens)
    row_valid = (
        (segment_ids(seg_lengths, local_pos) < doc_count).astype(jnp.float32).reshape(row_count, 1)
    )

    def forward_item(operands):
        queries_item, keys_item, values_item, docs_item, key_docs_item = operands

        def forward_one_block(block_operands):
            query_piece, docs_piece = block_operands
            weights_soft = soft_rows(
                masked_scores(query_piece, keys_item, docs_piece, key_docs_item, score_scale)
            )
            return matmul(weights_soft.astype(jnp.bfloat16), values_item)

        outputs = lax.map(
            forward_one_block,
            (
                queries_item.reshape(block_count, block_rows, head_dim),
                docs_item.reshape(block_count, block_rows),
            ),
        )
        return outputs.reshape(query_rows, head_dim)

    def backward_item(operands):
        queries_item, keys_item, values_item, grads_item, docs_item, key_docs_item = operands

        def backward_one_block(totals, block_operands):
            key_total, value_total = totals
            query_piece, grad_piece, docs_piece = block_operands
            weights_soft = soft_rows(
                masked_scores(query_piece, keys_item, docs_piece, key_docs_item, score_scale)
            )
            weights_low = weights_soft.astype(jnp.bfloat16)
            weight_grads = contract_cols(grad_piece, values_item)
            row_inner = jnp.sum(weights_soft * weight_grads, axis=-1, keepdims=True)
            score_grads = (weights_soft * (weight_grads - row_inner)).astype(jnp.bfloat16)
            query_grad = matmul(score_grads, keys_item) * score_scale
            key_total = key_total + contract_rows(score_grads, query_piece) * score_scale
            value_total = value_total + contract_rows(weights_low, grad_piece)
            return ((key_total, value_total), query_grad)

        zero_block = jnp.zeros((seq_length, head_dim), jnp.float32)
        totals, query_grads = lax.scan(
            backward_one_block,
            (zero_block, zero_block),
            (
                queries_item.reshape(block_count, block_rows, head_dim),
                grads_item.reshape(block_count, block_rows, head_dim),
                docs_item.reshape(block_count, block_rows),
            ),
        )
        return (query_grads.reshape(query_rows, head_dim), totals[0], totals[1])

    inputs = patches.astype(jnp.float32).reshape(row_count, features)
    norm_one_full, norm_one_pull = jax.vjp(layer_norm, inputs, norm1_gain, norm1_bias)
    norm_one = norm_one_full.astype(jnp.bfloat16)
    queries = matmul(norm_one, w_query).astype(jnp.bfloat16)
    keys_proj = matmul(norm_one, w_key).astype(jnp.bfloat16)
    values_proj = matmul(norm_one, w_value).astype(jnp.bfloat16)
    query_send = query_layout(queries)
    key_send = key_layout(keys_proj)
    value_send = key_layout(values_proj)
    query_heads, key_heads, value_heads = (
        lax.all_to_all(query_send, "blk", split_axis=0, concat_axis=1, tiled=True),
        lax.all_to_all(key_send, "blk", split_axis=0, concat_axis=1, tiled=True),
        lax.all_to_all(value_send, "blk", split_axis=0, concat_axis=1, tiled=True),
    )
    query_items = to_items(query_heads)
    key_items = to_items(key_heads)
    value_items = to_items(value_heads)
    attended_items = lax.map(
        forward_item, (query_items, key_items, value_items, query_docs, key_docs)
    )
    attended_items = (attended_items * query_valid[:, :, None]).astype(jnp.bfloat16)
    attended = token_layout(
        lax.all_to_all(from_items(attended_items), "blk", split_axis=1, concat_axis=0, tiled=True)
    )
    mixed_rows = inputs + matmul(attended, w_out)
    norm_two_full, norm_two_pull = jax.vjp(layer_norm, mixed_rows, norm2_gain, norm2_bias)
    norm_two = norm_two_full.astype(jnp.bfloat16)
    upper_proj = matmul(norm_two, w_up)
    active_full, gelu_pull = jax.vjp(gelu_exact, upper_proj)
    active = active_full.astype(jnp.bfloat16)
    result = mixed_rows + matmul(active, w_down)
    layer_out = result.astype(jnp.bfloat16).reshape(micro_count, tokens, features)
    dout_low = out_grad.reshape(row_count, features)
    down_grad = contract_rows(active, dout_low)
    active_grad = contract_cols(dout_low, w_down)
    upper_grad = gelu_pull(active_grad)[0].astype(jnp.bfloat16)
    up_grad = contract_rows(norm_two, upper_grad)
    norm_two_grad = contract_cols(upper_grad, w_up)
    mixed_part, gain_two_grad, bias_two_grad = norm_two_pull(norm_two_grad)
    mixed_grad = dout_low.astype(jnp.float32) + mixed_part
    mixed_low = mixed_grad.astype(jnp.bfloat16)
    out_proj_grad = contract_rows(attended, mixed_low)
    attended_grad = (contract_cols(mixed_low, w_out) * row_valid).astype(jnp.bfloat16)
    grad_send = query_layout(attended_grad)
    query_again, key_again, value_again, grad_heads = (
        lax.all_to_all(query_send, "blk", split_axis=0, concat_axis=1, tiled=True),
        lax.all_to_all(key_send, "blk", split_axis=0, concat_axis=1, tiled=True),
        lax.all_to_all(value_send, "blk", split_axis=0, concat_axis=1, tiled=True),
        lax.all_to_all(grad_send, "blk", split_axis=0, concat_axis=1, tiled=True),
    )
    back_queries = to_items(query_again)
    back_keys = to_items(key_again)
    back_values = to_items(value_again)
    grad_items = to_items(grad_heads)
    query_grad_items, key_grad_items, value_grad_items = lax.map(
        backward_item, (back_queries, back_keys, back_values, grad_items, query_docs, key_docs)
    )
    query_back, key_back, value_back = (
        lax.all_to_all(
            from_items(query_grad_items).astype(jnp.bfloat16),
            "blk",
            split_axis=1,
            concat_axis=0,
            tiled=True,
        ).astype(jnp.float32),
        lax.all_to_all(
            from_items(key_grad_items).astype(jnp.bfloat16),
            "blk",
            split_axis=1,
            concat_axis=0,
            tiled=True,
        ).astype(jnp.float32),
        lax.all_to_all(
            from_items(value_grad_items).astype(jnp.bfloat16),
            "blk",
            split_axis=1,
            concat_axis=0,
            tiled=True,
        ).astype(jnp.float32),
    )
    query_grad = token_layout(query_back).astype(jnp.bfloat16)
    key_grad = key_sum(key_back).astype(jnp.bfloat16)
    value_grad = key_sum(value_back).astype(jnp.bfloat16)
    query_proj_grad = contract_rows(norm_one, query_grad)
    key_proj_grad = contract_rows(norm_one, key_grad)
    value_proj_grad = contract_rows(norm_one, value_grad)
    norm_one_grad = (
        contract_cols(query_grad, w_query)
        + contract_cols(key_grad, w_key)
        + contract_cols(value_grad, w_value)
    )
    input_part, gain_one_grad, bias_one_grad = norm_one_pull(norm_one_grad)
    patches_grad = (
        (mixed_grad + input_part).astype(jnp.bfloat16).reshape(micro_count, tokens, features)
    )
    gradients = (
        query_proj_grad,
        key_proj_grad,
        value_proj_grad,
        out_proj_grad,
        up_grad,
        down_grad,
        gain_one_grad,
        bias_one_grad,
        gain_two_grad,
        bias_two_grad,
    )
    summed = (
        lax.psum_scatter(gradients[0], ("blk", "mb"), scatter_dimension=0, tiled=True),
        lax.psum_scatter(gradients[1], ("blk", "mb"), scatter_dimension=0, tiled=True),
        lax.psum_scatter(gradients[2], ("blk", "mb"), scatter_dimension=0, tiled=True),
        lax.psum_scatter(gradients[3], ("blk", "mb"), scatter_dimension=0, tiled=True),
        lax.psum_scatter(gradients[4], ("blk", "mb"), scatter_dimension=0, tiled=True),
        lax.psum_scatter(gradients[5], ("blk", "mb"), scatter_dimension=0, tiled=True),
        lax.psum_scatter(gradients[6], ("blk", "mb"), scatter_dimension=0, tiled=True),
        lax.psum_scatter(gradients[7], ("blk", "mb"), scatter_dimension=0, tiled=True),
        lax.psum_scatter(gradients[8], ("blk", "mb"), scatter_dimension=0, tiled=True),
        lax.psum_scatter(gradients[9], ("blk", "mb"), scatter_dimension=0, tiled=True),
    )
    return (
        layer_out,
        patches_grad,
        summed[0],
        summed[1],
        summed[2],
        summed[3],
        summed[4],
        summed[5],
        summed[6],
        summed[7],
        summed[8],
        summed[9],
    )


def _normalize(values):
    center = values - jnp.mean(values, axis=-1, keepdims=True)
    variance = jnp.mean(center * center, axis=-1, keepdims=True)
    inverse = lax.rsqrt(variance + epsilon)
    return center * inverse, inverse


def _normalize_back(grads, gain, unit, inverse):
    scaled = grads * gain
    mean_scaled = jnp.mean(scaled, axis=-1, keepdims=True)
    mean_product = jnp.mean(scaled * unit, axis=-1, keepdims=True)
    return (scaled - mean_scaled - unit * mean_product) * inverse


def _doc_ids(lengths_ref, micro, doc_count, positions):
    end = jnp.int32(0)
    ids = jnp.zeros_like(positions)
    for doc in range(doc_count):
        end = end + lengths_ref[micro, doc]
        ids = ids + (positions >= end).astype(jnp.int32)
    return ids


def _params(mib):
    return pltpu.CompilerParams(vmem_limit_bytes=mib << 20)


def _cost(microseconds):
    return pl.CostEstimate(flops=int(microseconds * 1e9) + 1, bytes_accessed=1, transcendentals=0)


def project_call(rows, gain, bias, w_query, w_key, w_value, blocks, cuts):
    row_count, features = rows.shape
    slot = features // blocks
    per_step = max(1, min(blocks, 512 // slot))
    wide = slot * per_step

    def kernel(rows_ref, gain_ref, bias_ref, wq_ref, wk_ref, wv_ref, send_ref, *refs):
        unit_refs, norm_ref = refs[:-1], refs[-1]


        @pl.when(pl.program_id(0) == 0)
        def _():
            unit, _unused = _normalize(rows_ref[...].astype(jnp.float32))
            for (first, last), unit_ref in zip(cuts, unit_refs):
                unit_ref[...] = unit[first:last].astype(jnp.bfloat16)
            norm_ref[...] = (unit * gain_ref[...] + bias_ref[...]).astype(jnp.bfloat16)

        for part, weight_ref in enumerate((wq_ref, wk_ref, wv_ref)):
            made = matmul(norm_ref[...], weight_ref[...]).astype(jnp.bfloat16)
            for piece in range(per_step):
                send_ref[piece, :, part * slot : (part + 1) * slot] = made[
                    :, piece * slot : (piece + 1) * slot
                ]

    whole = pl.BlockSpec((row_count, features), lambda i: (0, 0))
    vector = pl.BlockSpec((1, features), lambda i: (0, 0))
    columns = pl.BlockSpec((features, wide), lambda i: (0, i))
    return pl.pallas_call(
        kernel,
        grid=(blocks // per_step,),
        in_specs=[whole, vector, vector, columns, columns, columns],
        out_specs=[pl.BlockSpec((per_step, row_count, 3 * slot), lambda i: (i, 0, 0))]
        + [pl.BlockSpec((last - first, features), lambda i: (0, 0)) for first, last in cuts],
        out_shape=[jax.ShapeDtypeStruct((blocks, row_count, 3 * slot), jnp.bfloat16)]
        + [jax.ShapeDtypeStruct((last - first, features), jnp.bfloat16) for first, last in cuts],
        scratch_shapes=[pltpu.VMEM((row_count, features), jnp.bfloat16)],
        compiler_params=_params(60),
        cost_estimate=_cost(6),
        name="project",
    )(rows, gain, bias, w_query, w_key, w_value)


def _head_masks(slot, head_dim, dtype):
    lanes = lax.broadcasted_iota(jnp.int32, (1, slot), 1)
    return [(lanes // head_dim == head).astype(dtype) for head in range(slot // head_dim)]


def _key_range(lengths_ref, micro, doc_count, first_row, last_row, seq):
    low, high, end = jnp.int32(0), jnp.int32(seq), jnp.int32(0)
    for doc in range(doc_count):
        end = end + lengths_ref[micro, doc]
        low = jnp.where(end <= first_row, jnp.maximum(low, end), low)
        high = jnp.where(end >= last_row, jnp.minimum(high, end), high)
    return low, high


def _by_key_range(lengths_ref, micro, doc_count, step, rows, blocks, tokens, compute):
    low, high = _key_range(lengths_ref, micro, doc_count, step * rows, (step + 1) * rows, blocks * tokens)
    half = blocks // 2
    in_low, in_high = high <= half * tokens, low >= half * tokens

    @pl.when(in_low | in_high)
    def _():
        compute(jnp.where(in_low, 0, half), half)

    @pl.when(jnp.logical_not(in_low | in_high))
    def _():
        compute(0, blocks)


def attend_call(received, lengths, head_dim):
    blocks, micro_count, tokens, width = received.shape
    slot = width // 3
    doc_count = lengths.shape[1]
    step_blocks = max(1, min(blocks // 2, 512 // tokens))
    rows = step_blocks * tokens
    scale = 1.0 / math.sqrt(head_dim)

    def kernel(lengths_ref, data_ref, out_ref, exact_ref, log_ref):
        micro = pl.program_id(0)
        step = pl.program_id(1)
        row_docs = _doc_ids(
            lengths_ref, micro, doc_count, lax.broadcasted_iota(jnp.int32, (rows, 1), 0) + step * rows
        )
        queries = data_ref[pl.ds(step * step_blocks, step_blocks), 0, :, 0:slot].reshape(rows, slot) * scale

        def compute(first, count):
            seq = count * tokens
            key_docs = _doc_ids(
                lengths_ref, micro, doc_count, lax.broadcasted_iota(jnp.int32, (1, seq), 1) + first * tokens
            )
            same = row_docs == key_docs
            keys = data_ref[pl.ds(first, count), 0, :, slot : 2 * slot].reshape(seq, slot)
            values = data_ref[pl.ds(first, count), 0, :, 2 * slot : 3 * slot].reshape(seq, slot)
            total = jnp.zeros((rows, slot), jnp.float32)
            logs = jnp.zeros((rows, 128), jnp.float32)
            lanes = lax.broadcasted_iota(jnp.int32, (1, 128), 1)
            for head, (mask, mask_wide) in enumerate(
                zip(_head_masks(slot, head_dim, jnp.bfloat16), _head_masks(slot, head_dim, jnp.float32))
            ):
                scores = jnp.where(same, contract_cols(queries * mask, keys), masked_score)
                most = jnp.max(scores, axis=-1, keepdims=True)
                exponent = jnp.exp(scores - most)
                exponent_sum = jnp.sum(exponent, axis=-1, keepdims=True)
                share = 1.0 / exponent_sum
                logs = jnp.where(lanes == head, most + jnp.log(exponent_sum), logs)
                total = total + matmul(exponent.astype(jnp.bfloat16), values) * (share * mask_wide)
            total = jnp.where(row_docs < doc_count, total, 0.0)
            out_ref[...] = total.astype(jnp.bfloat16).reshape(step_blocks, 1, tokens, slot)
            exact_ref[...] = total.reshape(step_blocks, 1, tokens, slot)
            log_ref[0] = logs.T[0:8, :]

        _by_key_range(lengths_ref, micro, doc_count, step, rows, blocks, tokens, compute)

    return pl.pallas_call(
        kernel,
        grid=(micro_count, blocks // step_blocks),
        in_specs=[
            pl.BlockSpec(memory_space=pltpu.SMEM),
            pl.BlockSpec((blocks, 1, tokens, width), lambda m, s: (0, m, 0, 0)),
        ],
        out_specs=[
            pl.BlockSpec((step_blocks, 1, tokens, slot), lambda m, s: (s, m, 0, 0)),
            pl.BlockSpec((step_blocks, 1, tokens, slot), lambda m, s: (s, m, 0, 0)),
            pl.BlockSpec((1, 8, rows), lambda m, s: (m, 0, s)),
        ],
        out_shape=[
            jax.ShapeDtypeStruct((blocks, micro_count, tokens, slot), jnp.bfloat16),
            jax.ShapeDtypeStruct((blocks, micro_count, tokens, slot), jnp.float32),
            jax.ShapeDtypeStruct((micro_count, 8, blocks * tokens), jnp.float32),
        ],
        compiler_params=_params(32),
        cost_estimate=_cost(11),
        name="attend",
    )(lengths, received)


def attend_back_call(received, grads, attended, logs, lengths, micro, cost, head_dim):
    blocks, _, tokens, width = received.shape
    slot = width // 3
    doc_count = lengths.shape[1]
    step_blocks = max(1, min(blocks // 2, 512 // tokens))
    rows = step_blocks * tokens
    steps = blocks // step_blocks
    scale = 1.0 / math.sqrt(head_dim)

    def kernel(lengths_ref, data_ref, grads_ref, att_ref, log_ref, out_ref, key_total, value_total, turned):
        step = pl.program_id(0)

        @pl.when(step == 0)
        def _():
            key_total[...] = jnp.zeros_like(key_total)
            value_total[...] = jnp.zeros_like(value_total)
            for block in range(blocks):
                turned[block] = data_ref[block, 0, :, slot : 2 * slot].T

        row_docs = _doc_ids(
            lengths_ref, micro, doc_count, lax.broadcasted_iota(jnp.int32, (1, rows), 1) + step * rows
        )
        column_docs = _doc_ids(
            lengths_ref, micro, doc_count, lax.broadcasted_iota(jnp.int32, (rows, 1), 0) + step * rows
        )
        queries = data_ref[pl.ds(step * step_blocks, step_blocks), 0, :, 0:slot].reshape(rows, slot) * scale
        out_grads = grads_ref[...].reshape(rows, slot)
        out_grads = out_grads * (column_docs < doc_count).astype(jnp.float32).astype(jnp.bfloat16)

        inner = (out_grads.astype(jnp.float32) * att_ref[...].reshape(rows, slot)).T

        def compute(first, count):
            chunk = min(CHUNK, count)
            query_parts = [jnp.zeros((head_dim, rows), jnp.float32) for _ in range(slot // head_dim)]
            masks = _head_masks(slot, head_dim, jnp.bfloat16)
            for at in range(0, count, chunk):
                seq = chunk * tokens
                key_docs = _doc_ids(
                    lengths_ref,
                    micro,
                    doc_count,
                    lax.broadcasted_iota(jnp.int32, (seq, 1), 0) + (first + at) * tokens,
                )
                same = row_docs == key_docs
                keys = data_ref[pl.ds(first + at, chunk), 0, :, slot : 2 * slot].reshape(seq, slot)
                values = data_ref[pl.ds(first + at, chunk), 0, :, 2 * slot : 3 * slot].reshape(seq, slot)
                keys_turned = jnp.concatenate([turned[first + at + other] for other in range(chunk)], axis=1)
                key_made = jnp.zeros((seq, slot), jnp.float32)
                value_made = jnp.zeros((seq, slot), jnp.float32)
                for head, mask in enumerate(masks):
                    lanes = slice(head * head_dim, (head + 1) * head_dim)
                    queries_head, grads_head = queries * mask, out_grads * mask
                    scores = jnp.where(same, contract_cols(keys, queries_head), masked_score)
                    probs = jnp.exp(scores - log_ref[0, head : head + 1, :])
                    prob_grads = contract_cols(values, grads_head)
                    head_inner = jnp.sum(inner[lanes], axis=0, keepdims=True)
                    score_grads = (probs * (prob_grads - head_inner)).astype(jnp.bfloat16)
                    value_made = value_made + matmul(probs.astype(jnp.bfloat16), grads_head)
                    key_made = key_made + matmul(score_grads, queries_head)
                    query_parts[head] = query_parts[head] + matmul(keys_turned[lanes], score_grads)
                to = pl.ds(pl.multiple_of((first + at) * tokens, tokens), seq)
                key_total[to, :] += key_made
                value_total[to, :] += value_made
            query_grads = (jnp.concatenate(query_parts, axis=0).T * scale).astype(jnp.bfloat16).reshape(step_blocks, tokens, slot)
            out_ref[pl.ds(step * step_blocks, step_blocks), :, 0:slot] = query_grads

        _by_key_range(lengths_ref, micro, doc_count, step, rows, blocks, tokens, compute)

        @pl.when(step == steps - 1)
        def _():
            out_ref[:, :, slot : 2 * slot] = key_total[...].astype(jnp.bfloat16).reshape(blocks, tokens, slot)
            out_ref[:, :, 2 * slot :] = value_total[...].astype(jnp.bfloat16).reshape(blocks, tokens, slot)

    return pl.pallas_call(
        kernel,
        grid=(steps,),
        in_specs=[
            pl.BlockSpec(memory_space=pltpu.SMEM),
            pl.BlockSpec((blocks, 1, tokens, width), lambda s: (0, micro, 0, 0)),
            pl.BlockSpec((step_blocks, 1, tokens, slot), lambda s: (s, micro, 0, 0)),
            pl.BlockSpec((step_blocks, 1, tokens, slot), lambda s: (s, micro, 0, 0)),
            pl.BlockSpec((1, 8, rows), lambda s: (micro, 0, s)),
        ],
        out_specs=_fixed(blocks, tokens, width),
        out_shape=jax.ShapeDtypeStruct((blocks, tokens, width), jnp.bfloat16),
        scratch_shapes=[pltpu.VMEM((blocks * tokens, slot), jnp.float32)] * 2
        + [pltpu.VMEM((blocks, slot, tokens), jnp.bfloat16)],
        compiler_params=_params(60),
        cost_estimate=_cost(cost),
        name="attend_back",
    )(lengths, received, grads, attended, logs)


def _fixed(*shape):
    return pl.BlockSpec(shape, lambda *_unused: (0,) * len(shape))


def mix_call(attended, rows, gain, bias, w_out):
    blocks, row_count, slot = attended.shape
    features = rows.shape[1]

    def kernel(att_ref, rows_ref, gain_ref, bias_ref, wo_ref, mixed_ref, both_ref):
        for block in range(blocks):
            both_ref[1, :, block * slot : (block + 1) * slot] = att_ref[block]
        value = rows_ref[...].astype(jnp.float32) + matmul(both_ref[1], wo_ref[...])
        mixed_ref[...] = value
        unit, _unused = _normalize(value)
        both_ref[0] = (unit * gain_ref[...] + bias_ref[...]).astype(jnp.bfloat16)

    rows_spec, vector = _fixed(row_count, features), _fixed(1, features)
    return pl.pallas_call(
        kernel,
        grid=(1,),
        in_specs=[_fixed(blocks, row_count, slot), rows_spec, vector, vector, _fixed(features, features)],
        out_specs=[rows_spec, _fixed(2, row_count, features)],
        out_shape=[
            jax.ShapeDtypeStruct((row_count, features), jnp.float32),
            jax.ShapeDtypeStruct((2, row_count, features), jnp.bfloat16),
        ],
        compiler_params=_params(24),
        cost_estimate=_cost(4),
        name="mix",
    )(attended, rows, gain, bias, w_out)


def _hidden_parts(norm, out_grad, up_columns, down_rows):
    upper = matmul(norm, up_columns)
    active_grad = contract_cols(out_grad, down_rows)
    half = (1.0 + lax.erf(upper * (1.0 / math.sqrt(2.0)))) * 0.5
    slope = half + upper * jnp.exp(upper * upper * -0.5) * (1.0 / math.sqrt(2.0 * math.pi))
    return (upper * half).astype(jnp.bfloat16), (active_grad * slope).astype(jnp.bfloat16)


def middle_call(place, both, mixed, out_grad, gain, w_out, w_up, w_down, blocks, shares):
    row_count, features = mixed.shape
    hidden = w_up.shape[1]
    wide = min(1024, hidden)
    sub = min(512, wide)
    steps = hidden // wide
    slot, part = features // blocks, features // shares

    def kernel(place_ref, norm_ref, mixed_ref, grad_ref, gain_ref, wo_ref, wu_ref, wd_ref, *refs):
        out_ref, mixed_grad_ref, back_ref, sums_ref = refs[:4]
        low_refs, (total, grad_total, active_all, upper_all, low_all) = refs[4 : 4 + shares], refs[4 + shares :]
        step = pl.program_id(0)

        @pl.when(step == 0)
        def _():
            total[...] = mixed_ref[...]
            grad_total[...] = jnp.zeros_like(grad_total)

        for chunk in range(0, wide, sub):
            active, upper_grad = _hidden_parts(
                norm_ref[0], grad_ref[...], wu_ref[:, chunk : chunk + sub], wd_ref[chunk : chunk + sub, :]
            )
            active_all[:, chunk : chunk + sub] = active
            upper_all[:, chunk : chunk + sub] = upper_grad
        total[...] += matmul(active_all[...], wd_ref[...])
        grad_total[...] += contract_cols(upper_all[...], wu_ref[...])

        @pl.when(step == steps - 1)
        def _():
            out_ref[...] = total[...].astype(jnp.bfloat16)
            unit, inverse = _normalize(mixed_ref[...])
            grads = grad_total[...]
            sums_ref[0:1, :] = jnp.sum(grads * unit, axis=0, keepdims=True)
            sums_ref[1:2, :] = jnp.sum(grads, axis=0, keepdims=True)
            mixed_grad = grad_ref[...].astype(jnp.float32) + _normalize_back(grads, gain_ref[...], unit, inverse)
            mixed_grad_ref[...] = mixed_grad
            low = mixed_grad.astype(jnp.bfloat16)
            low_all[...] = low
            for share, low_ref in enumerate(low_refs):
                low_ref[...] = low_all[:, pl.ds(pl.multiple_of((place_ref[2] ^ share) * part, 128), part)]
            back = contract_cols(low, wo_ref[...]).astype(jnp.bfloat16)
            for block in range(blocks):
                back_ref[block] = back[:, block * slot : (block + 1) * slot]

    rows_spec = _fixed(row_count, features)
    return pl.pallas_call(
        kernel,
        grid_spec=pltpu.PrefetchScalarGridSpec(
            num_scalar_prefetch=1,
            grid=(steps,),
            in_specs=[
                _fixed(1, row_count, features),
                rows_spec,
                rows_spec,
                _fixed(1, features),
                _fixed(features, features),
                pl.BlockSpec((features, wide), lambda i, place: (0, i)),
                pl.BlockSpec((wide, features), lambda i, place: (i, 0)),
            ],
            out_specs=[rows_spec, rows_spec, _fixed(blocks, row_count, slot), _fixed(2, features)]
            + [_fixed(row_count, part)] * shares,
            scratch_shapes=[
                pltpu.VMEM((row_count, features), jnp.float32),
                pltpu.VMEM((row_count, features), jnp.float32),
                pltpu.VMEM((row_count, wide), jnp.bfloat16),
                pltpu.VMEM((row_count, wide), jnp.bfloat16),
                pltpu.VMEM((row_count, features), jnp.bfloat16),
            ],
        ),
        out_shape=[
            jax.ShapeDtypeStruct((row_count, features), jnp.bfloat16),
            jax.ShapeDtypeStruct((row_count, features), jnp.float32),
            jax.ShapeDtypeStruct((blocks, row_count, slot), jnp.bfloat16),
            jax.ShapeDtypeStruct((2, features), jnp.float32),
        ]
        + [jax.ShapeDtypeStruct((row_count, part), jnp.bfloat16)] * shares,
        compiler_params=_params(44),
        cost_estimate=_cost(20),
        name="middle",
    )(place, both, mixed, out_grad, gain, w_out, w_up, w_down)


def finish_call(received, patches, mixed_grad, gain, w_query, w_key, w_value, micro, before, cost):
    blocks, row_count, width = received.shape
    slot = width // 3
    features = patches.shape[2]
    per_step = max(1, min(blocks, 512 // slot))
    wide = slot * per_step
    steps = blocks // per_step

    def kernel(data_ref, rows_ref, mixed_ref, gain_ref, wq_ref, wk_ref, wv_ref, *refs):
        out_ref, total, side = refs[-3:]
        step = pl.program_id(0)

        @pl.when(step == 0)
        def _():
            total[...] = jnp.zeros_like(total)

        for part, weight_ref in enumerate((wq_ref, wk_ref, wv_ref)):
            for piece in range(per_step):
                side[part, :, piece * slot : (piece + 1) * slot] = data_ref[
                    piece, :, part * slot : (part + 1) * slot
                ]
            total[...] += contract_cols(side[part], weight_ref[...])

        @pl.when(step == steps - 1)
        def _():
            unit, inverse = _normalize(rows_ref[0].astype(jnp.float32))
            out_ref[0] = (
                mixed_ref[...] + _normalize_back(total[...], gain_ref[...], unit, inverse)
            ).astype(jnp.bfloat16)

    def fixed(*shape):
        return pl.BlockSpec(shape, lambda i: (0,) * len(shape))

    columns = pl.BlockSpec((features, wide), lambda i: (0, i))
    return pl.pallas_call(
        kernel,
        grid=(steps,),
        in_specs=[
            pl.BlockSpec((per_step, row_count, width), lambda i: (i, 0, 0)),
            pl.BlockSpec((1, row_count, features), lambda i: (micro, 0, 0)),
            pl.BlockSpec((row_count, features), lambda i: (micro, 0)),
            fixed(1, features),
            columns,
            columns,
            columns,
        ]
        + [pl.BlockSpec(memory_space=pl.ANY)] * (before is not None),
        out_specs=pl.BlockSpec((1, row_count, features), lambda i: (micro, 0, 0)),
        out_shape=jax.ShapeDtypeStruct(patches.shape, jnp.bfloat16),
        input_output_aliases={7: 0} if before is not None else {},
        scratch_shapes=[
            pltpu.VMEM((row_count, features), jnp.float32),
            pltpu.VMEM((3, row_count, wide), jnp.bfloat16),
        ],
        compiler_params=_params(60),
        cost_estimate=_cost(cost),
        name="finish",
    )(received, patches, mixed_grad, gain, w_query, w_key, w_value, *([before] if before is not None else []))


def grad_heads_call(place, units, cuts, places, made, gain, bias, sums, w_query, w_key, w_value, shares):
    micro_count = len(made)
    blocks, tokens, width = made[0].shape
    slot = width // 3
    features = gain.shape[1]
    group = features // (blocks * shares)
    full = width + 128
    kept = blocks * (shares // 2) * group

    def kernel(place_ref, *refs):
        unit_refs, refs = refs[: len(units)], refs[len(units) :]
        made_refs, refs = refs[:micro_count], refs[micro_count:]
        gain_ref, bias_ref, sums_ref, wq_ref, wk_ref, wv_ref, send_ref, keep_ref, spread, ordered = refs
        product = jnp.zeros((features, width), jnp.float32)
        column_sum = jnp.zeros((1, width), jnp.float32)
        for cut, (first, last) in enumerate(cuts):
            at = 0
            for relative in places:
                for micro, made_ref in enumerate(made_refs):
                    low, high = max(first - micro * tokens, 0), min(last - micro * tokens, tokens)
                    if low < high:
                        ordered[at : at + high - low, :] = made_ref[place_ref[0] ^ relative, low:high]
                        at += high - low
            half = at // 2
            for side in range(2):
                rows = ordered[side * half : (side + 1) * half, :]
                product = product + contract_rows(unit_refs[2 * cut + side][...], rows)
                column_sum = column_sum + jnp.sum(rows.astype(jnp.float32), axis=0, keepdims=True)
        vectors = jnp.concatenate(
            [gain_ref[...], bias_ref[...], sums_ref[...], jnp.zeros((124, features), jnp.float32)], axis=0
        ).T
        total = vectors[:, 0:1] * product + vectors[:, 1:2] * column_sum
        weights = jnp.concatenate([wq_ref[...], wk_ref[...], wv_ref[...]], axis=1).astype(jnp.float32)
        gain_sum = jnp.sum(weights * product, axis=1, keepdims=True)
        bias_sum = jnp.sum(weights * column_sum, axis=1, keepdims=True)
        lanes = lax.broadcasted_iota(jnp.int32, (1, 128), 1)
        norms = jnp.where(
            lanes == 0, gain_sum, jnp.where(lanes == 1, bias_sum, jnp.where(lanes < 4, vectors, 0.0))
        )
        spread[:, :, :, 0:width] = total.reshape(blocks, shares, group, width)
        spread[:, :, :, width:] = norms.reshape(blocks, shares, group, 128)
        core = place_ref[1] % 2
        for which, out_ref in enumerate((send_ref, keep_ref)):
            for share in range(0, shares, 2):
                for block in range(blocks):
                    out_ref[share // 2, block] = spread[block, share + (core if which else 1 - core)].astype(out_ref.dtype)

    def fixed(*shape):
        return pl.BlockSpec(shape, lambda i, place: (0,) * len(shape))

    columns = pl.BlockSpec((features, slot), lambda i, place: (0, place[0]))
    out = (shares // 2, blocks, group, full)
    return pl.pallas_call(
        kernel,
        grid_spec=pltpu.PrefetchScalarGridSpec(
            num_scalar_prefetch=1,
            grid=(1,),
            in_specs=[fixed(*part.shape) for part in (*units, *made)]
            + [fixed(1, features), fixed(1, features), fixed(2, features), columns, columns, columns],
            out_specs=[fixed(*out), fixed(*out)],
            scratch_shapes=[
                pltpu.VMEM((blocks, shares, group, full), jnp.float32),
                pltpu.VMEM((blocks * max(last - first for first, last in cuts), width), jnp.bfloat16),
            ],
        ),
        out_shape=[jax.ShapeDtypeStruct(out, jnp.bfloat16), jax.ShapeDtypeStruct(out, jnp.float32)],
        compiler_params=_params(60),
        cost_estimate=_cost(20),
        name="grad_heads",
    )(place, *units, *made, gain, bias, sums, w_query, w_key, w_value)


def assemble_call(place, parts, down_steps, blocks, owned):
    shares = len(parts)
    rows, width = parts[0].shape
    part = width - blocks * owned

    def kernel(place_ref, *refs):
        part_refs, (up_ref, out_ref) = refs[:shares], refs[shares:]
        for other, part_ref in enumerate(part_refs):
            share = place_ref[2] ^ other
            for at, block in enumerate(_ordered([_owner_stride(*step, shares) for step in down_steps])):
                to = pl.multiple_of((block + share % 2 + share // 2 * shares) * owned, 128)
                up_ref[:, pl.ds(to, owned)] = part_ref[:, at * owned : (at + 1) * owned].astype(jnp.float32)
            out_ref[:, pl.ds(pl.multiple_of(share * part, 128), part)] = part_ref[:, blocks * owned :].astype(jnp.float32)

    return pl.pallas_call(
        kernel,
        grid_spec=pltpu.PrefetchScalarGridSpec(
            num_scalar_prefetch=1,
            grid=(1,),
            in_specs=[_fixed(rows, width)] * shares,
            out_specs=[_fixed(rows, blocks * shares * owned), _fixed(rows, shares * part)],
        ),
        out_shape=[
            jax.ShapeDtypeStruct((rows, blocks * shares * owned), jnp.float32),
            jax.ShapeDtypeStruct((rows, shares * part), jnp.float32),
        ],
        compiler_params=_params(8),
        cost_estimate=_cost(0),
        name="assemble",
    )(place, *parts)


def _bits(count):
    return [1 << place for place in range(count.bit_length() - 1)]


def _ordered(bits):
    places = [0]
    for bit in bits:
        places = [at + step for at in places for step in (0, bit)]
    return places


def _ordered_low(bits):
    places = [0]
    for bit in bits:
        places = places + [at + bit for at in places]
    return places


def _paired(values, axis, bit):
    count = lax.axis_size(axis)
    return lax.ppermute(values, axis, [(i, i ^ bit) for i in range(count)])


def _bit_of(axis, bit):
    return (lax.axis_index(axis) // bit) % 2


def _mesh_bit(place, step):
    axis, bit = step
    return place[("blk", "mb").index(axis)] // bit % 2


def _owner_stride(axis, bit, shares):
    return bit * shares if axis == "blk" else bit


def _share_places(shares):
    return [0, 1, shares, shares + 1]


def _place_at(bits, step):
    places = _ordered(bits)
    at = jnp.int32(places[0])
    for other in range(1, len(places)):
        at = jnp.where(step == other, places[other], at)
    return at


def grad_middle_call(place, boths, out_grads, lows, w_up, w_down, down_steps, up_steps):
    shares = len(boths)
    _, row_count, features = boths[0].shape
    all_rows = shares * row_count
    hidden = w_up.shape[1]
    blocks = 1 << len(up_steps)
    owned, each = hidden // (blocks * shares), features // (blocks * shares)
    down_places = [_owner_stride(*step, shares) for step in down_steps]
    up_places = [_owner_stride(*step, shares) for step in up_steps]
    share_places = _share_places(shares)
    part = lows[0].shape[1]
    half = blocks // 2
    pair = min(2, half)
    half_steps = half // pair

    def kernel(place_ref, *refs):
        groups, refs = [refs[at * shares : (at + 1) * shares] for at in range(3)], refs[3 * shares :]
        up_refs, down_refs, refs = refs[:pair], refs[pair : 2 * pair], refs[2 * pair :]
        down_send, down_keep, up_send, up_keep, norm_turned, grad_all, active_all, upper_all, up_all = refs
        step = pl.program_id(0)
        mine = _mesh_bit(place_ref, up_steps[0])

        def spread():
            for at, block in enumerate(_ordered(up_places[1:])):
                for share, other in enumerate(share_places):
                    rows = slice((at * shares + share) * each, (at * shares + share + 1) * each)
                    up_send[rows, :] = up_all[block + other + up_places[0] * (1 - mine)].astype(jnp.bfloat16)
                    up_keep[rows, :] = up_all[block + other + up_places[0] * mine]

        @pl.when(step == 0)
        def _():
            for at in range(shares):
                rows = slice(at * row_count, (at + 1) * row_count)
                norm_turned[:, rows] = groups[0][at][0].T
                grad_all[rows, :] = groups[1][at][...]

        @pl.when(step < 2 * half_steps)
        def _():
            up_columns = jnp.concatenate([ref[...] for ref in up_refs], axis=1)
            down_rows = jnp.concatenate([ref[...] for ref in down_refs], axis=0)
            for at in range(shares):
                rows = slice(at * row_count, (at + 1) * row_count)
                active_all[rows, :], upper_all[rows, :] = _hidden_parts(
                    groups[0][at][0], groups[1][at][...], up_columns, down_rows
                )
            down_made = contract_rows(active_all[...], grad_all[...])

            @pl.when(step < half_steps)
            def _():
                down_send[...] = down_made.astype(jnp.bfloat16)

            @pl.when(step >= half_steps)
            def _():
                down_keep[...] = down_made

            up_all[...] = matmul(norm_turned[...], upper_all[...]).reshape(blocks * shares, each, pair * owned)
            spread()

        @pl.when(step == 2 * half_steps)
        def _():
            made = jnp.zeros((features, part), jnp.float32)
            for both_ref, low_ref in zip(groups[0], groups[2]):
                made = made + contract_rows(both_ref[1], low_ref[...])
            up_all[...] = made.reshape(blocks * shares, each, part)
            spread()

    def first_bit(i, place):
        return (_mesh_bit(place, down_steps[0]) + 1 + jnp.minimum(i, 2 * half_steps - 1) // half_steps) % 2

    def unit_block(i, place, at):
        inner = _place_at(down_places[1:], jnp.minimum(i, 2 * half_steps - 1) % half_steps * pair + at)
        return inner + down_places[0] * first_bit(i, place) + place[0] % 2 * shares + place[1] % 2

    ups = [
        pl.BlockSpec((features, owned), lambda i, place, at=at: (0, unit_block(i, place, at))) for at in range(pair)
    ]
    downs = [
        pl.BlockSpec((owned, features), lambda i, place, at=at: (unit_block(i, place, at), 0)) for at in range(pair)
    ]
    def up_block(i, place):
        return (0, jnp.where(i == 2 * half_steps, i, first_bit(i, place) * half_steps + i % half_steps))

    up_out = pl.BlockSpec((features // 2, pair * owned), up_block)
    shapes = [(half * owned, features), (features // 2, blocks * owned + part)]
    return pl.pallas_call(
        kernel,
        grid_spec=pltpu.PrefetchScalarGridSpec(
            num_scalar_prefetch=1,
            grid=(2 * half_steps + 1,),
            in_specs=[_fixed(2, row_count, features)] * shares
            + [_fixed(row_count, features)] * shares
            + [_fixed(row_count, part)] * shares
            + ups
            + downs,
            out_specs=[
                pl.BlockSpec((pair * owned, features), lambda i, place: (jnp.minimum(i, half_steps - 1), 0)),
                pl.BlockSpec((pair * owned, features), lambda i, place: (jnp.clip(i - half_steps, 0, half_steps - 1), 0)),
                up_out,
                up_out,
            ],
            scratch_shapes=[
                pltpu.VMEM((features, all_rows), jnp.bfloat16),
                pltpu.VMEM((all_rows, features), jnp.bfloat16),
                pltpu.VMEM((all_rows, pair * owned), jnp.bfloat16),
                pltpu.VMEM((all_rows, pair * owned), jnp.bfloat16),
                pltpu.VMEM((blocks * shares, each, pair * owned), jnp.float32),
            ],
        ),
        out_shape=[jax.ShapeDtypeStruct(shape, dtype) for shape in shapes for dtype in (jnp.bfloat16, jnp.float32)],
        compiler_params=_params(52),
        cost_estimate=_cost(20),
        name="grad_middle",
    )(place, *boths, *out_grads, *lows, *([w_up] * pair), *([w_down] * pair))


def halve_call(place, keep, received, step, cost):
    count, rows, columns = keep.shape
    half = count // 2

    def kernel(place_ref, keep_theirs, keep_mine, got_theirs, got_mine, theirs_ref, mine_ref):
        theirs_ref[...] = (keep_theirs[...] + got_theirs[...].astype(jnp.float32)).astype(jnp.bfloat16)
        mine_ref[...] = keep_mine[...] + got_mine[...].astype(jnp.float32)

    def block(which):
        return pl.BlockSpec(
            (1, rows, columns), lambda i, place: (i + half * ((_mesh_bit(place, step) + which) % 2), 0, 0)
        )

    out = pl.BlockSpec((1, rows, columns), lambda i, place: (i, 0, 0))
    return pl.pallas_call(
        kernel,
        grid_spec=pltpu.PrefetchScalarGridSpec(
            num_scalar_prefetch=1,
            grid=(half,),
            in_specs=[block(1), block(0), block(1), block(0)],
            out_specs=[out, out],
        ),
        out_shape=[
            jax.ShapeDtypeStruct((half, rows, columns), jnp.bfloat16),
            jax.ShapeDtypeStruct((half, rows, columns), jnp.float32),
        ],
        compiler_params=_params(16),
        cost_estimate=_cost(cost),
        name="halve",
    )(place, keep, keep, received, received)


def heads_total_call(keep, received):
    def kernel(keep_ref, got_ref, out_ref):
        out_ref[...] = (keep_ref[...] + got_ref[...].astype(jnp.float32)).astype(jnp.bfloat16)

    return pl.pallas_call(
        kernel,
        out_shape=jax.ShapeDtypeStruct(keep.shape, jnp.bfloat16),
        compiler_params=_params(8),
        cost_estimate=_cost(20),
        name="heads_total",
    )(keep, received)


def close_call(place, keep, received, shares):
    rows, width = keep.shape
    each = rows // shares

    def kernel(place_ref, keep_ref, got_ref, *refs):
        out_refs, total = refs[:-1], refs[-1]
        total[...] = (keep_ref[...] + got_ref[...].astype(jnp.float32)).reshape(shares, each, width)
        for share, out_ref in enumerate(out_refs):
            out_ref[...] = total[place_ref[2] ^ share].astype(jnp.bfloat16)

    return pl.pallas_call(
        kernel,
        grid_spec=pltpu.PrefetchScalarGridSpec(
            num_scalar_prefetch=1,
            grid=(1,),
            in_specs=[_fixed(rows, width)] * 2,
            out_specs=[_fixed(each, width)] * shares,
            scratch_shapes=[pltpu.VMEM((shares, each, width), jnp.float32)],
        ),
        out_shape=[jax.ShapeDtypeStruct((each, width), jnp.bfloat16)] * shares,
        compiler_params=_params(8),
        cost_estimate=_cost(6),
        name="close",
    )(place, keep, received)


def assemble_heads_call(parts, slot):
    blocks, rows, _ = parts.shape

    def kernel(parts_ref, *refs):
        weight_refs, norm_refs = refs[:3], refs[3:]
        for part, ref in enumerate(weight_refs):
            for block in range(blocks):
                ref[:, block * slot : (block + 1) * slot] = parts_ref[
                    block, :, part * slot : (part + 1) * slot
                ].astype(jnp.float32)
        sums = jnp.zeros((rows, 128), jnp.float32)
        for block in range(blocks):
            sums = sums + parts_ref[block, :, 3 * slot :].astype(jnp.float32)
        turned = jnp.concatenate([sums, jnp.zeros((128 - rows, 128), jnp.float32)], axis=0).T
        for at, ref in enumerate(norm_refs):
            ref[...] = turned[at : at + 1, 0:rows]

    return pl.pallas_call(
        kernel,
        out_shape=[jax.ShapeDtypeStruct((rows, blocks * slot), jnp.float32)] * 3
        + [jax.ShapeDtypeStruct((1, rows), jnp.float32)] * 4,
        compiler_params=_params(8),
        cost_estimate=_cost(0),
        name="assemble_heads",
    )(parts)


def fast_body(
    patches, seg_lengths, w_query, w_key, w_value, w_out, w_up, w_down,
    norm1_gain, norm1_bias, norm2_gain, norm2_bias, out_grad,
):
    micro_count, tokens, features = patches.shape
    hidden = w_up.shape[1]
    row_count = micro_count * tokens
    blocks, shares = lax.axis_size("blk"), lax.axis_size("mb")
    head_dim = features // H
    slot = features // blocks
    rows = patches.reshape(row_count, features)
    dout = out_grad.reshape(row_count, features)
    gain_one, bias_one, gain_two, bias_two = (
        value.reshape(1, features) for value in (norm1_gain, norm1_bias, norm2_gain, norm2_bias)
    )

    def swap(values):
        return lax.all_to_all(values, "blk", split_axis=0, concat_axis=0, tiled=True)

    def by_micro(values):
        return values.reshape(blocks, micro_count, tokens, values.shape[-1])

    at_blk, at_mb = lax.axis_index("blk"), lax.axis_index("mb")
    place = jnp.stack([at_blk, at_mb, at_mb % 2 + at_blk % 2 * 2]).astype(jnp.int32)
    blk_bits = _bits(blocks)
    down_steps = [("mb", 2), *(("blk", bit) for bit in blk_bits[1:])]
    up_steps = [down_steps[1], down_steps[0], *down_steps[2:]]
    each, owned, block_rows = features // (blocks * shares), hidden // (blocks * shares), features // blocks
    tie = lax.optimization_barrier

    def grown(values, bit):
        return jnp.concatenate([values, _paired(values, "blk", bit)], axis=0)

    def to_share(values, other):
        if other == 1:
            return _paired(values, "mb", 1)
        if other == 2:
            return _paired(values, "blk", 1)
        return lax.ppermute(values, ("blk", "mb"), [(i, i ^ (shares + 1)) for i in range(blocks * shares)])

    def shared(values):
        over = to_share(values, 2)
        return [values, to_share(values, 1), over, to_share(over, 1)]

    first_rows = max(16, tokens * 3 // 4 // 16 * 16)
    cuts = [(0, first_rows), (first_rows, row_count)]
    send, units_first, units_last = project_call(
        rows, gain_one, bias_one, w_query, w_key, w_value, blocks, cuts
    )
    received = by_micro(swap(send))
    dout_parts = [out_grad[micro] for micro in range(micro_count)]
    dout_over = [to_share(part, 2) for part in dout_parts]
    received, dout_over[0] = tie((received, dout_over[0]))
    units_first, received = tie((units_first, received))
    first_over = _paired(units_first, "blk", blk_bits[-1])
    own_attended, exact, logs = attend_call(received, seg_lengths, head_dim)
    attended, first_over, dout_over = tie((own_attended.reshape(blocks, row_count, slot), first_over, dout_over))
    units_first = jnp.concatenate([units_first, first_over], axis=0)
    dout_over = jnp.concatenate(dout_over, axis=0)
    attended, units_first, units_last, *douts = tie(
        (swap(attended), units_first, units_last, dout, to_share(dout, 1), dout_over, to_share(dout_over, 1))
    )
    for bit in blk_bits[-2:0:-1]:
        units_first = grown(units_first, bit)
    units_last = grown(units_last, blk_bits[-1])
    places = _ordered_low([*blk_bits[:0:-1], blk_bits[0]])

    mixed, both = mix_call(attended, rows, gain_two, bias_two, w_out)
    both_peer, both_over = to_share(both, 1), to_share(both, 2)
    layer_out, mixed_grad, back, sums_two, *lows = middle_call(
        place, both, mixed, dout, gain_two, w_out, w_up, w_down, blocks, shares
    )
    back, lows, units_first, units_last, both_peer, both_over = tie(
        (back, lows, units_first, units_last, both_peer, both_over)
    )
    boths = [both, both_peer, both_over, to_share(both_over, 1)]
    units_first_peer = _paired(units_first, "blk", blk_bits[0])
    for bit in blk_bits[-2:0:-1]:
        units_last = grown(units_last, bit)
    grads = by_micro(swap(back))
    lows = [lows[0]] + [to_share(lows[share], share) for share in range(1, shares)]
    down_theirs, down_keep, up_theirs, up_keep = grad_middle_call(
        place, boths, douts, lows, w_up, w_down, down_steps, up_steps
    )
    down_theirs, down_keep = (value.reshape(-1, owned, features) for value in (down_theirs, down_keep))
    up_theirs, up_keep = (value.reshape(-1, block_rows, value.shape[-1]) for value in (up_theirs, up_keep))
    down_received, up_received = _paired(down_theirs, *down_steps[0]), _paired(up_theirs, *up_steps[0])
    grads, down_keep, units_first_peer, units_last = tie((grads, down_keep, units_first_peer, units_last))
    units_last_peer = _paired(units_last, "blk", blk_bits[0])
    made = []
    for micro in range(micro_count):
        cost = 3 if micro == micro_count - 1 else 0
        made.append(attend_back_call(received, grads, exact, logs, seg_lengths, micro, cost, head_dim))
        grads, made[micro] = tie((grads, made[micro]))
    returned = [swap(made[0])]

    def then(done, *values):
        return tie((done, values))[1]

    returned += [swap(tie((values, returned[0]))[0]) for values in made[1:]]
    made = tie(made)
    up_theirs, up_keep = halve_call(place, *then(made[-1], up_keep, up_received), up_steps[1], 0)
    up_received = _paired(up_theirs, *up_steps[1])
    down_keep, down_received, units_last_peer = then(up_keep, down_keep, down_received, units_last_peer)
    down_theirs, down_keep = halve_call(place, down_keep, down_received, down_steps[1], 5)
    down_received = _paired(down_theirs, *down_steps[1])
    made = then(down_keep, *made)
    heads_send, heads_keep = grad_heads_call(
        place, (units_first, units_first_peer, units_last, units_last_peer), cuts, places,
        made, gain_one, bias_one, sums_two, w_query, w_key, w_value, shares,
    )
    pair = (shares // 2, -1, heads_keep.shape[-1])
    heads_received = _paired(heads_send, "mb", 1).reshape(pair)
    down_keep, down_received = then(heads_keep, down_keep, down_received)
    for step in down_steps[2:-1]:
        down_theirs, down_keep = halve_call(place, down_keep, down_received, step, 0)
        down_received = _paired(down_theirs, *step)
    down_theirs, down_keep = halve_call(place, down_keep, down_received, down_steps[-1], 0)
    up_keep, up_received = then(down_keep, up_keep, up_received)
    for step in up_steps[2:]:
        up_theirs, up_keep = halve_call(place, up_keep, up_received, step, 3)
        up_received = _paired(up_theirs, *step)
    heads_theirs, heads_keep = halve_call(
        place, *then(up_keep, heads_keep.reshape(pair), heads_received), ("mb", 2), 0
    )
    heads_theirs, down_theirs = tie((heads_theirs, down_theirs))
    heads_received = _paired(heads_theirs, "mb", 2)
    down_received = _paired(down_theirs, *down_steps[-1])
    finish = (patches, mixed_grad, gain_one, w_query, w_key, w_value)
    patches_grad = None
    for micro in range(micro_count - 1):
        first, heads_keep, heads_received = then(down_keep, returned[micro], heads_keep, heads_received)
        patches_grad = finish_call(first, *finish, micro, patches_grad, 0)
        heads_keep, heads_received = then(patches_grad, heads_keep, heads_received)
    returned[-1], heads_keep, heads_received = tie((returned[-1], heads_keep, heads_received))
    heads_total = heads_total_call(heads_keep[0], heads_received[0]).reshape(blocks, each, heads_keep.shape[-1])
    heads_parts = swap(heads_total)
    up_keep, up_received = then(heads_total, up_keep, up_received)
    parts = close_call(place, up_keep[0], up_received[0], shares)
    last = then(parts[0], returned[-1])[0]
    parts = [parts[0]] + [to_share(parts[share], share) for share in range(1, shares)]
    patches_grad = finish_call(last, *finish, micro_count - 1, patches_grad, 20)
    up_total, out_total = assemble_call(place, then(patches_grad, *parts), down_steps, blocks, owned)
    down_keep, down_received = then(up_total, down_keep, down_received)
    down_total = (down_keep + down_received.astype(jnp.float32))[0]
    query_total, key_total, value_total, *sums = assemble_heads_call(then(down_total, heads_parts)[0], slot)
    return (
        layer_out.reshape(patches.shape),
        patches_grad.reshape(patches.shape),
        query_total,
        key_total,
        value_total,
        out_total,
        up_total,
        down_total,
        *(value.reshape(each) for value in sums),
    )


def solution(mesh):
    in_specs = (
        P("mb", "blk", None),
        P("mb", None),
        P(),
        P(),
        P(),
        P(),
        P(),
        P(),
        P(),
        P(),
        P(),
        P(),
        P("mb", "blk", None),
    )
    out_specs = (
        P("mb", "blk", None),
        P("mb", "blk", None),
        P(("blk", "mb"), None),
        P(("blk", "mb"), None),
        P(("blk", "mb"), None),
        P(("blk", "mb"), None),
        P(("blk", "mb"), None),
        P(("blk", "mb"), None),
        P(("blk", "mb")),
        P(("blk", "mb")),
        P(("blk", "mb")),
        P(("blk", "mb")),
    )
    blocks, shares = mesh.shape["blk"], mesh.shape["mb"]
    paired = blocks >= 4 and blocks & (blocks - 1) == 0 and shares == 4
    chosen_body = fast_body if paired and H % blocks == 0 else body
    return jax.shard_map(chosen_body, mesh=mesh, in_specs=in_specs, out_specs=out_specs, check_vma=False)
```

```python
import math

import jax
import jax.numpy as jnp
from jax import lax
from jax.experimental import pallas as pl
from jax.experimental.pallas import tpu as pltpu
from jax.sharding import PartitionSpec as P

H = 16
CHUNK = 8


epsilon = 1e-05
masked_score = -1e30


def layer_norm(values, norm_gain, norm_bias):
    center = values - jnp.mean(values, axis=-1, keepdims=True)
    variance = jnp.mean(center * center, axis=-1, keepdims=True)
    return center * lax.rsqrt(variance + epsilon) * norm_gain + norm_bias


def gelu_exact(values):
    return jax.nn.gelu(values, approximate=False)


def matmul(left_side, right_side):
    return jnp.dot(left_side, right_side, preferred_element_type=jnp.float32)


def contract_rows(left_side, right_side):
    return lax.dot_general(
        left_side, right_side, (((0,), (0,)), ((), ())), preferred_element_type=jnp.float32
    )


def contract_cols(left_side, right_side):
    return lax.dot_general(
        left_side, right_side, (((1,), (1,)), ((), ())), preferred_element_type=jnp.float32
    )


def segment_ids(lengths, positions):
    doc_ends = jnp.cumsum(lengths, axis=-1)
    return jnp.sum((positions[None, :, None] >= doc_ends[:, None, :]).astype(jnp.int32), axis=-1)


def masked_scores(query_piece, keys_all, query_docs, key_docs, score_scale):
    scores = contract_cols(query_piece, keys_all) * score_scale
    return jnp.where(query_docs[:, None] == key_docs[None, :], scores, masked_score)


def soft_rows(scores):
    row_max = jnp.max(scores, axis=-1, keepdims=True)
    exponent = jnp.exp(scores - row_max)
    return exponent / jnp.sum(exponent, axis=-1, keepdims=True)


def body(
    patches,
    seg_lengths,
    w_query,
    w_key,
    w_value,
    w_out,
    w_up,
    w_down,
    norm1_gain,
    norm1_bias,
    norm2_gain,
    norm2_bias,
    out_grad,
):
    micro_count, tokens, features = patches.shape
    row_count = micro_count * tokens
    blocks = lax.axis_size("blk")
    block_index = lax.axis_index("blk")
    head_count = H
    head_dim = features // head_count
    repeat = max(1, blocks // head_count)
    per_slot = max(1, head_count // blocks)
    groups = head_count // per_slot
    rows_part = tokens // repeat
    query_rows = blocks * rows_part
    seq_length = blocks * tokens
    item_count = micro_count * per_slot
    block_rows = min(512, query_rows)
    block_count = query_rows // block_rows
    slot_width = micro_count * per_slot * head_dim
    score_scale = 1.0 / math.sqrt(head_dim)
    doc_count = seg_lengths.shape[1]

    def query_layout(values):
        shaped = values.reshape(micro_count, repeat, rows_part, groups, per_slot * head_dim)
        return shaped.transpose(3, 1, 2, 0, 4).reshape(blocks, rows_part, slot_width)

    def key_layout(values):
        shaped = values.reshape(micro_count, tokens, groups, per_slot * head_dim).transpose(
            2, 1, 0, 3
        )
        shaped = jnp.broadcast_to(
            shaped[:, None], (groups, repeat, tokens, micro_count, per_slot * head_dim)
        )
        return shaped.reshape(blocks, tokens, slot_width)

    def token_layout(values):
        shaped = values.reshape(groups, repeat, rows_part, micro_count, per_slot * head_dim)
        return shaped.transpose(3, 1, 2, 0, 4).reshape(row_count, features)

    def key_sum(values):
        shaped = values.reshape(groups, repeat, tokens, micro_count, per_slot * head_dim).sum(
            axis=1
        )
        return shaped.transpose(2, 1, 0, 3).reshape(row_count, features)

    def to_items(received):
        row_total = received.shape[1]
        shaped = received.reshape(row_total, micro_count, per_slot, head_dim).transpose(1, 2, 0, 3)
        return shaped.reshape(item_count, row_total, head_dim)

    def from_items(values):
        row_total = values.shape[1]
        shaped = values.reshape(micro_count, per_slot, row_total, head_dim).transpose(2, 0, 1, 3)
        return shaped.reshape(1, row_total, slot_width)

    row_ids = jnp.arange(query_rows)
    query_pos = (
        row_ids // rows_part * tokens + block_index % repeat * rows_part + row_ids % rows_part
    )
    query_docs = jnp.repeat(segment_ids(seg_lengths, query_pos), per_slot, axis=0)
    key_docs = jnp.repeat(segment_ids(seg_lengths, jnp.arange(seq_length)), per_slot, axis=0)
    query_valid = (query_docs < doc_count).astype(jnp.float32)
    local_pos = block_index * tokens + jnp.arange(tokens)
    row_valid = (
        (segment_ids(seg_lengths, local_pos) < doc_count).astype(jnp.float32).reshape(row_count, 1)
    )

    def forward_item(operands):
        queries_item, keys_item, values_item, docs_item, key_docs_item = operands

        def forward_one_block(block_operands):
            query_piece, docs_piece = block_operands
            weights_soft = soft_rows(
                masked_scores(query_piece, keys_item, docs_piece, key_docs_item, score_scale)
            )
            return matmul(weights_soft.astype(jnp.bfloat16), values_item)

        outputs = lax.map(
            forward_one_block,
            (
                queries_item.reshape(block_count, block_rows, head_dim),
                docs_item.reshape(block_count, block_rows),
            ),
        )
        return outputs.reshape(query_rows, head_dim)

    def backward_item(operands):
        queries_item, keys_item, values_item, grads_item, docs_item, key_docs_item = operands

        def backward_one_block(totals, block_operands):
            key_total, value_total = totals
            query_piece, grad_piece, docs_piece = block_operands
            weights_soft = soft_rows(
                masked_scores(query_piece, keys_item, docs_piece, key_docs_item, score_scale)
            )
            weights_low = weights_soft.astype(jnp.bfloat16)
            weight_grads = contract_cols(grad_piece, values_item)
            row_inner = jnp.sum(weights_soft * weight_grads, axis=-1, keepdims=True)
            score_grads = (weights_soft * (weight_grads - row_inner)).astype(jnp.bfloat16)
            query_grad = matmul(score_grads, keys_item) * score_scale
            key_total = key_total + contract_rows(score_grads, query_piece) * score_scale
            value_total = value_total + contract_rows(weights_low, grad_piece)
            return ((key_total, value_total), query_grad)

        zero_block = jnp.zeros((seq_length, head_dim), jnp.float32)
        totals, query_grads = lax.scan(
            backward_one_block,
            (zero_block, zero_block),
            (
                queries_item.reshape(block_count, block_rows, head_dim),
                grads_item.reshape(block_count, block_rows, head_dim),
                docs_item.reshape(block_count, block_rows),
            ),
        )
        return (query_grads.reshape(query_rows, head_dim), totals[0], totals[1])

    inputs = patches.astype(jnp.float32).reshape(row_count, features)
    norm_one_full, norm_one_pull = jax.vjp(layer_norm, inputs, norm1_gain, norm1_bias)
    norm_one = norm_one_full.astype(jnp.bfloat16)
    queries = matmul(norm_one, w_query).astype(jnp.bfloat16)
    keys_proj = matmul(norm_one, w_key).astype(jnp.bfloat16)
    values_proj = matmul(norm_one, w_value).astype(jnp.bfloat16)
    query_send = query_layout(queries)
    key_send = key_layout(keys_proj)
    value_send = key_layout(values_proj)
    query_heads, key_heads, value_heads = (
        lax.all_to_all(query_send, "blk", split_axis=0, concat_axis=1, tiled=True),
        lax.all_to_all(key_send, "blk", split_axis=0, concat_axis=1, tiled=True),
        lax.all_to_all(value_send, "blk", split_axis=0, concat_axis=1, tiled=True),
    )
    query_items = to_items(query_heads)
    key_items = to_items(key_heads)
    value_items = to_items(value_heads)
    attended_items = lax.map(
        forward_item, (query_items, key_items, value_items, query_docs, key_docs)
    )
    attended_items = (attended_items * query_valid[:, :, None]).astype(jnp.bfloat16)
    attended = token_layout(
        lax.all_to_all(from_items(attended_items), "blk", split_axis=1, concat_axis=0, tiled=True)
    )
    mixed_rows = inputs + matmul(attended, w_out)
    norm_two_full, norm_two_pull = jax.vjp(layer_norm, mixed_rows, norm2_gain, norm2_bias)
    norm_two = norm_two_full.astype(jnp.bfloat16)
    upper_proj = matmul(norm_two, w_up)
    active_full, gelu_pull = jax.vjp(gelu_exact, upper_proj)
    active = active_full.astype(jnp.bfloat16)
    result = mixed_rows + matmul(active, w_down)
    layer_out = result.astype(jnp.bfloat16).reshape(micro_count, tokens, features)
    dout_low = out_grad.reshape(row_count, features)
    down_grad = contract_rows(active, dout_low)
    active_grad = contract_cols(dout_low, w_down)
    upper_grad = gelu_pull(active_grad)[0].astype(jnp.bfloat16)
    up_grad = contract_rows(norm_two, upper_grad)
    norm_two_grad = contract_cols(upper_grad, w_up)
    mixed_part, gain_two_grad, bias_two_grad = norm_two_pull(norm_two_grad)
    mixed_grad = dout_low.astype(jnp.float32) + mixed_part
    mixed_low = mixed_grad.astype(jnp.bfloat16)
    out_proj_grad = contract_rows(attended, mixed_low)
    attended_grad = (contract_cols(mixed_low, w_out) * row_valid).astype(jnp.bfloat16)
    grad_send = query_layout(attended_grad)
    query_again, key_again, value_again, grad_heads = (
        lax.all_to_all(query_send, "blk", split_axis=0, concat_axis=1, tiled=True),
        lax.all_to_all(key_send, "blk", split_axis=0, concat_axis=1, tiled=True),
        lax.all_to_all(value_send, "blk", split_axis=0, concat_axis=1, tiled=True),
        lax.all_to_all(grad_send, "blk", split_axis=0, concat_axis=1, tiled=True),
    )
    back_queries = to_items(query_again)
    back_keys = to_items(key_again)
    back_values = to_items(value_again)
    grad_items = to_items(grad_heads)
    query_grad_items, key_grad_items, value_grad_items = lax.map(
        backward_item, (back_queries, back_keys, back_values, grad_items, query_docs, key_docs)
    )
    query_back, key_back, value_back = (
        lax.all_to_all(
            from_items(query_grad_items).astype(jnp.bfloat16),
            "blk",
            split_axis=1,
            concat_axis=0,
            tiled=True,
        ).astype(jnp.float32),
        lax.all_to_all(
            from_items(key_grad_items).astype(jnp.bfloat16),
            "blk",
            split_axis=1,
            concat_axis=0,
            tiled=True,
        ).astype(jnp.float32),
        lax.all_to_all(
            from_items(value_grad_items).astype(jnp.bfloat16),
            "blk",
            split_axis=1,
            concat_axis=0,
            tiled=True,
        ).astype(jnp.float32),
    )
    query_grad = token_layout(query_back).astype(jnp.bfloat16)
    key_grad = key_sum(key_back).astype(jnp.bfloat16)
    value_grad = key_sum(value_back).astype(jnp.bfloat16)
    query_proj_grad = contract_rows(norm_one, query_grad)
    key_proj_grad = contract_rows(norm_one, key_grad)
    value_proj_grad = contract_rows(norm_one, value_grad)
    norm_one_grad = (
        contract_cols(query_grad, w_query)
        + contract_cols(key_grad, w_key)
        + contract_cols(value_grad, w_value)
    )
    input_part, gain_one_grad, bias_one_grad = norm_one_pull(norm_one_grad)
    patches_grad = (
        (mixed_grad + input_part).astype(jnp.bfloat16).reshape(micro_count, tokens, features)
    )
    gradients = (
        query_proj_grad,
        key_proj_grad,
        value_proj_grad,
        out_proj_grad,
        up_grad,
        down_grad,
        gain_one_grad,
        bias_one_grad,
        gain_two_grad,
        bias_two_grad,
    )
    summed = (
        lax.psum_scatter(gradients[0], ("blk", "mb"), scatter_dimension=0, tiled=True),
        lax.psum_scatter(gradients[1], ("blk", "mb"), scatter_dimension=0, tiled=True),
        lax.psum_scatter(gradients[2], ("blk", "mb"), scatter_dimension=0, tiled=True),
        lax.psum_scatter(gradients[3], ("blk", "mb"), scatter_dimension=0, tiled=True),
        lax.psum_scatter(gradients[4], ("blk", "mb"), scatter_dimension=0, tiled=True),
        lax.psum_scatter(gradients[5], ("blk", "mb"), scatter_dimension=0, tiled=True),
        lax.psum_scatter(gradients[6], ("blk", "mb"), scatter_dimension=0, tiled=True),
        lax.psum_scatter(gradients[7], ("blk", "mb"), scatter_dimension=0, tiled=True),
        lax.psum_scatter(gradients[8], ("blk", "mb"), scatter_dimension=0, tiled=True),
        lax.psum_scatter(gradients[9], ("blk", "mb"), scatter_dimension=0, tiled=True),
    )
    return (
        layer_out,
        patches_grad,
        summed[0],
        summed[1],
        summed[2],
        summed[3],
        summed[4],
        summed[5],
        summed[6],
        summed[7],
        summed[8],
        summed[9],
    )


def _normalize(values):
    center = values - jnp.mean(values, axis=-1, keepdims=True)
    variance = jnp.mean(center * center, axis=-1, keepdims=True)
    inverse = lax.rsqrt(variance + epsilon)
    return center * inverse, inverse


def _normalize_back(grads, gain, unit, inverse):
    scaled = grads * gain
    mean_scaled = jnp.mean(scaled, axis=-1, keepdims=True)
    mean_product = jnp.mean(scaled * unit, axis=-1, keepdims=True)
    return (scaled - mean_scaled - unit * mean_product) * inverse


def _doc_ids(lengths_ref, micro, doc_count, positions):
    end = jnp.int32(0)
    ids = jnp.zeros_like(positions)
    for doc in range(doc_count):
        end = end + lengths_ref[micro, doc]
        ids = ids + (positions >= end).astype(jnp.int32)
    return ids


def _params(mib):
    return pltpu.CompilerParams(vmem_limit_bytes=mib << 20)


def _cost(microseconds):
    return pl.CostEstimate(flops=int(microseconds * 1e9) + 1, bytes_accessed=1, transcendentals=0)


def project_call(rows, gain, bias, w_query, w_key, w_value, blocks, cuts):
    row_count, features = rows.shape
    slot = features // blocks
    per_step = max(1, min(blocks, 512 // slot))
    wide = slot * per_step

    def kernel(rows_ref, gain_ref, bias_ref, wq_ref, wk_ref, wv_ref, send_ref, *refs):
        unit_refs, norm_ref = refs[:-1], refs[-1]


        @pl.when(pl.program_id(0) == 0)
        def _():
            unit, _unused = _normalize(rows_ref[...].astype(jnp.float32))
            for (first, last), unit_ref in zip(cuts, unit_refs):
                unit_ref[...] = unit[first:last].astype(jnp.bfloat16)
            norm_ref[...] = (unit * gain_ref[...] + bias_ref[...]).astype(jnp.bfloat16)

        for part, weight_ref in enumerate((wq_ref, wk_ref, wv_ref)):
            made = matmul(norm_ref[...], weight_ref[...]).astype(jnp.bfloat16)
            for piece in range(per_step):
                send_ref[piece, :, part * slot : (part + 1) * slot] = made[
                    :, piece * slot : (piece + 1) * slot
                ]

    whole = pl.BlockSpec((row_count, features), lambda i: (0, 0))
    vector = pl.BlockSpec((1, features), lambda i: (0, 0))
    columns = pl.BlockSpec((features, wide), lambda i: (0, i))
    return pl.pallas_call(
        kernel,
        grid=(blocks // per_step,),
        in_specs=[whole, vector, vector, columns, columns, columns],
        out_specs=[pl.BlockSpec((per_step, row_count, 3 * slot), lambda i: (i, 0, 0))]
        + [pl.BlockSpec((last - first, features), lambda i: (0, 0)) for first, last in cuts],
        out_shape=[jax.ShapeDtypeStruct((blocks, row_count, 3 * slot), jnp.bfloat16)]
        + [jax.ShapeDtypeStruct((last - first, features), jnp.bfloat16) for first, last in cuts],
        scratch_shapes=[pltpu.VMEM((row_count, features), jnp.bfloat16)],
        compiler_params=_params(60),
        cost_estimate=_cost(6),
        name="project",
    )(rows, gain, bias, w_query, w_key, w_value)


def _head_masks(slot, head_dim, dtype):
    lanes = lax.broadcasted_iota(jnp.int32, (1, slot), 1)
    return [(lanes // head_dim == head).astype(dtype) for head in range(slot // head_dim)]


def _key_range(lengths_ref, micro, doc_count, first_row, last_row, seq):
    low, high, end = jnp.int32(0), jnp.int32(seq), jnp.int32(0)
    for doc in range(doc_count):
        end = end + lengths_ref[micro, doc]
        low = jnp.where(end <= first_row, jnp.maximum(low, end), low)
        high = jnp.where(end >= last_row, jnp.minimum(high, end), high)
    return low, high


def _by_key_range(lengths_ref, micro, doc_count, step, rows, blocks, tokens, compute):
    low, high = _key_range(lengths_ref, micro, doc_count, step * rows, (step + 1) * rows, blocks * tokens)
    half = blocks // 2
    in_low, in_high = high <= half * tokens, low >= half * tokens

    @pl.when(in_low | in_high)
    def _():
        compute(jnp.where(in_low, 0, half), half)

    @pl.when(jnp.logical_not(in_low | in_high))
    def _():
        compute(0, blocks)


def attend_call(received, lengths, head_dim):
    blocks, micro_count, tokens, width = received.shape
    slot = width // 3
    doc_count = lengths.shape[1]
    step_blocks = max(1, min(blocks // 2, 512 // tokens))
    rows = step_blocks * tokens
    scale = 1.0 / math.sqrt(head_dim)

    def kernel(lengths_ref, data_ref, out_ref, exact_ref, log_ref):
        micro = pl.program_id(0)
        step = pl.program_id(1)
        row_docs = _doc_ids(
            lengths_ref, micro, doc_count, lax.broadcasted_iota(jnp.int32, (rows, 1), 0) + step * rows
        )
        queries = data_ref[pl.ds(step * step_blocks, step_blocks), 0, :, 0:slot].reshape(rows, slot) * scale

        def compute(first, count):
            seq = count * tokens
            key_docs = _doc_ids(
                lengths_ref, micro, doc_count, lax.broadcasted_iota(jnp.int32, (1, seq), 1) + first * tokens
            )
            same = row_docs == key_docs
            keys = data_ref[pl.ds(first, count), 0, :, slot : 2 * slot].reshape(seq, slot)
            values = data_ref[pl.ds(first, count), 0, :, 2 * slot : 3 * slot].reshape(seq, slot)
            total = jnp.zeros((rows, slot), jnp.float32)
            logs = jnp.zeros((rows, 128), jnp.float32)
            lanes = lax.broadcasted_iota(jnp.int32, (1, 128), 1)
            for head, (mask, mask_wide) in enumerate(
                zip(_head_masks(slot, head_dim, jnp.bfloat16), _head_masks(slot, head_dim, jnp.float32))
            ):
                scores = jnp.where(same, contract_cols(queries * mask, keys), masked_score)
                most = jnp.max(scores, axis=-1, keepdims=True)
                exponent = jnp.exp(scores - most)
                exponent_sum = jnp.sum(exponent, axis=-1, keepdims=True)
                share = 1.0 / exponent_sum
                logs = jnp.where(lanes == head, most + jnp.log(exponent_sum), logs)
                total = total + matmul(exponent.astype(jnp.bfloat16), values) * (share * mask_wide)
            total = jnp.where(row_docs < doc_count, total, 0.0)
            out_ref[...] = total.astype(jnp.bfloat16).reshape(step_blocks, 1, tokens, slot)
            exact_ref[...] = total.reshape(step_blocks, 1, tokens, slot)
            log_ref[0] = logs.T[0:8, :]

        _by_key_range(lengths_ref, micro, doc_count, step, rows, blocks, tokens, compute)

    return pl.pallas_call(
        kernel,
        grid=(micro_count, blocks // step_blocks),
        in_specs=[
            pl.BlockSpec(memory_space=pltpu.SMEM),
            pl.BlockSpec((blocks, 1, tokens, width), lambda m, s: (0, m, 0, 0)),
        ],
        out_specs=[
            pl.BlockSpec((step_blocks, 1, tokens, slot), lambda m, s: (s, m, 0, 0)),
            pl.BlockSpec((step_blocks, 1, tokens, slot), lambda m, s: (s, m, 0, 0)),
            pl.BlockSpec((1, 8, rows), lambda m, s: (m, 0, s)),
        ],
        out_shape=[
            jax.ShapeDtypeStruct((blocks, micro_count, tokens, slot), jnp.bfloat16),
            jax.ShapeDtypeStruct((blocks, micro_count, tokens, slot), jnp.float32),
            jax.ShapeDtypeStruct((micro_count, 8, blocks * tokens), jnp.float32),
        ],
        compiler_params=_params(32),
        cost_estimate=_cost(11),
        name="attend",
    )(lengths, received)


def attend_back_call(received, grads, attended, logs, lengths, micro, cost, head_dim):
    blocks, _, tokens, width = received.shape
    slot = width // 3
    doc_count = lengths.shape[1]
    step_blocks = max(1, min(blocks // 2, 512 // tokens))
    rows = step_blocks * tokens
    steps = blocks // step_blocks
    scale = 1.0 / math.sqrt(head_dim)

    def kernel(lengths_ref, data_ref, grads_ref, att_ref, log_ref, out_ref, key_total, value_total, turned):
        step = pl.program_id(0)

        @pl.when(step == 0)
        def _():
            key_total[...] = jnp.zeros_like(key_total)
            value_total[...] = jnp.zeros_like(value_total)
            for block in range(blocks):
                turned[block] = data_ref[block, 0, :, slot : 2 * slot].T

        row_docs = _doc_ids(
            lengths_ref, micro, doc_count, lax.broadcasted_iota(jnp.int32, (1, rows), 1) + step * rows
        )
        column_docs = _doc_ids(
            lengths_ref, micro, doc_count, lax.broadcasted_iota(jnp.int32, (rows, 1), 0) + step * rows
        )
        queries = data_ref[pl.ds(step * step_blocks, step_blocks), 0, :, 0:slot].reshape(rows, slot) * scale
        out_grads = grads_ref[...].reshape(rows, slot)
        out_grads = out_grads * (column_docs < doc_count).astype(jnp.float32).astype(jnp.bfloat16)

        inner = (out_grads.astype(jnp.float32) * att_ref[...].reshape(rows, slot)).T

        def compute(first, count):
            chunk = min(CHUNK, count)
            query_parts = [jnp.zeros((head_dim, rows), jnp.float32) for _ in range(slot // head_dim)]
            masks = _head_masks(slot, head_dim, jnp.bfloat16)
            for at in range(0, count, chunk):
                seq = chunk * tokens
                key_docs = _doc_ids(
                    lengths_ref,
                    micro,
                    doc_count,
                    lax.broadcasted_iota(jnp.int32, (seq, 1), 0) + (first + at) * tokens,
                )
                same = row_docs == key_docs
                keys = data_ref[pl.ds(first + at, chunk), 0, :, slot : 2 * slot].reshape(seq, slot)
                values = data_ref[pl.ds(first + at, chunk), 0, :, 2 * slot : 3 * slot].reshape(seq, slot)
                keys_turned = jnp.concatenate([turned[first + at + other] for other in range(chunk)], axis=1)
                key_made = jnp.zeros((seq, slot), jnp.float32)
                value_made = jnp.zeros((seq, slot), jnp.float32)
                for head, mask in enumerate(masks):
                    lanes = slice(head * head_dim, (head + 1) * head_dim)
                    queries_head, grads_head = queries * mask, out_grads * mask
                    scores = jnp.where(same, contract_cols(keys, queries_head), masked_score)
                    probs = jnp.exp(scores - log_ref[0, head : head + 1, :])
                    prob_grads = contract_cols(values, grads_head)
                    head_inner = jnp.sum(inner[lanes], axis=0, keepdims=True)
                    score_grads = (probs * (prob_grads - head_inner)).astype(jnp.bfloat16)
                    value_made = value_made + matmul(probs.astype(jnp.bfloat16), grads_head)
                    key_made = key_made + matmul(score_grads, queries_head)
                    query_parts[head] = query_parts[head] + matmul(keys_turned[lanes], score_grads)
                to = pl.ds(pl.multiple_of((first + at) * tokens, tokens), seq)
                key_total[to, :] += key_made
                value_total[to, :] += value_made
            query_grads = (jnp.concatenate(query_parts, axis=0).T * scale).astype(jnp.bfloat16).reshape(step_blocks, tokens, slot)
            out_ref[pl.ds(step * step_blocks, step_blocks), :, 0:slot] = query_grads

        _by_key_range(lengths_ref, micro, doc_count, step, rows, blocks, tokens, compute)

        @pl.when(step == steps - 1)
        def _():
            out_ref[:, :, slot : 2 * slot] = key_total[...].astype(jnp.bfloat16).reshape(blocks, tokens, slot)
            out_ref[:, :, 2 * slot :] = value_total[...].astype(jnp.bfloat16).reshape(blocks, tokens, slot)

    return pl.pallas_call(
        kernel,
        grid=(steps,),
        in_specs=[
            pl.BlockSpec(memory_space=pltpu.SMEM),
            pl.BlockSpec((blocks, 1, tokens, width), lambda s: (0, micro, 0, 0)),
            pl.BlockSpec((step_blocks, 1, tokens, slot), lambda s: (s, micro, 0, 0)),
            pl.BlockSpec((step_blocks, 1, tokens, slot), lambda s: (s, micro, 0, 0)),
            pl.BlockSpec((1, 8, rows), lambda s: (micro, 0, s)),
        ],
        out_specs=_fixed(blocks, tokens, width),
        out_shape=jax.ShapeDtypeStruct((blocks, tokens, width), jnp.bfloat16),
        scratch_shapes=[pltpu.VMEM((blocks * tokens, slot), jnp.float32)] * 2
        + [pltpu.VMEM((blocks, slot, tokens), jnp.bfloat16)],
        compiler_params=_params(60),
        cost_estimate=_cost(cost),
        name="attend_back",
    )(lengths, received, grads, attended, logs)


def _fixed(*shape):
    return pl.BlockSpec(shape, lambda *_unused: (0,) * len(shape))


def mix_call(attended, rows, gain, bias, w_out):
    blocks, row_count, slot = attended.shape
    features = rows.shape[1]

    def kernel(att_ref, rows_ref, gain_ref, bias_ref, wo_ref, mixed_ref, both_ref):
        for block in range(blocks):
            both_ref[1, :, block * slot : (block + 1) * slot] = att_ref[block]
        value = rows_ref[...].astype(jnp.float32) + matmul(both_ref[1], wo_ref[...])
        mixed_ref[...] = value
        unit, _unused = _normalize(value)
        both_ref[0] = (unit * gain_ref[...] + bias_ref[...]).astype(jnp.bfloat16)

    rows_spec, vector = _fixed(row_count, features), _fixed(1, features)
    return pl.pallas_call(
        kernel,
        grid=(1,),
        in_specs=[_fixed(blocks, row_count, slot), rows_spec, vector, vector, _fixed(features, features)],
        out_specs=[rows_spec, _fixed(2, row_count, features)],
        out_shape=[
            jax.ShapeDtypeStruct((row_count, features), jnp.float32),
            jax.ShapeDtypeStruct((2, row_count, features), jnp.bfloat16),
        ],
        compiler_params=_params(24),
        cost_estimate=_cost(4),
        name="mix",
    )(attended, rows, gain, bias, w_out)


def _hidden_parts(norm, out_grad, up_columns, down_rows):
    upper = matmul(norm, up_columns)
    active_grad = contract_cols(out_grad, down_rows)
    half = (1.0 + lax.erf(upper * (1.0 / math.sqrt(2.0)))) * 0.5
    slope = half + upper * jnp.exp(upper * upper * -0.5) * (1.0 / math.sqrt(2.0 * math.pi))
    return (upper * half).astype(jnp.bfloat16), (active_grad * slope).astype(jnp.bfloat16)


def middle_call(place, both, mixed, out_grad, gain, w_out, w_up, w_down, blocks, shares):
    row_count, features = mixed.shape
    hidden = w_up.shape[1]
    wide = min(1024, hidden)
    sub = min(512, wide)
    steps = hidden // wide
    slot, part = features // blocks, features // shares

    def kernel(place_ref, norm_ref, mixed_ref, grad_ref, gain_ref, wo_ref, wu_ref, wd_ref, *refs):
        out_ref, mixed_grad_ref, back_ref, sums_ref = refs[:4]
        low_refs, (total, grad_total, active_all, upper_all, low_all) = refs[4 : 4 + shares], refs[4 + shares :]
        step = pl.program_id(0)

        @pl.when(step == 0)
        def _():
            total[...] = mixed_ref[...]
            grad_total[...] = jnp.zeros_like(grad_total)

        for chunk in range(0, wide, sub):
            active, upper_grad = _hidden_parts(
                norm_ref[0], grad_ref[...], wu_ref[:, chunk : chunk + sub], wd_ref[chunk : chunk + sub, :]
            )
            active_all[:, chunk : chunk + sub] = active
            upper_all[:, chunk : chunk + sub] = upper_grad
        total[...] += matmul(active_all[...], wd_ref[...])
        grad_total[...] += contract_cols(upper_all[...], wu_ref[...])

        @pl.when(step == steps - 1)
        def _():
            out_ref[...] = total[...].astype(jnp.bfloat16)
            unit, inverse = _normalize(mixed_ref[...])
            grads = grad_total[...]
            sums_ref[0:1, :] = jnp.sum(grads * unit, axis=0, keepdims=True)
            sums_ref[1:2, :] = jnp.sum(grads, axis=0, keepdims=True)
            mixed_grad = grad_ref[...].astype(jnp.float32) + _normalize_back(grads, gain_ref[...], unit, inverse)
            mixed_grad_ref[...] = mixed_grad
            low = mixed_grad.astype(jnp.bfloat16)
            low_all[...] = low
            for share, low_ref in enumerate(low_refs):
                low_ref[...] = low_all[:, pl.ds(pl.multiple_of((place_ref[2] ^ share) * part, 128), part)]
            back = contract_cols(low, wo_ref[...]).astype(jnp.bfloat16)
            for block in range(blocks):
                back_ref[block] = back[:, block * slot : (block + 1) * slot]

    rows_spec = _fixed(row_count, features)
    return pl.pallas_call(
        kernel,
        grid_spec=pltpu.PrefetchScalarGridSpec(
            num_scalar_prefetch=1,
            grid=(steps,),
            in_specs=[
                _fixed(1, row_count, features),
                rows_spec,
                rows_spec,
                _fixed(1, features),
                _fixed(features, features),
                pl.BlockSpec((features, wide), lambda i, place: (0, i)),
                pl.BlockSpec((wide, features), lambda i, place: (i, 0)),
            ],
            out_specs=[rows_spec, rows_spec, _fixed(blocks, row_count, slot), _fixed(2, features)]
            + [_fixed(row_count, part)] * shares,
            scratch_shapes=[
                pltpu.VMEM((row_count, features), jnp.float32),
                pltpu.VMEM((row_count, features), jnp.float32),
                pltpu.VMEM((row_count, wide), jnp.bfloat16),
                pltpu.VMEM((row_count, wide), jnp.bfloat16),
                pltpu.VMEM((row_count, features), jnp.bfloat16),
            ],
        ),
        out_shape=[
            jax.ShapeDtypeStruct((row_count, features), jnp.bfloat16),
            jax.ShapeDtypeStruct((row_count, features), jnp.float32),
            jax.ShapeDtypeStruct((blocks, row_count, slot), jnp.bfloat16),
            jax.ShapeDtypeStruct((2, features), jnp.float32),
        ]
        + [jax.ShapeDtypeStruct((row_count, part), jnp.bfloat16)] * shares,
        compiler_params=_params(44),
        cost_estimate=_cost(20),
        name="middle",
    )(place, both, mixed, out_grad, gain, w_out, w_up, w_down)


def finish_call(received, patches, mixed_grad, gain, w_query, w_key, w_value, micro, before, cost):
    blocks, row_count, width = received.shape
    slot = width // 3
    features = patches.shape[2]
    per_step = max(1, min(blocks, 512 // slot))
    wide = slot * per_step
    steps = blocks // per_step

    def kernel(data_ref, rows_ref, mixed_ref, gain_ref, wq_ref, wk_ref, wv_ref, *refs):
        out_ref, total, side = refs[-3:]
        step = pl.program_id(0)

        @pl.when(step == 0)
        def _():
            total[...] = jnp.zeros_like(total)

        for part, weight_ref in enumerate((wq_ref, wk_ref, wv_ref)):
            for piece in range(per_step):
                side[part, :, piece * slot : (piece + 1) * slot] = data_ref[
                    piece, :, part * slot : (part + 1) * slot
                ]
            total[...] += contract_cols(side[part], weight_ref[...])

        @pl.when(step == steps - 1)
        def _():
            unit, inverse = _normalize(rows_ref[0].astype(jnp.float32))
            out_ref[0] = (
                mixed_ref[...] + _normalize_back(total[...], gain_ref[...], unit, inverse)
            ).astype(jnp.bfloat16)

    def fixed(*shape):
        return pl.BlockSpec(shape, lambda i: (0,) * len(shape))

    columns = pl.BlockSpec((features, wide), lambda i: (0, i))
    return pl.pallas_call(
        kernel,
        grid=(steps,),
        in_specs=[
            pl.BlockSpec((per_step, row_count, width), lambda i: (i, 0, 0)),
            pl.BlockSpec((1, row_count, features), lambda i: (micro, 0, 0)),
            pl.BlockSpec((row_count, features), lambda i: (micro, 0)),
            fixed(1, features),
            columns,
            columns,
            columns,
        ]
        + [pl.BlockSpec(memory_space=pl.ANY)] * (before is not None),
        out_specs=pl.BlockSpec((1, row_count, features), lambda i: (micro, 0, 0)),
        out_shape=jax.ShapeDtypeStruct(patches.shape, jnp.bfloat16),
        input_output_aliases={7: 0} if before is not None else {},
        scratch_shapes=[
            pltpu.VMEM((row_count, features), jnp.float32),
            pltpu.VMEM((3, row_count, wide), jnp.bfloat16),
        ],
        compiler_params=_params(60),
        cost_estimate=_cost(cost),
        name="finish",
    )(received, patches, mixed_grad, gain, w_query, w_key, w_value, *([before] if before is not None else []))


def grad_heads_call(place, units, cuts, places, made, gain, bias, sums, w_query, w_key, w_value, shares):
    micro_count = len(made)
    blocks, tokens, width = made[0].shape
    slot = width // 3
    features = gain.shape[1]
    group = features // (blocks * shares)
    full = width + 128
    kept = blocks * (shares // 2) * group

    def kernel(place_ref, *refs):
        unit_refs, refs = refs[: len(units)], refs[len(units) :]
        made_refs, refs = refs[:micro_count], refs[micro_count:]
        gain_ref, bias_ref, sums_ref, wq_ref, wk_ref, wv_ref, send_ref, keep_ref, spread, ordered = refs
        product = jnp.zeros((features, width), jnp.float32)
        column_sum = jnp.zeros((1, width), jnp.float32)
        for cut, (first, last) in enumerate(cuts):
            at = 0
            for relative in places:
                for micro, made_ref in enumerate(made_refs):
                    low, high = max(first - micro * tokens, 0), min(last - micro * tokens, tokens)
                    if low < high:
                        ordered[at : at + high - low, :] = made_ref[place_ref[0] ^ relative, low:high]
                        at += high - low
            half = at // 2
            for side in range(2):
                rows = ordered[side * half : (side + 1) * half, :]
                product = product + contract_rows(unit_refs[2 * cut + side][...], rows)
                column_sum = column_sum + jnp.sum(rows.astype(jnp.float32), axis=0, keepdims=True)
        vectors = jnp.concatenate(
            [gain_ref[...], bias_ref[...], sums_ref[...], jnp.zeros((124, features), jnp.float32)], axis=0
        ).T
        total = vectors[:, 0:1] * product + vectors[:, 1:2] * column_sum
        weights = jnp.concatenate([wq_ref[...], wk_ref[...], wv_ref[...]], axis=1).astype(jnp.float32)
        gain_sum = jnp.sum(weights * product, axis=1, keepdims=True)
        bias_sum = jnp.sum(weights * column_sum, axis=1, keepdims=True)
        lanes = lax.broadcasted_iota(jnp.int32, (1, 128), 1)
        norms = jnp.where(
            lanes == 0, gain_sum, jnp.where(lanes == 1, bias_sum, jnp.where(lanes < 4, vectors, 0.0))
        )
        spread[:, :, :, 0:width] = total.reshape(blocks, shares, group, width)
        spread[:, :, :, width:] = norms.reshape(blocks, shares, group, 128)
        core = place_ref[1] % 2
        for which, out_ref in enumerate((send_ref, keep_ref)):
            for share in range(0, shares, 2):
                for block in range(blocks):
                    out_ref[share // 2, block] = spread[block, share + (core if which else 1 - core)].astype(out_ref.dtype)

    def fixed(*shape):
        return pl.BlockSpec(shape, lambda i, place: (0,) * len(shape))

    columns = pl.BlockSpec((features, slot), lambda i, place: (0, place[0]))
    out = (shares // 2, blocks, group, full)
    return pl.pallas_call(
        kernel,
        grid_spec=pltpu.PrefetchScalarGridSpec(
            num_scalar_prefetch=1,
            grid=(1,),
            in_specs=[fixed(*part.shape) for part in (*units, *made)]
            + [fixed(1, features), fixed(1, features), fixed(2, features), columns, columns, columns],
            out_specs=[fixed(*out), fixed(*out)],
            scratch_shapes=[
                pltpu.VMEM((blocks, shares, group, full), jnp.float32),
                pltpu.VMEM((blocks * max(last - first for first, last in cuts), width), jnp.bfloat16),
            ],
        ),
        out_shape=[jax.ShapeDtypeStruct(out, jnp.bfloat16), jax.ShapeDtypeStruct(out, jnp.float32)],
        compiler_params=_params(60),
        cost_estimate=_cost(20),
        name="grad_heads",
    )(place, *units, *made, gain, bias, sums, w_query, w_key, w_value)


def assemble_call(place, parts, down_keep, down_received, heads, down_steps, blocks, owned):
    shares = len(parts)
    rows, width = parts[0].shape
    part = width - blocks * owned
    slot = (heads.shape[2] - 128) // 3

    def kernel(place_ref, *refs):
        part_refs, (keep_ref, got_ref, heads_ref, up_ref, out_ref, down_ref, *refs) = refs[:shares], refs[shares:]
        weight_refs, norm_refs = refs[:3], refs[3:]
        for other, part_ref in enumerate(part_refs):
            share = place_ref[2] ^ other
            for at, block in enumerate(_ordered([_owner_stride(*step, shares) for step in down_steps])):
                to = pl.multiple_of((block + share % 2 + share // 2 * shares) * owned, 128)
                up_ref[:, pl.ds(to, owned)] = part_ref[:, at * owned : (at + 1) * owned].astype(jnp.float32)
            out_ref[:, pl.ds(pl.multiple_of(share * part, 128), part)] = part_ref[:, blocks * owned :].astype(jnp.float32)
        down_ref[...] = keep_ref[...] + got_ref[...].astype(jnp.float32)
        for at, ref in enumerate(weight_refs):
            for block in range(blocks):
                ref[:, block * slot : (block + 1) * slot] = heads_ref[
                    block, :, at * slot : (at + 1) * slot
                ].astype(jnp.float32)
        sums = jnp.zeros((rows, 128), jnp.float32)
        for block in range(blocks):
            sums = sums + heads_ref[block, :, 3 * slot :].astype(jnp.float32)
        turned = jnp.concatenate([sums, jnp.zeros((128 - rows, 128), jnp.float32)], axis=0).T
        for at, ref in enumerate(norm_refs):
            ref[...] = turned[at : at + 1, 0:rows]

    shapes = [(rows, blocks * shares * owned), (rows, shares * part), down_keep.shape]
    shapes += [(rows, blocks * slot)] * 3 + [(1, rows)] * 4
    return pl.pallas_call(
        kernel,
        grid_spec=pltpu.PrefetchScalarGridSpec(
            num_scalar_prefetch=1,
            grid=(1,),
            in_specs=[_fixed(*array.shape) for array in (*parts, down_keep, down_received, heads)],
            out_specs=[_fixed(*shape) for shape in shapes],
        ),
        out_shape=[jax.ShapeDtypeStruct(shape, jnp.float32) for shape in shapes],
        compiler_params=_params(16),
        cost_estimate=_cost(0),
        name="assemble",
    )(place, *parts, down_keep, down_received, heads)


def _bits(count):
    return [1 << place for place in range(count.bit_length() - 1)]


def _ordered(bits):
    places = [0]
    for bit in bits:
        places = [at + step for at in places for step in (0, bit)]
    return places


def _ordered_low(bits):
    places = [0]
    for bit in bits:
        places = places + [at + bit for at in places]
    return places


def _paired(values, axis, bit):
    count = lax.axis_size(axis)
    return lax.ppermute(values, axis, [(i, i ^ bit) for i in range(count)])


def _bit_of(axis, bit):
    return (lax.axis_index(axis) // bit) % 2


def _mesh_bit(place, step):
    axis, bit = step
    return place[("blk", "mb").index(axis)] // bit % 2


def _owner_stride(axis, bit, shares):
    return bit * shares if axis == "blk" else bit


def _share_places(shares):
    return [0, 1, shares, shares + 1]


def _place_at(bits, step):
    places = _ordered(bits)
    at = jnp.int32(places[0])
    for other in range(1, len(places)):
        at = jnp.where(step == other, places[other], at)
    return at


def grad_middle_call(place, boths, out_grads, lows, w_up, w_down, down_steps, up_steps):
    shares = len(boths)
    _, row_count, features = boths[0].shape
    all_rows = shares * row_count
    hidden = w_up.shape[1]
    blocks = 1 << len(up_steps)
    owned, each = hidden // (blocks * shares), features // (blocks * shares)
    down_places = [_owner_stride(*step, shares) for step in down_steps]
    up_places = [_owner_stride(*step, shares) for step in up_steps]
    share_places = _share_places(shares)
    part = lows[0].shape[1]
    half = blocks // 2
    pair = min(2, half)
    half_steps = half // pair

    def kernel(place_ref, *refs):
        groups, refs = [refs[at * shares : (at + 1) * shares] for at in range(3)], refs[3 * shares :]
        up_refs, down_refs, refs = refs[:pair], refs[pair : 2 * pair], refs[2 * pair :]
        down_send, down_keep, up_send, up_keep, norm_turned, grad_all, active_all, upper_all, up_all = refs
        step = pl.program_id(0)
        mine = _mesh_bit(place_ref, up_steps[0])

        def spread():
            for at, block in enumerate(_ordered(up_places[1:])):
                for share, other in enumerate(share_places):
                    rows = slice((at * shares + share) * each, (at * shares + share + 1) * each)
                    up_send[rows, :] = up_all[block + other + up_places[0] * (1 - mine)].astype(jnp.bfloat16)
                    up_keep[rows, :] = up_all[block + other + up_places[0] * mine]

        @pl.when(step == 0)
        def _():
            for at in range(shares):
                rows = slice(at * row_count, (at + 1) * row_count)
                norm_turned[:, rows] = groups[0][at][0].T
                grad_all[rows, :] = groups[1][at][...]

        @pl.when(step < 2 * half_steps)
        def _():
            up_columns = jnp.concatenate([ref[...] for ref in up_refs], axis=1)
            down_rows = jnp.concatenate([ref[...] for ref in down_refs], axis=0)
            for at in range(shares):
                rows = slice(at * row_count, (at + 1) * row_count)
                active_all[rows, :], upper_all[rows, :] = _hidden_parts(
                    groups[0][at][0], groups[1][at][...], up_columns, down_rows
                )
            down_made = contract_rows(active_all[...], grad_all[...])

            @pl.when(step < half_steps)
            def _():
                down_send[...] = down_made.astype(jnp.bfloat16)

            @pl.when(step >= half_steps)
            def _():
                down_keep[...] = down_made

            up_all[...] = matmul(norm_turned[...], upper_all[...]).reshape(blocks * shares, each, pair * owned)
            spread()

        @pl.when(step == 2 * half_steps)
        def _():
            made = jnp.zeros((features, part), jnp.float32)
            for both_ref, low_ref in zip(groups[0], groups[2]):
                made = made + contract_rows(both_ref[1], low_ref[...])
            up_all[...] = made.reshape(blocks * shares, each, part)
            spread()

    def first_bit(i, place):
        return (_mesh_bit(place, down_steps[0]) + 1 + jnp.minimum(i, 2 * half_steps - 1) // half_steps) % 2

    def unit_block(i, place, at):
        inner = _place_at(down_places[1:], jnp.minimum(i, 2 * half_steps - 1) % half_steps * pair + at)
        return inner + down_places[0] * first_bit(i, place) + place[0] % 2 * shares + place[1] % 2

    ups = [
        pl.BlockSpec((features, owned), lambda i, place, at=at: (0, unit_block(i, place, at))) for at in range(pair)
    ]
    downs = [
        pl.BlockSpec((owned, features), lambda i, place, at=at: (unit_block(i, place, at), 0)) for at in range(pair)
    ]
    def up_block(i, place):
        return (0, jnp.where(i == 2 * half_steps, i, first_bit(i, place) * half_steps + i % half_steps))

    up_out = pl.BlockSpec((features // 2, pair * owned), up_block)
    shapes = [(half * owned, features), (features // 2, blocks * owned + part)]
    return pl.pallas_call(
        kernel,
        grid_spec=pltpu.PrefetchScalarGridSpec(
            num_scalar_prefetch=1,
            grid=(2 * half_steps + 1,),
            in_specs=[_fixed(2, row_count, features)] * shares
            + [_fixed(row_count, features)] * shares
            + [_fixed(row_count, part)] * shares
            + ups
            + downs,
            out_specs=[
                pl.BlockSpec((pair * owned, features), lambda i, place: (jnp.minimum(i, half_steps - 1), 0)),
                pl.BlockSpec((pair * owned, features), lambda i, place: (jnp.clip(i - half_steps, 0, half_steps - 1), 0)),
                up_out,
                up_out,
            ],
            scratch_shapes=[
                pltpu.VMEM((features, all_rows), jnp.bfloat16),
                pltpu.VMEM((all_rows, features), jnp.bfloat16),
                pltpu.VMEM((all_rows, pair * owned), jnp.bfloat16),
                pltpu.VMEM((all_rows, pair * owned), jnp.bfloat16),
                pltpu.VMEM((blocks * shares, each, pair * owned), jnp.float32),
            ],
        ),
        out_shape=[jax.ShapeDtypeStruct(shape, dtype) for shape in shapes for dtype in (jnp.bfloat16, jnp.float32)],
        compiler_params=_params(52),
        cost_estimate=_cost(20),
        name="grad_middle",
    )(place, *boths, *out_grads, *lows, *([w_up] * pair), *([w_down] * pair))


def halve_call(place, keep, received, step, cost):
    count, rows, columns = keep.shape
    half = count // 2

    def kernel(place_ref, keep_theirs, keep_mine, got_theirs, got_mine, theirs_ref, mine_ref):
        theirs_ref[...] = (keep_theirs[...] + got_theirs[...].astype(jnp.float32)).astype(jnp.bfloat16)
        mine_ref[...] = keep_mine[...] + got_mine[...].astype(jnp.float32)

    def block(which):
        return pl.BlockSpec(
            (1, rows, columns), lambda i, place: (i + half * ((_mesh_bit(place, step) + which) % 2), 0, 0)
        )

    out = pl.BlockSpec((1, rows, columns), lambda i, place: (i, 0, 0))
    return pl.pallas_call(
        kernel,
        grid_spec=pltpu.PrefetchScalarGridSpec(
            num_scalar_prefetch=1,
            grid=(half,),
            in_specs=[block(1), block(0), block(1), block(0)],
            out_specs=[out, out],
        ),
        out_shape=[
            jax.ShapeDtypeStruct((half, rows, columns), jnp.bfloat16),
            jax.ShapeDtypeStruct((half, rows, columns), jnp.float32),
        ],
        compiler_params=_params(16),
        cost_estimate=_cost(cost),
        name="halve",
    )(place, keep, keep, received, received)


def heads_total_call(keep, received):
    def kernel(keep_ref, got_ref, out_ref):
        out_ref[...] = (keep_ref[...] + got_ref[...].astype(jnp.float32)).astype(jnp.bfloat16)

    return pl.pallas_call(
        kernel,
        out_shape=jax.ShapeDtypeStruct(keep.shape, jnp.bfloat16),
        compiler_params=_params(8),
        cost_estimate=_cost(20),
        name="heads_total",
    )(keep, received)


def close_call(place, keep, received, shares):
    rows, width = keep.shape
    each = rows // shares

    def kernel(place_ref, keep_ref, got_ref, *refs):
        out_refs, total = refs[:-1], refs[-1]
        total[...] = (keep_ref[...] + got_ref[...].astype(jnp.float32)).reshape(shares, each, width)
        for share, out_ref in enumerate(out_refs):
            out_ref[...] = total[place_ref[2] ^ share].astype(jnp.bfloat16)

    return pl.pallas_call(
        kernel,
        grid_spec=pltpu.PrefetchScalarGridSpec(
            num_scalar_prefetch=1,
            grid=(1,),
            in_specs=[_fixed(rows, width)] * 2,
            out_specs=[_fixed(each, width)] * shares,
            scratch_shapes=[pltpu.VMEM((shares, each, width), jnp.float32)],
        ),
        out_shape=[jax.ShapeDtypeStruct((each, width), jnp.bfloat16)] * shares,
        compiler_params=_params(8),
        cost_estimate=_cost(6),
        name="close",
    )(place, keep, received)


def fast_body(
    patches, seg_lengths, w_query, w_key, w_value, w_out, w_up, w_down,
    norm1_gain, norm1_bias, norm2_gain, norm2_bias, out_grad,
):
    micro_count, tokens, features = patches.shape
    hidden = w_up.shape[1]
    row_count = micro_count * tokens
    blocks, shares = lax.axis_size("blk"), lax.axis_size("mb")
    head_dim = features // H
    slot = features // blocks
    rows = patches.reshape(row_count, features)
    dout = out_grad.reshape(row_count, features)
    gain_one, bias_one, gain_two, bias_two = (
        value.reshape(1, features) for value in (norm1_gain, norm1_bias, norm2_gain, norm2_bias)
    )

    def swap(values):
        return lax.all_to_all(values, "blk", split_axis=0, concat_axis=0, tiled=True)

    def by_micro(values):
        return values.reshape(blocks, micro_count, tokens, values.shape[-1])

    at_blk, at_mb = lax.axis_index("blk"), lax.axis_index("mb")
    place = jnp.stack([at_blk, at_mb, at_mb % 2 + at_blk % 2 * 2]).astype(jnp.int32)
    blk_bits = _bits(blocks)
    down_steps = [("mb", 2), *(("blk", bit) for bit in blk_bits[1:])]
    up_steps = [down_steps[1], down_steps[0], *down_steps[2:]]
    each, owned, block_rows = features // (blocks * shares), hidden // (blocks * shares), features // blocks
    tie = lax.optimization_barrier

    def grown(values, bit):
        return jnp.concatenate([values, _paired(values, "blk", bit)], axis=0)

    def to_share(values, other):
        if other == 1:
            return _paired(values, "mb", 1)
        if other == 2:
            return _paired(values, "blk", 1)
        return lax.ppermute(values, ("blk", "mb"), [(i, i ^ (shares + 1)) for i in range(blocks * shares)])

    def shared(values):
        over = to_share(values, 2)
        return [values, to_share(values, 1), over, to_share(over, 1)]

    first_rows = max(16, tokens * 3 // 4 // 16 * 16)
    cuts = [(0, first_rows), (first_rows, row_count)]
    send, units_first, units_last = project_call(
        rows, gain_one, bias_one, w_query, w_key, w_value, blocks, cuts
    )
    received = by_micro(swap(send))
    dout_parts = [out_grad[micro] for micro in range(micro_count)]
    dout_over = [to_share(part, 2) for part in dout_parts]
    received, dout_over[0] = tie((received, dout_over[0]))
    units_first, received = tie((units_first, received))
    first_over = _paired(units_first, "blk", blk_bits[-1])
    own_attended, exact, logs = attend_call(received, seg_lengths, head_dim)
    attended, first_over, dout_over = tie((own_attended.reshape(blocks, row_count, slot), first_over, dout_over))
    units_first = jnp.concatenate([units_first, first_over], axis=0)
    dout_over = jnp.concatenate(dout_over, axis=0)
    attended, units_first, units_last, *douts = tie(
        (swap(attended), units_first, units_last, dout, to_share(dout, 1), dout_over, to_share(dout_over, 1))
    )
    for bit in blk_bits[-2:0:-1]:
        units_first = grown(units_first, bit)
    units_last = grown(units_last, blk_bits[-1])
    places = _ordered_low([*blk_bits[:0:-1], blk_bits[0]])

    mixed, both = mix_call(attended, rows, gain_two, bias_two, w_out)
    both_peer, both_over = to_share(both, 1), to_share(both, 2)
    layer_out, mixed_grad, back, sums_two, *lows = middle_call(
        place, both, mixed, dout, gain_two, w_out, w_up, w_down, blocks, shares
    )
    back, lows, units_first, units_last, both_peer, both_over = tie(
        (back, lows, units_first, units_last, both_peer, both_over)
    )
    boths = [both, both_peer, both_over, to_share(both_over, 1)]
    units_first_peer = _paired(units_first, "blk", blk_bits[0])
    for bit in blk_bits[-2:0:-1]:
        units_last = grown(units_last, bit)
    grads = by_micro(swap(back))
    lows = [lows[0]] + [to_share(lows[share], share) for share in range(1, shares)]
    down_theirs, down_keep, up_theirs, up_keep = grad_middle_call(
        place, boths, douts, lows, w_up, w_down, down_steps, up_steps
    )
    down_theirs, down_keep = (value.reshape(-1, owned, features) for value in (down_theirs, down_keep))
    up_theirs, up_keep = (value.reshape(-1, block_rows, value.shape[-1]) for value in (up_theirs, up_keep))
    down_received, up_received = _paired(down_theirs, *down_steps[0]), _paired(up_theirs, *up_steps[0])
    grads, down_keep, units_first_peer, units_last = tie((grads, down_keep, units_first_peer, units_last))
    units_last_peer = _paired(units_last, "blk", blk_bits[0])
    made = []
    for micro in range(micro_count):
        cost = 3 if micro == micro_count - 1 else 0
        made.append(attend_back_call(received, grads, exact, logs, seg_lengths, micro, cost, head_dim))
        grads, made[micro] = tie((grads, made[micro]))
    returned = [swap(made[0])]

    def then(done, *values):
        return tie((done, values))[1]

    returned += [swap(tie((values, returned[0]))[0]) for values in made[1:]]
    made = tie(made)
    up_theirs, up_keep = halve_call(place, *then(made[-1], up_keep, up_received), up_steps[1], 0)
    up_received = _paired(up_theirs, *up_steps[1])
    down_keep, down_received, units_last_peer = then(up_keep, down_keep, down_received, units_last_peer)
    down_theirs, down_keep = halve_call(place, down_keep, down_received, down_steps[1], 5)
    down_received = _paired(down_theirs, *down_steps[1])
    made = then(down_keep, *made)
    heads_send, heads_keep = grad_heads_call(
        place, (units_first, units_first_peer, units_last, units_last_peer), cuts, places,
        made, gain_one, bias_one, sums_two, w_query, w_key, w_value, shares,
    )
    pair = (shares // 2, -1, heads_keep.shape[-1])
    heads_received = _paired(heads_send, "mb", 1).reshape(pair)
    down_keep, down_received = then(heads_keep, down_keep, down_received)
    for step in down_steps[2:-1]:
        down_theirs, down_keep = halve_call(place, down_keep, down_received, step, 0)
        down_received = _paired(down_theirs, *step)
    down_theirs, down_keep = halve_call(place, down_keep, down_received, down_steps[-1], 0)
    up_keep, up_received = then(down_keep, up_keep, up_received)
    for step in up_steps[2:]:
        up_theirs, up_keep = halve_call(place, up_keep, up_received, step, 3)
        up_received = _paired(up_theirs, *step)
    heads_theirs, heads_keep = halve_call(
        place, *then(up_keep, heads_keep.reshape(pair), heads_received), ("mb", 2), 0
    )
    heads_theirs, down_theirs = tie((heads_theirs, down_theirs))
    heads_received = _paired(heads_theirs, "mb", 2)
    down_received = _paired(down_theirs, *down_steps[-1])
    finish = (patches, mixed_grad, gain_one, w_query, w_key, w_value)
    patches_grad = None
    for micro in range(micro_count - 1):
        first, heads_keep, heads_received = then(down_keep, returned[micro], heads_keep, heads_received)
        patches_grad = finish_call(first, *finish, micro, patches_grad, 0)
        heads_keep, heads_received = then(patches_grad, heads_keep, heads_received)
    returned[-1], heads_keep, heads_received = tie((returned[-1], heads_keep, heads_received))
    heads_total = heads_total_call(heads_keep[0], heads_received[0]).reshape(blocks, each, heads_keep.shape[-1])
    heads_parts = swap(heads_total)
    up_keep, up_received = then(heads_total, up_keep, up_received)
    parts = close_call(place, up_keep[0], up_received[0], shares)
    last = then(parts[0], returned[-1])[0]
    parts = [parts[0]] + [to_share(parts[share], share) for share in range(1, shares)]
    patches_grad = finish_call(last, *finish, micro_count - 1, patches_grad, 20)
    *parts, down_keep, down_received, heads_parts = then(
        patches_grad, *parts, down_keep[0], down_received[0], heads_parts
    )
    up_total, out_total, down_total, query_total, key_total, value_total, *sums = assemble_call(
        place, parts, down_keep, down_received, heads_parts, down_steps, blocks, owned
    )
    return (
        layer_out.reshape(patches.shape),
        patches_grad.reshape(patches.shape),
        query_total,
        key_total,
        value_total,
        out_total,
        up_total,
        down_total,
        *(value.reshape(each) for value in sums),
    )


def solution(mesh):
    in_specs = (
        P("mb", "blk", None),
        P("mb", None),
        P(),
        P(),
        P(),
        P(),
        P(),
        P(),
        P(),
        P(),
        P(),
        P(),
        P("mb", "blk", None),
    )
    out_specs = (
        P("mb", "blk", None),
        P("mb", "blk", None),
        P(("blk", "mb"), None),
        P(("blk", "mb"), None),
        P(("blk", "mb"), None),
        P(("blk", "mb"), None),
        P(("blk", "mb"), None),
        P(("blk", "mb"), None),
        P(("blk", "mb")),
        P(("blk", "mb")),
        P(("blk", "mb")),
        P(("blk", "mb")),
    )
    blocks, shares = mesh.shape["blk"], mesh.shape["mb"]
    paired = blocks >= 4 and blocks & (blocks - 1) == 0 and shares == 4
    chosen_body = fast_body if paired and H % blocks == 0 else body
    return jax.shard_map(chosen_body, mesh=mesh, in_specs=in_specs, out_specs=out_specs, check_vma=False)
```

```python
import math

import jax
import jax.numpy as jnp
from jax import lax
from jax.experimental import pallas as pl
from jax.experimental.pallas import tpu as pltpu
from jax.sharding import PartitionSpec as P

H = 16
CHUNK = 8


epsilon = 1e-05
masked_score = -1e30


def layer_norm(values, norm_gain, norm_bias):
    center = values - jnp.mean(values, axis=-1, keepdims=True)
    variance = jnp.mean(center * center, axis=-1, keepdims=True)
    return center * lax.rsqrt(variance + epsilon) * norm_gain + norm_bias


def gelu_exact(values):
    return jax.nn.gelu(values, approximate=False)


def matmul(left_side, right_side):
    return jnp.dot(left_side, right_side, preferred_element_type=jnp.float32)


def contract_rows(left_side, right_side):
    return lax.dot_general(
        left_side, right_side, (((0,), (0,)), ((), ())), preferred_element_type=jnp.float32
    )


def contract_cols(left_side, right_side):
    return lax.dot_general(
        left_side, right_side, (((1,), (1,)), ((), ())), preferred_element_type=jnp.float32
    )


def segment_ids(lengths, positions):
    doc_ends = jnp.cumsum(lengths, axis=-1)
    return jnp.sum((positions[None, :, None] >= doc_ends[:, None, :]).astype(jnp.int32), axis=-1)


def masked_scores(query_piece, keys_all, query_docs, key_docs, score_scale):
    scores = contract_cols(query_piece, keys_all) * score_scale
    return jnp.where(query_docs[:, None] == key_docs[None, :], scores, masked_score)


def soft_rows(scores):
    row_max = jnp.max(scores, axis=-1, keepdims=True)
    exponent = jnp.exp(scores - row_max)
    return exponent / jnp.sum(exponent, axis=-1, keepdims=True)


def body(
    patches,
    seg_lengths,
    w_query,
    w_key,
    w_value,
    w_out,
    w_up,
    w_down,
    norm1_gain,
    norm1_bias,
    norm2_gain,
    norm2_bias,
    out_grad,
):
    micro_count, tokens, features = patches.shape
    row_count = micro_count * tokens
    blocks = lax.axis_size("blk")
    block_index = lax.axis_index("blk")
    head_count = H
    head_dim = features // head_count
    repeat = max(1, blocks // head_count)
    per_slot = max(1, head_count // blocks)
    groups = head_count // per_slot
    rows_part = tokens // repeat
    query_rows = blocks * rows_part
    seq_length = blocks * tokens
    item_count = micro_count * per_slot
    block_rows = min(512, query_rows)
    block_count = query_rows // block_rows
    slot_width = micro_count * per_slot * head_dim
    score_scale = 1.0 / math.sqrt(head_dim)
    doc_count = seg_lengths.shape[1]

    def query_layout(values):
        shaped = values.reshape(micro_count, repeat, rows_part, groups, per_slot * head_dim)
        return shaped.transpose(3, 1, 2, 0, 4).reshape(blocks, rows_part, slot_width)

    def key_layout(values):
        shaped = values.reshape(micro_count, tokens, groups, per_slot * head_dim).transpose(
            2, 1, 0, 3
        )
        shaped = jnp.broadcast_to(
            shaped[:, None], (groups, repeat, tokens, micro_count, per_slot * head_dim)
        )
        return shaped.reshape(blocks, tokens, slot_width)

    def token_layout(values):
        shaped = values.reshape(groups, repeat, rows_part, micro_count, per_slot * head_dim)
        return shaped.transpose(3, 1, 2, 0, 4).reshape(row_count, features)

    def key_sum(values):
        shaped = values.reshape(groups, repeat, tokens, micro_count, per_slot * head_dim).sum(
            axis=1
        )
        return shaped.transpose(2, 1, 0, 3).reshape(row_count, features)

    def to_items(received):
        row_total = received.shape[1]
        shaped = received.reshape(row_total, micro_count, per_slot, head_dim).transpose(1, 2, 0, 3)
        return shaped.reshape(item_count, row_total, head_dim)

    def from_items(values):
        row_total = values.shape[1]
        shaped = values.reshape(micro_count, per_slot, row_total, head_dim).transpose(2, 0, 1, 3)
        return shaped.reshape(1, row_total, slot_width)

    row_ids = jnp.arange(query_rows)
    query_pos = (
        row_ids // rows_part * tokens + block_index % repeat * rows_part + row_ids % rows_part
    )
    query_docs = jnp.repeat(segment_ids(seg_lengths, query_pos), per_slot, axis=0)
    key_docs = jnp.repeat(segment_ids(seg_lengths, jnp.arange(seq_length)), per_slot, axis=0)
    query_valid = (query_docs < doc_count).astype(jnp.float32)
    local_pos = block_index * tokens + jnp.arange(tokens)
    row_valid = (
        (segment_ids(seg_lengths, local_pos) < doc_count).astype(jnp.float32).reshape(row_count, 1)
    )

    def forward_item(operands):
        queries_item, keys_item, values_item, docs_item, key_docs_item = operands

        def forward_one_block(block_operands):
            query_piece, docs_piece = block_operands
            weights_soft = soft_rows(
                masked_scores(query_piece, keys_item, docs_piece, key_docs_item, score_scale)
            )
            return matmul(weights_soft.astype(jnp.bfloat16), values_item)

        outputs = lax.map(
            forward_one_block,
            (
                queries_item.reshape(block_count, block_rows, head_dim),
                docs_item.reshape(block_count, block_rows),
            ),
        )
        return outputs.reshape(query_rows, head_dim)

    def backward_item(operands):
        queries_item, keys_item, values_item, grads_item, docs_item, key_docs_item = operands

        def backward_one_block(totals, block_operands):
            key_total, value_total = totals
            query_piece, grad_piece, docs_piece = block_operands
            weights_soft = soft_rows(
                masked_scores(query_piece, keys_item, docs_piece, key_docs_item, score_scale)
            )
            weights_low = weights_soft.astype(jnp.bfloat16)
            weight_grads = contract_cols(grad_piece, values_item)
            row_inner = jnp.sum(weights_soft * weight_grads, axis=-1, keepdims=True)
            score_grads = (weights_soft * (weight_grads - row_inner)).astype(jnp.bfloat16)
            query_grad = matmul(score_grads, keys_item) * score_scale
            key_total = key_total + contract_rows(score_grads, query_piece) * score_scale
            value_total = value_total + contract_rows(weights_low, grad_piece)
            return ((key_total, value_total), query_grad)

        zero_block = jnp.zeros((seq_length, head_dim), jnp.float32)
        totals, query_grads = lax.scan(
            backward_one_block,
            (zero_block, zero_block),
            (
                queries_item.reshape(block_count, block_rows, head_dim),
                grads_item.reshape(block_count, block_rows, head_dim),
                docs_item.reshape(block_count, block_rows),
            ),
        )
        return (query_grads.reshape(query_rows, head_dim), totals[0], totals[1])

    inputs = patches.astype(jnp.float32).reshape(row_count, features)
    norm_one_full, norm_one_pull = jax.vjp(layer_norm, inputs, norm1_gain, norm1_bias)
    norm_one = norm_one_full.astype(jnp.bfloat16)
    queries = matmul(norm_one, w_query).astype(jnp.bfloat16)
    keys_proj = matmul(norm_one, w_key).astype(jnp.bfloat16)
    values_proj = matmul(norm_one, w_value).astype(jnp.bfloat16)
    query_send = query_layout(queries)
    key_send = key_layout(keys_proj)
    value_send = key_layout(values_proj)
    query_heads, key_heads, value_heads = (
        lax.all_to_all(query_send, "blk", split_axis=0, concat_axis=1, tiled=True),
        lax.all_to_all(key_send, "blk", split_axis=0, concat_axis=1, tiled=True),
        lax.all_to_all(value_send, "blk", split_axis=0, concat_axis=1, tiled=True),
    )
    query_items = to_items(query_heads)
    key_items = to_items(key_heads)
    value_items = to_items(value_heads)
    attended_items = lax.map(
        forward_item, (query_items, key_items, value_items, query_docs, key_docs)
    )
    attended_items = (attended_items * query_valid[:, :, None]).astype(jnp.bfloat16)
    attended = token_layout(
        lax.all_to_all(from_items(attended_items), "blk", split_axis=1, concat_axis=0, tiled=True)
    )
    mixed_rows = inputs + matmul(attended, w_out)
    norm_two_full, norm_two_pull = jax.vjp(layer_norm, mixed_rows, norm2_gain, norm2_bias)
    norm_two = norm_two_full.astype(jnp.bfloat16)
    upper_proj = matmul(norm_two, w_up)
    active_full, gelu_pull = jax.vjp(gelu_exact, upper_proj)
    active = active_full.astype(jnp.bfloat16)
    result = mixed_rows + matmul(active, w_down)
    layer_out = result.astype(jnp.bfloat16).reshape(micro_count, tokens, features)
    dout_low = out_grad.reshape(row_count, features)
    down_grad = contract_rows(active, dout_low)
    active_grad = contract_cols(dout_low, w_down)
    upper_grad = gelu_pull(active_grad)[0].astype(jnp.bfloat16)
    up_grad = contract_rows(norm_two, upper_grad)
    norm_two_grad = contract_cols(upper_grad, w_up)
    mixed_part, gain_two_grad, bias_two_grad = norm_two_pull(norm_two_grad)
    mixed_grad = dout_low.astype(jnp.float32) + mixed_part
    mixed_low = mixed_grad.astype(jnp.bfloat16)
    out_proj_grad = contract_rows(attended, mixed_low)
    attended_grad = (contract_cols(mixed_low, w_out) * row_valid).astype(jnp.bfloat16)
    grad_send = query_layout(attended_grad)
    query_again, key_again, value_again, grad_heads = (
        lax.all_to_all(query_send, "blk", split_axis=0, concat_axis=1, tiled=True),
        lax.all_to_all(key_send, "blk", split_axis=0, concat_axis=1, tiled=True),
        lax.all_to_all(value_send, "blk", split_axis=0, concat_axis=1, tiled=True),
        lax.all_to_all(grad_send, "blk", split_axis=0, concat_axis=1, tiled=True),
    )
    back_queries = to_items(query_again)
    back_keys = to_items(key_again)
    back_values = to_items(value_again)
    grad_items = to_items(grad_heads)
    query_grad_items, key_grad_items, value_grad_items = lax.map(
        backward_item, (back_queries, back_keys, back_values, grad_items, query_docs, key_docs)
    )
    query_back, key_back, value_back = (
        lax.all_to_all(
            from_items(query_grad_items).astype(jnp.bfloat16),
            "blk",
            split_axis=1,
            concat_axis=0,
            tiled=True,
        ).astype(jnp.float32),
        lax.all_to_all(
            from_items(key_grad_items).astype(jnp.bfloat16),
            "blk",
            split_axis=1,
            concat_axis=0,
            tiled=True,
        ).astype(jnp.float32),
        lax.all_to_all(
            from_items(value_grad_items).astype(jnp.bfloat16),
            "blk",
            split_axis=1,
            concat_axis=0,
            tiled=True,
        ).astype(jnp.float32),
    )
    query_grad = token_layout(query_back).astype(jnp.bfloat16)
    key_grad = key_sum(key_back).astype(jnp.bfloat16)
    value_grad = key_sum(value_back).astype(jnp.bfloat16)
    query_proj_grad = contract_rows(norm_one, query_grad)
    key_proj_grad = contract_rows(norm_one, key_grad)
    value_proj_grad = contract_rows(norm_one, value_grad)
    norm_one_grad = (
        contract_cols(query_grad, w_query)
        + contract_cols(key_grad, w_key)
        + contract_cols(value_grad, w_value)
    )
    input_part, gain_one_grad, bias_one_grad = norm_one_pull(norm_one_grad)
    patches_grad = (
        (mixed_grad + input_part).astype(jnp.bfloat16).reshape(micro_count, tokens, features)
    )
    gradients = (
        query_proj_grad,
        key_proj_grad,
        value_proj_grad,
        out_proj_grad,
        up_grad,
        down_grad,
        gain_one_grad,
        bias_one_grad,
        gain_two_grad,
        bias_two_grad,
    )
    summed = (
        lax.psum_scatter(gradients[0], ("blk", "mb"), scatter_dimension=0, tiled=True),
        lax.psum_scatter(gradients[1], ("blk", "mb"), scatter_dimension=0, tiled=True),
        lax.psum_scatter(gradients[2], ("blk", "mb"), scatter_dimension=0, tiled=True),
        lax.psum_scatter(gradients[3], ("blk", "mb"), scatter_dimension=0, tiled=True),
        lax.psum_scatter(gradients[4], ("blk", "mb"), scatter_dimension=0, tiled=True),
        lax.psum_scatter(gradients[5], ("blk", "mb"), scatter_dimension=0, tiled=True),
        lax.psum_scatter(gradients[6], ("blk", "mb"), scatter_dimension=0, tiled=True),
        lax.psum_scatter(gradients[7], ("blk", "mb"), scatter_dimension=0, tiled=True),
        lax.psum_scatter(gradients[8], ("blk", "mb"), scatter_dimension=0, tiled=True),
        lax.psum_scatter(gradients[9], ("blk", "mb"), scatter_dimension=0, tiled=True),
    )
    return (
        layer_out,
        patches_grad,
        summed[0],
        summed[1],
        summed[2],
        summed[3],
        summed[4],
        summed[5],
        summed[6],
        summed[7],
        summed[8],
        summed[9],
    )


def _normalize(values):
    center = values - jnp.mean(values, axis=-1, keepdims=True)
    variance = jnp.mean(center * center, axis=-1, keepdims=True)
    inverse = lax.rsqrt(variance + epsilon)
    return center * inverse, inverse


def _normalize_back(grads, gain, unit, inverse):
    scaled = grads * gain
    mean_scaled = jnp.mean(scaled, axis=-1, keepdims=True)
    mean_product = jnp.mean(scaled * unit, axis=-1, keepdims=True)
    return (scaled - mean_scaled - unit * mean_product) * inverse


def _doc_ids(lengths_ref, micro, doc_count, positions):
    end = jnp.int32(0)
    ids = jnp.zeros_like(positions)
    for doc in range(doc_count):
        end = end + lengths_ref[micro, doc]
        ids = ids + (positions >= end).astype(jnp.int32)
    return ids


def _params(mib):
    return pltpu.CompilerParams(vmem_limit_bytes=mib << 20)


def _cost(microseconds):
    return pl.CostEstimate(flops=int(microseconds * 1e9) + 1, bytes_accessed=1, transcendentals=0)


def project_call(rows, gain, bias, w_query, w_key, w_value, blocks, cuts):
    row_count, features = rows.shape
    slot = features // blocks
    per_step = max(1, min(blocks, 512 // slot))
    wide = slot * per_step

    def kernel(rows_ref, gain_ref, bias_ref, wq_ref, wk_ref, wv_ref, send_ref, *refs):
        unit_refs, norm_ref = refs[:-1], refs[-1]


        @pl.when(pl.program_id(0) == 0)
        def _():
            unit, _unused = _normalize(rows_ref[...].astype(jnp.float32))
            for (first, last), unit_ref in zip(cuts, unit_refs):
                unit_ref[...] = unit[first:last].astype(jnp.bfloat16)
            norm_ref[...] = (unit * gain_ref[...] + bias_ref[...]).astype(jnp.bfloat16)

        for part, weight_ref in enumerate((wq_ref, wk_ref, wv_ref)):
            made = matmul(norm_ref[...], weight_ref[...]).astype(jnp.bfloat16)
            for piece in range(per_step):
                send_ref[piece, :, part * slot : (part + 1) * slot] = made[
                    :, piece * slot : (piece + 1) * slot
                ]

    whole = pl.BlockSpec((row_count, features), lambda i: (0, 0))
    vector = pl.BlockSpec((1, features), lambda i: (0, 0))
    columns = pl.BlockSpec((features, wide), lambda i: (0, i))
    return pl.pallas_call(
        kernel,
        grid=(blocks // per_step,),
        in_specs=[whole, vector, vector, columns, columns, columns],
        out_specs=[pl.BlockSpec((per_step, row_count, 3 * slot), lambda i: (i, 0, 0))]
        + [pl.BlockSpec((last - first, features), lambda i: (0, 0)) for first, last in cuts],
        out_shape=[jax.ShapeDtypeStruct((blocks, row_count, 3 * slot), jnp.bfloat16)]
        + [jax.ShapeDtypeStruct((last - first, features), jnp.bfloat16) for first, last in cuts],
        scratch_shapes=[pltpu.VMEM((row_count, features), jnp.bfloat16)],
        compiler_params=_params(60),
        cost_estimate=_cost(6),
        name="project",
    )(rows, gain, bias, w_query, w_key, w_value)


def _head_masks(slot, head_dim, dtype):
    lanes = lax.broadcasted_iota(jnp.int32, (1, slot), 1)
    return [(lanes // head_dim == head).astype(dtype) for head in range(slot // head_dim)]


def _key_range(lengths_ref, micro, doc_count, first_row, last_row, seq):
    low, high, end = jnp.int32(0), jnp.int32(seq), jnp.int32(0)
    for doc in range(doc_count):
        end = end + lengths_ref[micro, doc]
        low = jnp.where(end <= first_row, jnp.maximum(low, end), low)
        high = jnp.where(end >= last_row, jnp.minimum(high, end), high)
    return low, high


def _by_key_range(lengths_ref, micro, doc_count, step, rows, blocks, tokens, compute):
    low, high = _key_range(lengths_ref, micro, doc_count, step * rows, (step + 1) * rows, blocks * tokens)
    half = blocks // 2
    in_low, in_high = high <= half * tokens, low >= half * tokens

    @pl.when(in_low | in_high)
    def _():
        compute(jnp.where(in_low, 0, half), half)

    @pl.when(jnp.logical_not(in_low | in_high))
    def _():
        compute(0, blocks)


def attend_call(received, lengths, head_dim):
    blocks, micro_count, tokens, width = received.shape
    slot = width // 3
    doc_count = lengths.shape[1]
    step_blocks = max(1, min(blocks // 2, 512 // tokens))
    rows = step_blocks * tokens
    scale = 1.0 / math.sqrt(head_dim)

    def kernel(lengths_ref, data_ref, out_ref, exact_ref, log_ref):
        micro = pl.program_id(0)
        step = pl.program_id(1)
        row_docs = _doc_ids(
            lengths_ref, micro, doc_count, lax.broadcasted_iota(jnp.int32, (rows, 1), 0) + step * rows
        )
        queries = data_ref[pl.ds(step * step_blocks, step_blocks), 0, :, 0:slot].reshape(rows, slot) * scale

        def compute(first, count):
            seq = count * tokens
            key_docs = _doc_ids(
                lengths_ref, micro, doc_count, lax.broadcasted_iota(jnp.int32, (1, seq), 1) + first * tokens
            )
            same = row_docs == key_docs
            keys = data_ref[pl.ds(first, count), 0, :, slot : 2 * slot].reshape(seq, slot)
            values = data_ref[pl.ds(first, count), 0, :, 2 * slot : 3 * slot].reshape(seq, slot)
            total = jnp.zeros((rows, slot), jnp.float32)
            logs = jnp.zeros((rows, 128), jnp.float32)
            lanes = lax.broadcasted_iota(jnp.int32, (1, 128), 1)
            for head, (mask, mask_wide) in enumerate(
                zip(_head_masks(slot, head_dim, jnp.bfloat16), _head_masks(slot, head_dim, jnp.float32))
            ):
                scores = jnp.where(same, contract_cols(queries * mask, keys), masked_score)
                most = jnp.max(scores, axis=-1, keepdims=True)
                exponent = jnp.exp(scores - most)
                exponent_sum = jnp.sum(exponent, axis=-1, keepdims=True)
                share = 1.0 / exponent_sum
                logs = jnp.where(lanes == head, most + jnp.log(exponent_sum), logs)
                total = total + matmul(exponent.astype(jnp.bfloat16), values) * (share * mask_wide)
            total = jnp.where(row_docs < doc_count, total, 0.0)
            out_ref[...] = total.astype(jnp.bfloat16).reshape(step_blocks, 1, tokens, slot)
            exact_ref[...] = total.reshape(step_blocks, 1, tokens, slot)
            log_ref[0] = logs.T[0:8, :]

        _by_key_range(lengths_ref, micro, doc_count, step, rows, blocks, tokens, compute)

    return pl.pallas_call(
        kernel,
        grid=(micro_count, blocks // step_blocks),
        in_specs=[
            pl.BlockSpec(memory_space=pltpu.SMEM),
            pl.BlockSpec((blocks, 1, tokens, width), lambda m, s: (0, m, 0, 0)),
        ],
        out_specs=[
            pl.BlockSpec((step_blocks, 1, tokens, slot), lambda m, s: (s, m, 0, 0)),
            pl.BlockSpec((step_blocks, 1, tokens, slot), lambda m, s: (s, m, 0, 0)),
            pl.BlockSpec((1, 8, rows), lambda m, s: (m, 0, s)),
        ],
        out_shape=[
            jax.ShapeDtypeStruct((blocks, micro_count, tokens, slot), jnp.bfloat16),
            jax.ShapeDtypeStruct((blocks, micro_count, tokens, slot), jnp.float32),
            jax.ShapeDtypeStruct((micro_count, 8, blocks * tokens), jnp.float32),
        ],
        compiler_params=_params(36),
        cost_estimate=_cost(11),
        name="attend",
    )(lengths, received)


def attend_back_call(received, grads, attended, logs, lengths, micro, cost, head_dim):
    blocks, _, tokens, width = received.shape
    slot = width // 3
    doc_count = lengths.shape[1]
    step_blocks = max(1, min(blocks // 2, 512 // tokens))
    rows = step_blocks * tokens
    steps = blocks // step_blocks
    scale = 1.0 / math.sqrt(head_dim)

    def kernel(lengths_ref, data_ref, grads_ref, att_ref, log_ref, out_ref, key_total, value_total, turned):
        step = pl.program_id(0)

        @pl.when(step == 0)
        def _():
            key_total[...] = jnp.zeros_like(key_total)
            value_total[...] = jnp.zeros_like(value_total)
            for block in range(blocks):
                turned[block] = data_ref[block, 0, :, slot : 2 * slot].T

        row_docs = _doc_ids(
            lengths_ref, micro, doc_count, lax.broadcasted_iota(jnp.int32, (1, rows), 1) + step * rows
        )
        column_docs = _doc_ids(
            lengths_ref, micro, doc_count, lax.broadcasted_iota(jnp.int32, (rows, 1), 0) + step * rows
        )
        queries = data_ref[pl.ds(step * step_blocks, step_blocks), 0, :, 0:slot].reshape(rows, slot) * scale
        out_grads = grads_ref[...].reshape(rows, slot)
        out_grads = out_grads * (column_docs < doc_count).astype(jnp.float32).astype(jnp.bfloat16)

        inner = (out_grads.astype(jnp.float32) * att_ref[...].reshape(rows, slot)).T

        def compute(first, count):
            chunk = min(CHUNK, count)
            query_parts = [jnp.zeros((head_dim, rows), jnp.float32) for _ in range(slot // head_dim)]
            masks = _head_masks(slot, head_dim, jnp.bfloat16)
            for at in range(0, count, chunk):
                seq = chunk * tokens
                key_docs = _doc_ids(
                    lengths_ref,
                    micro,
                    doc_count,
                    lax.broadcasted_iota(jnp.int32, (seq, 1), 0) + (first + at) * tokens,
                )
                same = row_docs == key_docs
                keys = data_ref[pl.ds(first + at, chunk), 0, :, slot : 2 * slot].reshape(seq, slot)
                values = data_ref[pl.ds(first + at, chunk), 0, :, 2 * slot : 3 * slot].reshape(seq, slot)
                keys_turned = jnp.concatenate([turned[first + at + other] for other in range(chunk)], axis=1)
                key_made = jnp.zeros((seq, slot), jnp.float32)
                value_made = jnp.zeros((seq, slot), jnp.float32)
                for head, mask in enumerate(masks):
                    lanes = slice(head * head_dim, (head + 1) * head_dim)
                    queries_head, grads_head = queries * mask, out_grads * mask
                    scores = jnp.where(same, contract_cols(keys, queries_head), masked_score)
                    probs = jnp.exp(scores - log_ref[0, head : head + 1, :])
                    prob_grads = contract_cols(values, grads_head)
                    head_inner = jnp.sum(inner[lanes], axis=0, keepdims=True)
                    score_grads = (probs * (prob_grads - head_inner)).astype(jnp.bfloat16)
                    value_made = value_made + matmul(probs.astype(jnp.bfloat16), grads_head)
                    key_made = key_made + matmul(score_grads, queries_head)
                    query_parts[head] = query_parts[head] + matmul(keys_turned[lanes], score_grads)
                to = pl.ds(pl.multiple_of((first + at) * tokens, tokens), seq)
                key_total[to, :] += key_made
                value_total[to, :] += value_made
            query_grads = (jnp.concatenate(query_parts, axis=0).T * scale).astype(jnp.bfloat16).reshape(step_blocks, tokens, slot)
            out_ref[pl.ds(step * step_blocks, step_blocks), :, 0:slot] = query_grads

        _by_key_range(lengths_ref, micro, doc_count, step, rows, blocks, tokens, compute)

        @pl.when(step == steps - 1)
        def _():
            out_ref[:, :, slot : 2 * slot] = key_total[...].astype(jnp.bfloat16).reshape(blocks, tokens, slot)
            out_ref[:, :, 2 * slot :] = value_total[...].astype(jnp.bfloat16).reshape(blocks, tokens, slot)

    return pl.pallas_call(
        kernel,
        grid=(steps,),
        in_specs=[
            pl.BlockSpec(memory_space=pltpu.SMEM),
            pl.BlockSpec((blocks, 1, tokens, width), lambda s: (0, micro, 0, 0)),
            pl.BlockSpec((step_blocks, 1, tokens, slot), lambda s: (s, micro, 0, 0)),
            pl.BlockSpec((step_blocks, 1, tokens, slot), lambda s: (s, micro, 0, 0)),
            pl.BlockSpec((1, 8, rows), lambda s: (micro, 0, s)),
        ],
        out_specs=_fixed(blocks, tokens, width),
        out_shape=jax.ShapeDtypeStruct((blocks, tokens, width), jnp.bfloat16),
        scratch_shapes=[pltpu.VMEM((blocks * tokens, slot), jnp.float32)] * 2
        + [pltpu.VMEM((blocks, slot, tokens), jnp.bfloat16)],
        compiler_params=_params(60),
        cost_estimate=_cost(cost),
        name="attend_back",
    )(lengths, received, grads, attended, logs)


def _fixed(*shape):
    return pl.BlockSpec(shape, lambda *_unused: (0,) * len(shape))


def mix_call(attended, rows, gain, bias, w_out):
    blocks, row_count, slot = attended.shape
    features = rows.shape[1]

    def kernel(att_ref, rows_ref, gain_ref, bias_ref, wo_ref, mixed_ref, both_ref):
        for block in range(blocks):
            both_ref[1, :, block * slot : (block + 1) * slot] = att_ref[block]
        value = rows_ref[...].astype(jnp.float32) + matmul(both_ref[1], wo_ref[...])
        mixed_ref[...] = value
        unit, _unused = _normalize(value)
        both_ref[0] = (unit * gain_ref[...] + bias_ref[...]).astype(jnp.bfloat16)

    rows_spec, vector = _fixed(row_count, features), _fixed(1, features)
    return pl.pallas_call(
        kernel,
        grid=(1,),
        in_specs=[_fixed(blocks, row_count, slot), rows_spec, vector, vector, _fixed(features, features)],
        out_specs=[rows_spec, _fixed(2, row_count, features)],
        out_shape=[
            jax.ShapeDtypeStruct((row_count, features), jnp.float32),
            jax.ShapeDtypeStruct((2, row_count, features), jnp.bfloat16),
        ],
        compiler_params=_params(24),
        cost_estimate=_cost(4),
        name="mix",
    )(attended, rows, gain, bias, w_out)


def _hidden_parts(norm, out_grad, up_columns, down_rows):
    upper = matmul(norm, up_columns)
    active_grad = contract_cols(out_grad, down_rows)
    half = (1.0 + lax.erf(upper * (1.0 / math.sqrt(2.0)))) * 0.5
    slope = half + upper * jnp.exp(upper * upper * -0.5) * (1.0 / math.sqrt(2.0 * math.pi))
    return (upper * half).astype(jnp.bfloat16), (active_grad * slope).astype(jnp.bfloat16)


def middle_call(place, both, mixed, out_grad, gain, w_out, w_up, w_down, blocks, shares):
    row_count, features = mixed.shape
    hidden = w_up.shape[1]
    wide = min(1024, hidden)
    sub = min(512, wide)
    steps = hidden // wide
    slot, part = features // blocks, features // shares

    def kernel(place_ref, norm_ref, mixed_ref, grad_ref, gain_ref, wo_ref, wu_ref, wd_ref, *refs):
        out_ref, mixed_grad_ref, back_ref, sums_ref = refs[:4]
        low_refs, (total, grad_total, active_all, upper_all, low_all) = refs[4 : 4 + shares], refs[4 + shares :]
        step = pl.program_id(0)

        @pl.when(step == 0)
        def _():
            total[...] = mixed_ref[...]
            grad_total[...] = jnp.zeros_like(grad_total)

        for chunk in range(0, wide, sub):
            active, upper_grad = _hidden_parts(
                norm_ref[0], grad_ref[...], wu_ref[:, chunk : chunk + sub], wd_ref[chunk : chunk + sub, :]
            )
            active_all[:, chunk : chunk + sub] = active
            upper_all[:, chunk : chunk + sub] = upper_grad
        total[...] += matmul(active_all[...], wd_ref[...])
        grad_total[...] += contract_cols(upper_all[...], wu_ref[...])

        @pl.when(step == steps - 1)
        def _():
            out_ref[...] = total[...].astype(jnp.bfloat16)
            unit, inverse = _normalize(mixed_ref[...])
            grads = grad_total[...]
            sums_ref[0:1, :] = jnp.sum(grads * unit, axis=0, keepdims=True)
            sums_ref[1:2, :] = jnp.sum(grads, axis=0, keepdims=True)
            mixed_grad = grad_ref[...].astype(jnp.float32) + _normalize_back(grads, gain_ref[...], unit, inverse)
            mixed_grad_ref[...] = mixed_grad
            low = mixed_grad.astype(jnp.bfloat16)
            low_all[...] = low
            for share, low_ref in enumerate(low_refs):
                low_ref[...] = low_all[:, pl.ds(pl.multiple_of((place_ref[2] ^ share) * part, 128), part)]
            back = contract_cols(low, wo_ref[...]).astype(jnp.bfloat16)
            for block in range(blocks):
                back_ref[block] = back[:, block * slot : (block + 1) * slot]

    rows_spec = _fixed(row_count, features)
    return pl.pallas_call(
        kernel,
        grid_spec=pltpu.PrefetchScalarGridSpec(
            num_scalar_prefetch=1,
            grid=(steps,),
            in_specs=[
                _fixed(1, row_count, features),
                rows_spec,
                rows_spec,
                _fixed(1, features),
                _fixed(features, features),
                pl.BlockSpec((features, wide), lambda i, place: (0, i)),
                pl.BlockSpec((wide, features), lambda i, place: (i, 0)),
            ],
            out_specs=[rows_spec, rows_spec, _fixed(blocks, row_count, slot), _fixed(2, features)]
            + [_fixed(row_count, part)] * shares,
            scratch_shapes=[
                pltpu.VMEM((row_count, features), jnp.float32),
                pltpu.VMEM((row_count, features), jnp.float32),
                pltpu.VMEM((row_count, wide), jnp.bfloat16),
                pltpu.VMEM((row_count, wide), jnp.bfloat16),
                pltpu.VMEM((row_count, features), jnp.bfloat16),
            ],
        ),
        out_shape=[
            jax.ShapeDtypeStruct((row_count, features), jnp.bfloat16),
            jax.ShapeDtypeStruct((row_count, features), jnp.float32),
            jax.ShapeDtypeStruct((blocks, row_count, slot), jnp.bfloat16),
            jax.ShapeDtypeStruct((2, features), jnp.float32),
        ]
        + [jax.ShapeDtypeStruct((row_count, part), jnp.bfloat16)] * shares,
        compiler_params=_params(44),
        cost_estimate=_cost(20),
        name="middle",
    )(place, both, mixed, out_grad, gain, w_out, w_up, w_down)


def finish_call(received, patches, mixed_grad, gain, w_query, w_key, w_value, micro, before, cost):
    blocks, row_count, width = received.shape
    slot = width // 3
    features = patches.shape[2]
    per_step = max(1, min(blocks, 512 // slot))
    wide = slot * per_step
    steps = blocks // per_step

    def kernel(data_ref, rows_ref, mixed_ref, gain_ref, wq_ref, wk_ref, wv_ref, *refs):
        out_ref, total, side = refs[-3:]
        step = pl.program_id(0)

        @pl.when(step == 0)
        def _():
            total[...] = jnp.zeros_like(total)

        for part, weight_ref in enumerate((wq_ref, wk_ref, wv_ref)):
            for piece in range(per_step):
                side[part, :, piece * slot : (piece + 1) * slot] = data_ref[
                    piece, :, part * slot : (part + 1) * slot
                ]
            total[...] += contract_cols(side[part], weight_ref[...])

        @pl.when(step == steps - 1)
        def _():
            unit, inverse = _normalize(rows_ref[0].astype(jnp.float32))
            out_ref[0] = (
                mixed_ref[...] + _normalize_back(total[...], gain_ref[...], unit, inverse)
            ).astype(jnp.bfloat16)

    def fixed(*shape):
        return pl.BlockSpec(shape, lambda i: (0,) * len(shape))

    columns = pl.BlockSpec((features, wide), lambda i: (0, i))
    return pl.pallas_call(
        kernel,
        grid=(steps,),
        in_specs=[
            pl.BlockSpec((per_step, row_count, width), lambda i: (i, 0, 0)),
            pl.BlockSpec((1, row_count, features), lambda i: (micro, 0, 0)),
            pl.BlockSpec((row_count, features), lambda i: (micro, 0)),
            fixed(1, features),
            columns,
            columns,
            columns,
        ]
        + [pl.BlockSpec(memory_space=pl.ANY)] * (before is not None),
        out_specs=pl.BlockSpec((1, row_count, features), lambda i: (micro, 0, 0)),
        out_shape=jax.ShapeDtypeStruct(patches.shape, jnp.bfloat16),
        input_output_aliases={7: 0} if before is not None else {},
        scratch_shapes=[
            pltpu.VMEM((row_count, features), jnp.float32),
            pltpu.VMEM((3, row_count, wide), jnp.bfloat16),
        ],
        compiler_params=_params(60),
        cost_estimate=_cost(cost),
        name="finish",
    )(received, patches, mixed_grad, gain, w_query, w_key, w_value, *([before] if before is not None else []))


def grad_heads_call(place, units, cuts, places, made, gain, bias, sums, w_query, w_key, w_value, shares):
    micro_count = len(made)
    blocks, tokens, width = made[0].shape
    slot = width // 3
    features = gain.shape[1]
    group = features // (blocks * shares)
    full = width + 128
    kept = blocks * (shares // 2) * group

    def kernel(place_ref, *refs):
        unit_refs, refs = refs[: len(units)], refs[len(units) :]
        made_refs, refs = refs[:micro_count], refs[micro_count:]
        gain_ref, bias_ref, sums_ref, wq_ref, wk_ref, wv_ref, send_ref, keep_ref, spread, ordered = refs
        product = jnp.zeros((features, width), jnp.float32)
        column_sum = jnp.zeros((1, width), jnp.float32)
        for cut, (first, last) in enumerate(cuts):
            at = 0
            for relative in places:
                for micro, made_ref in enumerate(made_refs):
                    low, high = max(first - micro * tokens, 0), min(last - micro * tokens, tokens)
                    if low < high:
                        ordered[at : at + high - low, :] = made_ref[place_ref[0] ^ relative, low:high]
                        at += high - low
            half = at // 2
            for side in range(2):
                rows = ordered[side * half : (side + 1) * half, :]
                product = product + contract_rows(unit_refs[2 * cut + side][...], rows)
                column_sum = column_sum + jnp.sum(rows.astype(jnp.float32), axis=0, keepdims=True)
        vectors = jnp.concatenate(
            [gain_ref[...], bias_ref[...], sums_ref[...], jnp.zeros((124, features), jnp.float32)], axis=0
        ).T
        total = vectors[:, 0:1] * product + vectors[:, 1:2] * column_sum
        weights = jnp.concatenate([wq_ref[...], wk_ref[...], wv_ref[...]], axis=1).astype(jnp.float32)
        gain_sum = jnp.sum(weights * product, axis=1, keepdims=True)
        bias_sum = jnp.sum(weights * column_sum, axis=1, keepdims=True)
        lanes = lax.broadcasted_iota(jnp.int32, (1, 128), 1)
        norms = jnp.where(
            lanes == 0, gain_sum, jnp.where(lanes == 1, bias_sum, jnp.where(lanes < 4, vectors, 0.0))
        )
        spread[:, :, :, 0:width] = total.reshape(blocks, shares, group, width)
        spread[:, :, :, width:] = norms.reshape(blocks, shares, group, 128)
        core = place_ref[1] % 2
        for which, out_ref in enumerate((send_ref, keep_ref)):
            for share in range(0, shares, 2):
                for block in range(blocks):
                    out_ref[share // 2, block] = spread[block, share + (core if which else 1 - core)].astype(out_ref.dtype)

    def fixed(*shape):
        return pl.BlockSpec(shape, lambda i, place: (0,) * len(shape))

    columns = pl.BlockSpec((features, slot), lambda i, place: (0, place[0]))
    out = (shares // 2, blocks, group, full)
    return pl.pallas_call(
        kernel,
        grid_spec=pltpu.PrefetchScalarGridSpec(
            num_scalar_prefetch=1,
            grid=(1,),
            in_specs=[fixed(*part.shape) for part in (*units, *made)]
            + [fixed(1, features), fixed(1, features), fixed(2, features), columns, columns, columns],
            out_specs=[fixed(*out), fixed(*out)],
            scratch_shapes=[
                pltpu.VMEM((blocks, shares, group, full), jnp.float32),
                pltpu.VMEM((blocks * max(last - first for first, last in cuts), width), jnp.bfloat16),
            ],
        ),
        out_shape=[jax.ShapeDtypeStruct(out, jnp.bfloat16), jax.ShapeDtypeStruct(out, jnp.float32)],
        compiler_params=_params(60),
        cost_estimate=_cost(20),
        name="grad_heads",
    )(place, *units, *made, gain, bias, sums, w_query, w_key, w_value)


def assemble_call(place, parts, down_keep, down_received, heads, down_steps, blocks, owned):
    shares = len(parts)
    rows, width = parts[0].shape
    part = width - blocks * owned
    slot = (heads.shape[2] - 128) // 3

    def kernel(place_ref, *refs):
        part_refs, (keep_ref, got_ref, heads_ref, up_ref, out_ref, down_ref, *refs) = refs[:shares], refs[shares:]
        weight_refs, norm_refs = refs[:3], refs[3:]
        for other, part_ref in enumerate(part_refs):
            share = place_ref[2] ^ other
            for at, block in enumerate(_ordered([_owner_stride(*step, shares) for step in down_steps])):
                to = pl.multiple_of((block + share % 2 + share // 2 * shares) * owned, 128)
                up_ref[:, pl.ds(to, owned)] = part_ref[:, at * owned : (at + 1) * owned].astype(jnp.float32)
            out_ref[:, pl.ds(pl.multiple_of(share * part, 128), part)] = part_ref[:, blocks * owned :].astype(jnp.float32)
        down_ref[...] = keep_ref[...] + got_ref[...].astype(jnp.float32)
        for at, ref in enumerate(weight_refs):
            for block in range(blocks):
                ref[:, block * slot : (block + 1) * slot] = heads_ref[
                    block, :, at * slot : (at + 1) * slot
                ].astype(jnp.float32)
        sums = jnp.zeros((rows, 128), jnp.float32)
        for block in range(blocks):
            sums = sums + heads_ref[block, :, 3 * slot :].astype(jnp.float32)
        turned = jnp.concatenate([sums, jnp.zeros((128 - rows, 128), jnp.float32)], axis=0).T
        for at, ref in enumerate(norm_refs):
            ref[...] = turned[at : at + 1, 0:rows]

    shapes = [(rows, blocks * shares * owned), (rows, shares * part), down_keep.shape]
    shapes += [(rows, blocks * slot)] * 3 + [(1, rows)] * 4
    return pl.pallas_call(
        kernel,
        grid_spec=pltpu.PrefetchScalarGridSpec(
            num_scalar_prefetch=1,
            grid=(1,),
            in_specs=[_fixed(*array.shape) for array in (*parts, down_keep, down_received, heads)],
            out_specs=[_fixed(*shape) for shape in shapes],
        ),
        out_shape=[jax.ShapeDtypeStruct(shape, jnp.float32) for shape in shapes],
        compiler_params=_params(16),
        cost_estimate=_cost(0),
        name="assemble",
    )(place, *parts, down_keep, down_received, heads)


def _bits(count):
    return [1 << place for place in range(count.bit_length() - 1)]


def _ordered(bits):
    places = [0]
    for bit in bits:
        places = [at + step for at in places for step in (0, bit)]
    return places


def _ordered_low(bits):
    places = [0]
    for bit in bits:
        places = places + [at + bit for at in places]
    return places


def _paired(values, axis, bit):
    count = lax.axis_size(axis)
    return lax.ppermute(values, axis, [(i, i ^ bit) for i in range(count)])


def _bit_of(axis, bit):
    return (lax.axis_index(axis) // bit) % 2


def _mesh_bit(place, step):
    axis, bit = step
    return place[("blk", "mb").index(axis)] // bit % 2


def _owner_stride(axis, bit, shares):
    return bit * shares if axis == "blk" else bit


def _share_places(shares):
    return [0, 1, shares, shares + 1]


def _place_at(bits, step):
    places = _ordered(bits)
    at = jnp.int32(places[0])
    for other in range(1, len(places)):
        at = jnp.where(step == other, places[other], at)
    return at


def grad_middle_call(place, boths, out_grads, lows, w_up, w_down, down_steps, up_steps):
    shares = len(boths)
    _, row_count, features = boths[0].shape
    all_rows = shares * row_count
    hidden = w_up.shape[1]
    blocks = 1 << len(up_steps)
    owned, each = hidden // (blocks * shares), features // (blocks * shares)
    down_places = [_owner_stride(*step, shares) for step in down_steps]
    up_places = [_owner_stride(*step, shares) for step in up_steps]
    share_places = _share_places(shares)
    part = lows[0].shape[1]
    half = blocks // 2
    pair = min(2, half)
    half_steps = half // pair

    def kernel(place_ref, *refs):
        groups, refs = [refs[at * shares : (at + 1) * shares] for at in range(3)], refs[3 * shares :]
        up_refs, down_refs, refs = refs[:pair], refs[pair : 2 * pair], refs[2 * pair :]
        down_send, down_keep, up_send, up_keep, norm_turned, grad_all, active_all, upper_all, up_all = refs
        step = pl.program_id(0)
        mine = _mesh_bit(place_ref, up_steps[0])

        def spread():
            for at, block in enumerate(_ordered(up_places[1:])):
                for share, other in enumerate(share_places):
                    rows = slice((at * shares + share) * each, (at * shares + share + 1) * each)
                    up_send[rows, :] = up_all[block + other + up_places[0] * (1 - mine)].astype(jnp.bfloat16)
                    up_keep[rows, :] = up_all[block + other + up_places[0] * mine]

        @pl.when(step == 0)
        def _():
            for at in range(shares):
                rows = slice(at * row_count, (at + 1) * row_count)
                norm_turned[:, rows] = groups[0][at][0].T
                grad_all[rows, :] = groups[1][at][...]

        @pl.when(step < 2 * half_steps)
        def _():
            up_columns = jnp.concatenate([ref[...] for ref in up_refs], axis=1)
            down_rows = jnp.concatenate([ref[...] for ref in down_refs], axis=0)
            for at in range(shares):
                rows = slice(at * row_count, (at + 1) * row_count)
                active_all[rows, :], upper_all[rows, :] = _hidden_parts(
                    groups[0][at][0], groups[1][at][...], up_columns, down_rows
                )
            down_made = contract_rows(active_all[...], grad_all[...])

            @pl.when(step < half_steps)
            def _():
                down_send[...] = down_made.astype(jnp.bfloat16)

            @pl.when(step >= half_steps)
            def _():
                down_keep[...] = down_made

            up_all[...] = matmul(norm_turned[...], upper_all[...]).reshape(blocks * shares, each, pair * owned)
            spread()

        @pl.when(step == 2 * half_steps)
        def _():
            made = jnp.zeros((features, part), jnp.float32)
            for both_ref, low_ref in zip(groups[0], groups[2]):
                made = made + contract_rows(both_ref[1], low_ref[...])
            up_all[...] = made.reshape(blocks * shares, each, part)
            spread()

    def first_bit(i, place):
        return (_mesh_bit(place, down_steps[0]) + 1 + jnp.minimum(i, 2 * half_steps - 1) // half_steps) % 2

    def unit_block(i, place, at):
        inner = _place_at(down_places[1:], jnp.minimum(i, 2 * half_steps - 1) % half_steps * pair + at)
        return inner + down_places[0] * first_bit(i, place) + place[0] % 2 * shares + place[1] % 2

    ups = [
        pl.BlockSpec((features, owned), lambda i, place, at=at: (0, unit_block(i, place, at))) for at in range(pair)
    ]
    downs = [
        pl.BlockSpec((owned, features), lambda i, place, at=at: (unit_block(i, place, at), 0)) for at in range(pair)
    ]
    def up_block(i, place):
        return (0, jnp.where(i == 2 * half_steps, i, first_bit(i, place) * half_steps + i % half_steps))

    up_out = pl.BlockSpec((features // 2, pair * owned), up_block)
    shapes = [(half * owned, features), (features // 2, blocks * owned + part)]
    return pl.pallas_call(
        kernel,
        grid_spec=pltpu.PrefetchScalarGridSpec(
            num_scalar_prefetch=1,
            grid=(2 * half_steps + 1,),
            in_specs=[_fixed(2, row_count, features)] * shares
            + [_fixed(row_count, features)] * shares
            + [_fixed(row_count, part)] * shares
            + ups
            + downs,
            out_specs=[
                pl.BlockSpec((pair * owned, features), lambda i, place: (jnp.minimum(i, half_steps - 1), 0)),
                pl.BlockSpec((pair * owned, features), lambda i, place: (jnp.clip(i - half_steps, 0, half_steps - 1), 0)),
                up_out,
                up_out,
            ],
            scratch_shapes=[
                pltpu.VMEM((features, all_rows), jnp.bfloat16),
                pltpu.VMEM((all_rows, features), jnp.bfloat16),
                pltpu.VMEM((all_rows, pair * owned), jnp.bfloat16),
                pltpu.VMEM((all_rows, pair * owned), jnp.bfloat16),
                pltpu.VMEM((blocks * shares, each, pair * owned), jnp.float32),
            ],
        ),
        out_shape=[jax.ShapeDtypeStruct(shape, dtype) for shape in shapes for dtype in (jnp.bfloat16, jnp.float32)],
        compiler_params=_params(52),
        cost_estimate=_cost(20),
        name="grad_middle",
    )(place, *boths, *out_grads, *lows, *([w_up] * pair), *([w_down] * pair))


def halve_call(place, keep, received, step, cost):
    count, rows, columns = keep.shape
    half = count // 2

    def kernel(place_ref, keep_theirs, keep_mine, got_theirs, got_mine, theirs_ref, mine_ref):
        theirs_ref[...] = (keep_theirs[...] + got_theirs[...].astype(jnp.float32)).astype(jnp.bfloat16)
        mine_ref[...] = keep_mine[...] + got_mine[...].astype(jnp.float32)

    def block(which):
        return pl.BlockSpec(
            (1, rows, columns), lambda i, place: (i + half * ((_mesh_bit(place, step) + which) % 2), 0, 0)
        )

    out = pl.BlockSpec((1, rows, columns), lambda i, place: (i, 0, 0))
    return pl.pallas_call(
        kernel,
        grid_spec=pltpu.PrefetchScalarGridSpec(
            num_scalar_prefetch=1,
            grid=(half,),
            in_specs=[block(1), block(0), block(1), block(0)],
            out_specs=[out, out],
        ),
        out_shape=[
            jax.ShapeDtypeStruct((half, rows, columns), jnp.bfloat16),
            jax.ShapeDtypeStruct((half, rows, columns), jnp.float32),
        ],
        compiler_params=_params(16),
        cost_estimate=_cost(cost),
        name="halve",
    )(place, keep, keep, received, received)


def heads_total_call(keep, received):
    def kernel(keep_ref, got_ref, out_ref):
        out_ref[...] = (keep_ref[...] + got_ref[...].astype(jnp.float32)).astype(jnp.bfloat16)

    return pl.pallas_call(
        kernel,
        out_shape=jax.ShapeDtypeStruct(keep.shape, jnp.bfloat16),
        compiler_params=_params(8),
        cost_estimate=_cost(20),
        name="heads_total",
    )(keep, received)


def close_call(place, keep, received, shares):
    rows, width = keep.shape
    each = rows // shares

    def kernel(place_ref, keep_ref, got_ref, *refs):
        out_refs, total = refs[:-1], refs[-1]
        total[...] = (keep_ref[...] + got_ref[...].astype(jnp.float32)).reshape(shares, each, width)
        for share, out_ref in enumerate(out_refs):
            out_ref[...] = total[place_ref[2] ^ share].astype(jnp.bfloat16)

    return pl.pallas_call(
        kernel,
        grid_spec=pltpu.PrefetchScalarGridSpec(
            num_scalar_prefetch=1,
            grid=(1,),
            in_specs=[_fixed(rows, width)] * 2,
            out_specs=[_fixed(each, width)] * shares,
            scratch_shapes=[pltpu.VMEM((shares, each, width), jnp.float32)],
        ),
        out_shape=[jax.ShapeDtypeStruct((each, width), jnp.bfloat16)] * shares,
        compiler_params=_params(8),
        cost_estimate=_cost(6),
        name="close",
    )(place, keep, received)


def fast_body(
    patches, seg_lengths, w_query, w_key, w_value, w_out, w_up, w_down,
    norm1_gain, norm1_bias, norm2_gain, norm2_bias, out_grad,
):
    micro_count, tokens, features = patches.shape
    hidden = w_up.shape[1]
    row_count = micro_count * tokens
    blocks, shares = lax.axis_size("blk"), lax.axis_size("mb")
    head_dim = features // H
    slot = features // blocks
    rows = patches.reshape(row_count, features)
    dout = out_grad.reshape(row_count, features)
    gain_one, bias_one, gain_two, bias_two = (
        value.reshape(1, features) for value in (norm1_gain, norm1_bias, norm2_gain, norm2_bias)
    )

    def swap(values):
        return lax.all_to_all(values, "blk", split_axis=0, concat_axis=0, tiled=True)

    def by_micro(values):
        return values.reshape(blocks, micro_count, tokens, values.shape[-1])

    at_blk, at_mb = lax.axis_index("blk"), lax.axis_index("mb")
    place = jnp.stack([at_blk, at_mb, at_mb % 2 + at_blk % 2 * 2]).astype(jnp.int32)
    blk_bits = _bits(blocks)
    down_steps = [("mb", 2), *(("blk", bit) for bit in blk_bits[1:])]
    up_steps = [down_steps[1], down_steps[0], *down_steps[2:]]
    each, owned, block_rows = features // (blocks * shares), hidden // (blocks * shares), features // blocks
    tie = lax.optimization_barrier

    def grown(values, bit):
        return jnp.concatenate([values, _paired(values, "blk", bit)], axis=0)

    def to_share(values, other):
        if other == 1:
            return _paired(values, "mb", 1)
        if other == 2:
            return _paired(values, "blk", 1)
        return lax.ppermute(values, ("blk", "mb"), [(i, i ^ (shares + 1)) for i in range(blocks * shares)])

    def shared(values):
        over = to_share(values, 2)
        return [values, to_share(values, 1), over, to_share(over, 1)]

    first_rows = max(16, tokens * 3 // 4 // 16 * 16)
    cuts = [(0, first_rows), (first_rows, row_count)]
    send, units_first, units_last = project_call(
        rows, gain_one, bias_one, w_query, w_key, w_value, blocks, cuts
    )
    received = by_micro(swap(send))
    dout_parts = [out_grad[micro] for micro in range(micro_count)]
    dout_over = [to_share(part, 2) for part in dout_parts]
    received, dout_over[0] = tie((received, dout_over[0]))
    units_first, received = tie((units_first, received))
    first_over = _paired(units_first, "blk", blk_bits[-1])
    own_attended, exact, logs = attend_call(received, seg_lengths, head_dim)
    attended, first_over, dout_over = tie((own_attended.reshape(blocks, row_count, slot), first_over, dout_over))
    units_first = jnp.concatenate([units_first, first_over], axis=0)
    dout_over = jnp.concatenate(dout_over, axis=0)
    attended, units_first, units_last, *douts = tie(
        (swap(attended), units_first, units_last, dout, to_share(dout, 1), dout_over, to_share(dout_over, 1))
    )
    for bit in blk_bits[-2:0:-1]:
        units_first = grown(units_first, bit)
    units_last = grown(units_last, blk_bits[-1])
    places = _ordered_low([*blk_bits[:0:-1], blk_bits[0]])

    mixed, both = mix_call(attended, rows, gain_two, bias_two, w_out)
    both_peer, both_over = to_share(both, 1), to_share(both, 2)
    layer_out, mixed_grad, back, sums_two, *lows = middle_call(
        place, both, mixed, dout, gain_two, w_out, w_up, w_down, blocks, shares
    )
    back, lows, units_first, units_last, both_peer, both_over = tie(
        (back, lows, units_first, units_last, both_peer, both_over)
    )
    boths = [both, both_peer, both_over, to_share(both_over, 1)]
    units_first_peer = _paired(units_first, "blk", blk_bits[0])
    for bit in blk_bits[-2:0:-1]:
        units_last = grown(units_last, bit)
    grads = by_micro(swap(back))
    lows = [lows[0]] + [to_share(lows[share], share) for share in range(1, shares)]
    down_theirs, down_keep, up_theirs, up_keep = grad_middle_call(
        place, boths, douts, lows, w_up, w_down, down_steps, up_steps
    )
    down_theirs, down_keep = (value.reshape(-1, owned, features) for value in (down_theirs, down_keep))
    up_theirs, up_keep = (value.reshape(-1, block_rows, value.shape[-1]) for value in (up_theirs, up_keep))
    down_received, up_received = _paired(down_theirs, *down_steps[0]), _paired(up_theirs, *up_steps[0])
    grads, down_keep, units_first_peer, units_last = tie((grads, down_keep, units_first_peer, units_last))
    units_last_peer = _paired(units_last, "blk", blk_bits[0])
    made = []
    for micro in range(micro_count):
        cost = 3 if micro == micro_count - 1 else 0
        made.append(attend_back_call(received, grads, exact, logs, seg_lengths, micro, cost, head_dim))
        grads, made[micro] = tie((grads, made[micro]))
    returned = [swap(made[0])]

    def then(done, *values):
        return tie((done, values))[1]

    returned += [swap(tie((values, returned[0]))[0]) for values in made[1:]]
    made = tie(made)
    up_theirs, up_keep = halve_call(place, *then(made[-1], up_keep, up_received), up_steps[1], 0)
    up_received = _paired(up_theirs, *up_steps[1])
    down_keep, down_received, units_last_peer = then(up_keep, down_keep, down_received, units_last_peer)
    down_theirs, down_keep = halve_call(place, down_keep, down_received, down_steps[1], 5)
    down_received = _paired(down_theirs, *down_steps[1])
    made = then(down_keep, *made)
    heads_send, heads_keep = grad_heads_call(
        place, (units_first, units_first_peer, units_last, units_last_peer), cuts, places,
        made, gain_one, bias_one, sums_two, w_query, w_key, w_value, shares,
    )
    pair = (shares // 2, -1, heads_keep.shape[-1])
    heads_received = _paired(heads_send, "mb", 1).reshape(pair)
    down_keep, down_received = then(heads_keep, down_keep, down_received)
    for step in down_steps[2:-1]:
        down_theirs, down_keep = halve_call(place, down_keep, down_received, step, 0)
        down_received = _paired(down_theirs, *step)
    down_theirs, down_keep = halve_call(place, down_keep, down_received, down_steps[-1], 0)
    up_keep, up_received = then(down_keep, up_keep, up_received)
    for step in up_steps[2:]:
        up_theirs, up_keep = halve_call(place, up_keep, up_received, step, 3)
        up_received = _paired(up_theirs, *step)
    heads_theirs, heads_keep = halve_call(
        place, *then(up_keep, heads_keep.reshape(pair), heads_received), ("mb", 2), 0
    )
    heads_theirs, down_theirs = tie((heads_theirs, down_theirs))
    heads_received = _paired(heads_theirs, "mb", 2)
    down_received = _paired(down_theirs, *down_steps[-1])
    finish = (patches, mixed_grad, gain_one, w_query, w_key, w_value)
    patches_grad = None
    for micro in range(micro_count - 1):
        first, heads_keep, heads_received = then(down_keep, returned[micro], heads_keep, heads_received)
        patches_grad = finish_call(first, *finish, micro, patches_grad, 0)
        heads_keep, heads_received = then(patches_grad, heads_keep, heads_received)
    returned[-1], heads_keep, heads_received = tie((returned[-1], heads_keep, heads_received))
    heads_total = heads_total_call(heads_keep[0], heads_received[0]).reshape(blocks, each, heads_keep.shape[-1])
    heads_parts = swap(heads_total)
    up_keep, up_received = then(heads_total, up_keep, up_received)
    parts = close_call(place, up_keep[0], up_received[0], shares)
    last = then(parts[0], returned[-1])[0]
    parts = [parts[0]] + [to_share(parts[share], share) for share in range(1, shares)]
    patches_grad = finish_call(last, *finish, micro_count - 1, patches_grad, 20)
    *parts, down_keep, down_received, heads_parts = then(
        patches_grad, *parts, down_keep[0], down_received[0], heads_parts
    )
    up_total, out_total, down_total, query_total, key_total, value_total, *sums = assemble_call(
        place, parts, down_keep, down_received, heads_parts, down_steps, blocks, owned
    )
    return (
        layer_out.reshape(patches.shape),
        patches_grad.reshape(patches.shape),
        query_total,
        key_total,
        value_total,
        out_total,
        up_total,
        down_total,
        *(value.reshape(each) for value in sums),
    )


def solution(mesh):
    in_specs = (
        P("mb", "blk", None),
        P("mb", None),
        P(),
        P(),
        P(),
        P(),
        P(),
        P(),
        P(),
        P(),
        P(),
        P(),
        P("mb", "blk", None),
    )
    out_specs = (
        P("mb", "blk", None),
        P("mb", "blk", None),
        P(("blk", "mb"), None),
        P(("blk", "mb"), None),
        P(("blk", "mb"), None),
        P(("blk", "mb"), None),
        P(("blk", "mb"), None),
        P(("blk", "mb"), None),
        P(("blk", "mb")),
        P(("blk", "mb")),
        P(("blk", "mb")),
        P(("blk", "mb")),
    )
    blocks, shares = mesh.shape["blk"], mesh.shape["mb"]
    paired = blocks >= 4 and blocks & (blocks - 1) == 0 and shares == 4
    chosen_body = fast_body if paired and H % blocks == 0 else body
    return jax.shard_map(chosen_body, mesh=mesh, in_specs=in_specs, out_specs=out_specs, check_vma=False)
```
